32 devices in a mesh: blk: 8 (over z, x), group: 4 (over y, core).
Axes of the slice: x: 2, y: 2, z: 4, core: 2. Of those that a mesh axis runs over, the one named last changes fastest.
Arguments:
- queries: bfloat16 [8, 2048, 2560], P('blk', 'group'), may hold values from -6 to 6
- new_keys: bfloat16 [8, 2048, 256], P('blk', 'group'), may hold values from -15 to 15
- new_values: bfloat16 [8, 2048, 256], P('blk', 'group'), may hold values from -4 to 4
- key_cache: bfloat16 [320, 128, 256], P('blk', 'group'), may hold values from -4 to 4
- value_cache: bfloat16 [320, 128, 256], P('blk', 'group'), may hold values from -4 to 4
- out_weight: bfloat16 [2560, 2560], replicated, may hold values from -0.375 to 0.375
- lengths: int32 [8], replicated, may hold values from 0 to 30720, as said below
- page_table: int32 [8, 32], replicated, may hold values from 0 to 319, as said below
Outputs:
- hidden_states: bfloat16 [8, 2048, 2560], P('blk', 'group')
- key_cache_out: bfloat16 [320, 128, 256], P('blk', 'group')
- value_cache_out: bfloat16 [320, 128, 256], P('blk', 'group')
The draws below stay inside these ranges and needn't reach their ends.
Inputs may be any that keep to these rules, and one draw needn't show every extreme that they name: `lengths`: multiples of 2048; some request has length 0 and some has 30720. `page_table`: all entries differ; page p lies on blk index p // 40; columns below 16 hold the request's last 16 pages before its group in order (pages that hold no part of a request where its length is short), the others the pages of its group in order; of one request's first 16 entries at most 2 lie on one blk index, of its last 16 at most 2, and both bounds are reached for every request.
All inputs are finite; a program needn't handle non-finite values.
Results may differ from the reference program's by a relative error of at most 0.009.
Values may be sent and summed in bfloat16 or wider, within the bound.
No kernel may reach another device: no remote copies, remote signals or barrier semaphores. Data moves between devices by JAX's collectives and lax.ppermute only.
A program may use at most 256 MiB of HBM per device.

```python
import jax
import jax.numpy as jnp
from jax import lax

D = 2560
HEADS = 10
HD = 256
PAGE = 128
OLD_PAGES = 16
MAX_GROUPS = 16
GROUP = 2048
REQUESTS = 8
WINDOW = 2048
NEW_PAGES = 16
SLOTS = 32
PAGES_DEV = 40
PAGES = 320


def draw_lengths(key, part):
    counts = jax.random.randint(jax.random.fold_in(key, 11), (REQUESTS,), 0, MAX_GROUPS)
    shuffled = jax.random.permutation(jax.random.fold_in(key, 12), REQUESTS)
    counts = counts.at[shuffled[0]].set(0).at[shuffled[1]].set(MAX_GROUPS - 1)
    return (counts * GROUP).astype(jnp.int32)


def draw_page_table(key, part):
    spread = jax.random.permutation(jax.random.fold_in(key, 21), REQUESTS)
    offset_perm = jax.random.permutation(jax.random.fold_in(key, 22), REQUESTS)
    column = jnp.arange(SLOTS, dtype=jnp.int32)
    owner_of = (spread[column % REQUESTS][None, :] + offset_perm[:, None]) % REQUESTS
    subkeys = jax.random.split(jax.random.fold_in(key, 23), REQUESTS)
    local_perm = jax.vmap(lambda subkey: jax.random.permutation(subkey, PAGES_DEV))(subkeys)
    return (owner_of * PAGES_DEV + local_perm[owner_of, column[None, :]]).astype(jnp.int32)


def draw_queries(key, part):
    array_shape = (REQUESTS, GROUP, HEADS * HD)
    result = 1.5 * jnp.clip(jax.random.normal(jax.random.fold_in(key, 1), array_shape, jnp.float32), -4.0, 4.0)
    return result.astype(jnp.bfloat16)


def draw_new_keys(key, part):
    array_shape = (REQUESTS, GROUP, HD)
    result = jnp.clip(jax.random.normal(jax.random.fold_in(key, 3), array_shape, jnp.float32), -4.0, 4.0)
    return result.astype(jnp.bfloat16)


def level_of(key, shape, shards, smallest, top_value):
    def one(axis_at, parts):
        steps = jax.random.uniform(jax.random.fold_in(jax.random.fold_in(key, 6), axis_at), (parts,), jnp.float32, smallest / len(shards), top_value / len(shards))
        return jnp.repeat(jnp.exp(steps), shape[axis_at] // parts).reshape((-1,) + (1,) * (len(shape) - axis_at - 1))

    level = one(*shards[0])
    for cut in shards[1:]:
        level = level * one(*cut)
    return level


def gaussian(own_key, extent, width, reach, cuts=(), kind=jnp.bfloat16):
    loudness = level_of(own_key, extent, cuts, -0.22, 0.18) if cuts else 1.0
    values = jax.random.normal(own_key, extent, jnp.float32) * width * loudness
    return jnp.minimum(jnp.maximum(values, -reach), reach).astype(kind)


def setup_inputs(seed: int = 0) -> dict:
    arg_keys = jax.random.split(jax.random.key(seed), 9)
    queries = draw_queries(jax.random.fold_in(arg_keys[8], 71), 0)
    new_keys = draw_new_keys(jax.random.fold_in(arg_keys[8], 71), 0)
    new_values = gaussian(arg_keys[2], (REQUESTS, GROUP, HD), 1.0, 4.0, ((0, 8), (1, 4)))
    key_cache = gaussian(arg_keys[3], (PAGES, PAGE, HD), 1.0, 4.0, ((0, 8), (1, 4)))
    value_cache = gaussian(arg_keys[4], (PAGES, PAGE, HD), 1.0, 4.0, ((0, 8), (1, 4)))
    out_weight = gaussian(arg_keys[5], (HEADS * HD, D), HD ** -0.5, 0.375)
    lengths = draw_lengths(jax.random.fold_in(arg_keys[8], 71), 0)
    page_table = draw_page_table(jax.random.fold_in(arg_keys[8], 71), 0)
    return dict(queries=queries, new_keys=new_keys, new_values=new_values, key_cache=key_cache, value_cache=value_cache, out_weight=out_weight, lengths=lengths, page_table=page_table)


masked_score = -1e30


def rotate(values, positions):
    quarter = values.shape[-1] // 4
    freq_table = 10000.0 ** (-jnp.arange(quarter, dtype=jnp.float32) / quarter)
    angles = positions.astype(jnp.float32)[..., None] * freq_table
    cosine = jnp.cos(angles)
    sine_part = jnp.sin(angles)
    leading = values[..., :quarter]
    trailing = values[..., quarter:2 * quarter]
    return jnp.concatenate([leading * cosine - trailing * sine_part, trailing * cosine + leading * sine_part, values[..., 2 * quarter:]], axis=-1)


def reference(queries, new_keys, new_values, key_cache, value_cache, out_weight, lengths, page_table):
    offsets = jnp.arange(GROUP, dtype=jnp.int32)
    positions = lengths[:, None] + offsets[None, :]
    roped_keys = rotate(new_keys.astype(jnp.float32), positions).astype(jnp.bfloat16)
    roped_queries = rotate(queries.astype(jnp.float32).reshape(REQUESTS, GROUP, HEADS, HD), positions[:, :, None]).astype(jnp.bfloat16)
    fresh_slots = page_table[:, OLD_PAGES:].reshape(-1)
    key_cache_out = key_cache.at[fresh_slots].set(roped_keys.reshape(REQUESTS * NEW_PAGES, PAGE, HD))
    value_cache_out = value_cache.at[fresh_slots].set(new_values.reshape(REQUESTS * NEW_PAGES, PAGE, HD))
    window_index = jnp.arange(WINDOW, dtype=jnp.int32)
    score_scale = HD ** -0.5

    def one_request(inputs):
        query_block, fresh_keys, fresh_values, length, table_row = inputs
        old_keys = key_cache[table_row[:OLD_PAGES]].reshape(WINDOW, HD)
        old_values = value_cache[table_row[:OLD_PAGES]].reshape(WINDOW, HD)
        key_rows = jnp.concatenate([old_keys, fresh_keys], axis=0).astype(jnp.float32)
        value_rows = jnp.concatenate([old_values, fresh_values], axis=0).astype(jnp.float32)
        old_visible = (window_index[None, :] > offsets[:, None]) & ((length - WINDOW + window_index[None, :]) >= 0)
        new_visible = offsets[None, :] <= offsets[:, None]
        visible = jnp.concatenate([old_visible, new_visible], axis=1)
        scores = jnp.einsum("thd,kd->thk", query_block.astype(jnp.float32), key_rows) * score_scale
        scores = jnp.where(visible[:, None, :], scores, masked_score)
        row_max = jnp.max(scores, axis=2, keepdims=True)
        weights = jnp.where(visible[:, None, :], jnp.exp(scores - row_max), 0.0)
        row_total = jnp.sum(weights, axis=2, keepdims=True)
        rounded = lax.optimization_barrier(weights.astype(jnp.bfloat16))
        attended = jnp.einsum("thk,kd->thd", rounded.astype(jnp.float32), value_rows) / row_total
        attended = attended.astype(jnp.bfloat16).reshape(GROUP, HEADS * HD)
        return jnp.dot(attended, out_weight, preferred_element_type=jnp.float32).astype(jnp.bfloat16)

    hidden_states = lax.map(one_request, (roped_queries, roped_keys, new_values, lengths, page_table))
    return (hidden_states, key_cache_out, value_cache_out)
```

```python
import jax
import jax.numpy as jnp
from jax import lax
from jax.experimental import pallas as pl
from jax.experimental.pallas import tpu as pltpu
from jax.sharding import PartitionSpec as P

masked_score = -1e30
half = 256
vmem_limit = 36 * 1024 * 1024
any_spec = pl.BlockSpec(memory_space=pl.ANY)
smem_spec = pl.BlockSpec(memory_space=pltpu.SMEM)
vmem_spec = pl.BlockSpec(memory_space=pltpu.VMEM)


def params():
    return pltpu.CompilerParams(vmem_limit_bytes=vmem_limit)


def turn(values, cosine, sine):
    front = values[:, :128].astype(jnp.float32)
    turned = front * cosine + pltpu.roll(front, 64, 1) * sine
    return turned


def pick_old_kernel(slots_ref, key_ref, value_ref, out_ref, sem):
    requests, cap = slots_ref.shape
    for r in range(requests):
        for c in range(cap):
            page = slots_ref[r, c]
            pltpu.make_async_copy(key_ref.at[page], out_ref.at[r, c, 0], sem).start()
            pltpu.make_async_copy(value_ref.at[page], out_ref.at[r, c, 1], sem).start()
    pltpu.make_async_copy(out_ref, out_ref, sem).wait()


def pick_old(slots, key_cache, value_cache):
    requests, cap = slots.shape
    return pl.pallas_call(
        pick_old_kernel,
        out_shape=jax.ShapeDtypeStruct((requests, cap, 2) + key_cache.shape[1:], jnp.bfloat16),
        in_specs=[smem_spec, any_spec, any_spec],
        out_specs=any_spec,
        scratch_shapes=[pltpu.SemaphoreType.DMA],
        compiler_params=params(),
        name="pick_old",
    )(slots, key_cache, value_cache)


def fresh_kernel(keys_ref, values_ref, cos_ref, sin_ref, out_ref):
    keys = keys_ref[...]
    out_ref[0, :, :128] = turn(keys, cos_ref[...], sin_ref[...]).astype(jnp.bfloat16)
    out_ref[0, :, 128:] = keys[:, 128:]
    out_ref[1] = values_ref[...]


def make_fresh(keys, values, cosine, sine):
    return pl.pallas_call(
        fresh_kernel,
        out_shape=jax.ShapeDtypeStruct((2,) + keys.shape, jnp.bfloat16),
        in_specs=[vmem_spec] * 4,
        out_specs=vmem_spec,
        compiler_params=params(),
        name="fresh",
    )(keys, values, cosine, sine)


def pick_new_kernel(info_ref, slots_ref, own_ref, core_ref, far_ref, far_core_ref, out_ref, sem):
    owners, cap = slots_ref.shape
    group_index = info_ref[0]
    rows = out_ref.shape[3]
    page_len = rows * 4
    block_pages = own_ref.shape[1] // page_len
    for o in range(owners):
        for c in range(cap):
            page = slots_ref[o, c]
            source = (page // block_pages) ^ group_index
            start = pl.multiple_of((page % block_pages) * page_len + rows * group_index, 32)
            for number, ref in enumerate((own_ref, core_ref, far_ref, far_core_ref)):

                @pl.when(source == number)
                def _():
                    pltpu.make_async_copy(
                        ref.at[:, pl.ds(start, rows), :], out_ref.at[o, c], sem
                    ).start()

    pltpu.make_async_copy(out_ref, out_ref, sem).wait()


def pick_new(info, slots, sources, rows):
    owners, cap = slots.shape
    return pl.pallas_call(
        pick_new_kernel,
        out_shape=jax.ShapeDtypeStruct(
            (owners, cap, 2, rows, sources[0].shape[2]), jnp.bfloat16
        ),
        in_specs=[smem_spec, smem_spec] + [any_spec] * 4,
        out_specs=any_spec,
        scratch_shapes=[pltpu.SemaphoreType.DMA],
        compiler_params=params(),
        name="pick_new",
    )(info, slots, *sources)


def lane_sums(weights):
    total = weights[:, :128]
    for start in range(128, weights.shape[1], 128):
        total = total + weights[:, start : start + 128]
    return total


def score(query, keys):
    return lax.dot_general(query, keys, (((1,), (1,)), ((), ())), preferred_element_type=jnp.float32)


def fresh_mask():
    row = lax.broadcasted_iota(jnp.int32, (half, half), 0)
    column = lax.broadcasted_iota(jnp.int32, (half, half), 1)
    return column <= row


def old_mask(pair):
    row = lax.broadcasted_iota(jnp.int32, (half, 128), 0)
    column = lax.broadcasted_iota(jnp.int32, (half, 128), 1)
    return column + (column // 64) * 64 + 64 * pair > row


def fetch_old(block, rest, slots_ref, sources, lows, kv_ref, sem):
    first = 4 * block
    later = list(range(first + 4, 16))
    order = later + [first + 2, first + 3, first, first + 1]
    for place, page in enumerate(order):
        slot = slots_ref[page]
        for source, low in zip(sources, lows):
            row = pl.multiple_of(rest + 64 * place + 32 * low, 32)
            pltpu.make_async_copy(source.at[slot], kv_ref.at[:, pl.ds(row, 32), :], sem).start()


def first_kernel(
    info_ref, slots_ref, query_ref, cos_ref, sin_ref, own_ref, core_ref, far_ref, far_core_ref,
    old_own_ref, old_core_ref, roped_ref, acc_ref, max_ref, sum_ref, kv_ref, sem,
):
    group_index = info_ref[0]
    has_old = info_ref[1]
    heads = acc_ref.shape[0]
    sources = (own_ref, core_ref, far_ref, far_core_ref)

    def run(block, with_old):
        low = block % 2
        rest = 512 * (block + 1)
        total = rest + (64 * (16 - 4 * block) if with_old else 0)
        own = sources[0]
        pltpu.make_async_copy(own.at[:, pl.ds(256, 256), :], kv_ref.at[:, pl.ds(0, 256), :], sem).start()
        pltpu.make_async_copy(own.at[:, pl.ds(0, 256), :], kv_ref.at[:, pl.ds(256, 256), :], sem).start()
        for earlier in range(block):
            pltpu.make_async_copy(
                sources[earlier ^ block], kv_ref.at[:, pl.ds(512 * (earlier + 1), 512), :], sem
            ).start()
        if with_old:
            fetch_old(block, rest, slots_ref, (old_own_ref, old_core_ref), (low, 1 - low), kv_ref, sem)
        filled = kv_ref.at[:, pl.ds(0, total), :]
        pltpu.make_async_copy(filled, filled, sem).wait()
        lower = fresh_mask()
        upper = old_mask(block // 2)

        def head(h, carry):
            columns = pl.ds(pl.multiple_of(h * 256, 256), 256)
            for part in range(2):
                rows = pl.ds(part * half, half)
                raw = query_ref[rows, columns]
                front = turn(raw, cos_ref[rows, :], sin_ref[rows, :])
                query = jnp.concatenate(
                    [(front * 0.0625).astype(jnp.bfloat16), raw[:, 128:] * jnp.bfloat16(0.0625)], axis=1
                )
                roped_ref[h, rows, :] = query
                start = 256 if part == 0 else 0
                stop = total - 128 if with_old and part == 1 else total
                keys = kv_ref[0, pl.ds(start, stop - start), :]
                values = kv_ref[1, pl.ds(start, stop - start), :]
                scores = score(query, keys)
                pieces = [jnp.where(lower, scores[:, :256], masked_score)]
                if with_old:
                    pieces.append(scores[:, 256 : stop - start - 128])
                    pieces.append(jnp.where(upper, scores[:, stop - start - 128 :], masked_score))
                elif stop - start > 256:
                    pieces.append(scores[:, 256:])
                scores = jnp.concatenate(pieces, axis=1) if len(pieces) > 1 else pieces[0]
                top = jnp.max(scores, axis=1, keepdims=True)
                weights = jnp.exp(scores - top)
                acc_ref[h, rows, :] = jnp.dot(
                    weights.astype(jnp.bfloat16), values, preferred_element_type=jnp.float32
                )
                max_ref[h, rows, :] = jnp.broadcast_to(top, (half, 128))
                sum_ref[h, rows, :] = lane_sums(weights)
            return carry

        lax.fori_loop(0, heads, head, 0)

    for block in range(4):
        for with_old in (False, True):

            @pl.when((group_index == block) & (has_old == int(with_old)))
            def _(block=block, with_old=with_old):
                run(block, with_old)


def first_part(info, slots, queries, cosine, sine, sources, old_own, old_core):
    tokens, width = queries.shape
    heads = width // 256
    return pl.pallas_call(
        first_kernel,
        out_shape=(
            pltpu.VMEM((heads, tokens, 256), jnp.bfloat16),
            pltpu.VMEM((heads, tokens, 256), jnp.float32),
            pltpu.VMEM((heads, tokens, 128), jnp.float32),
            pltpu.VMEM((heads, tokens, 128), jnp.float32),
        ),
        in_specs=[smem_spec, smem_spec, vmem_spec, vmem_spec, vmem_spec] + [any_spec] * 6,
        out_specs=(vmem_spec,) * 4,
        scratch_shapes=[pltpu.VMEM((2, 2304, 256), jnp.bfloat16), pltpu.SemaphoreType.DMA],
        compiler_params=params(),
        name="attend_first",
    )(info, slots, queries, cosine, sine, *sources, old_own, old_core)


def second_kernel(
    info_ref, slots_ref, pool_ref, roped_ref, acc_ref, max_ref, sum_ref, far_ref, far_core_ref,
    weight_ref, arrived_ref, key_ref, value_ref, hidden_ref, key_out_ref, value_out_ref,
    kv_ref, attended_ref, w_ref, stage_ref, sem, weight_sems, pool_sem, out_sems,
):
    group_index = info_ref[0]
    has_old = info_ref[1]
    heads = acc_ref.shape[0]
    chunks = weight_ref.shape[1] // 512

    def weight_copy(n):
        return pltpu.make_async_copy(
            weight_ref.at[:, pl.ds(n * 512, 512)], w_ref.at[n], weight_sems.at[n]
        )

    def run(block):
        fetch_old(
            block, 0, slots_ref, (far_ref, far_core_ref), (block % 2, 1 - block % 2), kv_ref, sem
        )

    def attend(block):
        total = 64 * (16 - 4 * block)
        filled = kv_ref.at[:, pl.ds(0, total), :]
        pltpu.make_async_copy(filled, filled, sem).wait()
        upper = old_mask(1 - block // 2)

        def head(h, carry):
            columns = pl.ds(pl.multiple_of(h * 256, 256), 256)
            for part in range(2):
                rows = pl.ds(part * half, half)
                stop = total - 128 * part
                scores = score(roped_ref[h, rows, :], kv_ref[0, pl.ds(0, stop), :])
                last = jnp.where(upper, scores[:, stop - 128 :], masked_score)
                scores = (
                    jnp.concatenate([scores[:, : stop - 128], last], axis=1) if stop > 128 else last
                )
                before = max_ref[h, rows, :][:, :1]
                top = jnp.maximum(before, jnp.max(scores, axis=1, keepdims=True))
                factor = jnp.exp(before - top)
                weights = jnp.exp(scores - top)
                total_sum = jnp.sum(sum_ref[h, rows, :] * factor + lane_sums(weights), axis=1, keepdims=True)
                mixed = acc_ref[h, rows, :] * factor + jnp.dot(
                    weights.astype(jnp.bfloat16), kv_ref[1, pl.ds(0, stop), :],
                    preferred_element_type=jnp.float32,
                )
                attended_ref[rows, columns] = (mixed / total_sum).astype(jnp.bfloat16)
            return carry

        lax.fori_loop(0, heads, head, 0)

    for block in range(4):

        @pl.when((group_index == block) & (has_old == 1))
        def _(block=block):
            run(block)

    for n in range(chunks):
        weight_copy(n).start()

    def place(page, carry):
        slot = pool_ref[page]

        @pl.when(slot >= 0)
        def _():
            pltpu.make_async_copy(arrived_ref.at[slot, 0], key_out_ref.at[page], pool_sem).start()
            pltpu.make_async_copy(arrived_ref.at[slot, 1], value_out_ref.at[page], pool_sem).start()

        @pl.when(slot < 0)
        def _():
            pltpu.make_async_copy(key_ref.at[page], key_out_ref.at[page], pool_sem).start()
            pltpu.make_async_copy(value_ref.at[page], value_out_ref.at[page], pool_sem).start()

        return carry

    lax.fori_loop(0, key_ref.shape[0], place, 0)

    for block in range(4):

        @pl.when((group_index == block) & (has_old == 1))
        def _(block=block):
            attend(block)

    @pl.when(has_old == 0)
    def _():
        def head(h, carry):
            columns = pl.ds(pl.multiple_of(h * 256, 256), 256)
            total_sum = jnp.sum(sum_ref[h], axis=1, keepdims=True)
            attended_ref[:, columns] = (acc_ref[h] / total_sum).astype(jnp.bfloat16)
            return carry

        lax.fori_loop(0, heads, head, 0)

    for n in range(chunks):
        weight_copy(n).wait()
        stage_ref[n] = jnp.dot(
            attended_ref[...], w_ref[n], preferred_element_type=jnp.float32
        ).astype(jnp.bfloat16)
        pltpu.make_async_copy(stage_ref.at[n], hidden_ref.at[:, pl.ds(n * 512, 512)], out_sems.at[n]).start()
    for n in range(chunks):
        pltpu.make_async_copy(stage_ref.at[n], hidden_ref.at[:, pl.ds(n * 512, 512)], out_sems.at[n]).wait()
    pltpu.make_async_copy(key_out_ref, key_out_ref, pool_sem).wait()
    pltpu.make_async_copy(value_out_ref, value_out_ref, pool_sem).wait()


def second_part(info, slots, pool, state, far, far_core, weight, arrived, key_cache, value_cache):
    heads, tokens, _ = state[0].shape
    width = weight.shape[1]
    chunks = width // 512
    state = [pltpu.with_memory_space_constraint(part, pltpu.VMEM) for part in state]
    return pl.pallas_call(
        second_kernel,
        out_shape=(
            jax.ShapeDtypeStruct((tokens, width), jnp.bfloat16),
            jax.ShapeDtypeStruct(key_cache.shape, jnp.bfloat16),
            jax.ShapeDtypeStruct(value_cache.shape, jnp.bfloat16),
        ),
        in_specs=[smem_spec] * 3 + [vmem_spec] * 4 + [any_spec] * 6,
        out_specs=(any_spec,) * 3,
        scratch_shapes=[
            pltpu.VMEM((2, 1024, 256), jnp.bfloat16),
            pltpu.VMEM((tokens, weight.shape[0]), jnp.bfloat16),
            pltpu.VMEM((chunks, weight.shape[0], 512), jnp.bfloat16),
            pltpu.VMEM((chunks, tokens, 512), jnp.bfloat16),
            pltpu.SemaphoreType.DMA,
            pltpu.SemaphoreType.DMA((chunks,)),
            pltpu.SemaphoreType.DMA,
            pltpu.SemaphoreType.DMA((chunks,)),
        ],
        compiler_params=params(),
        name="attend_second",
    )(info, slots, pool, *state, far, far_core, weight, arrived, key_cache, value_cache)


def body(queries, new_keys, new_values, key_cache, value_cache, out_weight, lengths, page_table):
    blk_count = lax.axis_size("blk")
    blk_index = lax.axis_index("blk")
    group_count = lax.axis_size("group")
    group_index = lax.axis_index("group")
    tok_rows = queries.shape[1]
    pages_here, page_rows, head_dim = key_cache.shape
    slot_count = page_table.shape[1]
    fresh_pages = tok_rows * group_count // (page_rows * group_count)
    window_pages = slot_count - fresh_pages
    cap_old = (window_pages + blk_count - 1) // blk_count
    cap_new = (fresh_pages + blk_count - 1) // blk_count

    owner = page_table // pages_here
    local = page_table % pages_here
    columns = jnp.arange(slot_count, dtype=jnp.int32)
    same_kind = (columns[:, None] >= window_pages) == (columns[None, :] >= window_pages)
    earlier = same_kind & (columns[None, :] < columns[:, None])
    rank = jnp.sum(
        (earlier[None] & (owner[:, None, :] == owner[:, :, None])).astype(jnp.int32), axis=2
    )
    here = owner == blk_index
    ranks_old = jnp.arange(cap_old, dtype=jnp.int32)
    old_send = jnp.sum(
        jnp.where(
            here[:, None, :window_pages] & (rank[:, None, :window_pages] == ranks_old[None, :, None]),
            local[:, None, :window_pages],
            0,
        ),
        axis=2,
    )
    my_owner = owner[blk_index]
    my_rank = rank[blk_index]
    old_slots = my_owner[:window_pages] * cap_old + my_rank[:window_pages]
    new_slots = my_owner[window_pages:] * cap_new + my_rank[window_pages:]
    new_send = jnp.sum(
        jnp.where(
            new_slots[None, :] == jnp.arange(blk_count * cap_new, dtype=jnp.int32)[:, None],
            jnp.arange(fresh_pages, dtype=jnp.int32)[None, :],
            0,
        ),
        axis=1,
    ).reshape(blk_count, cap_new)
    sent_as = jnp.arange(blk_count, dtype=jnp.int32)[:, None] * cap_new + rank[:, window_pages:]
    lands = here[:, window_pages:].reshape(1, -1) & (
        local[:, window_pages:].reshape(1, -1) == jnp.arange(pages_here, dtype=jnp.int32)[:, None]
    )
    pool = jnp.max(jnp.where(lands, sent_as.reshape(1, -1), -1), axis=1)
    length = lengths[blk_index]
    info = jnp.stack([group_index, (length > 0).astype(jnp.int32)])

    old_out = pick_old(old_send, key_cache, value_cache)
    old_own = lax.all_to_all(old_out, "blk", split_axis=0, concat_axis=0, tiled=True)
    old_own = old_own.reshape((blk_count * cap_old,) + old_own.shape[2:])

    positions = length + group_index * tok_rows + jnp.arange(tok_rows, dtype=jnp.int32)
    quarter = head_dim // 4
    freq_table = 10000.0 ** (-jnp.arange(quarter, dtype=jnp.float32) / quarter)
    angles = positions.astype(jnp.float32)[:, None] * freq_table
    cosine = jnp.cos(angles)
    sine = jnp.sin(angles)
    cosine = jnp.concatenate([cosine, cosine], axis=1)
    sine = jnp.concatenate([-sine, sine], axis=1)
    fresh = make_fresh(new_keys[0], new_values[0], cosine, sine)

    swap_core = [(0, 1), (1, 0), (2, 3), (3, 2)]
    swap_chip = [(0, 2), (2, 0), (1, 3), (3, 1)]
    far = lax.ppermute(fresh, "group", swap_chip)
    core = lax.ppermute(fresh, "group", swap_core)
    far_core = lax.ppermute(far, "group", swap_core)
    sources = (fresh, core, far, far_core)

    old_far = lax.ppermute(old_own, "group", swap_chip)
    old_core = lax.ppermute(old_own, "group", swap_core)
    old_far_core = lax.ppermute(old_far, "group", swap_core)

    new_out = pick_new(info, new_send, sources, page_rows)
    arrived = lax.all_to_all(new_out, "blk", split_axis=0, concat_axis=0, tiled=True)
    arrived = arrived.reshape((blk_count * cap_new,) + arrived.shape[2:])

    state = first_part(
        info, old_slots, queries[0], cosine, sine, sources, old_own, old_core
    )
    hidden, key_out, value_out = second_part(
        info, old_slots, pool, state, old_far, old_far_core, out_weight, arrived, key_cache, value_cache
    )
    return (hidden[None], key_out, value_out)


def solution(mesh):
    return jax.shard_map(
        body,
        mesh=mesh,
        in_specs=(
            P("blk", "group", None),
            P("blk", "group", None),
            P("blk", "group", None),
            P("blk", "group", None),
            P("blk", "group", None),
            P(),
            P(),
            P(),
        ),
        out_specs=(P("blk", "group", None), P("blk", "group", None), P("blk", "group", None)),
        check_vma=False,
    )
```

```python
import jax
import jax.numpy as jnp
from jax import lax
from jax.experimental import pallas as pl
from jax.experimental.pallas import tpu as pltpu
from jax.sharding import PartitionSpec as P

masked_score = -1e30
half = 256
pair_rows = 512
vmem_limit = 56 * 1024 * 1024
hbm_spec = pl.BlockSpec(memory_space=pltpu.HBM)
smem_spec = pl.BlockSpec(memory_space=pltpu.SMEM)
vmem_spec = pl.BlockSpec(memory_space=pltpu.VMEM)


def params(limit=vmem_limit):
    return pltpu.CompilerParams(vmem_limit_bytes=limit)


def in_hbm(*arrays):
    return [pltpu.with_memory_space_constraint(array, pltpu.HBM) for array in arrays]


def turn(values, cosine, sine):
    front = values[:, :128].astype(jnp.float32)
    return front * cosine + pltpu.roll(front, 64, 1) * sine


def pick_old_kernel(table_ref, key_ref, value_ref, out_ref, sem):
    requests, cap = out_ref.shape[:2]
    pages = key_ref.shape[0]
    low = lax.axis_index("blk") * pages
    window = table_ref.shape[1] // 2
    for r in range(requests):
        count = jnp.int32(0)
        chosen = [jnp.int32(0)] * cap
        for j in range(window):
            page = table_ref[r, j] - low
            inside = (page >= 0) & (page < pages)
            chosen = [jnp.where(inside & (count == c), page, chosen[c]) for c in range(cap)]
            count = count + inside.astype(jnp.int32)
        for c in range(cap):
            pltpu.make_async_copy(key_ref.at[chosen[c]], out_ref.at[r, c, 0], sem).start()
            pltpu.make_async_copy(value_ref.at[chosen[c]], out_ref.at[r, c, 1], sem).start()
    pltpu.make_async_copy(out_ref, out_ref, sem).wait()


def pick_old(page_table, cap, key_cache, value_cache):
    requests = page_table.shape[0]
    return pl.pallas_call(
        pick_old_kernel,
        out_shape=pltpu.HBM((requests, cap, 2) + key_cache.shape[1:], jnp.bfloat16),
        in_specs=[smem_spec, hbm_spec, hbm_spec],
        out_specs=hbm_spec,
        scratch_shapes=[pltpu.SemaphoreType.DMA],
        compiler_params=params(),
        name="pick_old",
    )(page_table, *in_hbm(key_cache, value_cache))


def rotate_kernel(keys_ref, cos_ref, sin_ref, out_ref):
    keys = keys_ref[...]
    out_ref[:, :128] = turn(keys, cos_ref[...], sin_ref[...]).astype(jnp.bfloat16)
    out_ref[:, 128:] = keys[:, 128:]


def rotate_keys(keys, cosine, sine):
    return pl.pallas_call(
        rotate_kernel,
        out_shape=jax.ShapeDtypeStruct(keys.shape, jnp.bfloat16),
        in_specs=[vmem_spec] * 3,
        out_specs=vmem_spec,
        compiler_params=params(),
        name="rotate_keys",
    )(keys, cosine, sine)


def find_slots(table_ref, row, first, count, owners, cap, pages, slots_ref, counts_ref):
    def clear(o, carry):
        counts_ref[o] = 0
        return carry

    lax.fori_loop(0, owners, clear, 0)
    for j in range(count):
        owner = table_ref[row, first + j] // pages
        rank = counts_ref[owner]
        counts_ref[owner] = rank + 1
        slots_ref[j] = owner * cap + rank


def pick_new_kernel(
    pages, table_ref, key_0, key_1, key_2, key_3, value_0, value_1, value_2, value_3,
    out_ref, slots_ref, counts_ref, sem,
):
    keys = (key_0, key_1, key_2, key_3)
    values = (value_0, value_1, value_2, value_3)
    owners = counts_ref.shape[0]
    cap = out_ref.shape[0] // owners
    rows = out_ref.shape[2]
    page_len = rows * 4
    block_pages = key_0.shape[0] // page_len
    count = block_pages * 4
    group_index = lax.axis_index("group")
    find_slots(
        table_ref, lax.axis_index("blk"), table_ref.shape[1] - count, count, owners, cap, pages,
        slots_ref, counts_ref,
    )
    start = rows * group_index
    for mine in range(4):

        @pl.when(group_index == mine)
        def _(mine=mine):
            for page in range(count):
                source = (page // block_pages) ^ mine
                first = (page % block_pages) * page_len + rows * mine
                slot = slots_ref[page]
                pltpu.make_async_copy(
                    keys[source].at[pl.ds(first, rows), :], out_ref.at[slot, 0], sem
                ).start()
                pltpu.make_async_copy(
                    values[source].at[pl.ds(first, rows), :], out_ref.at[slot, 1], sem
                ).start()

    sent = out_ref.at[pl.ds(0, count)]
    pltpu.make_async_copy(sent, sent, sem).wait()


def pick_new(page_table, blk_count, cap, pages, rows, keys, values):
    window = page_table.shape[1] // 2
    return pl.pallas_call(
        lambda *refs: pick_new_kernel(pages, *refs),
        out_shape=pltpu.HBM((blk_count * cap, 2, rows, keys[0].shape[1]), jnp.bfloat16),
        in_specs=[smem_spec] + [hbm_spec] * 8,
        out_specs=hbm_spec,
        scratch_shapes=[
            pltpu.SMEM((window,), jnp.int32),
            pltpu.SMEM((blk_count,), jnp.int32),
            pltpu.SemaphoreType.DMA,
        ],
        compiler_params=params(),
        name="pick_new",
    )(page_table, *in_hbm(*keys, *values))


def lane_fold(values, combine):
    total = values[:, :128]
    for start in range(128, values.shape[1], 128):
        total = combine(total, values[:, start : start + 128])
    return total


def score(query, keys):
    return lax.dot_general(query, keys, (((1,), (1,)), ((), ())), preferred_element_type=jnp.float32)


def fresh_mask():
    row = lax.broadcasted_iota(jnp.int32, (pair_rows, half), 0) & (half - 1)
    column = lax.broadcasted_iota(jnp.int32, (pair_rows, half), 1)
    return column <= row


def old_mask(pair):
    row = lax.broadcasted_iota(jnp.int32, (pair_rows, 128), 0) & (half - 1)
    column = lax.broadcasted_iota(jnp.int32, (pair_rows, 128), 1)
    return column + (column // 64) * 64 + 64 * pair > row


def join(pieces):
    pieces = [piece for piece in pieces if piece.shape[1]]
    return jnp.concatenate(pieces, axis=1) if len(pieces) > 1 else pieces[0]


def halves(values):
    return values.reshape(2, half, values.shape[1])


def fetch_old(block, rest, slots_ref, sources, lows, kv_ref, sem):
    first = 4 * block
    order = list(range(first + 4, 16)) + [first + 2, first + 3, first, first + 1]
    for place, page in enumerate(order):
        slot = slots_ref[page]
        for source, low in zip(sources, lows):
            row = rest + 64 * place + 32 * low
            pltpu.make_async_copy(source.at[slot], kv_ref.at[:, pl.ds(row, 32), :], sem).start()


def pipeline(pairs, scores, softmax, gather, finished):
    scores(0, 0)
    scores(0, 1)
    softmax(0, 0)

    def step(i, carry):
        scores(i + 1, 0)
        softmax(i, 1)
        gather(i, 0)
        scores(i + 1, 1)
        softmax(i + 1, 0)
        gather(i, 1)
        finished(i)
        return carry

    lax.fori_loop(0, pairs - 1, step, 0)
    softmax(pairs - 1, 1)
    gather(pairs - 1, 0)
    gather(pairs - 1, 1)
    finished(pairs - 1)


def first_kernel(
    pages, cap, table_ref, lengths_ref, query_ref, cos_ref, sin_ref,
    key_0, key_1, key_2, key_3, value_0, value_1, value_2, value_3, old_own_ref, old_core_ref,
    roped_out, acc_out, stat_out,
    q_ref, roped_ref, acc_ref, stat_ref, kv_ref, s_0, s_1, top_0, top_1, p_0, p_1,
    slots_ref, counts_ref, query_sem, sem, out_sem,
):
    group_index = lax.axis_index("group")
    blk_index = lax.axis_index("blk")
    has_old = lengths_ref[blk_index] > 0
    keys = (key_0, key_1, key_2, key_3)
    values = (value_0, value_1, value_2, value_3)
    s_refs, top_refs, p_refs = (s_0, s_1), (top_0, top_1), (p_0, p_1)
    pairs = acc_ref.shape[0] // 2
    query_copy = pltpu.make_async_copy(query_ref, q_ref, query_sem)
    query_copy.start()
    find_slots(
        table_ref, blk_index, 0, table_ref.shape[1] // 2, counts_ref.shape[0], cap, pages,
        slots_ref, counts_ref,
    )

    def run(block, with_old):
        rest = 512 * (block + 1)
        total = rest + (64 * (16 - 4 * block) if with_old else 0)
        for number, sources in enumerate((keys, values)):
            target = kv_ref.at[number]
            for low in range(2):
                pltpu.make_async_copy(
                    sources[0].at[pl.ds(256 - 256 * low, 256), :], target.at[pl.ds(256 * low, 256), :], sem
                ).start()
            for earlier in range(block):
                pltpu.make_async_copy(
                    sources[earlier ^ block], target.at[pl.ds(512 * (earlier + 1), 512), :], sem
                ).start()
        if with_old:
            low = block % 2
            fetch_old(block, rest, slots_ref, (old_own_ref, old_core_ref), (low, 1 - low), kv_ref, sem)
        query_copy.wait()
        filled = kv_ref.at[:, pl.ds(0, total), :]
        pltpu.make_async_copy(filled, filled, sem).wait()

        def key_range(part):
            start = 256 if part == 0 else 0
            stop = total - 128 if with_old and part == 1 else total
            return start, stop - start

        def scores(i, part):
            start, size = key_range(part)
            rows = pl.ds(part * half, half)
            query = []
            for one in range(2):
                column = pl.multiple_of(i * 512 + one * 256, 256)
                raw = q_ref[rows, pl.ds(column, 256)]
                front = turn(raw, cos_ref[rows, :], sin_ref[rows, :])
                query.append(
                    jnp.concatenate(
                        [(front * 0.0625).astype(jnp.bfloat16), raw[:, 128:] * jnp.bfloat16(0.0625)],
                        axis=1,
                    )
                )
            query = jnp.concatenate(query, axis=0)
            roped_ref[pl.ds(i * 2, 2), rows, :] = halves(query)
            result = score(query, kv_ref[0, pl.ds(start, size), :])
            pieces = [jnp.where(fresh_mask(), result[:, :256], masked_score)]
            if with_old:
                pieces.append(result[:, 256 : size - 128])
                pieces.append(jnp.where(old_mask(block // 2), result[:, size - 128 :], masked_score))
            else:
                pieces.append(result[:, 256:])
            result = join(pieces)
            s_refs[part][:, :size] = result
            top_refs[part][...] = lane_fold(result, jnp.maximum)

        def softmax(i, part):
            _, size = key_range(part)
            rows = pl.ds(part * half, half)
            top = jnp.max(top_refs[part][...], axis=1, keepdims=True)
            weights = jnp.exp(s_refs[part][:, :size] - top)
            p_refs[part][:, :size] = weights.astype(jnp.bfloat16)
            sums = jnp.sum(lane_fold(weights, jnp.add), axis=1, keepdims=True)
            lane = lax.broadcasted_iota(jnp.int32, (pair_rows, 128), 1)
            stat_ref[pl.ds(i * 2, 2), rows, :] = halves(jnp.where(lane < 64, top, sums))

        def gather(i, part):
            start, size = key_range(part)
            rows = pl.ds(part * half, half)
            acc_ref[pl.ds(i * 2, 2), rows, :] = halves(
                jnp.dot(
                    p_refs[part][:, :size], kv_ref[1, pl.ds(start, size), :],
                    preferred_element_type=jnp.float32,
                )
            )

        def finished(i):
            for source, target in ((roped_ref, roped_out), (acc_ref, acc_out), (stat_ref, stat_out)):
                some = pl.ds(i * 2, 2)
                pltpu.make_async_copy(source.at[some], target.at[some], out_sem).start()

        pipeline(pairs, scores, softmax, gather, finished)

    for block in range(4):
        for with_old in (False, True):

            @pl.when((group_index == block) & (has_old == with_old))
            def _(block=block, with_old=with_old):
                run(block, with_old)

    for source, target in ((roped_ref, roped_out), (acc_ref, acc_out), (stat_ref, stat_out)):
        pltpu.make_async_copy(source, target, out_sem).wait()


def first_part(page_table, lengths, blk_count, cap, pages, queries, cosine, sine, keys, values, old_own, old_core):
    tokens, width = queries.shape
    heads = width // 256
    widest = 4 * 512 + 256
    return pl.pallas_call(
        lambda *refs: first_kernel(pages, cap, *refs),
        out_shape=(
            pltpu.HBM((heads, tokens, 256), jnp.bfloat16),
            pltpu.HBM((heads, tokens, 256), jnp.float32),
            pltpu.HBM((heads, tokens, 128), jnp.float32),
        ),
        in_specs=[smem_spec, smem_spec, hbm_spec, vmem_spec, vmem_spec] + [hbm_spec] * 10,
        out_specs=(hbm_spec,) * 3,
        scratch_shapes=[
            pltpu.VMEM((tokens, width), jnp.bfloat16),
            pltpu.VMEM((heads, tokens, 256), jnp.bfloat16),
            pltpu.VMEM((heads, tokens, 256), jnp.float32),
            pltpu.VMEM((heads, tokens, 128), jnp.float32),
            pltpu.VMEM((2, widest, 256), jnp.bfloat16),
            pltpu.VMEM((pair_rows, widest), jnp.float32),
            pltpu.VMEM((pair_rows, widest), jnp.float32),
            pltpu.VMEM((pair_rows, 128), jnp.float32),
            pltpu.VMEM((pair_rows, 128), jnp.float32),
            pltpu.VMEM((pair_rows, widest), jnp.bfloat16),
            pltpu.VMEM((pair_rows, widest), jnp.bfloat16),
            pltpu.SMEM((page_table.shape[1] // 2,), jnp.int32),
            pltpu.SMEM((blk_count,), jnp.int32),
            pltpu.SemaphoreType.DMA,
            pltpu.SemaphoreType.DMA,
            pltpu.SemaphoreType.DMA,
        ],
        compiler_params=params(),
        name="attend_first",
    )(page_table, lengths, *in_hbm(queries), cosine, sine, *in_hbm(*keys, *values, old_own, old_core))


def second_kernel(
    cap_old, cap_new, table_ref, lengths_ref, roped_in, acc_in, stat_in, far_ref, far_core_ref,
    weight_ref, arrived_ref, key_ref, value_ref, hidden_ref, key_out_ref, value_out_ref,
    roped_ref, acc_ref, stat_ref, kv_ref, s_0, s_1, top_0, top_1, p_0, p_1, old_0, old_1, inv_0, inv_1,
    attended_ref, w_ref, stage_ref, slots_ref, counts_ref,
    state_sems, sem, weight_sem, pool_sem, page_sem, out_sems,
):
    group_index = lax.axis_index("group")
    blk_index = lax.axis_index("blk")
    has_old = lengths_ref[blk_index] > 0
    pages = key_ref.shape[0]
    requests, slots = table_ref.shape
    pairs = acc_ref.shape[0] // 2
    s_refs, top_refs, p_refs = (s_0, s_1), (top_0, top_1), (p_0, p_1)
    old_refs, inv_refs = (old_0, old_1), (inv_0, inv_1)
    chunks = stage_ref.shape[0]
    chunk = stage_ref.shape[2]

    def state_copies(i):
        some = pl.ds(i * 2, 2)
        return [
            pltpu.make_async_copy(source.at[some], target.at[some], state_sems.at[number, i])
            for number, (source, target) in enumerate(
                ((roped_in, roped_ref), (acc_in, acc_ref), (stat_in, stat_ref))
            )
        ]

    def fetch(block):
        low = block % 2
        fetch_old(block, 0, slots_ref, (far_ref, far_core_ref), (low, 1 - low), kv_ref, sem)

    def attend(block):
        total = 64 * (16 - 4 * block)
        filled = kv_ref.at[:, pl.ds(0, total), :]
        pltpu.make_async_copy(filled, filled, sem).wait()

        def scores(i, part):
            if part == 0:
                for copy in state_copies(i):
                    copy.wait()
            rows = pl.ds(part * half, half)
            size = total - 128 * part
            query = roped_ref[pl.ds(i * 2, 2), rows, :].reshape(pair_rows, 256)
            result = score(query, kv_ref[0, pl.ds(0, size), :])
            last = jnp.where(old_mask(1 - block // 2), result[:, size - 128 :], masked_score)
            result = join([result[:, : size - 128], last])
            s_refs[part][:, :size] = result
            top_refs[part][...] = lane_fold(result, jnp.maximum)

        def softmax(i, part):
            rows = pl.ds(part * half, half)
            size = total - 128 * part
            stat = stat_ref[pl.ds(i * 2, 2), rows, :].reshape(pair_rows, 128)
            before = stat[:, :1]
            top = jnp.maximum(before, jnp.max(top_refs[part][...], axis=1, keepdims=True))
            weights = jnp.exp(s_refs[part][:, :size] - top)
            p_refs[part][:, :size] = weights.astype(jnp.bfloat16)
            factor = jnp.exp(before - top)
            sums = stat[:, 64:65] * factor + jnp.sum(lane_fold(weights, jnp.add), axis=1, keepdims=True)
            inverse = 1.0 / sums
            old_refs[part][...] = jnp.broadcast_to(factor * inverse, (pair_rows, 128))
            inv_refs[part][...] = jnp.broadcast_to(inverse, (pair_rows, 128))

        def gather(i, part):
            rows = pl.ds(part * half, half)
            size = total - 128 * part
            fresh = jnp.dot(
                p_refs[part][:, :size], kv_ref[1, pl.ds(0, size), :], preferred_element_type=jnp.float32
            )
            before = acc_ref[pl.ds(i * 2, 2), rows, :].reshape(pair_rows, 256)
            old, inverse = old_refs[part][...], inv_refs[part][...]
            mixed = before * join([old, old]) + fresh * join([inverse, inverse])
            mixed = mixed.astype(jnp.bfloat16)
            for one in range(2):
                column = pl.multiple_of(i * 512 + one * 256, 256)
                attended_ref[rows, pl.ds(column, 256)] = mixed[one * half : (one + 1) * half]

        pipeline(pairs, scores, softmax, gather, lambda i: None)

    find_slots(
        table_ref, blk_index, 0, slots // 2, counts_ref.shape[0], cap_old, pages, slots_ref, counts_ref
    )
    for block in range(4):

        @pl.when((group_index == block) & has_old)
        def _(block=block):
            fetch(block)

    for i in range(pairs):
        for copy in state_copies(i):
            copy.start()
    weight_copy = pltpu.make_async_copy(weight_ref, w_ref, weight_sem)
    weight_copy.start()
    pool_copies = [
        pltpu.make_async_copy(key_ref, key_out_ref, pool_sem.at[0]),
        pltpu.make_async_copy(value_ref, value_out_ref, pool_sem.at[1]),
    ]
    for copy in pool_copies:
        copy.start()

    for block in range(4):

        @pl.when((group_index == block) & has_old)
        def _(block=block):
            attend(block)

    @pl.when(jnp.logical_not(has_old))
    def _():
        for i in range(pairs):
            for copy in state_copies(i):
                copy.wait()

        def head(h, carry):
            columns = pl.ds(pl.multiple_of(h * 256, 256), 256)
            attended_ref[:, columns] = (acc_ref[h] * (1.0 / stat_ref[h][:, 64:65])).astype(jnp.bfloat16)
            return carry

        lax.fori_loop(0, pairs * 2, head, 0)

    for copy in pool_copies:
        copy.wait()
    low = blk_index * pages

    def place(r, placed):
        rank = jnp.int32(0)
        for j in range(slots // 2, slots):
            page = table_ref[r, j] - low
            inside = (page >= 0) & (page < pages)

            @pl.when(inside)
            def _(page=page, rank=rank):
                slot = r * cap_new + rank
                pltpu.make_async_copy(arrived_ref.at[slot, 0], key_out_ref.at[page], page_sem).start()
                pltpu.make_async_copy(arrived_ref.at[slot, 1], value_out_ref.at[page], page_sem).start()

            rank = rank + inside.astype(jnp.int32)
        return placed + rank

    placed = lax.fori_loop(0, requests, place, jnp.int32(0))

    weight_copy.wait()

    def project(n, carry):
        columns = pl.ds(pl.multiple_of(n * chunk, chunk), chunk)
        stage_ref[n] = jnp.dot(
            attended_ref[...], w_ref[:, columns], preferred_element_type=jnp.float32
        ).astype(jnp.bfloat16)
        pltpu.make_async_copy(stage_ref.at[n], hidden_ref.at[:, columns], out_sems.at[n]).start()
        return carry

    lax.fori_loop(0, chunks, project, 0)
    for n in range(chunks):
        pltpu.make_async_copy(
            stage_ref.at[n], hidden_ref.at[:, pl.ds(n * chunk, chunk)], out_sems.at[n]
        ).wait()

    def settle(n, carry):
        pltpu.make_async_copy(arrived_ref.at[0, 0], key_out_ref.at[0], page_sem).wait()
        pltpu.make_async_copy(arrived_ref.at[0, 1], value_out_ref.at[0], page_sem).wait()
        return carry

    lax.fori_loop(0, placed, settle, 0)


def second_part(
    page_table, lengths, blk_count, cap_old, cap_new, state, far, far_core, weight, arrived, key_cache, value_cache
):
    heads, tokens, _ = state[0].shape
    width = weight.shape[1]
    chunk = 256
    widest = 1024
    return pl.pallas_call(
        lambda *refs: second_kernel(cap_old, cap_new, *refs),
        out_shape=(
            pltpu.HBM((tokens, width), jnp.bfloat16),
            pltpu.HBM(key_cache.shape, jnp.bfloat16),
            pltpu.HBM(value_cache.shape, jnp.bfloat16),
        ),
        in_specs=[smem_spec] * 2 + [hbm_spec] * 9,
        out_specs=(hbm_spec,) * 3,
        scratch_shapes=[
            pltpu.VMEM((heads, tokens, 256), jnp.bfloat16),
            pltpu.VMEM((heads, tokens, 256), jnp.float32),
            pltpu.VMEM((heads, tokens, 128), jnp.float32),
            pltpu.VMEM((2, widest, 256), jnp.bfloat16),
            pltpu.VMEM((pair_rows, widest), jnp.float32),
            pltpu.VMEM((pair_rows, widest), jnp.float32),
            pltpu.VMEM((pair_rows, 128), jnp.float32),
            pltpu.VMEM((pair_rows, 128), jnp.float32),
            pltpu.VMEM((pair_rows, widest), jnp.bfloat16),
            pltpu.VMEM((pair_rows, widest), jnp.bfloat16),
            pltpu.VMEM((pair_rows, 128), jnp.float32),
            pltpu.VMEM((pair_rows, 128), jnp.float32),
            pltpu.VMEM((pair_rows, 128), jnp.float32),
            pltpu.VMEM((pair_rows, 128), jnp.float32),
            pltpu.VMEM((tokens, weight.shape[0]), jnp.bfloat16),
            pltpu.VMEM(weight.shape, jnp.bfloat16),
            pltpu.VMEM((width // chunk, tokens, chunk), jnp.bfloat16),
            pltpu.SMEM((page_table.shape[1] // 2,), jnp.int32),
            pltpu.SMEM((blk_count,), jnp.int32),
            pltpu.SemaphoreType.DMA((3, heads // 2)),
            pltpu.SemaphoreType.DMA,
            pltpu.SemaphoreType.DMA,
            pltpu.SemaphoreType.DMA((2,)),
            pltpu.SemaphoreType.DMA,
            pltpu.SemaphoreType.DMA((width // chunk,)),
        ],
        compiler_params=params(),
        name="attend_second",
    )(page_table, lengths, *in_hbm(*state, far, far_core, weight, arrived, key_cache, value_cache))


def body(queries, new_keys, new_values, key_cache, value_cache, out_weight, lengths, page_table):
    blk_count = lax.axis_size("blk")
    blk_index = lax.axis_index("blk")
    group_index = lax.axis_index("group")
    tok_rows = queries.shape[1]
    pages_here, page_rows, head_dim = key_cache.shape
    window_pages = page_table.shape[1] // 2
    cap = (window_pages + blk_count - 1) // blk_count

    swap_core = [(0, 1), (1, 0), (2, 3), (3, 2)]
    swap_chip = [(0, 2), (2, 0), (1, 3), (3, 1)]

    def swap(value, pairs):
        return lax.ppermute(value, "group", pairs)

    value_own = new_values[0]
    value_far = swap(value_own, swap_chip)

    positions = lengths[blk_index] + group_index * tok_rows + jnp.arange(tok_rows, dtype=jnp.int32)
    quarter = head_dim // 4
    freq_table = 10000.0 ** (-jnp.arange(quarter, dtype=jnp.float32) / quarter)
    angles = positions.astype(jnp.float32)[:, None] * freq_table
    cosine = jnp.cos(angles)
    sine = jnp.sin(angles)
    cosine = jnp.concatenate([cosine, cosine], axis=1)
    sine = jnp.concatenate([-sine, sine], axis=1)
    key_own = rotate_keys(new_keys[0], cosine, sine)
    key_far = swap(key_own, swap_chip)

    table, _ = lax.optimization_barrier((page_table, key_own))
    old_out = pick_old(table, cap, key_cache, value_cache)
    old_own = lax.all_to_all(old_out, "blk", split_axis=0, concat_axis=0, tiled=True)
    old_own = old_own.reshape((blk_count * cap,) + old_own.shape[2:])
    old_far = swap(old_own, swap_chip)
    old_core = swap(old_own, swap_core)

    value_core = swap(value_own, swap_core)
    key_core = swap(key_own, swap_core)
    value_far_core = swap(value_far, swap_core)
    key_far_core = swap(key_far, swap_core)
    keys = (key_own, key_core, key_far, key_far_core)
    values = (value_own, value_core, value_far, value_far_core)

    new_out = pick_new(page_table, blk_count, cap, pages_here, page_rows, keys, values)
    arrived = lax.all_to_all(new_out, "blk", split_axis=0, concat_axis=0, tiled=True)

    state = first_part(
        page_table, lengths, blk_count, cap, pages_here, queries[0], cosine, sine, keys, values,
        old_own, old_core,
    )
    old_far_core = swap(old_far, swap_core)
    hidden, key_out, value_out = second_part(
        page_table, lengths, blk_count, cap, cap, state, old_far, old_far_core, out_weight, arrived,
        key_cache, value_cache,
    )
    return (hidden[None], key_out, value_out)


def solution(mesh):
    return jax.shard_map(
        body,
        mesh=mesh,
        in_specs=(
            P("blk", "group", None),
            P("blk", "group", None),
            P("blk", "group", None),
            P("blk", "group", None),
            P("blk", "group", None),
            P(),
            P(),
            P(),
        ),
        out_specs=(P("blk", "group", None), P("blk", "group", None), P("blk", "group", None)),
        check_vma=False,
    )
```

```python
import jax
import jax.numpy as jnp
import numpy as np
from jax import lax
from jax.experimental import pallas as pl
from jax.experimental.pallas import tpu as pltpu
from jax.sharding import PartitionSpec as P

masked_score = -1e30
step_keys = 512
hbm_spec = pl.BlockSpec(memory_space=pltpu.HBM)
smem_spec = pl.BlockSpec(memory_space=pltpu.SMEM)
vmem_spec = pl.BlockSpec(memory_space=pltpu.VMEM)
small_limit = 8 * 1024 * 1024
large_limit = 56 * 1024 * 1024


def params(limit):
    return pltpu.CompilerParams(vmem_limit_bytes=limit)


def in_hbm(*arrays):
    return [pltpu.with_memory_space_constraint(array, pltpu.HBM) for array in arrays]


def turn(values, cosine, sine):
    front = values[:, :128].astype(jnp.float32)
    return front * cosine + pltpu.roll(front, 64, 1) * sine


def join(pieces):
    return jnp.concatenate(pieces, axis=1)


def rotate_kernel(lengths_ref, freq_ref, keys_ref, out_ref, cos_ref, sin_ref):
    rows = keys_ref.shape[0]
    start = lengths_ref[lax.axis_index("blk")] + lax.axis_index("group") * rows
    positions = start + lax.broadcasted_iota(jnp.int32, (rows, 128), 0)
    angles = positions.astype(jnp.float32) * freq_ref[...]
    lane = lax.broadcasted_iota(jnp.int32, (rows, 128), 1)
    cosine = jnp.cos(angles)
    sine = jnp.sin(angles)
    sine = jnp.where(lane < 64, -sine, sine)
    cos_ref[...] = cosine
    sin_ref[...] = sine
    keys = keys_ref[...]
    out_ref[:, :128] = turn(keys, cosine, sine).astype(jnp.bfloat16)
    out_ref[:, 128:] = keys[:, 128:]


def rotate_keys(lengths, keys):
    rows, head_dim = keys.shape
    quarter = head_dim // 4
    freq_table = np.float32(10000.0) ** (-np.arange(quarter, dtype=np.float32) / np.float32(quarter))
    freq_table = np.concatenate([freq_table, freq_table])[None].astype(np.float32)
    table = jax.ShapeDtypeStruct((rows, 128), jnp.float32)
    return pl.pallas_call(
        rotate_kernel,
        out_shape=(jax.ShapeDtypeStruct(keys.shape, jnp.bfloat16), table, table),
        in_specs=[smem_spec, vmem_spec, vmem_spec],
        out_specs=(vmem_spec,) * 3,
        compiler_params=params(small_limit),
        name="rotate_keys",
    )(lengths, jnp.asarray(freq_table), keys)


def pick_old_kernel(table_ref, key_ref, value_ref, out_ref, sem):
    requests, cap = out_ref.shape[:2]
    pages = key_ref.shape[0]
    low = lax.axis_index("blk") * pages
    window = table_ref.shape[1] // 2
    for r in range(requests):
        count = jnp.int32(0)
        chosen = [jnp.int32(0)] * cap
        for j in range(window):
            page = table_ref[r, j] - low
            inside = (page >= 0) & (page < pages)
            chosen = [jnp.where(inside & (count == c), page, chosen[c]) for c in range(cap)]
            count = count + inside.astype(jnp.int32)
        for c in range(cap):
            pltpu.make_async_copy(key_ref.at[chosen[c]], out_ref.at[r, c, 0], sem).start()
            pltpu.make_async_copy(value_ref.at[chosen[c]], out_ref.at[r, c, 1], sem).start()
    pltpu.make_async_copy(out_ref, out_ref, sem).wait()


def pick_old(page_table, cap, key_cache, value_cache):
    requests = page_table.shape[0]
    return pl.pallas_call(
        pick_old_kernel,
        out_shape=jax.ShapeDtypeStruct((requests, cap, 2) + key_cache.shape[1:], jnp.bfloat16),
        in_specs=[smem_spec, hbm_spec, hbm_spec],
        out_specs=vmem_spec,
        scratch_shapes=[pltpu.SemaphoreType.DMA],
        compiler_params=params(small_limit),
        name="pick_old",
    )(page_table, *in_hbm(key_cache, value_cache))


def owner_of(page, pages, owners):
    factor = (1 << 20) // pages + 1
    assert all((p * factor) >> 20 == p // pages for p in range(pages * owners))
    assert pages * owners * factor < 1 << 31
    return (page * factor) >> 20


def find_slots(table_ref, first, count, cap, pages, slots_ref, counts_ref):
    owners = counts_ref.shape[0]
    row = lax.axis_index("blk")
    for o in range(owners):
        counts_ref[o] = 0
    for j in range(count):
        owner = owner_of(table_ref[row, first + j], pages, owners)
        rank = counts_ref[owner]
        counts_ref[owner] = rank + 1
        slots_ref[j] = owner * cap + rank


def pick_new_kernel(
    pages, table_ref, key_0, key_1, key_2, key_3, value_0, value_1, value_2, value_3,
    out_ref, slots_ref, counts_ref, sem,
):
    sources = ((key_0, value_0), (key_1, value_1), (key_2, value_2), (key_3, value_3))
    cap = out_ref.shape[0] // counts_ref.shape[0]
    rows = out_ref.shape[2]
    page_len = rows * 4
    block_pages = key_0.shape[0] // page_len
    count = block_pages * 4
    group_index = lax.axis_index("group")
    find_slots(table_ref, table_ref.shape[1] - count, count, cap, pages, slots_ref, counts_ref)
    for number, pair in enumerate(sources):
        block = number ^ group_index

        for place in range(block_pages):
            slot = slots_ref[block * block_pages + place]
            first = pl.multiple_of(place * page_len + rows * group_index, 32)
            for kind in range(2):
                pltpu.make_async_copy(
                    pair[kind].at[pl.ds(first, rows), :], out_ref.at[slot, kind], sem
                ).start()
    sent = out_ref.at[pl.ds(0, count)]
    pltpu.make_async_copy(sent, sent, sem).wait()


def pick_new(page_table, blk_count, cap, pages, rows, keys, values):
    window = page_table.shape[1] // 2
    return pl.pallas_call(
        lambda *refs: pick_new_kernel(pages, *refs),
        out_shape=jax.ShapeDtypeStruct((blk_count * cap, 2, rows, keys[0].shape[1]), jnp.bfloat16),
        in_specs=[smem_spec] + [hbm_spec] * 8,
        out_specs=vmem_spec,
        scratch_shapes=[
            pltpu.SMEM((window,), jnp.int32),
            pltpu.SMEM((blk_count,), jnp.int32),
            pltpu.SemaphoreType.DMA,
        ],
        compiler_params=params(small_limit),
        name="pick_new",
    )(page_table, *in_hbm(*keys, *values))


def lane_fold(values, combine):
    total = values[:, :128]
    for start in range(128, values.shape[1], 128):
        total = combine(total, values[:, start : start + 128])
    return total


def old_bias(rows, pair):
    row = lax.broadcasted_iota(jnp.int32, (rows, 256), 0)
    column = lax.broadcasted_iota(jnp.int32, (rows, 256), 1)
    return jnp.where(column + (column // 64) * 64 + 64 * pair > row, 0.0, masked_score)


def fetch_page(slot, row, sources, low, kv_ref, sem):
    for number, source in enumerate(sources):
        place = pl.multiple_of(row + 32 * (low ^ number), 32)
        pltpu.make_async_copy(source.at[slot], kv_ref.at[:, pl.ds(place, 32), :], sem).start()


def wait_rows(kv_ref, steps, most, sem):
    for n in range(1, most + 1):

        @pl.when(steps == n)
        def _(n=n):
            filled = kv_ref.at[:, pl.ds(0, n * step_keys), :]
            pltpu.make_async_copy(filled, filled, sem).wait()


def attention(heads, steps, roped_ref, kv_ref, bias_ref, s_refs, most_refs, top_ref, sum_ref, acc_ref, begin, finish):
    last_bias = bias_ref.shape[0] - 1

    def scores(h, c, which):
        keys = kv_ref[0, pl.ds(pl.multiple_of(c * step_keys, step_keys), step_keys), :]
        result = lax.dot_general(
            roped_ref[h], keys, (((1,), (1,)), ((), ())), preferred_element_type=jnp.float32
        )
        result = result + bias_ref[jnp.minimum(c, last_bias)]
        s_refs[which][c] = result
        most_refs[which][...] = jnp.maximum(most_refs[which][...], lane_fold(result, jnp.maximum))

    def weigh(c, which):
        top = top_ref[...]
        weights = jnp.exp(s_refs[which][c] - join([top] * (step_keys // 128)))
        sum_ref[...] += lane_fold(weights, jnp.add)
        values = kv_ref[1, pl.ds(pl.multiple_of(c * step_keys, step_keys), step_keys), :]
        acc_ref[...] += jnp.dot(
            weights.astype(jnp.bfloat16), values, preferred_element_type=jnp.float32
        )

    def settle(which):
        top_ref[...] = jnp.broadcast_to(
            jnp.max(most_refs[which][...], axis=1, keepdims=True), top_ref.shape
        )
        sum_ref[...] = jnp.zeros_like(sum_ref)
        acc_ref[...] = jnp.zeros_like(acc_ref)

    def loop(work):
        def step(c, carry):
            work(c)
            return carry

        lax.fori_loop(0, steps, step, 0)

    begin(0, most_refs[0])
    loop(lambda c: scores(0, c, 0))

    def two(i, carry):
        h = i * 2
        begin(h + 1, most_refs[1])
        settle(0)

        def first_work(c):
            weigh(c, 0)
            scores(h + 1, c, 1)

        loop(first_work)
        finish(h)
        settle(1)

        @pl.when(h + 2 < heads)
        def _():
            begin(h + 2, most_refs[0])

            def second_work(c):
                weigh(c, 1)
                scores(h + 2, c, 0)

            loop(second_work)

        @pl.when(h + 2 >= heads)
        def _():
            loop(lambda c: weigh(c, 1))

        finish(h + 1)
        return carry

    lax.fori_loop(0, heads // 2, two, 0)


def first_kernel(
    pages, cap, table_ref, lengths_ref, query_ref, cos_ref, sin_ref,
    key_0, key_1, key_2, key_3, value_0, value_1, value_2, value_3, old_own_ref, old_core_ref,
    roped_out, acc_out, stat_out,
    q_ref, roped_ref, acc_ref, stat_ref, kv_ref, s_0, s_1, most_0, most_1, top_ref, sum_ref, head_ref,
    bias_ref, slots_ref, counts_ref, query_sem, sem, out_sem,
):
    group_index = lax.axis_index("group")
    has_old = lengths_ref[lax.axis_index("blk")] > 0
    heads, rows = roped_ref.shape[:2]
    block_pages = slots_ref.shape[0] // 4
    even = 1 - group_index % 2
    query_copy = pltpu.make_async_copy(query_ref, q_ref, query_sem)
    query_copy.start()
    steps = jnp.where(has_old, 3 + group_index // 2, group_index + 1)

    for number, refs in enumerate(((key_0, key_1, key_2, key_3), (value_0, value_1, value_2, value_3))):
        target = kv_ref.at[number]
        pltpu.make_async_copy(refs[0], target.at[pl.ds(0, rows), :], sem).start()
        for other in range(1, 4):
            block = group_index ^ other

            @pl.when(block < group_index)
            def _(block=block, other=other, refs=refs, target=target):
                start = rows + jnp.where(has_old, 256 * even, 0) + rows * block
                pltpu.make_async_copy(
                    refs[other], target.at[pl.ds(pl.multiple_of(start, 256), rows), :], sem
                ).start()

    @pl.when(has_old)
    def _():
        find_slots(table_ref, 0, 4 * block_pages, cap, pages, slots_ref, counts_ref)
        later = rows + 256 * even + rows * group_index

        def page(j, carry):
            block = j // block_pages
            row = jnp.where(block == group_index, rows, later + 256 * (block - group_index - 1))
            row = row + 64 * (j % block_pages)

            @pl.when((block > group_index) | ((block == group_index) & (even == 1)))
            def _():
                fetch_page(slots_ref[j], row, (old_own_ref, old_core_ref), group_index % 2, kv_ref, sem)

            return carry

        lax.fori_loop(0, 4 * block_pages, page, 0)

    row = lax.broadcasted_iota(jnp.int32, (rows, step_keys), 0)
    column = lax.broadcasted_iota(jnp.int32, (rows, step_keys), 1)
    bias_ref[0] = jnp.where(column <= row, 0.0, masked_score)
    bias_ref[1] = jnp.zeros((rows, step_keys), jnp.float32)
    bias_ref[2] = jnp.zeros((rows, step_keys), jnp.float32)

    @pl.when(has_old & (even == 1))
    def _():
        bias_ref[1, :, :256] = old_bias(rows, group_index // 2)

    query_copy.wait()

    def rope(h, carry):
        raw = q_ref[:, pl.ds(pl.multiple_of(h * 256, 256), 256)]
        front = turn(raw, cos_ref[...], sin_ref[...])
        roped_ref[h, :, :128] = (front * 0.0625).astype(jnp.bfloat16)
        roped_ref[h, :, 128:] = raw[:, 128:] * jnp.bfloat16(0.0625)
        return carry

    lax.fori_loop(0, heads, rope, 0)
    roped_copy = pltpu.make_async_copy(roped_ref, roped_out, query_sem)
    roped_copy.start()
    wait_rows(kv_ref, steps, 4, sem)

    def begin(h, most_ref):
        most_ref[...] = jnp.full_like(most_ref, masked_score)

    def finish(h):
        lane = lax.broadcasted_iota(jnp.int32, (rows, 128), 1)
        sums = jnp.sum(sum_ref[...], axis=1, keepdims=True)
        stat_ref[h] = jnp.where(lane < 64, top_ref[...], sums)
        acc_ref[h] = head_ref[...]
        pltpu.make_async_copy(acc_ref.at[h], acc_out.at[h], out_sem).start()
        pltpu.make_async_copy(stat_ref.at[h], stat_out.at[h], out_sem).start()

    attention(
        heads, steps, roped_ref, kv_ref, bias_ref, (s_0, s_1), (most_0, most_1), top_ref, sum_ref,
        head_ref, begin, finish,
    )
    roped_copy.wait()
    pltpu.make_async_copy(acc_ref, acc_out, out_sem).wait()
    pltpu.make_async_copy(stat_ref, stat_out, out_sem).wait()


def working(rows, steps, biases):
    return [
        pltpu.VMEM((steps, rows, step_keys), jnp.float32),
        pltpu.VMEM((steps, rows, step_keys), jnp.float32),
        pltpu.VMEM((rows, 128), jnp.float32),
        pltpu.VMEM((rows, 128), jnp.float32),
        pltpu.VMEM((rows, 128), jnp.float32),
        pltpu.VMEM((rows, 128), jnp.float32),
        pltpu.VMEM((rows, 256), jnp.float32),
        pltpu.VMEM((biases, rows, step_keys), jnp.float32),
    ]


def first_part(page_table, lengths, blk_count, cap, pages, queries, cosine, sine, keys, values, old_own, old_core):
    rows, width = queries.shape
    heads = width // 256
    return pl.pallas_call(
        lambda *refs: first_kernel(pages, cap, *refs),
        out_shape=(
            pltpu.HBM((heads, rows, 256), jnp.bfloat16),
            pltpu.HBM((heads, rows, 256), jnp.float32),
            pltpu.HBM((heads, rows, 128), jnp.float32),
        ),
        in_specs=[smem_spec, smem_spec, hbm_spec, vmem_spec, vmem_spec] + [hbm_spec] * 10,
        out_specs=(hbm_spec,) * 3,
        scratch_shapes=[
            pltpu.VMEM((rows, width), jnp.bfloat16),
            pltpu.VMEM((heads, rows, 256), jnp.bfloat16),
            pltpu.VMEM((heads, rows, 256), jnp.float32),
            pltpu.VMEM((heads, rows, 128), jnp.float32),
            pltpu.VMEM((2, 4 * step_keys, 256), jnp.bfloat16),
        ]
        + working(rows, 4, 3)
        + [
            pltpu.SMEM((page_table.shape[1] // 2,), jnp.int32),
            pltpu.SMEM((blk_count,), jnp.int32),
            pltpu.SemaphoreType.DMA,
            pltpu.SemaphoreType.DMA,
            pltpu.SemaphoreType.DMA,
        ],
        compiler_params=params(large_limit),
        name="attend_first",
    )(page_table, lengths, *in_hbm(queries), cosine, sine, *in_hbm(*keys, *values, old_own, old_core))


def second_kernel(
    cap, table_ref, lengths_ref, roped_in, acc_in, stat_in, own_ref, core_ref, far_ref, far_core_ref,
    weight_ref, arrived_ref, key_ref, value_ref, hidden_ref, key_out_ref, value_out_ref,
    roped_ref, acc_ref, stat_ref, kv_ref, s_0, s_1, most_0, most_1, top_ref, sum_ref, head_ref,
    bias_ref, attended_ref, w_ref, stage_ref, key_pool, value_pool, slots_ref, counts_ref,
    state_sems, sem, weight_sem, pool_sems, page_sem, out_sems,
):
    group_index = lax.axis_index("group")
    blk_index = lax.axis_index("blk")
    has_old = lengths_ref[blk_index] > 0
    pages = key_ref.shape[0]
    requests, slots = table_ref.shape
    heads, rows = roped_ref.shape[:2]
    block_pages = slots // 8
    chunks = stage_ref.shape[0]
    chunk = stage_ref.shape[2]
    odd = group_index % 2
    steps = jnp.where(has_old, 2 - group_index // 2, 0)

    @pl.when(has_old)
    def _():
        find_slots(table_ref, 0, slots // 2, cap, pages, slots_ref, counts_ref)

        def page(j, carry):
            block = j // block_pages
            row = jnp.where(block == group_index, 0, 256 * (odd + block - group_index))
            row = row + 64 * (j % block_pages)

            @pl.when(block >= group_index)
            def _():
                fetch_page(slots_ref[j], row, (far_ref, far_core_ref), odd, kv_ref, sem)

            @pl.when((block == group_index) & (odd == 1))
            def _():
                fetch_page(slots_ref[j], row + 256, (own_ref, core_ref), odd, kv_ref, sem)

            return carry

        lax.fori_loop(0, slots // 2, page, 0)

    def state_copies(h):
        return [
            pltpu.make_async_copy(source.at[h], target.at[h], state_sems.at[number, h])
            for number, (source, target) in enumerate(
                ((roped_in, roped_ref), (stat_in, stat_ref), (acc_in, acc_ref))
            )
        ]

    pool_loads = [
        pltpu.make_async_copy(key_ref, key_pool, pool_sems.at[0]),
        pltpu.make_async_copy(value_ref, value_pool, pool_sems.at[1]),
    ]
    pool_stores = [
        pltpu.make_async_copy(key_pool, key_out_ref, pool_sems.at[0]),
        pltpu.make_async_copy(value_pool, value_out_ref, pool_sems.at[1]),
    ]
    for h in range(2):
        for copy in state_copies(h):
            copy.start()
    for copy in pool_loads:
        copy.start()
    for h in range(2, heads):
        for copy in state_copies(h):
            copy.start()
    weight_copy = pltpu.make_async_copy(weight_ref, w_ref, weight_sem)
    weight_copy.start()

    bias_ref[...] = jnp.zeros_like(bias_ref)
    bias_ref[0, :, :256] = old_bias(rows, 1 - group_index // 2)

    @pl.when(odd == 1)
    def _():
        bias_ref[0, :, 256:] = old_bias(rows, group_index // 2)

    for copy in pool_loads:
        copy.wait()
    low = blk_index * pages

    def place(r, placed):
        rank = jnp.int32(0)
        for j in range(slots // 2, slots):
            page = table_ref[r, j] - low
            inside = (page >= 0) & (page < pages)

            @pl.when(inside)
            def _(page=page, rank=rank):
                slot = r * cap + rank
                pltpu.make_async_copy(arrived_ref.at[slot, 0], key_pool.at[page], page_sem).start()
                pltpu.make_async_copy(arrived_ref.at[slot, 1], value_pool.at[page], page_sem).start()

            rank = rank + inside.astype(jnp.int32)
        return placed + rank

    placed = lax.fori_loop(0, requests, place, jnp.int32(0))
    wait_rows(kv_ref, steps, 2, sem)
    lane = lax.broadcasted_iota(jnp.int32, (rows, 128), 1)

    def begin(h, most_ref):
        for copy in state_copies(h):
            copy.wait()
        most_ref[...] = jnp.where(lane < 64, stat_ref[h], masked_score)

    def finish(h):
        stat = stat_ref[h]
        top = top_ref[...]
        factor = jnp.exp(stat[:, :1] - top)
        sums = stat[:, 64:65] * factor + jnp.sum(sum_ref[...], axis=1, keepdims=True)
        inverse = 1.0 / sums
        old = factor * inverse
        mixed = acc_ref[h] * join([old, old]) + head_ref[...] * join([inverse, inverse])
        attended_ref[:, pl.ds(pl.multiple_of(h * 256, 256), 256)] = mixed.astype(jnp.bfloat16)

    attention(
        heads, steps, roped_ref, kv_ref, bias_ref, (s_0, s_1), (most_0, most_1), top_ref, sum_ref,
        head_ref, begin, finish,
    )

    def settle(n, carry):
        pltpu.make_async_copy(arrived_ref.at[0, 0], key_pool.at[0], page_sem).wait()
        pltpu.make_async_copy(arrived_ref.at[0, 1], value_pool.at[0], page_sem).wait()
        return carry

    lax.fori_loop(0, placed, settle, 0)
    for copy in pool_stores:
        copy.start()
    weight_copy.wait()

    def project(n, carry):
        columns = pl.ds(pl.multiple_of(n * chunk, chunk), chunk)
        stage_ref[n] = jnp.dot(
            attended_ref[...], w_ref[:, columns], preferred_element_type=jnp.float32
        ).astype(jnp.bfloat16)
        pltpu.make_async_copy(stage_ref.at[n], hidden_ref.at[:, columns], out_sems.at[n]).start()
        return carry

    lax.fori_loop(0, chunks, project, 0)
    for n in range(chunks):
        pltpu.make_async_copy(
            stage_ref.at[n], hidden_ref.at[:, pl.ds(n * chunk, chunk)], out_sems.at[n]
        ).wait()
    for copy in pool_stores:
        copy.wait()


def second_part(page_table, lengths, blk_count, cap, state, olds, weight, arrived, key_cache, value_cache):
    heads, rows, _ = state[0].shape
    width = weight.shape[1]
    chunk = 256
    return pl.pallas_call(
        lambda *refs: second_kernel(cap, *refs),
        out_shape=(
            pltpu.HBM((rows, width), jnp.bfloat16),
            pltpu.HBM(key_cache.shape, jnp.bfloat16),
            pltpu.HBM(value_cache.shape, jnp.bfloat16),
        ),
        in_specs=[smem_spec] * 2 + [hbm_spec] * 11,
        out_specs=(hbm_spec,) * 3,
        scratch_shapes=[
            pltpu.VMEM((heads, rows, 256), jnp.bfloat16),
            pltpu.VMEM((heads, rows, 256), jnp.float32),
            pltpu.VMEM((heads, rows, 128), jnp.float32),
            pltpu.VMEM((2, 2 * step_keys, 256), jnp.bfloat16),
        ]
        + working(rows, 2, 2)
        + [
            pltpu.VMEM((rows, weight.shape[0]), jnp.bfloat16),
            pltpu.VMEM(weight.shape, jnp.bfloat16),
            pltpu.VMEM((width // chunk, rows, chunk), jnp.bfloat16),
            pltpu.VMEM(key_cache.shape, jnp.bfloat16),
            pltpu.VMEM(value_cache.shape, jnp.bfloat16),
            pltpu.SMEM((page_table.shape[1] // 2,), jnp.int32),
            pltpu.SMEM((blk_count,), jnp.int32),
            pltpu.SemaphoreType.DMA((3, heads)),
            pltpu.SemaphoreType.DMA,
            pltpu.SemaphoreType.DMA,
            pltpu.SemaphoreType.DMA((2,)),
            pltpu.SemaphoreType.DMA,
            pltpu.SemaphoreType.DMA((width // chunk,)),
        ],
        compiler_params=params(large_limit),
        name="attend_second",
    )(page_table, lengths, *in_hbm(*state, *olds, weight, arrived, key_cache, value_cache))


def body(queries, new_keys, new_values, key_cache, value_cache, out_weight, lengths, page_table):
    blk_count = lax.axis_size("blk")
    pages_here, page_rows, _ = key_cache.shape
    window_pages = page_table.shape[1] // 2
    cap = (window_pages + blk_count - 1) // blk_count

    swap_core = [(0, 1), (1, 0), (2, 3), (3, 2)]
    swap_chip = [(0, 2), (2, 0), (1, 3), (3, 1)]

    def swap(value, pairs):
        return lax.ppermute(value, "group", pairs)

    value_own = new_values[0]
    value_far = swap(value_own, swap_chip)
    key_own, cosine, sine = rotate_keys(lengths, new_keys[0])
    key_far = swap(key_own, swap_chip)

    table, _ = lax.optimization_barrier((page_table, key_own))
    old_out = pick_old(table, cap, key_cache, value_cache)
    old_own = lax.all_to_all(old_out, "blk", split_axis=0, concat_axis=0, tiled=True)
    old_own = old_own.reshape((blk_count * cap,) + old_own.shape[2:])
    old_far = swap(old_own, swap_chip)
    old_core = swap(old_own, swap_core)

    value_core = swap(value_own, swap_core)
    key_core = swap(key_own, swap_core)
    value_far_core = swap(value_far, swap_core)
    key_far_core = swap(key_far, swap_core)
    keys = (key_own, key_core, key_far, key_far_core)
    values = (value_own, value_core, value_far, value_far_core)

    new_out = pick_new(page_table, blk_count, cap, pages_here, page_rows, keys, values)
    arrived = lax.all_to_all(new_out, "blk", split_axis=0, concat_axis=0, tiled=True)

    state = first_part(
        page_table, lengths, blk_count, cap, pages_here, queries[0], cosine, sine, keys, values,
        old_own, old_core,
    )
    old_far_core = swap(old_far, swap_core)
    hidden, key_out, value_out = second_part(
        page_table, lengths, blk_count, cap, state, (old_own, old_core, old_far, old_far_core),
        out_weight, arrived, key_cache, value_cache,
    )
    return (hidden[None], key_out, value_out)


def solution(mesh):
    return jax.shard_map(
        body,
        mesh=mesh,
        in_specs=(
            P("blk", "group", None),
            P("blk", "group", None),
            P("blk", "group", None),
            P("blk", "group", None),
            P("blk", "group", None),
            P(),
            P(),
            P(),
        ),
        out_specs=(P("blk", "group", None), P("blk", "group", None), P("blk", "group", None)),
        check_vma=False,
    )
```

```python
import jax
import jax.numpy as jnp
import numpy as np
from jax import lax
from jax.experimental import pallas as pl
from jax.experimental.pallas import tpu as pltpu
from jax.sharding import PartitionSpec as P

masked_score = -1e30
step_keys = 512
step_slots = 16
hbm_spec = pl.BlockSpec(memory_space=pltpu.HBM)
smem_spec = pl.BlockSpec(memory_space=pltpu.SMEM)
vmem_spec = pl.BlockSpec(memory_space=pltpu.VMEM)
small_limit = 16 * 1024 * 1024
large_limit = 56 * 1024 * 1024


def params(limit):
    return pltpu.CompilerParams(vmem_limit_bytes=limit)


def in_hbm(*arrays):
    return [pltpu.with_memory_space_constraint(array, pltpu.HBM) for array in arrays]


def turn(values, cosine, sine):
    front = values[:, :128].astype(jnp.float32)
    return front * cosine + pltpu.roll(front, 64, 1) * sine


def join(pieces):
    return jnp.concatenate(pieces, axis=1)


def pages_here(table_ref, r, first, count, cap, pages):
    low = lax.axis_index("blk") * pages
    found = jnp.int32(0)
    chosen = [jnp.int32(0)] * cap
    for j in range(first, first + count):
        page = table_ref[r, j] - low
        inside = (page >= 0) & (page < pages)
        chosen = [jnp.where(inside & (found == c), page, chosen[c]) for c in range(cap)]
        found = found + inside.astype(jnp.int32)
    return chosen, found


def pick_old_kernel(table_ref, key_ref, value_ref, out_ref, sem):
    requests, cap = out_ref.shape[:2]
    for r in range(requests):
        chosen, _ = pages_here(table_ref, r, 0, table_ref.shape[1] // 2, cap, key_ref.shape[0])
        for c in range(cap):
            pltpu.make_async_copy(key_ref.at[chosen[c]], out_ref.at[r, c, 0], sem).start()
            pltpu.make_async_copy(value_ref.at[chosen[c]], out_ref.at[r, c, 1], sem).start()
    pltpu.make_async_copy(out_ref, out_ref, sem).wait()


def pick_old(page_table, cap, key_cache, value_cache):
    requests = page_table.shape[0]
    return pl.pallas_call(
        pick_old_kernel,
        out_shape=jax.ShapeDtypeStruct((requests, cap, 2) + key_cache.shape[1:], jnp.bfloat16),
        in_specs=[smem_spec, hbm_spec, hbm_spec],
        out_specs=vmem_spec,
        scratch_shapes=[pltpu.SemaphoreType.DMA],
        compiler_params=params(small_limit),
        name="pick_old",
    )(page_table, *in_hbm(key_cache, value_cache))


def owner_of(page, pages, owners):
    factor = (1 << 20) // pages + 1
    assert all((p * factor) >> 20 == p // pages for p in range(pages * owners))
    assert pages * owners * factor < 1 << 31
    return (page * factor) >> 20


def find_slots(table_ref, first, count, cap, pages, counts_ref):
    owners = counts_ref.shape[0]
    row = lax.axis_index("blk")
    for o in range(owners):
        counts_ref[o] = 0
    slots = []
    for j in range(count):
        owner = owner_of(table_ref[row, first + j], pages, owners)
        rank = counts_ref[owner]
        counts_ref[owner] = rank + 1
        slots.append(owner * cap + rank)
    return slots


def pack_kernel(
    pages, cap, table_ref, lengths_ref, freq_ref, keys_ref, values_ref, old_ref,
    both_ref, one_ref, two_ref, cos_ref, sin_ref, counts_ref, sem,
):
    rows = keys_ref.shape[0]
    slots = rows // 32
    for j, slot in enumerate(find_slots(table_ref, 0, slots, cap, pages, counts_ref)):
        pltpu.make_async_copy(old_ref.at[slot], both_ref.at[slots + j], sem).start()
    group_index = lax.axis_index("group")
    start = lengths_ref[lax.axis_index("blk")] + group_index * rows
    positions = start + lax.broadcasted_iota(jnp.int32, (rows, 128), 0)
    angles = positions.astype(jnp.float32) * freq_ref[...]
    lane = lax.broadcasted_iota(jnp.int32, (rows, 128), 1)
    cosine = jnp.cos(angles)
    sine = jnp.sin(angles)
    sine = jnp.where(lane < 64, -sine, sine)
    cos_ref[...] = cosine
    sin_ref[...] = sine
    keys = keys_ref[...]
    turned = join([turn(keys, cosine, sine).astype(jnp.bfloat16), keys[:, 128:]])
    both_ref[:slots, 0] = turned.reshape(slots, 32, 256)
    both_ref[:slots, 1] = values_ref[...].reshape(slots, 32, 256)
    sorted_ref = both_ref.at[pl.ds(slots, slots)]
    pltpu.make_async_copy(sorted_ref, sorted_ref, sem).wait()

    @pl.when(group_index < 2)
    def _():
        one_ref[...] = both_ref[:slots]
        two_ref[...] = both_ref[slots + slots // 2 :]

    @pl.when(group_index >= 2)
    def _():
        one_ref[...] = both_ref[slots:]
        for page in range(slots // 4):
            two_ref[2 * page : 2 * page + 2] = both_ref[4 * page : 4 * page + 2]


def pack(page_table, lengths, blk_count, cap, pages, keys, values, old):
    rows, head_dim = keys.shape
    slots = rows // 32
    quarter = head_dim // 4
    freq_table = np.float32(10000.0) ** (-np.arange(quarter, dtype=np.float32) / np.float32(quarter))
    freq_table = np.concatenate([freq_table, freq_table])[None].astype(np.float32)
    return pl.pallas_call(
        lambda *refs: pack_kernel(pages, cap, *refs),
        out_shape=(
            jax.ShapeDtypeStruct((2 * slots, 2, 32, head_dim), jnp.bfloat16),
            jax.ShapeDtypeStruct((slots, 2, 32, head_dim), jnp.bfloat16),
            jax.ShapeDtypeStruct((slots // 2, 2, 32, head_dim), jnp.bfloat16),
            jax.ShapeDtypeStruct((rows, 128), jnp.float32),
            jax.ShapeDtypeStruct((rows, 128), jnp.float32),
        ),
        in_specs=[smem_spec, smem_spec, vmem_spec, vmem_spec, vmem_spec, hbm_spec],
        out_specs=(vmem_spec,) * 5,
        scratch_shapes=[pltpu.SMEM((blk_count,), jnp.int32), pltpu.SemaphoreType.DMA],
        compiler_params=params(small_limit),
        name="pack",
    )(page_table, lengths, jnp.asarray(freq_table), keys, values, *in_hbm(old))


def rope_kernel(query_ref, cos_ref, sin_ref, out_ref):
    raw = query_ref[...]
    front = turn(raw, cos_ref[...], sin_ref[...])
    out_ref[0, :, :128] = (front * 0.0625).astype(jnp.bfloat16)
    out_ref[0, :, 128:] = raw[:, 128:] * jnp.bfloat16(0.0625)


def rotate_queries(queries, cosine, sine):
    rows, width = queries.shape
    heads = width // 256
    return pl.pallas_call(
        rope_kernel,
        out_shape=pltpu.HBM((heads, rows, 256), jnp.bfloat16),
        grid=(heads,),
        in_specs=[
            pl.BlockSpec((rows, 256), lambda h: (0, h)),
            pl.BlockSpec((rows, 128), lambda h: (0, 0)),
            pl.BlockSpec((rows, 128), lambda h: (0, 0)),
        ],
        out_specs=pl.BlockSpec((1, rows, 256), lambda h: (h, 0, 0)),
        compiler_params=params(small_limit),
        cost_estimate=pl.CostEstimate(flops=8 * rows * width, bytes_accessed=4 * rows * width, transcendentals=0),
        name="rotate_queries",
    )(queries, cosine, sine)


def pick_new_kernel(
    pages, cap, table_ref, both_ref, core_ref, one_ref, one_core_ref, two_ref, two_core_ref,
    out_ref, slots_ref, counts_ref, sem,
):
    count = slots_ref.shape[0]
    block_pages = count // 4
    group_index = lax.axis_index("group")
    for j, slot in enumerate(find_slots(table_ref, table_ref.shape[1] - count, count, cap, pages, counts_ref)):
        slots_ref[j] = slot

    def send(ref, block, stride):
        for place in range(block_pages):
            source = ref.at[stride * place + group_index]
            target = out_ref.at[slots_ref[block * block_pages + place]]
            pltpu.make_async_copy(source, target, sem).start()

    send(both_ref, group_index, 4)
    send(core_ref, group_index ^ 1, 4)

    @pl.when(group_index < 2)
    def _():
        send(two_ref, group_index ^ 2, 2)
        send(two_core_ref, group_index ^ 3, 2)

    @pl.when(group_index >= 2)
    def _():
        send(one_ref, group_index ^ 2, 4)
        send(one_core_ref, group_index ^ 3, 4)

    sent = out_ref.at[pl.ds(0, count)]
    pltpu.make_async_copy(sent, sent, sem).wait()


def pick_new(page_table, blk_count, cap, pages, sources):
    window = page_table.shape[1] // 2
    return pl.pallas_call(
        lambda *refs: pick_new_kernel(pages, cap, *refs),
        out_shape=jax.ShapeDtypeStruct((blk_count * cap,) + sources[0].shape[1:], jnp.bfloat16),
        in_specs=[smem_spec] + [hbm_spec] * 6,
        out_specs=vmem_spec,
        scratch_shapes=[
            pltpu.SMEM((window,), jnp.int32),
            pltpu.SMEM((blk_count,), jnp.int32),
            pltpu.SemaphoreType.DMA,
        ],
        compiler_params=params(small_limit),
        name="pick_new",
    )(page_table, *in_hbm(*sources))


def lane_fold(values, combine):
    total = values[:, :128]
    for start in range(128, values.shape[1], 128):
        total = combine(total, values[:, start : start + 128])
    return total


def old_bias(rows, quarter):
    row = lax.broadcasted_iota(jnp.int32, (rows, 256), 0)
    column = lax.broadcasted_iota(jnp.int32, (rows, 256), 1)
    held = quarter ^ (column // 128)
    position = ((column % 128) // 32) * 128 + 32 * held + column % 32
    return jnp.where(position > row, 0.0, masked_score)


def fetch(source, first, kv_ref, place, count, sem):
    for kind in range(2):
        pltpu.make_async_copy(
            source.at[pl.ds(first, count), kind], kv_ref.at[kind, pl.ds(place, count)], sem
        ).start()


def fetch_pair(sources, first, kv_ref, place, sem):
    fetch(sources[0], first, kv_ref, place, 4, sem)
    fetch(sources[1], first, kv_ref, place + 4, 4, sem)


def wait_rows(kv_ref, steps, most, sem):
    for n in range(1, most + 1):

        @pl.when(steps == n)
        def _(n=n):
            filled = kv_ref.at[:, pl.ds(0, n * step_slots)]
            pltpu.make_async_copy(filled, filled, sem).wait()


def attention(heads, steps, roped_ref, kv_ref, bias_ref, s_refs, most_refs, top_ref, sum_ref, acc_of, begin, finish):
    last_bias = bias_ref.shape[0] - 1
    rows = roped_ref.shape[1]
    parts = 2
    part_rows = rows // parts

    def block(kind, c):
        return kv_ref[kind, pl.ds(c * step_slots, step_slots)].reshape(step_keys, 256)

    def scores(h, c, which, part, keys):
        some = pl.ds(part * part_rows, part_rows)
        result = lax.dot_general(
            roped_ref[h, some, :], keys, (((1,), (1,)), ((), ())), preferred_element_type=jnp.float32
        )
        result = result + bias_ref[jnp.minimum(c, last_bias), some, :]
        s_refs[which][c, some, :] = result
        most_refs[which][some, :] = jnp.maximum(most_refs[which][some, :], lane_fold(result, jnp.maximum))

    def exponentials(c, which, part):
        some = pl.ds(part * part_rows, part_rows)
        weights = jnp.exp(s_refs[which][c, some, :] - join([top_ref[some, :]] * (step_keys // 128)))
        sum_ref[some, :] += lane_fold(weights, jnp.add)
        return weights.astype(jnp.bfloat16)

    def gather(h, part, weights, values):
        some = pl.ds(part * part_rows, part_rows)
        acc_of(h)[some, :] += jnp.dot(weights, values, preferred_element_type=jnp.float32)

    def settle(h, which):
        top_ref[...] = jnp.broadcast_to(
            jnp.max(most_refs[which][...], axis=1, keepdims=True), top_ref.shape
        )
        sum_ref[...] = jnp.zeros_like(sum_ref)
        acc = acc_of(h)
        acc[...] = jnp.zeros(acc.shape, jnp.float32)

    def loop(h, which, following):
        def step(c, carry):
            keys = block(0, c)
            values = block(1, c)
            weights = None
            for part in range(parts):
                if following:
                    scores(h + 1, c, 1 - which, part, keys)
                if weights is not None:
                    gather(h, part - 1, weights, values)
                weights = exponentials(c, which, part)
            gather(h, parts - 1, weights, values)
            return carry

        lax.fori_loop(0, steps, step, 0)

    def first_scores(c, carry):
        for part in range(parts):
            scores(0, c, 0, part, block(0, c))
        return carry

    begin(0, most_refs[0])
    lax.fori_loop(0, steps, first_scores, 0)

    def two(i, carry):
        h = i * 2
        begin(h + 1, most_refs[1])
        settle(h, 0)
        loop(h, 0, True)
        finish(h)
        settle(h + 1, 1)

        @pl.when(h + 2 < heads)
        def _():
            begin(h + 2, most_refs[0])
            loop(h + 1, 1, True)

        @pl.when(h + 2 >= heads)
        def _():
            loop(h + 1, 1, False)

        finish(h + 1)
        return carry

    lax.fori_loop(0, heads // 2, two, 0)


def first_kernel(
    lengths_ref, roped_in, both_ref, core_ref, acc_out, stat_out,
    roped_ref, acc_ref, stat_ref, kv_ref, s_0, s_1, most_0, most_1, top_ref, sum_ref,
    bias_ref, roped_sem, sem, out_sem,
):
    group_index = lax.axis_index("group")
    has_old = lengths_ref[lax.axis_index("blk")] > 0
    heads, rows = roped_ref.shape[:2]
    odd = group_index % 2
    roped_copy = pltpu.make_async_copy(roped_in, roped_ref, roped_sem)
    roped_copy.start()
    steps = jnp.where(has_old, 3 - group_index // 2, 1 + odd)
    fetch(both_ref, 0, kv_ref, 0, 16, sem)

    @pl.when(odd == 1)
    def _():
        fetch(core_ref, 0, kv_ref, 16, 16, sem)

    @pl.when(has_old)
    def _():
        for block in range(4):

            @pl.when((block == group_index) & (odd == 0))
            def _(block=block):
                fetch_pair((both_ref, core_ref), 16 + 4 * block, kv_ref, 16, sem)

            @pl.when(block > group_index)
            def _(block=block):
                place = 24 + 8 * odd + 8 * (block - 1 - group_index)
                fetch_pair((both_ref, core_ref), 16 + 4 * block, kv_ref, place, sem)

    row = lax.broadcasted_iota(jnp.int32, (rows, step_keys), 0)
    column = lax.broadcasted_iota(jnp.int32, (rows, step_keys), 1)
    bias_ref[0] = jnp.where(column <= row, 0.0, masked_score)
    bias_ref[1] = jnp.zeros((rows, step_keys), jnp.float32)
    bias_ref[2] = jnp.zeros((rows, step_keys), jnp.float32)

    @pl.when(has_old & (odd == 0))
    def _():
        bias_ref[1, :, :256] = old_bias(rows, group_index)

    roped_copy.wait()
    wait_rows(kv_ref, steps, 3, sem)

    def begin(h, most_ref):
        most_ref[...] = jnp.full_like(most_ref, masked_score)

    def finish(h):
        lane = lax.broadcasted_iota(jnp.int32, (rows, 128), 1)
        sums = jnp.sum(sum_ref[...], axis=1, keepdims=True)
        stat_ref[h] = jnp.where(lane < 64, top_ref[...], sums)
        pltpu.make_async_copy(acc_ref.at[h], acc_out.at[h], out_sem).start()
        pltpu.make_async_copy(stat_ref.at[h], stat_out.at[h], out_sem).start()

    attention(
        heads, steps, roped_ref, kv_ref, bias_ref, (s_0, s_1), (most_0, most_1), top_ref, sum_ref,
        lambda h: acc_ref.at[h], begin, finish,
    )
    pltpu.make_async_copy(acc_ref, acc_out, out_sem).wait()
    pltpu.make_async_copy(stat_ref, stat_out, out_sem).wait()


def working(rows, steps, biases):
    return [
        pltpu.VMEM((2, steps * step_slots, 32, 256), jnp.bfloat16),
        pltpu.VMEM((steps, rows, step_keys), jnp.float32),
        pltpu.VMEM((steps, rows, step_keys), jnp.float32),
        pltpu.VMEM((rows, 128), jnp.float32),
        pltpu.VMEM((rows, 128), jnp.float32),
        pltpu.VMEM((rows, 128), jnp.float32),
        pltpu.VMEM((rows, 128), jnp.float32),
        pltpu.VMEM((biases, rows, step_keys), jnp.float32),
    ]


def first_part(lengths, roped, both, core):
    heads, rows, _ = roped.shape
    return pl.pallas_call(
        first_kernel,
        out_shape=(
            pltpu.HBM((heads, rows, 256), jnp.float32),
            pltpu.HBM((heads, rows, 128), jnp.float32),
        ),
        in_specs=[smem_spec] + [hbm_spec] * 3,
        out_specs=(hbm_spec,) * 2,
        scratch_shapes=[
            pltpu.VMEM((heads, rows, 256), jnp.bfloat16),
            pltpu.VMEM((heads, rows, 256), jnp.float32),
            pltpu.VMEM((heads, rows, 128), jnp.float32),
        ]
        + working(rows, 3, 3)
        + [pltpu.SemaphoreType.DMA] * 3,
        compiler_params=params(large_limit),
        cost_estimate=pl.CostEstimate(
            flops=4 * heads * rows * 1536 * 256, bytes_accessed=1 << 24, transcendentals=heads * rows * 1536
        ),
        name="attend_first",
    )(lengths, *in_hbm(roped, both, core))


def second_kernel(
    cap, table_ref, lengths_ref, roped_in, acc_in, stat_in, both_ref, core_ref, one_ref, one_core_ref,
    two_ref, two_core_ref, weight_ref, arrived_ref, key_ref, value_ref,
    hidden_ref, key_out_ref, value_out_ref,
    roped_ref, acc_ref, stat_ref, kv_ref, s_0, s_1, most_0, most_1, top_ref, sum_ref,
    bias_ref, head_ref, attended_ref, w_ref, stage_ref, key_pool, value_pool,
    state_sems, sem, weight_sem, pool_sems, page_sem, out_sems,
):
    group_index = lax.axis_index("group")
    has_old = lengths_ref[lax.axis_index("blk")] > 0
    pages = key_ref.shape[0]
    requests, slots = table_ref.shape
    heads, rows = roped_ref.shape[:2]
    chunks = stage_ref.shape[0]
    chunk = stage_ref.shape[2]
    odd = group_index % 2
    chip = group_index // 2
    steps = 2 * chip + jnp.where(has_old, 2 - chip, 0)

    def state_copies(h):
        return [
            pltpu.make_async_copy(source.at[h], target.at[h], state_sems.at[number, h])
            for number, (source, target) in enumerate(
                ((roped_in, roped_ref), (stat_in, stat_ref), (acc_in, acc_ref))
            )
        ]

    pool_loads = [
        pltpu.make_async_copy(key_ref, key_pool, pool_sems.at[0]),
        pltpu.make_async_copy(value_ref, value_pool, pool_sems.at[1]),
    ]
    pool_stores = [
        pltpu.make_async_copy(key_pool, key_out_ref, pool_sems.at[0]),
        pltpu.make_async_copy(value_pool, value_out_ref, pool_sems.at[1]),
    ]
    for copy in pool_loads:
        copy.start()

    @pl.when(has_old)
    def _():
        for block in range(4):
            if block < 2:
                fars = (one_ref, one_core_ref)

                @pl.when((chip == 0) & (block == group_index))
                def _(block=block, fars=fars):
                    fetch_pair(fars, 4 * block, kv_ref, 0, sem)

            for number, fars in enumerate(((one_ref, one_core_ref), (two_ref, two_core_ref))):
                if block < 2 and number == 1:
                    continue
                page = 4 * block - 8 * number

                @pl.when((chip == number) & (block == group_index) & (block >= 2))
                def _(fars=fars, page=page):
                    fetch_pair(fars, page, kv_ref, 0, sem)

                @pl.when((chip == number) & (block > group_index))
                def _(block=block, fars=fars, page=page):
                    fetch_pair(fars, page, kv_ref, 8 * (odd + block - group_index), sem)

            @pl.when((block == group_index) & (odd == 1))
            def _(block=block):
                fetch_pair((both_ref, core_ref), 16 + 4 * block, kv_ref, 8, sem)

    @pl.when(chip == 1)
    def _():
        place = jnp.where(has_old, 16, 0)
        fetch(one_ref, 0, kv_ref, place, 16, sem)
        fetch(one_core_ref, 0, kv_ref, place + 16, 16, sem)

    for h in range(heads):
        for copy in state_copies(h):
            copy.start()
    weight_copy = pltpu.make_async_copy(weight_ref, w_ref, weight_sem)
    weight_copy.start()

    bias_ref[...] = jnp.zeros_like(bias_ref)

    @pl.when(has_old)
    def _():
        bias_ref[0, :, :256] = old_bias(rows, group_index ^ 2)

        @pl.when(odd == 1)
        def _():
            bias_ref[0, :, 256:] = old_bias(rows, group_index)

    for copy in pool_loads:
        copy.wait()
    placed = jnp.int32(0)
    for r in range(requests):
        chosen, found = pages_here(table_ref, r, slots // 2, slots // 2, cap, pages)
        placed = placed + found
        for c in range(cap):

            @pl.when(found > c)
            def _(page=chosen[c], slot=r * cap + c):
                pltpu.make_async_copy(arrived_ref.at[slot, 0], key_pool.at[page], page_sem).start()
                pltpu.make_async_copy(arrived_ref.at[slot, 1], value_pool.at[page], page_sem).start()

    wait_rows(kv_ref, steps, 3, sem)
    lane = lax.broadcasted_iota(jnp.int32, (rows, 128), 1)

    def begin(h, most_ref):
        for copy in state_copies(h):
            copy.wait()
        most_ref[...] = jnp.where(lane < 64, stat_ref[h], masked_score)

    def finish(h):
        stat = stat_ref[h]
        top = top_ref[...]
        factor = jnp.exp(stat[:, :1] - top)
        sums = stat[:, 64:65] * factor + jnp.sum(sum_ref[...], axis=1, keepdims=True)
        inverse = 1.0 / sums
        old = factor * inverse
        mixed = acc_ref[h] * join([old, old]) + head_ref[...] * join([inverse, inverse])
        attended_ref[:, pl.ds(pl.multiple_of(h * 256, 256), 256)] = mixed.astype(jnp.bfloat16)

    attention(
        heads, steps, roped_ref, kv_ref, bias_ref, (s_0, s_1), (most_0, most_1), top_ref, sum_ref,
        lambda h: head_ref, begin, finish,
    )

    def settle(n, carry):
        pltpu.make_async_copy(arrived_ref.at[0, 0], key_pool.at[0], page_sem).wait()
        pltpu.make_async_copy(arrived_ref.at[0, 1], value_pool.at[0], page_sem).wait()
        return carry

    lax.fori_loop(0, placed, settle, 0)
    for copy in pool_stores:
        copy.start()
    weight_copy.wait()

    def project(n, carry):
        columns = pl.ds(pl.multiple_of(n * chunk, chunk), chunk)
        stage_ref[n] = jnp.dot(
            attended_ref[...], w_ref[:, columns], preferred_element_type=jnp.float32
        ).astype(jnp.bfloat16)
        pltpu.make_async_copy(stage_ref.at[n], hidden_ref.at[:, columns], out_sems.at[n]).start()
        return carry

    lax.fori_loop(0, chunks, project, 0)
    for n in range(chunks):
        pltpu.make_async_copy(
            stage_ref.at[n], hidden_ref.at[:, pl.ds(n * chunk, chunk)], out_sems.at[n]
        ).wait()
    for copy in pool_stores:
        copy.wait()


def second_part(page_table, lengths, cap, state, slots, weight, arrived, key_cache, value_cache):
    heads, rows, _ = state[0].shape
    width = weight.shape[1]
    chunk = 512
    return pl.pallas_call(
        lambda *refs: second_kernel(cap, *refs),
        out_shape=(
            pltpu.HBM((rows, width), jnp.bfloat16),
            pltpu.HBM(key_cache.shape, jnp.bfloat16),
            pltpu.HBM(value_cache.shape, jnp.bfloat16),
        ),
        in_specs=[smem_spec] * 2 + [hbm_spec] * 13,
        out_specs=(hbm_spec,) * 3,
        scratch_shapes=[
            pltpu.VMEM((heads, rows, 256), jnp.bfloat16),
            pltpu.VMEM((heads, rows, 256), jnp.float32),
            pltpu.VMEM((heads, rows, 128), jnp.float32),
        ]
        + working(rows, 3, 2)
        + [
            pltpu.VMEM((rows, 256), jnp.float32),
            pltpu.VMEM((rows, weight.shape[0]), jnp.bfloat16),
            pltpu.VMEM(weight.shape, jnp.bfloat16),
            pltpu.VMEM((width // chunk, rows, chunk), jnp.bfloat16),
            pltpu.VMEM(key_cache.shape, jnp.bfloat16),
            pltpu.VMEM(value_cache.shape, jnp.bfloat16),
            pltpu.SemaphoreType.DMA((3, heads)),
            pltpu.SemaphoreType.DMA,
            pltpu.SemaphoreType.DMA,
            pltpu.SemaphoreType.DMA((2,)),
            pltpu.SemaphoreType.DMA,
            pltpu.SemaphoreType.DMA((width // chunk,)),
        ],
        compiler_params=params(large_limit),
        name="attend_second",
    )(page_table, lengths, *in_hbm(*state, *slots, weight, arrived, key_cache, value_cache))


def body(queries, new_keys, new_values, key_cache, value_cache, out_weight, lengths, page_table):
    blk_count = lax.axis_size("blk")
    pages = key_cache.shape[0]
    window_pages = page_table.shape[1] // 2
    cap = (window_pages + blk_count - 1) // blk_count

    def other_core(value):
        return lax.ppermute(value, "group", [(0, 1), (1, 0), (2, 3), (3, 2)])

    def other_chip(value):
        return lax.ppermute(value, "group", [(0, 2), (2, 0), (1, 3), (3, 1)])

    old = pick_old(page_table, cap, key_cache, value_cache)
    old = lax.all_to_all(old, "blk", split_axis=0, concat_axis=0, tiled=True)
    old = old.reshape((blk_count * cap,) + old.shape[2:])
    both, one, two, cosine, sine = pack(
        page_table, lengths, blk_count, cap, pages, new_keys[0], new_values[0], old
    )
    one = other_chip(one)
    core = other_core(both)
    two = other_chip(two)
    roped = rotate_queries(queries[0], cosine, sine)
    acc, stat = first_part(lengths, roped, both, core)
    one_core = other_core(one)
    two_core = other_core(two)
    slots = (both, core, one, one_core, two, two_core)
    late_table, _ = lax.optimization_barrier((page_table, stat))
    new = pick_new(late_table, blk_count, cap, pages, slots)
    arrived = lax.all_to_all(new, "blk", split_axis=0, concat_axis=0, tiled=True)
    hidden, key_out, value_out = second_part(
        page_table, lengths, cap, (roped, acc, stat), slots, out_weight, arrived, key_cache, value_cache
    )
    return (hidden[None], key_out, value_out)


def solution(mesh):
    return jax.shard_map(
        body,
        mesh=mesh,
        in_specs=(
            P("blk", "group", None),
            P("blk", "group", None),
            P("blk", "group", None),
            P("blk", "group", None),
            P("blk", "group", None),
            P(),
            P(),
            P(),
        ),
        out_specs=(P("blk", "group", None), P("blk", "group", None), P("blk", "group", None)),
        check_vma=False,
    )
```

```python
import jax
import jax.numpy as jnp
import numpy as np
from jax import lax
from jax.experimental import pallas as pl
from jax.experimental.pallas import tpu as pltpu
from jax.sharding import PartitionSpec as P

masked_score = -1e30
step_keys = 512
step_slots = 16
hbm_spec = pl.BlockSpec(memory_space=pltpu.HBM)
smem_spec = pl.BlockSpec(memory_space=pltpu.SMEM)
vmem_spec = pl.BlockSpec(memory_space=pltpu.VMEM)
small_limit = 16 * 1024 * 1024
head_pair = 2
large_limit = 56 * 1024 * 1024


def params(limit):
    return pltpu.CompilerParams(vmem_limit_bytes=limit)


def in_hbm(*arrays):
    return [pltpu.with_memory_space_constraint(array, pltpu.HBM) for array in arrays]


def turn(values, cosine, sine):
    front = values[:, :128].astype(jnp.float32)
    return front * cosine + pltpu.roll(front, 64, 1) * sine


def join(pieces):
    return jnp.concatenate(pieces, axis=1)


def pages_here(table_ref, r, first, count, cap, pages):
    low = lax.axis_index("blk") * pages
    found = jnp.int32(0)
    chosen = [jnp.int32(0)] * cap
    for j in range(first, first + count):
        page = table_ref[r, j] - low
        inside = (page >= 0) & (page < pages)
        chosen = [jnp.where(inside & (found == c), page, chosen[c]) for c in range(cap)]
        found = found + inside.astype(jnp.int32)
    return chosen, found


def pick_old_kernel(table_ref, key_ref, value_ref, out_ref, sem):
    requests, cap = out_ref.shape[:2]
    for r in range(requests):
        chosen, _ = pages_here(table_ref, r, 0, table_ref.shape[1] // 2, cap, key_ref.shape[0])
        for c in range(cap):
            pltpu.make_async_copy(key_ref.at[chosen[c]], out_ref.at[r, c, 0], sem).start()
            pltpu.make_async_copy(value_ref.at[chosen[c]], out_ref.at[r, c, 1], sem).start()
    pltpu.make_async_copy(out_ref, out_ref, sem).wait()


def pick_old(page_table, cap, key_cache, value_cache):
    requests = page_table.shape[0]
    return pl.pallas_call(
        pick_old_kernel,
        out_shape=jax.ShapeDtypeStruct((requests, cap, 2) + key_cache.shape[1:], jnp.bfloat16),
        in_specs=[smem_spec, hbm_spec, hbm_spec],
        out_specs=vmem_spec,
        scratch_shapes=[pltpu.SemaphoreType.DMA],
        compiler_params=params(small_limit),
        name="pick_old",
    )(page_table, *in_hbm(key_cache, value_cache))


def owner_of(page, pages, owners):
    factor = (1 << 20) // pages + 1
    assert all((p * factor) >> 20 == p // pages for p in range(pages * owners))
    assert pages * owners * factor < 1 << 31
    return (page * factor) >> 20


def find_slots(table_ref, first, count, cap, pages, counts_ref):
    owners = counts_ref.shape[0]
    row = lax.axis_index("blk")
    for o in range(owners):
        counts_ref[o] = 0
    slots = []
    for j in range(count):
        owner = owner_of(table_ref[row, first + j], pages, owners)
        rank = counts_ref[owner]
        counts_ref[owner] = rank + 1
        slots.append(owner * cap + rank)
    return slots


def rotate_kernel(lengths_ref, freq_ref, keys_ref, values_ref, out_ref, cos_ref, sin_ref):
    rows = keys_ref.shape[0]
    slots = rows // 32
    start = lengths_ref[lax.axis_index("blk")] + lax.axis_index("group") * rows
    positions = start + lax.broadcasted_iota(jnp.int32, (rows, 128), 0)
    angles = positions.astype(jnp.float32) * freq_ref[...]
    lane = lax.broadcasted_iota(jnp.int32, (rows, 128), 1)
    cosine = jnp.cos(angles)
    sine = jnp.sin(angles)
    sine = jnp.where(lane < 64, -sine, sine)
    cos_ref[...] = cosine
    sin_ref[...] = sine
    keys = keys_ref[...]
    turned = join([turn(keys, cosine, sine).astype(jnp.bfloat16), keys[:, 128:]])
    out_ref[:, 0] = turned.reshape(slots, 32, 256)
    out_ref[:, 1] = values_ref[...].reshape(slots, 32, 256)


def rotate_keys(lengths, keys, values):
    rows, head_dim = keys.shape
    quarter = head_dim // 4
    freq_table = np.float32(10000.0) ** (-np.arange(quarter, dtype=np.float32) / np.float32(quarter))
    freq_table = np.concatenate([freq_table, freq_table])[None].astype(np.float32)
    return pl.pallas_call(
        rotate_kernel,
        out_shape=(
            jax.ShapeDtypeStruct((rows // 32, 2, 32, head_dim), jnp.bfloat16),
            jax.ShapeDtypeStruct((rows, 128), jnp.float32),
            jax.ShapeDtypeStruct((rows, 128), jnp.float32),
        ),
        in_specs=[smem_spec, vmem_spec, vmem_spec, vmem_spec],
        out_specs=(vmem_spec,) * 3,
        compiler_params=params(small_limit),
        name="rotate_keys",
    )(lengths, jnp.asarray(freq_table), keys, values)


def sort_kernel(pages, cap, table_ref, old_ref, out_ref, counts_ref, sem):
    count = out_ref.shape[0]
    for j, slot in enumerate(find_slots(table_ref, 0, count, cap, pages, counts_ref)):
        pltpu.make_async_copy(old_ref.at[slot], out_ref.at[j], sem).start()
    pltpu.make_async_copy(out_ref, out_ref, sem).wait()


def sort_old(page_table, blk_count, cap, pages, old):
    window = page_table.shape[1] // 2
    return pl.pallas_call(
        lambda *refs: sort_kernel(pages, cap, *refs),
        out_shape=jax.ShapeDtypeStruct((window,) + old.shape[1:], jnp.bfloat16),
        in_specs=[smem_spec, hbm_spec],
        out_specs=vmem_spec,
        scratch_shapes=[pltpu.SMEM((blk_count,), jnp.int32), pltpu.SemaphoreType.DMA],
        compiler_params=params(small_limit),
        name="sort_old",
    )(page_table, *in_hbm(old))


def pick_new_kernel(pages, cap, table_ref, own_ref, core_ref, far_ref, far_core_ref, out_ref, slots_ref, counts_ref, sem):
    count = slots_ref.shape[0]
    block_pages = count // 4
    group_index = lax.axis_index("group")
    for j, slot in enumerate(find_slots(table_ref, table_ref.shape[1] - count, count, cap, pages, counts_ref)):
        slots_ref[j] = slot
    for number, ref in enumerate((own_ref, core_ref, far_ref, far_core_ref)):
        block = group_index ^ number
        for place in range(block_pages):
            source = ref.at[4 * place + group_index]
            target = out_ref.at[slots_ref[block * block_pages + place]]
            pltpu.make_async_copy(source, target, sem).start()
    sent = out_ref.at[pl.ds(0, count)]
    pltpu.make_async_copy(sent, sent, sem).wait()


def pick_new(page_table, blk_count, cap, pages, sources):
    window = page_table.shape[1] // 2
    return pl.pallas_call(
        lambda *refs: pick_new_kernel(pages, cap, *refs),
        out_shape=jax.ShapeDtypeStruct((blk_count * cap,) + sources[0].shape[1:], jnp.bfloat16),
        in_specs=[smem_spec] + [hbm_spec] * 4,
        out_specs=vmem_spec,
        scratch_shapes=[
            pltpu.SMEM((window,), jnp.int32),
            pltpu.SMEM((blk_count,), jnp.int32),
            pltpu.SemaphoreType.DMA,
        ],
        compiler_params=params(small_limit),
        name="pick_new",
    )(page_table, *in_hbm(*sources))


def lane_fold(values, combine):
    total = values[:, :128]
    for start in range(128, values.shape[1], 128):
        total = combine(total, values[:, start : start + 128])
    return total


def old_bias(rows, quarter):
    row = lax.broadcasted_iota(jnp.int32, (rows, 256), 0)
    column = lax.broadcasted_iota(jnp.int32, (rows, 256), 1)
    held = quarter ^ (column // 128)
    position = ((column % 128) // 32) * 128 + 32 * held + column % 32
    return jnp.where(position > row, 0.0, masked_score)


def fetch(source, first, kv_ref, place, count, sem):
    for kind in range(2):
        pltpu.make_async_copy(
            source.at[pl.ds(first, count), kind], kv_ref.at[kind, pl.ds(place, count)], sem
        ).start()


def fetch_pair(sources, first, kv_ref, place, sem):
    fetch(sources[0], first, kv_ref, place, 4, sem)
    fetch(sources[1], first, kv_ref, place + 4, 4, sem)


def wait_rows(kv_ref, steps, most, sem):
    for n in range(1, most + 1):

        @pl.when(steps == n)
        def _(n=n):
            filled = kv_ref.at[:, pl.ds(0, n * step_slots)]
            pltpu.make_async_copy(filled, filled, sem).wait()


def attention(steps, roped_ref, kv_ref, bias_ref, s_refs, most_refs, top_ref, sum_ref, sum_of_values, begin, finish):
    items, rows, _ = roped_ref.shape
    last_bias = bias_ref.shape[0] - 1

    def block(kind, c):
        return kv_ref[kind, pl.ds(c * step_slots, step_slots)].reshape(step_keys, 256)

    def scores(t, c, which):
        result = lax.dot_general(
            roped_ref[t], block(0, c), (((1,), (1,)), ((), ())), preferred_element_type=jnp.float32
        )
        bias = bias_ref[jnp.minimum(c, last_bias)]
        result = (result.reshape(head_pair, rows // head_pair, step_keys) + bias).reshape(rows, step_keys)
        s_refs[which][c] = result
        most_refs[which][...] = jnp.maximum(most_refs[which][...], lane_fold(result, jnp.maximum))

    def weigh(c, which):
        weights = jnp.exp(s_refs[which][c] - join([top_ref[...]] * (step_keys // 128)))
        sum_ref[...] += lane_fold(weights, jnp.add)
        sum_of_values[...] += jnp.dot(
            weights.astype(jnp.bfloat16), block(1, c), preferred_element_type=jnp.float32
        )

    def settle(which):
        top_ref[...] = jnp.broadcast_to(
            jnp.max(most_refs[which][...], axis=1, keepdims=True), top_ref.shape
        )
        sum_ref[...] = jnp.zeros_like(sum_ref)
        sum_of_values[...] = jnp.zeros_like(sum_of_values)

    def loop(work):
        def step(c, carry):
            work(c)
            return carry

        lax.fori_loop(0, steps, step, 0)

    def one(t, which):
        begin(t + 1, most_refs[1 - which])
        settle(which)

        def work(c):
            weigh(c, which)
            scores(t + 1, c, 1 - which)

        loop(work)
        finish(t)

    def two(i, carry):
        one(2 * i, 0)
        one(2 * i + 1, 1)
        return carry

    begin(0, most_refs[0])
    loop(lambda c: scores(0, c, 0))
    pairs = (items - 1) // 2
    lax.fori_loop(0, pairs, two, 0)
    last = 2 * pairs
    if last < items - 1:
        one(last, 0)
        last += 1
    settle(last % 2)
    loop(lambda c: weigh(c, last % 2))
    finish(last)


def working(rows, steps, biases):
    return [
        pltpu.VMEM((2, steps * step_slots, 32, 256), jnp.bfloat16),
        pltpu.VMEM((steps, head_pair * rows, step_keys), jnp.float32),
        pltpu.VMEM((steps, head_pair * rows, step_keys), jnp.float32),
        pltpu.VMEM((head_pair * rows, 128), jnp.float32),
        pltpu.VMEM((head_pair * rows, 128), jnp.float32),
        pltpu.VMEM((head_pair * rows, 128), jnp.float32),
        pltpu.VMEM((head_pair * rows, 128), jnp.float32),
        pltpu.VMEM((head_pair * rows, 256), jnp.float32),
        pltpu.VMEM((biases, rows, step_keys), jnp.float32),
    ]


def state_shapes(items, rows):
    return [
        pltpu.VMEM((items, head_pair * rows, 256), jnp.bfloat16),
        pltpu.VMEM((items, head_pair * rows, 256), jnp.float32),
        pltpu.VMEM((items, head_pair * rows, 128), jnp.float32),
    ]


def state_out(items, rows):
    return (
        pltpu.HBM((items, head_pair * rows, 256), jnp.float32),
        pltpu.HBM((items, head_pair * rows, 128), jnp.float32),
    )


def cost(items, rows, keys):
    pairs = items * head_pair * rows * keys
    return pl.CostEstimate(flops=4 * pairs * 256, bytes_accessed=1 << 24, transcendentals=pairs)


def diagonal_kernel(
    query_ref, cos_ref, sin_ref, own_ref, roped_out, acc_out, stat_out,
    q_ref, roped_ref, acc_ref, stat_ref, kv_ref, s_0, s_1, most_0, most_1, top_ref, sum_ref, values_ref,
    bias_ref, query_sem, sem, out_sem,
):
    rows = q_ref.shape[0]
    items = roped_ref.shape[0]
    query_copy = pltpu.make_async_copy(query_ref, q_ref, query_sem)
    query_copy.start()
    fetch(own_ref, 0, kv_ref, 0, step_slots, sem)
    row = lax.broadcasted_iota(jnp.int32, (rows, step_keys), 0)
    column = lax.broadcasted_iota(jnp.int32, (rows, step_keys), 1)
    bias_ref[0] = jnp.where(column <= row, 0.0, masked_score)
    query_copy.wait()

    def rope(t, carry):
        for one in range(head_pair):
            raw = q_ref[:, pl.ds(pl.multiple_of((t * head_pair + one) * 256, 256), 256)]
            front = turn(raw, cos_ref[...], sin_ref[...])
            some = pl.ds(one * rows, rows)
            roped_ref[t, some, :128] = (front * 0.0625).astype(jnp.bfloat16)
            roped_ref[t, some, 128:] = raw[:, 128:] * jnp.bfloat16(0.0625)
        return carry

    lax.fori_loop(0, items, rope, 0)
    roped_copy = pltpu.make_async_copy(roped_ref, roped_out, query_sem)
    roped_copy.start()
    pltpu.make_async_copy(kv_ref, kv_ref, sem).wait()

    def begin(t, most_ref):
        most_ref[...] = jnp.full_like(most_ref, masked_score)

    def finish(t):
        lane = lax.broadcasted_iota(jnp.int32, stat_ref.shape[1:], 1)
        sums = jnp.sum(sum_ref[...], axis=1, keepdims=True)
        stat_ref[t] = jnp.where(lane < 64, top_ref[...], sums)
        acc_ref[t] = values_ref[...]
        pltpu.make_async_copy(acc_ref.at[t], acc_out.at[t], out_sem).start()
        pltpu.make_async_copy(stat_ref.at[t], stat_out.at[t], out_sem).start()

    attention(
        1, roped_ref, kv_ref, bias_ref, (s_0, s_1), (most_0, most_1), top_ref, sum_ref, values_ref,
        begin, finish,
    )
    roped_copy.wait()
    pltpu.make_async_copy(acc_ref, acc_out, out_sem).wait()
    pltpu.make_async_copy(stat_ref, stat_out, out_sem).wait()


def diagonal_part(queries, cosine, sine, own):
    rows, width = queries.shape
    items = width // (256 * head_pair)
    return pl.pallas_call(
        diagonal_kernel,
        out_shape=(pltpu.HBM((items, head_pair * rows, 256), jnp.bfloat16),) + state_out(items, rows),
        in_specs=[hbm_spec, vmem_spec, vmem_spec, hbm_spec],
        out_specs=(hbm_spec,) * 3,
        scratch_shapes=[pltpu.VMEM((rows, width), jnp.bfloat16)]
        + state_shapes(items, rows)
        + working(rows, 1, 1)
        + [pltpu.SemaphoreType.DMA] * 3,
        compiler_params=params(large_limit),
        cost_estimate=cost(items, rows, 512),
        name="attend_diagonal",
    )(*in_hbm(queries), cosine, sine, *in_hbm(own))


def state_copies(t, sources, targets, sems):
    return [
        pltpu.make_async_copy(source.at[t], target.at[t], sems.at[number, t])
        for number, (source, target) in enumerate(zip(sources, targets))
    ]


def near_kernel(
    lengths_ref, roped_in, acc_in, stat_in, core_ref, far_ref, far_core_ref, old_ref, old_core_ref,
    acc_out, stat_out,
    roped_ref, acc_ref, stat_ref, kv_ref, s_0, s_1, most_0, most_1, top_ref, sum_ref, values_ref,
    bias_ref, state_sems, sem, out_sem,
):
    group_index = lax.axis_index("group")
    has_old = lengths_ref[lax.axis_index("blk")] > 0
    items = roped_ref.shape[0]
    rows = bias_ref.shape[1]
    odd = group_index % 2
    chip = group_index // 2
    steps = jnp.where(has_old, 2 + chip, odd + 2 * chip)
    olds = (old_ref, old_core_ref)

    @pl.when(odd == 1)
    def _():
        fetch(core_ref, 0, kv_ref, 0, 16, sem)

    @pl.when(has_old)
    def _():
        for block in range(4):

            @pl.when((block == group_index) & (odd == 0))
            def _(block=block):
                fetch_pair(olds, 4 * block, kv_ref, 0, sem)

            @pl.when(block > group_index)
            def _(block=block):
                fetch_pair(olds, 4 * block, kv_ref, 8 * (odd + block - group_index), sem)

    @pl.when(chip == 1)
    def _():
        place = jnp.where(has_old, 16, 16 * odd)
        fetch(far_ref, 0, kv_ref, place, 16, sem)
        fetch(far_core_ref, 0, kv_ref, place + 16, 16, sem)

    def copies(t):
        return state_copies(t, (roped_in, stat_in, acc_in), (roped_ref, stat_ref, acc_ref), state_sems)

    for t in range(items):
        for copy in copies(t):
            copy.start()
    bias_ref[...] = jnp.zeros_like(bias_ref)

    @pl.when(has_old & (odd == 0))
    def _():
        bias_ref[0, :, :256] = old_bias(rows, group_index)

    wait_rows(kv_ref, steps, 3, sem)
    lane = lax.broadcasted_iota(jnp.int32, stat_ref.shape[1:], 1)

    def begin(t, most_ref):
        for copy in copies(t):
            copy.wait()
        most_ref[...] = jnp.where(lane < 64, stat_ref[t], masked_score)

    def finish(t):
        stat = stat_ref[t]
        top = top_ref[...]
        factor = jnp.exp(stat[:, :1] - top)
        sums = stat[:, 64:65] * factor + jnp.sum(sum_ref[...], axis=1, keepdims=True)
        stat_ref[t] = jnp.where(lane < 64, top, sums)
        acc_ref[t] = acc_ref[t] * join([factor, factor]) + values_ref[...]
        pltpu.make_async_copy(acc_ref.at[t], acc_out.at[t], out_sem).start()
        pltpu.make_async_copy(stat_ref.at[t], stat_out.at[t], out_sem).start()

    attention(
        steps, roped_ref, kv_ref, bias_ref, (s_0, s_1), (most_0, most_1), top_ref, sum_ref, values_ref,
        begin, finish,
    )
    pltpu.make_async_copy(acc_ref, acc_out, out_sem).wait()
    pltpu.make_async_copy(stat_ref, stat_out, out_sem).wait()


def near_part(lengths, state, slots):
    items, pair_rows, _ = state[0].shape
    rows = pair_rows // head_pair
    return pl.pallas_call(
        near_kernel,
        out_shape=state_out(items, rows),
        in_specs=[smem_spec] + [hbm_spec] * 8,
        out_specs=(hbm_spec,) * 2,
        scratch_shapes=state_shapes(items, rows)
        + working(rows, 3, 2)
        + [pltpu.SemaphoreType.DMA((3, items))]
        + [pltpu.SemaphoreType.DMA] * 2,
        compiler_params=params(large_limit),
        cost_estimate=cost(items, rows, 1024),
        name="attend_near",
    )(lengths, *in_hbm(*state, *slots))


def far_kernel(
    cap, table_ref, lengths_ref, roped_in, acc_in, stat_in, old_ref, old_core_ref, far_ref, far_core_ref,
    weight_ref, arrived_ref, key_ref, value_ref,
    hidden_ref, key_out_ref, value_out_ref,
    roped_ref, acc_ref, stat_ref, kv_ref, s_0, s_1, most_0, most_1, top_ref, sum_ref, values_ref,
    bias_ref, attended_ref, w_ref, stage_ref, key_pool, value_pool,
    state_sems, sem, weight_sem, pool_sems, page_sem, out_sems,
):
    group_index = lax.axis_index("group")
    has_old = lengths_ref[lax.axis_index("blk")] > 0
    pages = key_ref.shape[0]
    requests, slots = table_ref.shape
    items = roped_ref.shape[0]
    rows = bias_ref.shape[1]
    chunks = stage_ref.shape[0]
    chunk = stage_ref.shape[2]
    odd = group_index % 2
    steps = jnp.where(has_old, 2 - group_index // 2, 0)

    def copies(t):
        return state_copies(t, (roped_in, stat_in, acc_in), (roped_ref, stat_ref, acc_ref), state_sems)

    pool_loads = [
        pltpu.make_async_copy(key_ref, key_pool, pool_sems.at[0]),
        pltpu.make_async_copy(value_ref, value_pool, pool_sems.at[1]),
    ]
    pool_stores = [
        pltpu.make_async_copy(key_pool, key_out_ref, pool_sems.at[0]),
        pltpu.make_async_copy(value_pool, value_out_ref, pool_sems.at[1]),
    ]
    for copy in pool_loads:
        copy.start()

    @pl.when(has_old)
    def _():
        for block in range(4):

            @pl.when(block == group_index)
            def _(block=block):
                fetch_pair((far_ref, far_core_ref), 4 * block, kv_ref, 0, sem)

            @pl.when((block == group_index) & (odd == 1))
            def _(block=block):
                fetch_pair((old_ref, old_core_ref), 4 * block, kv_ref, 8, sem)

            @pl.when(block > group_index)
            def _(block=block):
                place = 8 * (odd + block - group_index)
                fetch_pair((far_ref, far_core_ref), 4 * block, kv_ref, place, sem)

    for t in range(items):
        for copy in copies(t):
            copy.start()
    weight_copy = pltpu.make_async_copy(weight_ref, w_ref, weight_sem)
    weight_copy.start()

    bias_ref[1] = jnp.zeros(bias_ref.shape[1:], jnp.float32)
    bias_ref[0, :, :256] = old_bias(rows, group_index ^ 2)
    bias_ref[0, :, 256:] = jnp.zeros((rows, 256), jnp.float32)

    @pl.when(odd == 1)
    def _():
        bias_ref[0, :, 256:] = old_bias(rows, group_index)

    for copy in pool_loads:
        copy.wait()
    placed = jnp.int32(0)
    for r in range(requests):
        chosen, found = pages_here(table_ref, r, slots // 2, slots // 2, cap, pages)
        placed = placed + found
        for c in range(cap):

            @pl.when(found > c)
            def _(page=chosen[c], slot=r * cap + c):
                pltpu.make_async_copy(arrived_ref.at[slot, 0], key_pool.at[page], page_sem).start()
                pltpu.make_async_copy(arrived_ref.at[slot, 1], value_pool.at[page], page_sem).start()

    wait_rows(kv_ref, steps, 2, sem)
    lane = lax.broadcasted_iota(jnp.int32, stat_ref.shape[1:], 1)

    def begin(t, most_ref):
        for copy in copies(t):
            copy.wait()
        most_ref[...] = jnp.where(lane < 64, stat_ref[t], masked_score)

    def finish(t):
        stat = stat_ref[t]
        factor = jnp.exp(stat[:, :1] - top_ref[...])
        sums = stat[:, 64:65] * factor + jnp.sum(sum_ref[...], axis=1, keepdims=True)
        inverse = 1.0 / sums
        old = factor * inverse
        mixed = acc_ref[t] * join([old, old]) + values_ref[...] * join([inverse, inverse])
        mixed = mixed.astype(jnp.bfloat16)
        for one in range(head_pair):
            column = pl.multiple_of((t * head_pair + one) * 256, 256)
            attended_ref[:, pl.ds(column, 256)] = mixed[one * rows : (one + 1) * rows]

    attention(
        steps, roped_ref, kv_ref, bias_ref, (s_0, s_1), (most_0, most_1), top_ref, sum_ref, values_ref,
        begin, finish,
    )

    def settle(n, carry):
        pltpu.make_async_copy(arrived_ref.at[0, 0], key_pool.at[0], page_sem).wait()
        pltpu.make_async_copy(arrived_ref.at[0, 1], value_pool.at[0], page_sem).wait()
        return carry

    lax.fori_loop(0, placed, settle, 0)
    for copy in pool_stores:
        copy.start()
    weight_copy.wait()

    def project(n, carry):
        columns = pl.ds(pl.multiple_of(n * chunk, chunk), chunk)
        stage_ref[n] = jnp.dot(
            attended_ref[...], w_ref[:, columns], preferred_element_type=jnp.float32
        ).astype(jnp.bfloat16)
        pltpu.make_async_copy(stage_ref.at[n], hidden_ref.at[:, columns], out_sems.at[n]).start()
        return carry

    lax.fori_loop(0, chunks, project, 0)
    for n in range(chunks):
        pltpu.make_async_copy(
            stage_ref.at[n], hidden_ref.at[:, pl.ds(n * chunk, chunk)], out_sems.at[n]
        ).wait()
    for copy in pool_stores:
        copy.wait()


def far_part(page_table, lengths, cap, state, slots, weight, arrived, key_cache, value_cache):
    items, pair_rows, _ = state[0].shape
    rows = pair_rows // head_pair
    width = weight.shape[1]
    chunk = 512
    return pl.pallas_call(
        lambda *refs: far_kernel(cap, *refs),
        out_shape=(
            pltpu.HBM((rows, width), jnp.bfloat16),
            pltpu.HBM(key_cache.shape, jnp.bfloat16),
            pltpu.HBM(value_cache.shape, jnp.bfloat16),
        ),
        in_specs=[smem_spec] * 2 + [hbm_spec] * 11,
        out_specs=(hbm_spec,) * 3,
        scratch_shapes=state_shapes(items, rows)
        + working(rows, 2, 2)
        + [
            pltpu.VMEM((rows, weight.shape[0]), jnp.bfloat16),
            pltpu.VMEM(weight.shape, jnp.bfloat16),
            pltpu.VMEM((width // chunk, rows, chunk), jnp.bfloat16),
            pltpu.VMEM(key_cache.shape, jnp.bfloat16),
            pltpu.VMEM(value_cache.shape, jnp.bfloat16),
            pltpu.SemaphoreType.DMA((3, items)),
            pltpu.SemaphoreType.DMA,
            pltpu.SemaphoreType.DMA,
            pltpu.SemaphoreType.DMA((2,)),
            pltpu.SemaphoreType.DMA,
            pltpu.SemaphoreType.DMA((width // chunk,)),
        ],
        compiler_params=params(large_limit),
        cost_estimate=cost(items, rows, 1536),
        name="attend_far",
    )(page_table, lengths, *in_hbm(*state, *slots, weight, arrived, key_cache, value_cache))


def after(value, *others):
    return lax.optimization_barrier((value,) + others)[0]


def body(queries, new_keys, new_values, key_cache, value_cache, out_weight, lengths, page_table):
    blk_count = lax.axis_size("blk")
    pages = key_cache.shape[0]
    window_pages = page_table.shape[1] // 2
    cap = (window_pages + blk_count - 1) // blk_count

    def other_core(value):
        return lax.ppermute(value, "group", [(0, 1), (1, 0), (2, 3), (3, 2)])

    def other_chip(value):
        return lax.ppermute(value, "group", [(0, 2), (2, 0), (1, 3), (3, 1)])

    picked = pick_old(page_table, cap, key_cache, value_cache)
    old = lax.all_to_all(picked, "blk", split_axis=0, concat_axis=0, tiled=True)
    old = old.reshape((blk_count * cap,) + old.shape[2:])

    fresh, cosine, sine = rotate_keys(lengths, new_keys[0], new_values[0])
    fresh_far = other_chip(fresh)
    fresh_core = other_core(fresh)
    roped, acc, stat = diagonal_part(after(queries[0], picked), cosine, sine, fresh)

    old = sort_old(after(page_table, stat), blk_count, cap, pages, old)
    old_far = other_chip(old)
    old_core = other_core(old)
    fresh_far_core = other_core(fresh_far)
    new = pick_new(page_table, blk_count, cap, pages, (fresh, fresh_core, fresh_far, fresh_far_core))
    arrived = lax.all_to_all(new, "blk", split_axis=0, concat_axis=0, tiled=True)
    acc, stat = near_part(
        after(lengths, new), (roped, acc, stat), (fresh_core, fresh_far, fresh_far_core, old, old_core)
    )
    old_far_core = other_core(old_far)
    hidden, key_out, value_out = far_part(
        page_table, lengths, cap, (roped, acc, stat), (old, old_core, old_far, old_far_core),
        out_weight, arrived, key_cache, value_cache,
    )
    return (hidden[None], key_out, value_out)


def solution(mesh):
    return jax.shard_map(
        body,
        mesh=mesh,
        in_specs=(
            P("blk", "group", None),
            P("blk", "group", None),
            P("blk", "group", None),
            P("blk", "group", None),
            P("blk", "group", None),
            P(),
            P(),
            P(),
        ),
        out_specs=(P("blk", "group", None), P("blk", "group", None), P("blk", "group", None)),
        check_vma=False,
    )
```

```python
import jax
import jax.numpy as jnp
import numpy as np
from jax import lax
from jax.experimental import pallas as pl
from jax.experimental.pallas import tpu as pltpu
from jax.sharding import PartitionSpec as P

masked_score = -1e30
step_keys = 512
step_slots = 16
any_spec = pl.BlockSpec(memory_space=pl.ANY)
hbm_spec = pl.BlockSpec(memory_space=pltpu.HBM)
smem_spec = pl.BlockSpec(memory_space=pltpu.SMEM)
vmem_spec = pl.BlockSpec(memory_space=pltpu.VMEM)
small_limit = 16 * 1024 * 1024
head_pair = 2
large_limit = 58 * 1024 * 1024


def params(limit):
    return pltpu.CompilerParams(vmem_limit_bytes=limit)


def in_hbm(*arrays):
    return [pltpu.with_memory_space_constraint(array, pltpu.HBM) for array in arrays]


def turn(values, cosine, sine):
    front = values[:, :128].astype(jnp.float32)
    return front * cosine + pltpu.roll(front, 64, 1) * sine


def join(pieces):
    return jnp.concatenate(pieces, axis=1)


def pages_here(table_ref, r, first, count, cap, pages):
    low = lax.axis_index("blk") * pages
    found = jnp.int32(0)
    chosen = [jnp.int32(0)] * cap
    for j in range(first, first + count):
        page = table_ref[r, j] - low
        inside = (page >= 0) & (page < pages)
        chosen = [jnp.where(inside & (found == c), page, chosen[c]) for c in range(cap)]
        found = found + inside.astype(jnp.int32)
    return chosen, found


def pick_old_kernel(table_ref, key_ref, value_ref, out_ref, sem):
    requests, cap = out_ref.shape[:2]
    for r in range(requests):
        chosen, _ = pages_here(table_ref, r, 0, table_ref.shape[1] // 2, cap, key_ref.shape[0])
        for c in range(cap):
            pltpu.make_async_copy(key_ref.at[chosen[c]], out_ref.at[r, c, 0], sem).start()
            pltpu.make_async_copy(value_ref.at[chosen[c]], out_ref.at[r, c, 1], sem).start()
    pltpu.make_async_copy(out_ref, out_ref, sem).wait()


def pick_old(page_table, cap, key_cache, value_cache):
    requests = page_table.shape[0]
    return pl.pallas_call(
        pick_old_kernel,
        out_shape=jax.ShapeDtypeStruct((requests, cap, 2) + key_cache.shape[1:], jnp.bfloat16),
        in_specs=[smem_spec, hbm_spec, hbm_spec],
        out_specs=vmem_spec,
        scratch_shapes=[pltpu.SemaphoreType.DMA],
        compiler_params=params(small_limit),
        name="pick_old",
    )(page_table, *in_hbm(key_cache, value_cache))


def owner_of(page, pages, owners):
    factor = (1 << 20) // pages + 1
    assert all((p * factor) >> 20 == p // pages for p in range(pages * owners))
    assert pages * owners * factor < 1 << 31
    return (page * factor) >> 20


def find_slots(table_ref, first, count, cap, pages, counts_ref):
    owners = counts_ref.shape[0]
    row = lax.axis_index("blk")
    for o in range(owners):
        counts_ref[o] = 0
    slots = []
    for j in range(count):
        owner = owner_of(table_ref[row, first + j], pages, owners)
        rank = counts_ref[owner]
        counts_ref[owner] = rank + 1
        slots.append(owner * cap + rank)
    return slots


def rotate_kernel(lengths_ref, freq_ref, keys_ref, values_ref, out_ref, cos_ref, sin_ref):
    rows = keys_ref.shape[0]
    slots = rows // 32
    start = lengths_ref[lax.axis_index("blk")] + lax.axis_index("group") * rows
    positions = start + lax.broadcasted_iota(jnp.int32, (rows, 128), 0)
    angles = positions.astype(jnp.float32) * freq_ref[...]
    lane = lax.broadcasted_iota(jnp.int32, (rows, 128), 1)
    cosine = jnp.cos(angles)
    sine = jnp.sin(angles)
    sine = jnp.where(lane < 64, -sine, sine)
    cos_ref[...] = cosine
    sin_ref[...] = sine
    keys = keys_ref[...]
    turned = join([turn(keys, cosine, sine).astype(jnp.bfloat16), keys[:, 128:]])
    out_ref[:, 0] = turned.reshape(slots, 32, 256)
    out_ref[:, 1] = values_ref[...].reshape(slots, 32, 256)


def rotate_keys(lengths, keys, values):
    rows, head_dim = keys.shape
    quarter = head_dim // 4
    freq_table = np.float32(10000.0) ** (-np.arange(quarter, dtype=np.float32) / np.float32(quarter))
    freq_table = np.concatenate([freq_table, freq_table])[None].astype(np.float32)
    return pl.pallas_call(
        rotate_kernel,
        out_shape=(
            pltpu.HBM((rows // 32, 2, 32, head_dim), jnp.bfloat16),
            pltpu.HBM((rows, 128), jnp.float32),
            pltpu.HBM((rows, 128), jnp.float32),
        ),
        in_specs=[smem_spec, vmem_spec, vmem_spec, vmem_spec],
        out_specs=(vmem_spec,) * 3,
        compiler_params=params(small_limit),
        name="rotate_keys",
    )(lengths, jnp.asarray(freq_table), keys, values)


def sort_kernel(pages, cap, table_ref, old_ref, out_ref, counts_ref, sem):
    count = out_ref.shape[0]
    for j, slot in enumerate(find_slots(table_ref, 0, count, cap, pages, counts_ref)):
        pltpu.make_async_copy(old_ref.at[slot], out_ref.at[j], sem).start()
    pltpu.make_async_copy(out_ref, out_ref, sem).wait()


def sort_old(page_table, blk_count, cap, pages, old):
    window = page_table.shape[1] // 2
    return pl.pallas_call(
        lambda *refs: sort_kernel(pages, cap, *refs),
        out_shape=jax.ShapeDtypeStruct((window,) + old.shape[1:], jnp.bfloat16),
        in_specs=[smem_spec, hbm_spec],
        out_specs=vmem_spec,
        scratch_shapes=[pltpu.SMEM((blk_count,), jnp.int32), pltpu.SemaphoreType.DMA],
        compiler_params=params(small_limit),
        name="sort_old",
    )(page_table, *in_hbm(old))


def pick_new_kernel(pages, cap, table_ref, own_ref, core_ref, far_ref, far_core_ref, out_ref, slots_ref, counts_ref, sem):
    count = slots_ref.shape[0]
    block_pages = count // 4
    group_index = lax.axis_index("group")
    for j, slot in enumerate(find_slots(table_ref, table_ref.shape[1] - count, count, cap, pages, counts_ref)):
        slots_ref[j] = slot
    for number, ref in enumerate((own_ref, core_ref, far_ref, far_core_ref)):
        block = group_index ^ number
        for place in range(block_pages):
            source = ref.at[4 * place + group_index]
            target = out_ref.at[slots_ref[block * block_pages + place]]
            pltpu.make_async_copy(source, target, sem).start()
    sent = out_ref.at[pl.ds(0, count)]
    pltpu.make_async_copy(sent, sent, sem).wait()


def pick_new(page_table, blk_count, cap, pages, sources):
    window = page_table.shape[1] // 2
    return pl.pallas_call(
        lambda *refs: pick_new_kernel(pages, cap, *refs),
        out_shape=jax.ShapeDtypeStruct((blk_count * cap,) + sources[0].shape[1:], jnp.bfloat16),
        in_specs=[smem_spec] + [any_spec] * 4,
        out_specs=vmem_spec,
        scratch_shapes=[
            pltpu.SMEM((window,), jnp.int32),
            pltpu.SMEM((blk_count,), jnp.int32),
            pltpu.SemaphoreType.DMA,
        ],
        compiler_params=params(small_limit),
        name="pick_new",
    )(page_table, *sources)


def lane_fold(values, combine):
    total = values[:, :128]
    for start in range(128, values.shape[1], 128):
        total = combine(total, values[:, start : start + 128])
    return total


def old_bias(rows, quarter):
    row = lax.broadcasted_iota(jnp.int32, (rows, 256), 0)
    column = lax.broadcasted_iota(jnp.int32, (rows, 256), 1)
    held = quarter ^ (column // 128)
    position = ((column % 128) // 32) * 128 + 32 * held + column % 32
    return jnp.where(position > row, 0.0, masked_score)


def fetch(source, first, kv_ref, place, count, sem):
    for kind in range(2):
        pltpu.make_async_copy(
            source.at[pl.ds(first, count), kind], kv_ref.at[kind, pl.ds(place, count)], sem
        ).start()


def fetch_pair(sources, first, kv_ref, place, sem):
    fetch(sources[0], first, kv_ref, place, 4, sem)
    fetch(sources[1], first, kv_ref, place + 4, 4, sem)


def wait_rows(kv_ref, steps, most, sem):
    for n in range(1, most + 1):

        @pl.when(steps == n)
        def _(n=n):
            filled = kv_ref.at[:, pl.ds(0, n * step_slots)]
            pltpu.make_async_copy(filled, filled, sem).wait()


def attention(steps, roped_ref, kv_ref, bias_ref, s_refs, most_refs, top_ref, sum_ref, sum_of_values, begin, finish):
    items, rows, _ = roped_ref.shape
    last_bias = bias_ref.shape[0] - 1

    def block(kind, c):
        return kv_ref[kind, pl.ds(c * step_slots, step_slots)].reshape(step_keys, 256)

    def scores(t, c, which):
        result = lax.dot_general(
            roped_ref[t], block(0, c), (((1,), (1,)), ((), ())), preferred_element_type=jnp.float32
        )
        bias = bias_ref[jnp.minimum(c, last_bias)]
        result = (result.reshape(head_pair, rows // head_pair, step_keys) + bias).reshape(rows, step_keys)
        s_refs[which][c] = result
        most_refs[which][...] = jnp.maximum(most_refs[which][...], lane_fold(result, jnp.maximum))

    def weigh(c, which):
        weights = jnp.exp(s_refs[which][c] - join([top_ref[...]] * (step_keys // 128)))
        sum_ref[...] += lane_fold(weights, jnp.add)
        sum_of_values[...] += jnp.dot(
            weights.astype(jnp.bfloat16), block(1, c), preferred_element_type=jnp.float32
        )

    def settle(which):
        top_ref[...] = jnp.broadcast_to(
            jnp.max(most_refs[which][...], axis=1, keepdims=True), top_ref.shape
        )
        sum_ref[...] = jnp.zeros_like(sum_ref)
        sum_of_values[...] = jnp.zeros_like(sum_of_values)

    def loop(work):
        def step(c, carry):
            work(c)
            return carry

        lax.fori_loop(0, steps, step, 0)

    def one(t, which):
        begin(t + 1, most_refs[1 - which])
        settle(which)

        def work(c):
            weigh(c, which)
            scores(t + 1, c, 1 - which)

        loop(work)
        finish(t)

    def two(i, carry):
        one(2 * i, 0)
        one(2 * i + 1, 1)
        return carry

    begin(0, most_refs[0])
    loop(lambda c: scores(0, c, 0))
    pairs = (items - 1) // 2
    lax.fori_loop(0, pairs, two, 0)
    last = 2 * pairs
    if last < items - 1:
        one(last, 0)
        last += 1
    settle(last % 2)
    loop(lambda c: weigh(c, last % 2))
    finish(last)


def working(rows, steps, biases):
    return [
        pltpu.VMEM((2, steps * step_slots, 32, 256), jnp.bfloat16),
        pltpu.VMEM((steps, head_pair * rows, step_keys), jnp.float32),
        pltpu.VMEM((steps, head_pair * rows, step_keys), jnp.float32),
        pltpu.VMEM((head_pair * rows, 128), jnp.float32),
        pltpu.VMEM((head_pair * rows, 128), jnp.float32),
        pltpu.VMEM((head_pair * rows, 128), jnp.float32),
        pltpu.VMEM((head_pair * rows, 128), jnp.float32),
        pltpu.VMEM((head_pair * rows, 256), jnp.float32),
        pltpu.VMEM((biases, rows, step_keys), jnp.float32),
    ]


def state_shapes(items, rows):
    return [
        pltpu.VMEM((items, head_pair * rows, 256), jnp.bfloat16),
        pltpu.VMEM((items, head_pair * rows, 256), jnp.float32),
        pltpu.VMEM((items, head_pair * rows, 128), jnp.float32),
    ]


def state_out(items, rows):
    return (
        pltpu.HBM((items, head_pair * rows, 256), jnp.float32),
        pltpu.HBM((items, head_pair * rows, 128), jnp.float32),
    )


def cost(items, rows, keys):
    pairs = items * head_pair * rows * keys
    return pl.CostEstimate(flops=4 * pairs * 256, bytes_accessed=1 << 24, transcendentals=pairs)


def diagonal_kernel(
    query_ref, cos_ref, sin_ref, own_ref, roped_out, acc_out, stat_out,
    q_ref, roped_ref, acc_ref, stat_ref, kv_ref, s_0, s_1, most_0, most_1, top_ref, sum_ref, values_ref,
    bias_ref, query_sem, sem, out_sem,
):
    rows = q_ref.shape[0]
    items = roped_ref.shape[0]
    query_copy = pltpu.make_async_copy(query_ref, q_ref, query_sem)
    query_copy.start()
    fetch(own_ref, 0, kv_ref, 0, step_slots, sem)
    row = lax.broadcasted_iota(jnp.int32, (rows, step_keys), 0)
    column = lax.broadcasted_iota(jnp.int32, (rows, step_keys), 1)
    bias_ref[0] = jnp.where(column <= row, 0.0, masked_score)
    query_copy.wait()

    def rope(t, carry):
        for one in range(head_pair):
            raw = q_ref[:, pl.ds(pl.multiple_of((t * head_pair + one) * 256, 256), 256)]
            front = turn(raw, cos_ref[...], sin_ref[...])
            some = pl.ds(one * rows, rows)
            roped_ref[t, some, :128] = (front * 0.0625).astype(jnp.bfloat16)
            roped_ref[t, some, 128:] = raw[:, 128:] * jnp.bfloat16(0.0625)
        return carry

    lax.fori_loop(0, items, rope, 0)
    roped_copy = pltpu.make_async_copy(roped_ref, roped_out, query_sem)
    roped_copy.start()
    pltpu.make_async_copy(kv_ref, kv_ref, sem).wait()

    def begin(t, most_ref):
        most_ref[...] = jnp.full_like(most_ref, masked_score)

    def finish(t):
        lane = lax.broadcasted_iota(jnp.int32, stat_ref.shape[1:], 1)
        sums = jnp.sum(sum_ref[...], axis=1, keepdims=True)
        stat_ref[t] = jnp.where(lane < 64, top_ref[...], sums)
        acc_ref[t] = values_ref[...]
        pltpu.make_async_copy(acc_ref.at[t], acc_out.at[t], out_sem).start()
        pltpu.make_async_copy(stat_ref.at[t], stat_out.at[t], out_sem).start()

    attention(
        1, roped_ref, kv_ref, bias_ref, (s_0, s_1), (most_0, most_1), top_ref, sum_ref, values_ref,
        begin, finish,
    )
    roped_copy.wait()
    pltpu.make_async_copy(acc_ref, acc_out, out_sem).wait()
    pltpu.make_async_copy(stat_ref, stat_out, out_sem).wait()


def diagonal_part(queries, cosine, sine, own):
    rows, width = queries.shape
    items = width // (256 * head_pair)
    return pl.pallas_call(
        diagonal_kernel,
        out_shape=(pltpu.HBM((items, head_pair * rows, 256), jnp.bfloat16),) + state_out(items, rows),
        in_specs=[hbm_spec, vmem_spec, vmem_spec, hbm_spec],
        out_specs=(hbm_spec,) * 3,
        scratch_shapes=[pltpu.VMEM((rows, width), jnp.bfloat16)]
        + state_shapes(items, rows)
        + working(rows, 1, 1)
        + [pltpu.SemaphoreType.DMA] * 3,
        compiler_params=params(large_limit),
        cost_estimate=cost(items, rows, 512),
        name="attend_diagonal",
    )(*in_hbm(queries), cosine, sine, *in_hbm(own))


def rest_kernel(
    cap, table_ref, lengths_ref, roped_in, acc_in, stat_in, core_ref, far_ref, far_core_ref,
    old_ref, old_core_ref, old_far_ref, old_far_core_ref, weight_ref, arrived_ref, key_ref, value_ref,
    hidden_ref, key_out_ref, value_out_ref,
    roped_ref, acc_ref, stat_ref, kv_ref, s_0, s_1, most_0, most_1, top_ref, sum_ref, values_ref,
    bias_ref, w_ref, stage_ref, key_pool, value_pool,
    state_sems, sem, weight_sem, pool_sems, page_sem, out_sems,
):
    group_index = lax.axis_index("group")
    has_old = lengths_ref[lax.axis_index("blk")] > 0
    pages = key_ref.shape[0]
    requests, slots = table_ref.shape
    items = roped_ref.shape[0]
    rows = bias_ref.shape[1]
    chunk = stage_ref.shape[2]
    chunks = w_ref.shape[1] // chunk
    odd = group_index % 2
    chip = group_index // 2
    steps = jnp.where(has_old, 4, odd + 2 * chip)
    base = jnp.where(has_old, 16, 0)
    near = (old_ref, old_core_ref)
    far = (old_far_ref, old_far_core_ref)

    def copies(t):
        return [
            pltpu.make_async_copy(source.at[t], target.at[t], state_sems.at[number, t])
            for number, (source, target) in enumerate(
                ((roped_in, roped_ref), (stat_in, stat_ref), (acc_in, acc_ref))
            )
        ]

    pool_loads = [
        pltpu.make_async_copy(key_ref, key_pool, pool_sems.at[0]),
        pltpu.make_async_copy(value_ref, value_pool, pool_sems.at[1]),
    ]
    pool_stores = [
        pltpu.make_async_copy(key_pool, key_out_ref, pool_sems.at[0]),
        pltpu.make_async_copy(value_pool, value_out_ref, pool_sems.at[1]),
    ]
    for copy in copies(0):
        copy.start()

    @pl.when(odd == 1)
    def _():
        fetch(core_ref, 0, kv_ref, base, 16, sem)

    @pl.when(chip == 1)
    def _():
        place = base + 16 * jnp.where(has_old, 1, odd)
        fetch(far_ref, 0, kv_ref, place, 16, sem)
        fetch(far_core_ref, 0, kv_ref, place + 16, 16, sem)

    @pl.when(has_old)
    def _():
        for block in range(4):

            @pl.when(block >= group_index)
            def _(block=block):
                gap = jnp.where(block == group_index, 0, odd)
                place = 16 * (gap + block - group_index)
                fetch_pair(near, 4 * block, kv_ref, place, sem)
                fetch_pair(far, 4 * block, kv_ref, place + 8, sem)

    for copy in pool_loads:
        copy.start()
    for t in range(1, items):
        for copy in copies(t):
            copy.start()
    weight_copy = pltpu.make_async_copy(weight_ref, w_ref, weight_sem)
    weight_copy.start()

    bias_ref[...] = jnp.zeros_like(bias_ref)

    @pl.when(has_old)
    def _():
        bias_ref[0, :, :256] = old_bias(rows, group_index)
        bias_ref[0, :, 256:] = old_bias(rows, group_index ^ 2)

    for copy in pool_loads:
        copy.wait()
    placed = jnp.int32(0)
    for r in range(requests):
        chosen, found = pages_here(table_ref, r, slots // 2, slots // 2, cap, pages)
        placed = placed + found
        for c in range(cap):

            @pl.when(found > c)
            def _(page=chosen[c], slot=r * cap + c):
                pltpu.make_async_copy(arrived_ref.at[slot, 0], key_pool.at[page], page_sem).start()
                pltpu.make_async_copy(arrived_ref.at[slot, 1], value_pool.at[page], page_sem).start()

    wait_rows(kv_ref, steps, 4, sem)
    lane = lax.broadcasted_iota(jnp.int32, stat_ref.shape[1:], 1)

    def begin(t, most_ref):
        for copy in copies(t):
            copy.wait()
        most_ref[...] = jnp.where(lane < 64, stat_ref[t], masked_score)

    def finish(t):
        stat = stat_ref[t]
        factor = jnp.exp(stat[:, :1] - top_ref[...])
        sums = stat[:, 64:65] * factor + jnp.sum(sum_ref[...], axis=1, keepdims=True)
        inverse = 1.0 / sums
        old = factor * inverse
        mixed = acc_ref[t] * join([old, old]) + values_ref[...] * join([inverse, inverse])
        roped_ref[t] = mixed.astype(jnp.bfloat16)

    attention(
        steps, roped_ref, kv_ref, bias_ref, (s_0, s_1), (most_0, most_1), top_ref, sum_ref, values_ref,
        begin, finish,
    )

    def settle(n, carry):
        pltpu.make_async_copy(arrived_ref.at[0, 0], key_pool.at[0], page_sem).wait()
        pltpu.make_async_copy(arrived_ref.at[0, 1], value_pool.at[0], page_sem).wait()
        return carry

    lax.fori_loop(0, placed, settle, 0)
    for copy in pool_stores:
        copy.start()
    weight_copy.wait()

    def out_copy(n, columns):
        return pltpu.make_async_copy(stage_ref.at[n % 2], hidden_ref.at[:, columns], out_sems.at[n % 2])

    def project(n, carry):
        columns = pl.ds(pl.multiple_of(n * chunk, chunk), chunk)

        @pl.when(n >= 2)
        def _():
            out_copy(n, columns).wait()

        attended = join(
            [
                roped_ref[t, one * rows : (one + 1) * rows, :]
                for t in range(items)
                for one in range(head_pair)
            ]
        )
        stage_ref[n % 2] = jnp.dot(
            attended, w_ref[:, columns], preferred_element_type=jnp.float32
        ).astype(jnp.bfloat16)
        out_copy(n, columns).start()
        return carry

    lax.fori_loop(0, chunks, project, 0)
    for n in range(2):
        out_copy(n, pl.ds(0, chunk)).wait()
    for copy in pool_stores:
        copy.wait()


def rest_part(page_table, lengths, cap, state, slots, weight, arrived, key_cache, value_cache):
    items, pair_rows, _ = state[0].shape
    rows = pair_rows // head_pair
    width = weight.shape[1]
    chunk = 512
    return pl.pallas_call(
        lambda *refs: rest_kernel(cap, *refs),
        out_shape=(
            pltpu.HBM((rows, width), jnp.bfloat16),
            pltpu.HBM(key_cache.shape, jnp.bfloat16),
            pltpu.HBM(value_cache.shape, jnp.bfloat16),
        ),
        in_specs=[smem_spec] * 2 + [hbm_spec] * 3 + [any_spec] * 7 + [hbm_spec] * 4,
        out_specs=(hbm_spec,) * 3,
        scratch_shapes=state_shapes(items, rows)
        + working(rows, 4, 2)
        + [
            pltpu.VMEM(weight.shape, jnp.bfloat16),
            pltpu.VMEM((2, rows, chunk), jnp.bfloat16),
            pltpu.VMEM(key_cache.shape, jnp.bfloat16),
            pltpu.VMEM(value_cache.shape, jnp.bfloat16),
            pltpu.SemaphoreType.DMA((3, items)),
            pltpu.SemaphoreType.DMA,
            pltpu.SemaphoreType.DMA,
            pltpu.SemaphoreType.DMA((2,)),
            pltpu.SemaphoreType.DMA,
            pltpu.SemaphoreType.DMA((2,)),
        ],
        compiler_params=params(large_limit),
        cost_estimate=cost(items, rows, 2560),
        name="attend_rest",
    )(page_table, lengths, *in_hbm(*state), *slots, *in_hbm(weight, arrived, key_cache, value_cache))


def after(value, *others):
    return lax.optimization_barrier((value,) + others)[0]


def body(queries, new_keys, new_values, key_cache, value_cache, out_weight, lengths, page_table):
    blk_count = lax.axis_size("blk")
    pages = key_cache.shape[0]
    window_pages = page_table.shape[1] // 2
    cap = (window_pages + blk_count - 1) // blk_count

    def other_core(value):
        return lax.ppermute(value, "group", [(0, 1), (1, 0), (2, 3), (3, 2)])

    def other_chip(value):
        return lax.ppermute(value, "group", [(0, 2), (2, 0), (1, 3), (3, 1)])

    picked = pick_old(page_table, cap, key_cache, value_cache)
    old = lax.all_to_all(picked, "blk", split_axis=0, concat_axis=0, tiled=True)
    old = old.reshape((blk_count * cap,) + old.shape[2:])

    fresh, cosine, sine = rotate_keys(lengths, new_keys[0], new_values[0])
    fresh_far = other_chip(fresh)
    fresh_core = other_core(fresh)
    roped, acc, stat = diagonal_part(after(queries[0], picked), cosine, sine, fresh)

    old = sort_old(after(page_table, stat), blk_count, cap, pages, old)
    old_far = other_chip(old)
    old_core = other_core(old)
    fresh_far_core = other_core(after(fresh_far, stat))
    new = pick_new(page_table, blk_count, cap, pages, (fresh, fresh_core, fresh_far, fresh_far_core))
    arrived = lax.all_to_all(new, "blk", split_axis=0, concat_axis=0, tiled=True)
    old_far_core = other_core(after(old_far, new))
    hidden, key_out, value_out = rest_part(
        page_table, lengths, cap, (roped, acc, stat),
        (fresh_core, fresh_far, fresh_far_core, old, old_core, old_far, old_far_core),
        out_weight, arrived, key_cache, value_cache,
    )
    return (hidden[None], key_out, value_out)


def solution(mesh):
    return jax.shard_map(
        body,
        mesh=mesh,
        in_specs=(
            P("blk", "group", None),
            P("blk", "group", None),
            P("blk", "group", None),
            P("blk", "group", None),
            P("blk", "group", None),
            P(),
            P(),
            P(),
        ),
        out_specs=(P("blk", "group", None), P("blk", "group", None), P("blk", "group", None)),
        check_vma=False,
    )
```

```python
import jax
import jax.numpy as jnp
import numpy as np
from jax import lax
from jax.experimental import pallas as pl
from jax.experimental.pallas import tpu as pltpu
from jax.sharding import PartitionSpec as P

masked_score = -1e30
step_keys = 512
step_slots = 16
any_spec = pl.BlockSpec(memory_space=pl.ANY)
hbm_spec = pl.BlockSpec(memory_space=pltpu.HBM)
smem_spec = pl.BlockSpec(memory_space=pltpu.SMEM)
vmem_spec = pl.BlockSpec(memory_space=pltpu.VMEM)
small_limit = 16 * 1024 * 1024
head_pair = 2
large_limit = 58 * 1024 * 1024


def params(limit):
    return pltpu.CompilerParams(vmem_limit_bytes=limit)


def in_hbm(*arrays):
    return [pltpu.with_memory_space_constraint(array, pltpu.HBM) for array in arrays]


def turn(values, cosine, sine):
    front = values[:, :128].astype(jnp.float32)
    return front * cosine + pltpu.roll(front, 64, 1) * sine


def join(pieces):
    return jnp.concatenate(pieces, axis=1)


def pages_here(table_ref, r, first, count, cap, pages):
    low = lax.axis_index("blk") * pages
    found = jnp.int32(0)
    chosen = [jnp.int32(0)] * cap
    for j in range(first, first + count):
        page = table_ref[r, j] - low
        inside = (page >= 0) & (page < pages)
        chosen = [jnp.where(inside & (found == c), page, chosen[c]) for c in range(cap)]
        found = found + inside.astype(jnp.int32)
    return chosen, found


def pick_old_kernel(table_ref, key_ref, value_ref, out_ref, sem):
    requests, cap = out_ref.shape[:2]
    for r in range(requests):
        chosen, _ = pages_here(table_ref, r, 0, table_ref.shape[1] // 2, cap, key_ref.shape[0])
        for c in range(cap):
            pltpu.make_async_copy(key_ref.at[chosen[c]], out_ref.at[r, c, 0], sem).start()
            pltpu.make_async_copy(value_ref.at[chosen[c]], out_ref.at[r, c, 1], sem).start()
    pltpu.make_async_copy(out_ref, out_ref, sem).wait()


def pick_old(page_table, cap, key_cache, value_cache):
    requests = page_table.shape[0]
    return pl.pallas_call(
        pick_old_kernel,
        out_shape=jax.ShapeDtypeStruct((requests, cap, 2) + key_cache.shape[1:], jnp.bfloat16),
        in_specs=[smem_spec, hbm_spec, hbm_spec],
        out_specs=vmem_spec,
        scratch_shapes=[pltpu.SemaphoreType.DMA],
        compiler_params=params(small_limit),
        name="pick_old",
    )(page_table, *in_hbm(key_cache, value_cache))


def owner_of(page, pages, owners):
    factor = (1 << 20) // pages + 1
    assert all((p * factor) >> 20 == p // pages for p in range(pages * owners))
    assert pages * owners * factor < 1 << 31
    return (page * factor) >> 20


def find_slots(table_ref, first, count, cap, pages, counts_ref):
    owners = counts_ref.shape[0]
    row = lax.axis_index("blk")
    for o in range(owners):
        counts_ref[o] = 0
    slots = []
    for j in range(count):
        owner = owner_of(table_ref[row, first + j], pages, owners)
        rank = counts_ref[owner]
        counts_ref[owner] = rank + 1
        slots.append(owner * cap + rank)
    return slots


def rotate_kernel(lengths_ref, freq_ref, keys_ref, values_ref, out_ref, cos_ref, sin_ref):
    rows = keys_ref.shape[0]
    slots = rows // 32
    start = lengths_ref[lax.axis_index("blk")] + lax.axis_index("group") * rows
    positions = start + lax.broadcasted_iota(jnp.int32, (rows, 128), 0)
    angles = positions.astype(jnp.float32) * freq_ref[...]
    lane = lax.broadcasted_iota(jnp.int32, (rows, 128), 1)
    cosine = jnp.cos(angles)
    sine = jnp.sin(angles)
    sine = jnp.where(lane < 64, -sine, sine)
    cos_ref[...] = cosine
    sin_ref[...] = sine
    keys = keys_ref[...]
    turned = join([turn(keys, cosine, sine).astype(jnp.bfloat16), keys[:, 128:]])
    out_ref[:, 0] = turned.reshape(slots, 32, 256)
    out_ref[:, 1] = values_ref[...].reshape(slots, 32, 256)


def rotate_keys(lengths, keys, values):
    rows, head_dim = keys.shape
    quarter = head_dim // 4
    freq_table = np.float32(10000.0) ** (-np.arange(quarter, dtype=np.float32) / np.float32(quarter))
    freq_table = np.concatenate([freq_table, freq_table])[None].astype(np.float32)
    return pl.pallas_call(
        rotate_kernel,
        out_shape=(
            pltpu.HBM((rows // 32, 2, 32, head_dim), jnp.bfloat16),
            pltpu.HBM((rows, 128), jnp.float32),
            pltpu.HBM((rows, 128), jnp.float32),
        ),
        in_specs=[smem_spec, vmem_spec, vmem_spec, vmem_spec],
        out_specs=(vmem_spec,) * 3,
        compiler_params=params(small_limit),
        name="rotate_keys",
    )(lengths, jnp.asarray(freq_table), keys, values)


def sort_kernel(pages, cap, table_ref, old_ref, out_ref, counts_ref, sem):
    count = out_ref.shape[0]
    for j, slot in enumerate(find_slots(table_ref, 0, count, cap, pages, counts_ref)):
        pltpu.make_async_copy(old_ref.at[slot], out_ref.at[j], sem).start()
    pltpu.make_async_copy(out_ref, out_ref, sem).wait()


def sort_old(page_table, blk_count, cap, pages, old):
    window = page_table.shape[1] // 2
    return pl.pallas_call(
        lambda *refs: sort_kernel(pages, cap, *refs),
        out_shape=jax.ShapeDtypeStruct((window,) + old.shape[1:], jnp.bfloat16),
        in_specs=[smem_spec, hbm_spec],
        out_specs=vmem_spec,
        scratch_shapes=[pltpu.SMEM((blk_count,), jnp.int32), pltpu.SemaphoreType.DMA],
        compiler_params=params(small_limit),
        name="sort_old",
    )(page_table, *in_hbm(old))


def pick_new_kernel(
    pages, cap, table_ref, own_ref, core_ref, far_ref, far_core_ref, out_ref, targets_ref,
    slots_ref, counts_ref, sem,
):
    count = slots_ref.shape[0]
    block_pages = count // 4
    group_index = lax.axis_index("group")
    for j, slot in enumerate(find_slots(table_ref, table_ref.shape[1] - count, count, cap, pages, counts_ref)):
        slots_ref[j] = slot
    for number, ref in enumerate((own_ref, core_ref, far_ref, far_core_ref)):
        block = group_index ^ number
        for place in range(block_pages):
            source = ref.at[4 * place + group_index]
            target = out_ref.at[slots_ref[block * block_pages + place]]
            pltpu.make_async_copy(source, target, sem).start()
    for r in range(table_ref.shape[0]):
        chosen, found = pages_here(table_ref, r, table_ref.shape[1] - count, count, cap, pages)
        for c in range(cap):
            targets_ref[r * cap + c] = jnp.where(found > c, chosen[c], -1)
    sent = out_ref.at[pl.ds(0, count)]
    pltpu.make_async_copy(sent, sent, sem).wait()


def pick_new(page_table, blk_count, cap, pages, sources):
    window = page_table.shape[1] // 2
    return pl.pallas_call(
        lambda *refs: pick_new_kernel(pages, cap, *refs),
        out_shape=(
            jax.ShapeDtypeStruct((blk_count * cap,) + sources[0].shape[1:], jnp.bfloat16),
            jax.ShapeDtypeStruct((blk_count * cap,), jnp.int32),
        ),
        in_specs=[smem_spec] + [any_spec] * 4,
        out_specs=(vmem_spec, smem_spec),
        scratch_shapes=[
            pltpu.SMEM((window,), jnp.int32),
            pltpu.SMEM((blk_count,), jnp.int32),
            pltpu.SemaphoreType.DMA,
        ],
        compiler_params=params(small_limit),
        name="pick_new",
    )(page_table, *sources)


def lane_fold(values, combine):
    total = values[:, :128]
    for start in range(128, values.shape[1], 128):
        total = combine(total, values[:, start : start + 128])
    return total


def old_bias(rows, quarter):
    row = lax.broadcasted_iota(jnp.int32, (rows, 256), 0)
    column = lax.broadcasted_iota(jnp.int32, (rows, 256), 1)
    held = quarter ^ (column // 128)
    position = ((column % 128) // 32) * 128 + 32 * held + column % 32
    return jnp.where(position > row, 0.0, masked_score)


def fetch(source, first, kv_ref, place, count, sem):
    for kind in range(2):
        pltpu.make_async_copy(
            source.at[pl.ds(first, count), kind], kv_ref.at[kind, pl.ds(place, count)], sem
        ).start()


def fetch_pair(sources, first, kv_ref, place, sem):
    fetch(sources[0], first, kv_ref, place, 4, sem)
    fetch(sources[1], first, kv_ref, place + 4, 4, sem)


def wait_rows(kv_ref, steps, most, sem):
    for n in range(1, most + 1):

        @pl.when(steps == n)
        def _(n=n):
            filled = kv_ref.at[:, pl.ds(0, n * step_slots)]
            pltpu.make_async_copy(filled, filled, sem).wait()


def attention(steps, roped_ref, kv_ref, bias_ref, s_refs, most_refs, top_ref, sum_ref, sum_of_values, begin, finish):
    items, rows, _ = roped_ref.shape

    def block(kind, c):
        return kv_ref[kind, pl.ds(c * step_slots, step_slots)].reshape(step_keys, 256)

    def scores(t, c, which, masked):
        result = lax.dot_general(
            roped_ref[t], block(0, c), (((1,), (1,)), ((), ())), preferred_element_type=jnp.float32
        )
        if masked:
            result = result.reshape(head_pair, rows // head_pair, step_keys) + bias_ref[...]
            result = result.reshape(rows, step_keys)
        s_refs[which][c] = result
        most_refs[which][...] = jnp.maximum(most_refs[which][...], lane_fold(result, jnp.maximum))

    def weigh(c, which):
        weights = jnp.exp(s_refs[which][c] - join([top_ref[...]] * (step_keys // 128)))
        sum_ref[...] += lane_fold(weights, jnp.add)
        sum_of_values[...] += jnp.dot(
            weights.astype(jnp.bfloat16), block(1, c), preferred_element_type=jnp.float32
        )

    def settle(which):
        top_ref[...] = jnp.broadcast_to(
            jnp.max(most_refs[which][...], axis=1, keepdims=True), top_ref.shape
        )
        sum_ref[...] = jnp.zeros_like(sum_ref)
        sum_of_values[...] = jnp.zeros_like(sum_of_values)

    def loop(work):
        def step(c, carry):
            work(c, False)
            return carry

        if isinstance(steps, int):
            for c in range(steps):
                work(c, c == 0)
            return

        @pl.when(steps > 0)
        def _():
            work(0, True)

        lax.fori_loop(1, steps, step, 0)

    def one(t, which):
        begin(t + 1, most_refs[1 - which])
        settle(which)

        def work(c, masked):
            weigh(c, which)
            scores(t + 1, c, 1 - which, masked)

        loop(work)
        finish(t)

    def two(i, carry):
        one(2 * i, 0)
        one(2 * i + 1, 1)
        return carry

    begin(0, most_refs[0])
    loop(lambda c, masked: scores(0, c, 0, masked))
    pairs = (items - 1) // 2
    lax.fori_loop(0, pairs, two, 0)
    last = 2 * pairs
    if last < items - 1:
        one(last, 0)
        last += 1
    settle(last % 2)
    loop(lambda c, masked: weigh(c, last % 2))
    finish(last)


def working(rows, steps):
    return [
        pltpu.VMEM((2, steps * step_slots, 32, 256), jnp.bfloat16),
        pltpu.VMEM((steps, head_pair * rows, step_keys), jnp.float32),
        pltpu.VMEM((steps, head_pair * rows, step_keys), jnp.float32),
        pltpu.VMEM((head_pair * rows, 128), jnp.float32),
        pltpu.VMEM((head_pair * rows, 128), jnp.float32),
        pltpu.VMEM((head_pair * rows, 128), jnp.float32),
        pltpu.VMEM((head_pair * rows, 128), jnp.float32),
        pltpu.VMEM((head_pair * rows, 256), jnp.float32),
        pltpu.VMEM((rows, step_keys), jnp.float32),
    ]


def state_shapes(items, rows):
    return [
        pltpu.VMEM((items, head_pair * rows, 256), jnp.bfloat16),
        pltpu.VMEM((items, head_pair * rows, 256), jnp.float32),
        pltpu.VMEM((items, head_pair * rows, 128), jnp.float32),
    ]


def state_out(items, rows):
    return (
        pltpu.HBM((items, head_pair * rows, 256), jnp.float32),
        pltpu.HBM((items, head_pair * rows, 128), jnp.float32),
    )


def cost(items, rows, keys):
    pairs = items * head_pair * rows * keys
    return pl.CostEstimate(flops=4 * pairs * 256, bytes_accessed=1 << 24, transcendentals=pairs)


def diagonal_kernel(
    query_ref, cos_ref, sin_ref, own_ref, roped_out, acc_out, stat_out,
    q_ref, roped_ref, acc_ref, stat_ref, kv_ref, s_0, s_1, most_0, most_1, top_ref, sum_ref, values_ref,
    bias_ref, query_sem, sem, out_sem,
):
    rows = q_ref.shape[0]
    items = roped_ref.shape[0]
    query_copy = pltpu.make_async_copy(query_ref, q_ref, query_sem)
    query_copy.start()
    fetch(own_ref, 0, kv_ref, 0, step_slots, sem)
    row = lax.broadcasted_iota(jnp.int32, (rows, step_keys), 0)
    column = lax.broadcasted_iota(jnp.int32, (rows, step_keys), 1)
    bias_ref[...] = jnp.where(column <= row, 0.0, masked_score)
    query_copy.wait()

    def rope(t, carry):
        for one in range(head_pair):
            raw = q_ref[:, pl.ds(pl.multiple_of((t * head_pair + one) * 256, 256), 256)]
            front = turn(raw, cos_ref[...], sin_ref[...])
            some = pl.ds(one * rows, rows)
            roped_ref[t, some, :128] = (front * 0.0625).astype(jnp.bfloat16)
            roped_ref[t, some, 128:] = raw[:, 128:] * jnp.bfloat16(0.0625)
        return carry

    lax.fori_loop(0, items, rope, 0)
    roped_copy = pltpu.make_async_copy(roped_ref, roped_out, query_sem)
    roped_copy.start()
    pltpu.make_async_copy(kv_ref, kv_ref, sem).wait()

    def begin(t, most_ref):
        most_ref[...] = jnp.full_like(most_ref, masked_score)

    def finish(t):
        lane = lax.broadcasted_iota(jnp.int32, stat_ref.shape[1:], 1)
        sums = jnp.sum(sum_ref[...], axis=1, keepdims=True)
        stat_ref[t] = jnp.where(lane < 64, top_ref[...], sums)
        acc_ref[t] = values_ref[...]
        pltpu.make_async_copy(acc_ref.at[t], acc_out.at[t], out_sem).start()
        pltpu.make_async_copy(stat_ref.at[t], stat_out.at[t], out_sem).start()

    attention(
        1, roped_ref, kv_ref, bias_ref, (s_0, s_1), (most_0, most_1), top_ref, sum_ref, values_ref,
        begin, finish,
    )
    roped_copy.wait()
    pltpu.make_async_copy(acc_ref, acc_out, out_sem).wait()
    pltpu.make_async_copy(stat_ref, stat_out, out_sem).wait()


def diagonal_part(queries, cosine, sine, own):
    rows, width = queries.shape
    items = width // (256 * head_pair)
    return pl.pallas_call(
        diagonal_kernel,
        out_shape=(pltpu.HBM((items, head_pair * rows, 256), jnp.bfloat16),) + state_out(items, rows),
        in_specs=[hbm_spec, vmem_spec, vmem_spec, hbm_spec],
        out_specs=(hbm_spec,) * 3,
        scratch_shapes=[pltpu.VMEM((rows, width), jnp.bfloat16)]
        + state_shapes(items, rows)
        + working(rows, 1)
        + [pltpu.SemaphoreType.DMA] * 3,
        compiler_params=params(large_limit),
        cost_estimate=cost(items, rows, 512),
        name="attend_diagonal",
    )(*in_hbm(queries), cosine, sine, *in_hbm(own))


def rest_kernel(
    lengths_ref, roped_in, acc_in, stat_in, core_ref, far_ref, far_core_ref,
    old_ref, old_core_ref, old_far_ref, old_far_core_ref, weight_ref, key_ref, value_ref,
    hidden_ref, key_out_ref, value_out_ref,
    roped_ref, acc_ref, stat_ref, kv_ref, s_0, s_1, most_0, most_1, top_ref, sum_ref, values_ref,
    bias_ref, w_ref, stage_ref, key_pool, value_pool,
    state_sems, sem, weight_sem, pool_sems, out_sems,
):
    group_index = lax.axis_index("group")
    has_old = lengths_ref[lax.axis_index("blk")] > 0
    items = roped_ref.shape[0]
    rows = bias_ref.shape[0]
    chunk = stage_ref.shape[2]
    chunks = w_ref.shape[1] // chunk
    odd = group_index % 2
    chip = group_index // 2
    steps = jnp.where(has_old, 4, odd + 2 * chip)
    base = jnp.where(has_old, 16, 0)
    near = (old_ref, old_core_ref)
    far = (old_far_ref, old_far_core_ref)

    def copies(t):
        return [
            pltpu.make_async_copy(source.at[t], target.at[t], state_sems.at[number, t])
            for number, (source, target) in enumerate(
                ((roped_in, roped_ref), (stat_in, stat_ref), (acc_in, acc_ref))
            )
        ]

    pool_loads = [
        pltpu.make_async_copy(key_ref, key_pool, pool_sems.at[0]),
        pltpu.make_async_copy(value_ref, value_pool, pool_sems.at[1]),
    ]
    pool_stores = [
        pltpu.make_async_copy(key_pool, key_out_ref, pool_sems.at[0]),
        pltpu.make_async_copy(value_pool, value_out_ref, pool_sems.at[1]),
    ]
    for copy in copies(0):
        copy.start()

    @pl.when(odd == 1)
    def _():
        fetch(core_ref, 0, kv_ref, base, 16, sem)

    @pl.when(chip == 1)
    def _():
        place = base + 16 * jnp.where(has_old, 1, odd)
        fetch(far_ref, 0, kv_ref, place, 16, sem)
        fetch(far_core_ref, 0, kv_ref, place + 16, 16, sem)

    @pl.when(has_old)
    def _():
        for block in range(4):

            @pl.when(block >= group_index)
            def _(block=block):
                gap = jnp.where(block == group_index, 0, odd)
                place = 16 * (gap + block - group_index)
                fetch_pair(near, 4 * block, kv_ref, place, sem)
                fetch_pair(far, 4 * block, kv_ref, place + 8, sem)

    for copy in pool_loads:
        copy.start()
    for t in range(1, items):
        for copy in copies(t):
            copy.start()
    weight_copy = pltpu.make_async_copy(weight_ref, w_ref, weight_sem)
    weight_copy.start()

    bias_ref[...] = jnp.zeros_like(bias_ref)

    @pl.when(has_old)
    def _():
        bias_ref[:, :256] = old_bias(rows, group_index)
        bias_ref[:, 256:] = old_bias(rows, group_index ^ 2)

    wait_rows(kv_ref, steps, 4, sem)
    lane = lax.broadcasted_iota(jnp.int32, stat_ref.shape[1:], 1)

    def begin(t, most_ref):
        for copy in copies(t):
            copy.wait()
        most_ref[...] = jnp.where(lane < 64, stat_ref[t], masked_score)

    def finish(t):
        stat = stat_ref[t]
        factor = jnp.exp(stat[:, :1] - top_ref[...])
        sums = stat[:, 64:65] * factor + jnp.sum(sum_ref[...], axis=1, keepdims=True)
        inverse = 1.0 / sums
        old = factor * inverse
        mixed = acc_ref[t] * join([old, old]) + values_ref[...] * join([inverse, inverse])
        roped_ref[t] = mixed.astype(jnp.bfloat16)

    attention(
        steps, roped_ref, kv_ref, bias_ref, (s_0, s_1), (most_0, most_1), top_ref, sum_ref, values_ref,
        begin, finish,
    )

    for copy in pool_loads:
        copy.wait()
    for copy in pool_stores:
        copy.start()
    weight_copy.wait()

    def out_copy(n, columns):
        return pltpu.make_async_copy(stage_ref.at[n % 2], hidden_ref.at[:, columns], out_sems.at[n % 2])

    def project(n, carry):
        columns = pl.ds(pl.multiple_of(n * chunk, chunk), chunk)

        @pl.when(n >= 2)
        def _():
            out_copy(n, columns).wait()

        attended = join(
            [
                roped_ref[t, one * rows : (one + 1) * rows, :]
                for t in range(items)
                for one in range(head_pair)
            ]
        )
        stage_ref[n % 2] = jnp.dot(
            attended, w_ref[:, columns], preferred_element_type=jnp.float32
        ).astype(jnp.bfloat16)
        out_copy(n, columns).start()
        return carry

    lax.fori_loop(0, chunks, project, 0)
    for n in range(2):
        out_copy(n, pl.ds(0, chunk)).wait()
    for copy in pool_stores:
        copy.wait()


def rest_part(lengths, state, slots, weight, key_cache, value_cache):
    items, pair_rows, _ = state[0].shape
    rows = pair_rows // head_pair
    width = weight.shape[1]
    chunk = 512
    return pl.pallas_call(
        rest_kernel,
        out_shape=(
            pltpu.HBM((rows, width), jnp.bfloat16),
            pltpu.HBM(key_cache.shape, jnp.bfloat16),
            pltpu.HBM(value_cache.shape, jnp.bfloat16),
        ),
        in_specs=[smem_spec] + [hbm_spec] * 3 + [any_spec] * 7 + [hbm_spec] * 3,
        out_specs=(hbm_spec,) * 3,
        scratch_shapes=state_shapes(items, rows)
        + working(rows, 4)
        + [
            pltpu.VMEM(weight.shape, jnp.bfloat16),
            pltpu.VMEM((2, rows, chunk), jnp.bfloat16),
            pltpu.VMEM(key_cache.shape, jnp.bfloat16),
            pltpu.VMEM(value_cache.shape, jnp.bfloat16),
            pltpu.SemaphoreType.DMA((3, items)),
            pltpu.SemaphoreType.DMA,
            pltpu.SemaphoreType.DMA,
            pltpu.SemaphoreType.DMA((2,)),
            pltpu.SemaphoreType.DMA((2,)),
        ],
        compiler_params=params(large_limit),
        cost_estimate=cost(items, rows, 2560),
        name="attend_rest",
    )(lengths, *in_hbm(*state), *slots, *in_hbm(weight, key_cache, value_cache))


def place_kernel(targets_ref, arrived_ref, key_in, value_in, key_ref, value_ref, buffer_ref, load_sem, sem):
    load = pltpu.make_async_copy(arrived_ref, buffer_ref, load_sem)
    load.start()
    load.wait()

    def each(act):
        for slot in range(targets_ref.shape[0]):
            page = targets_ref[slot]

            @pl.when(page >= 0)
            def _(slot=slot, page=page):
                for kind, out_ref in enumerate((key_ref, value_ref)):
                    act(pltpu.make_async_copy(buffer_ref.at[slot, kind], out_ref.at[page], sem))

    each(lambda copy: copy.start())
    each(lambda copy: copy.wait())


def place_new(targets, arrived, key_pool, value_pool):
    return pl.pallas_call(
        place_kernel,
        out_shape=(
            pltpu.HBM(key_pool.shape, jnp.bfloat16),
            pltpu.HBM(value_pool.shape, jnp.bfloat16),
        ),
        in_specs=[smem_spec] + [hbm_spec] * 3,
        out_specs=(hbm_spec,) * 2,
        input_output_aliases={2: 0, 3: 1},
        scratch_shapes=[
            pltpu.VMEM(arrived.shape, jnp.bfloat16),
            pltpu.SemaphoreType.DMA,
            pltpu.SemaphoreType.DMA,
        ],
        compiler_params=params(small_limit),
        name="place_new",
    )(targets, *in_hbm(arrived, key_pool, value_pool))


def after(value, *others):
    return lax.optimization_barrier((value,) + others)[0]


def body(queries, new_keys, new_values, key_cache, value_cache, out_weight, lengths, page_table):
    blk_count = lax.axis_size("blk")
    pages = key_cache.shape[0]
    window_pages = page_table.shape[1] // 2
    cap = (window_pages + blk_count - 1) // blk_count

    def other_core(value):
        return lax.ppermute(value, "group", [(0, 1), (1, 0), (2, 3), (3, 2)])

    def other_chip(value):
        return lax.ppermute(value, "group", [(0, 2), (2, 0), (1, 3), (3, 1)])

    picked = pick_old(page_table, cap, key_cache, value_cache)
    old = lax.all_to_all(picked, "blk", split_axis=0, concat_axis=0, tiled=True)
    old = old.reshape((blk_count * cap,) + old.shape[2:])

    fresh, cosine, sine = rotate_keys(lengths, new_keys[0], new_values[0])
    fresh_far = other_chip(fresh)
    fresh_core = other_core(fresh)
    roped, acc, stat = diagonal_part(after(queries[0], picked), cosine, sine, fresh)

    old = sort_old(after(page_table, stat), blk_count, cap, pages, old)
    old_far = other_chip(old)
    old_core = other_core(old)
    fresh_far_core = other_core(after(fresh_far, old))
    new, targets = pick_new(
        page_table, blk_count, cap, pages, (fresh, fresh_core, fresh_far, fresh_far_core)
    )
    arrived = lax.all_to_all(new, "blk", split_axis=0, concat_axis=0, tiled=True)
    old_far_core = other_core(after(old_far, new))
    hidden, key_out, value_out = rest_part(
        lengths, (roped, acc, stat),
        (fresh_core, fresh_far, fresh_far_core, old, old_core, old_far, old_far_core),
        out_weight, key_cache, value_cache,
    )
    key_out, value_out = place_new(targets, arrived, key_out, value_out)
    return (hidden[None], key_out, value_out)


def solution(mesh):
    return jax.shard_map(
        body,
        mesh=mesh,
        in_specs=(
            P("blk", "group", None),
            P("blk", "group", None),
            P("blk", "group", None),
            P("blk", "group", None),
            P("blk", "group", None),
            P(),
            P(),
            P(),
        ),
        out_specs=(P("blk", "group", None), P("blk", "group", None), P("blk", "group", None)),
        check_vma=False,
    )
```

```python
import jax
import jax.numpy as jnp
import numpy as np
from jax import lax
from jax.experimental import pallas as pl
from jax.experimental.pallas import tpu as pltpu
from jax.sharding import PartitionSpec as P

masked_score = -1e30
step_keys = 512
step_slots = 16
any_spec = pl.BlockSpec(memory_space=pl.ANY)
hbm_spec = pl.BlockSpec(memory_space=pltpu.HBM)
smem_spec = pl.BlockSpec(memory_space=pltpu.SMEM)
vmem_spec = pl.BlockSpec(memory_space=pltpu.VMEM)
small_limit = 16 * 1024 * 1024
head_pair = 2
large_limit = 58 * 1024 * 1024


light = pl.CostEstimate(flops=1, bytes_accessed=1, transcendentals=0)


def params(limit):
    return pltpu.CompilerParams(vmem_limit_bytes=limit)


def in_hbm(*arrays):
    return [pltpu.with_memory_space_constraint(array, pltpu.HBM) for array in arrays]


def turn(values, cosine, sine):
    front = values[:, :128].astype(jnp.float32)
    return front * cosine + pltpu.roll(front, 64, 1) * sine


def join(pieces):
    return jnp.concatenate(pieces, axis=1)


def pages_here(table_ref, r, first, count, cap, pages):
    low = lax.axis_index("blk") * pages
    found = jnp.int32(0)
    chosen = [jnp.int32(0)] * cap
    for j in range(first, first + count):
        page = table_ref[r, j] - low
        inside = (page >= 0) & (page < pages)
        chosen = [jnp.where(inside & (found == c), page, chosen[c]) for c in range(cap)]
        found = found + inside.astype(jnp.int32)
    return chosen, found


def pick_old_kernel(table_ref, key_ref, value_ref, out_ref, sem):
    requests, cap = out_ref.shape[:2]
    for r in range(requests):
        chosen, _ = pages_here(table_ref, r, 0, table_ref.shape[1] // 2, cap, key_ref.shape[0])
        for c in range(cap):
            pltpu.make_async_copy(key_ref.at[chosen[c]], out_ref.at[r, c, 0], sem).start()
            pltpu.make_async_copy(value_ref.at[chosen[c]], out_ref.at[r, c, 1], sem).start()
    pltpu.make_async_copy(out_ref, out_ref, sem).wait()


def pick_old(page_table, cap, key_cache, value_cache):
    requests = page_table.shape[0]
    return pl.pallas_call(
        pick_old_kernel,
        out_shape=jax.ShapeDtypeStruct((requests, cap, 2) + key_cache.shape[1:], jnp.bfloat16),
        in_specs=[smem_spec, hbm_spec, hbm_spec],
        out_specs=vmem_spec,
        scratch_shapes=[pltpu.SemaphoreType.DMA],
        cost_estimate=light,
        compiler_params=params(small_limit),
        name="pick_old",
    )(page_table, *in_hbm(key_cache, value_cache))


def owner_of(page, pages, owners):
    factor = (1 << 20) // pages + 1
    assert all((p * factor) >> 20 == p // pages for p in range(pages * owners))
    assert pages * owners * factor < 1 << 31
    return (page * factor) >> 20


def find_slots(table_ref, first, count, cap, pages, counts_ref):
    owners = counts_ref.shape[0]
    row = lax.axis_index("blk")
    for o in range(owners):
        counts_ref[o] = 0
    slots = []
    for j in range(count):
        owner = owner_of(table_ref[row, first + j], pages, owners)
        rank = counts_ref[owner]
        counts_ref[owner] = rank + 1
        slots.append(owner * cap + rank)
    return slots


def rotate_kernel(lengths_ref, freq_ref, keys_ref, values_ref, out_ref, cos_ref, sin_ref):
    rows = keys_ref.shape[0]
    slots = rows // 32
    start = lengths_ref[lax.axis_index("blk")] + lax.axis_index("group") * rows
    positions = start + lax.broadcasted_iota(jnp.int32, (rows, 128), 0)
    angles = positions.astype(jnp.float32) * freq_ref[...]
    lane = lax.broadcasted_iota(jnp.int32, (rows, 128), 1)
    cosine = jnp.cos(angles)
    sine = jnp.sin(angles)
    sine = jnp.where(lane < 64, -sine, sine)
    cos_ref[...] = cosine
    sin_ref[...] = sine
    keys = keys_ref[...]
    turned = join([turn(keys, cosine, sine).astype(jnp.bfloat16), keys[:, 128:]])
    out_ref[:, 0] = turned.reshape(slots, 32, 256)
    out_ref[:, 1] = values_ref[...].reshape(slots, 32, 256)


def rotate_keys(lengths, keys, values):
    rows, head_dim = keys.shape
    quarter = head_dim // 4
    freq_table = np.float32(10000.0) ** (-np.arange(quarter, dtype=np.float32) / np.float32(quarter))
    freq_table = np.concatenate([freq_table, freq_table])[None].astype(np.float32)
    return pl.pallas_call(
        rotate_kernel,
        out_shape=(
            pltpu.HBM((rows // 32, 2, 32, head_dim), jnp.bfloat16),
            pltpu.HBM((rows, 128), jnp.float32),
            pltpu.HBM((rows, 128), jnp.float32),
        ),
        in_specs=[smem_spec, vmem_spec, vmem_spec, vmem_spec],
        out_specs=(vmem_spec,) * 3,
        cost_estimate=light,
        compiler_params=params(small_limit),
        name="rotate_keys",
    )(lengths, jnp.asarray(freq_table), keys, values)


def sort_kernel(pages, cap, table_ref, old_ref, out_ref, counts_ref, sem):
    count = out_ref.shape[0]
    for j, slot in enumerate(find_slots(table_ref, 0, count, cap, pages, counts_ref)):
        pltpu.make_async_copy(old_ref.at[slot], out_ref.at[j], sem).start()
    pltpu.make_async_copy(out_ref, out_ref, sem).wait()


def sort_old(page_table, blk_count, cap, pages, old):
    window = page_table.shape[1] // 2
    return pl.pallas_call(
        lambda *refs: sort_kernel(pages, cap, *refs),
        out_shape=jax.ShapeDtypeStruct((window,) + old.shape[1:], jnp.bfloat16),
        in_specs=[smem_spec, hbm_spec],
        out_specs=vmem_spec,
        scratch_shapes=[pltpu.SMEM((blk_count,), jnp.int32), pltpu.SemaphoreType.DMA],
        cost_estimate=light,
        compiler_params=params(small_limit),
        name="sort_old",
    )(page_table, *in_hbm(old))


def pick_new_kernel(
    pages, cap, table_ref, own_ref, core_ref, far_ref, far_core_ref, out_ref, targets_ref,
    slots_ref, counts_ref, sem,
):
    count = slots_ref.shape[0]
    block_pages = count // 4
    group_index = lax.axis_index("group")
    for j, slot in enumerate(find_slots(table_ref, table_ref.shape[1] - count, count, cap, pages, counts_ref)):
        slots_ref[j] = slot
    for number, ref in enumerate((own_ref, core_ref, far_ref, far_core_ref)):
        block = group_index ^ number
        for place in range(block_pages):
            source = ref.at[4 * place + group_index]
            target = out_ref.at[slots_ref[block * block_pages + place]]
            pltpu.make_async_copy(source, target, sem).start()
    for r in range(table_ref.shape[0]):
        chosen, found = pages_here(table_ref, r, table_ref.shape[1] - count, count, cap, pages)
        for c in range(cap):
            targets_ref[r * cap + c] = jnp.where(found > c, chosen[c], -1)
    sent = out_ref.at[pl.ds(0, count)]
    pltpu.make_async_copy(sent, sent, sem).wait()


def pick_new(page_table, blk_count, cap, pages, sources):
    window = page_table.shape[1] // 2
    return pl.pallas_call(
        lambda *refs: pick_new_kernel(pages, cap, *refs),
        out_shape=(
            jax.ShapeDtypeStruct((blk_count * cap,) + sources[0].shape[1:], jnp.bfloat16),
            jax.ShapeDtypeStruct((blk_count * cap,), jnp.int32),
        ),
        in_specs=[smem_spec] + [any_spec] * 4,
        out_specs=(vmem_spec, smem_spec),
        scratch_shapes=[
            pltpu.SMEM((window,), jnp.int32),
            pltpu.SMEM((blk_count,), jnp.int32),
            pltpu.SemaphoreType.DMA,
        ],
        cost_estimate=light,
        compiler_params=params(small_limit),
        name="pick_new",
    )(page_table, *sources)


def lane_fold(values, combine):
    total = values[:, :128]
    for start in range(128, values.shape[1], 128):
        total = combine(total, values[:, start : start + 128])
    return total


def old_bias(rows, quarter):
    row = lax.broadcasted_iota(jnp.int32, (rows, 256), 0)
    column = lax.broadcasted_iota(jnp.int32, (rows, 256), 1)
    held = quarter ^ (column // 128)
    position = ((column % 128) // 32) * 128 + 32 * held + column % 32
    return jnp.where(position > row, 0.0, masked_score)


def fetch(source, first, kv_ref, place, count, sem):
    for kind in range(2):
        pltpu.make_async_copy(
            source.at[pl.ds(first, count), kind], kv_ref.at[kind, pl.ds(place, count)], sem
        ).start()


def fetch_pair(sources, first, kv_ref, place, sem):
    fetch(sources[0], first, kv_ref, place, 4, sem)
    fetch(sources[1], first, kv_ref, place + 4, 4, sem)


def wait_rows(kv_ref, steps, most, sem):
    for n in range(1, most + 1):

        @pl.when(steps == n)
        def _(n=n):
            filled = kv_ref.at[:, pl.ds(0, n * step_slots)]
            pltpu.make_async_copy(filled, filled, sem).wait()


def attention(steps, roped_ref, kv_ref, bias_ref, s_refs, most_refs, top_ref, sum_ref, sum_of_values, begin, finish):
    items, rows, _ = roped_ref.shape

    def block(kind, c):
        return kv_ref[kind, pl.ds(c * step_slots, step_slots)].reshape(step_keys, 256)

    def scores(t, c, which, masked):
        result = lax.dot_general(
            roped_ref[t], block(0, c), (((1,), (1,)), ((), ())), preferred_element_type=jnp.float32
        )
        if masked:
            result = result.reshape(head_pair, rows // head_pair, step_keys) + bias_ref[...]
            result = result.reshape(rows, step_keys)
        s_refs[which][c] = result
        most_refs[which][...] = jnp.maximum(most_refs[which][...], lane_fold(result, jnp.maximum))

    def weigh(c, which):
        weights = jnp.exp(s_refs[which][c] - join([top_ref[...]] * (step_keys // 128)))
        sum_ref[...] += lane_fold(weights, jnp.add)
        sum_of_values[...] += jnp.dot(
            weights.astype(jnp.bfloat16), block(1, c), preferred_element_type=jnp.float32
        )

    def settle(which):
        top_ref[...] = jnp.broadcast_to(
            jnp.max(most_refs[which][...], axis=1, keepdims=True), top_ref.shape
        )
        sum_ref[...] = jnp.zeros_like(sum_ref)
        sum_of_values[...] = jnp.zeros_like(sum_of_values)

    def loop(work):
        def step(c, carry):
            work(c, False)
            return carry

        if isinstance(steps, int):
            for c in range(steps):
                work(c, c == 0)
            return

        @pl.when(steps > 0)
        def _():
            work(0, True)

        lax.fori_loop(1, steps, step, 0)

    def one(t, which):
        begin(t + 1, most_refs[1 - which])
        settle(which)

        def work(c, masked):
            weigh(c, which)
            scores(t + 1, c, 1 - which, masked)

        loop(work)
        finish(t)

    def two(i, carry):
        one(2 * i, 0)
        one(2 * i + 1, 1)
        return carry

    begin(0, most_refs[0])
    loop(lambda c, masked: scores(0, c, 0, masked))
    pairs = (items - 1) // 2
    lax.fori_loop(0, pairs, two, 0)
    last = 2 * pairs
    if last < items - 1:
        one(last, 0)
        last += 1
    settle(last % 2)
    loop(lambda c, masked: weigh(c, last % 2))
    finish(last)


def working(rows, steps):
    return [
        pltpu.VMEM((2, steps * step_slots, 32, 256), jnp.bfloat16),
        pltpu.VMEM((steps, head_pair * rows, step_keys), jnp.float32),
        pltpu.VMEM((steps, head_pair * rows, step_keys), jnp.float32),
        pltpu.VMEM((head_pair * rows, 128), jnp.float32),
        pltpu.VMEM((head_pair * rows, 128), jnp.float32),
        pltpu.VMEM((head_pair * rows, 128), jnp.float32),
        pltpu.VMEM((head_pair * rows, 128), jnp.float32),
        pltpu.VMEM((head_pair * rows, 256), jnp.float32),
        pltpu.VMEM((rows, step_keys), jnp.float32),
    ]


def state_shapes(items, rows):
    return [
        pltpu.VMEM((items, head_pair * rows, 256), jnp.bfloat16),
        pltpu.VMEM((items, head_pair * rows, 256), jnp.float32),
        pltpu.VMEM((items, head_pair * rows, 128), jnp.float32),
    ]


def state_out(items, rows):
    return (
        pltpu.HBM((items, head_pair * rows, 256), jnp.float32),
        pltpu.HBM((items, head_pair * rows, 128), jnp.float32),
    )


def diagonal_kernel(
    query_ref, cos_ref, sin_ref, own_ref, roped_out, acc_out, stat_out,
    q_ref, roped_ref, acc_ref, stat_ref, kv_ref, s_0, s_1, most_0, most_1, top_ref, sum_ref, values_ref,
    bias_ref, query_sem, sem, out_sem,
):
    rows = q_ref.shape[0]
    items = roped_ref.shape[0]
    query_copy = pltpu.make_async_copy(query_ref, q_ref, query_sem)
    query_copy.start()
    fetch(own_ref, 0, kv_ref, 0, step_slots, sem)
    row = lax.broadcasted_iota(jnp.int32, (rows, step_keys), 0)
    column = lax.broadcasted_iota(jnp.int32, (rows, step_keys), 1)
    bias_ref[...] = jnp.where(column <= row, 0.0, masked_score)
    query_copy.wait()

    def rope(t, carry):
        for one in range(head_pair):
            raw = q_ref[:, pl.ds(pl.multiple_of((t * head_pair + one) * 256, 256), 256)]
            front = turn(raw, cos_ref[...], sin_ref[...])
            some = pl.ds(one * rows, rows)
            roped_ref[t, some, :128] = (front * 0.0625).astype(jnp.bfloat16)
            roped_ref[t, some, 128:] = raw[:, 128:] * jnp.bfloat16(0.0625)
        return carry

    lax.fori_loop(0, items, rope, 0)
    roped_copy = pltpu.make_async_copy(roped_ref, roped_out, query_sem)
    roped_copy.start()
    pltpu.make_async_copy(kv_ref, kv_ref, sem).wait()

    def begin(t, most_ref):
        most_ref[...] = jnp.full_like(most_ref, masked_score)

    def finish(t):
        lane = lax.broadcasted_iota(jnp.int32, stat_ref.shape[1:], 1)
        sums = jnp.sum(sum_ref[...], axis=1, keepdims=True)
        stat_ref[t] = jnp.where(lane < 64, top_ref[...], sums)
        acc_ref[t] = values_ref[...]
        pltpu.make_async_copy(acc_ref.at[t], acc_out.at[t], out_sem).start()
        pltpu.make_async_copy(stat_ref.at[t], stat_out.at[t], out_sem).start()

    attention(
        1, roped_ref, kv_ref, bias_ref, (s_0, s_1), (most_0, most_1), top_ref, sum_ref, values_ref,
        begin, finish,
    )
    roped_copy.wait()
    pltpu.make_async_copy(acc_ref, acc_out, out_sem).wait()
    pltpu.make_async_copy(stat_ref, stat_out, out_sem).wait()


def diagonal_part(queries, cosine, sine, own):
    rows, width = queries.shape
    items = width // (256 * head_pair)
    return pl.pallas_call(
        diagonal_kernel,
        out_shape=(pltpu.HBM((items, head_pair * rows, 256), jnp.bfloat16),) + state_out(items, rows),
        in_specs=[hbm_spec, vmem_spec, vmem_spec, hbm_spec],
        out_specs=(hbm_spec,) * 3,
        scratch_shapes=[pltpu.VMEM((rows, width), jnp.bfloat16)]
        + state_shapes(items, rows)
        + working(rows, 1)
        + [pltpu.SemaphoreType.DMA] * 3,
        cost_estimate=light,
        compiler_params=params(large_limit),
        name="attend_diagonal",
    )(*in_hbm(queries), cosine, sine, *in_hbm(own))


def rest_kernel(
    lengths_ref, roped_in, acc_in, stat_in, core_ref, far_ref, far_core_ref,
    old_ref, old_core_ref, old_far_ref, old_far_core_ref, weight_ref, key_ref, value_ref,
    hidden_ref, key_out_ref, value_out_ref,
    roped_ref, acc_ref, stat_ref, kv_ref, s_0, s_1, most_0, most_1, top_ref, sum_ref, values_ref,
    bias_ref, w_ref, stage_ref, key_pool, value_pool,
    state_sems, sem, weight_sem, pool_sems, out_sems,
):
    group_index = lax.axis_index("group")
    has_old = lengths_ref[lax.axis_index("blk")] > 0
    items = roped_ref.shape[0]
    rows = bias_ref.shape[0]
    chunk = stage_ref.shape[2]
    chunks = w_ref.shape[1] // chunk
    odd = group_index % 2
    chip = group_index // 2
    steps = jnp.where(has_old, 4, odd + 2 * chip)
    base = jnp.where(has_old, 16, 0)
    near = (old_ref, old_core_ref)
    far = (old_far_ref, old_far_core_ref)

    def copies(t):
        return [
            pltpu.make_async_copy(source.at[t], target.at[t], state_sems.at[number, t])
            for number, (source, target) in enumerate(
                ((roped_in, roped_ref), (stat_in, stat_ref), (acc_in, acc_ref))
            )
        ]

    pool_loads = [
        pltpu.make_async_copy(key_ref, key_pool, pool_sems.at[0]),
        pltpu.make_async_copy(value_ref, value_pool, pool_sems.at[1]),
    ]
    pool_stores = [
        pltpu.make_async_copy(key_pool, key_out_ref, pool_sems.at[0]),
        pltpu.make_async_copy(value_pool, value_out_ref, pool_sems.at[1]),
    ]
    for copy in copies(0):
        copy.start()

    @pl.when(odd == 1)
    def _():
        fetch(core_ref, 0, kv_ref, base, 16, sem)

    @pl.when(chip == 1)
    def _():
        place = base + 16 * jnp.where(has_old, 1, odd)
        fetch(far_ref, 0, kv_ref, place, 16, sem)
        fetch(far_core_ref, 0, kv_ref, place + 16, 16, sem)

    @pl.when(has_old)
    def _():
        for block in range(4):

            @pl.when(block >= group_index)
            def _(block=block):
                gap = jnp.where(block == group_index, 0, odd)
                place = 16 * (gap + block - group_index)
                fetch_pair(near, 4 * block, kv_ref, place, sem)
                fetch_pair(far, 4 * block, kv_ref, place + 8, sem)

    for copy in pool_loads:
        copy.start()
    for t in range(1, items):
        for copy in copies(t):
            copy.start()
    weight_copy = pltpu.make_async_copy(weight_ref, w_ref, weight_sem)
    weight_copy.start()

    bias_ref[...] = jnp.zeros_like(bias_ref)

    @pl.when(has_old)
    def _():
        bias_ref[:, :256] = old_bias(rows, group_index)
        bias_ref[:, 256:] = old_bias(rows, group_index ^ 2)

    wait_rows(kv_ref, steps, 4, sem)
    lane = lax.broadcasted_iota(jnp.int32, stat_ref.shape[1:], 1)

    def begin(t, most_ref):
        for copy in copies(t):
            copy.wait()
        most_ref[...] = jnp.where(lane < 64, stat_ref[t], masked_score)

    def finish(t):
        stat = stat_ref[t]
        factor = jnp.exp(stat[:, :1] - top_ref[...])
        sums = stat[:, 64:65] * factor + jnp.sum(sum_ref[...], axis=1, keepdims=True)
        inverse = 1.0 / sums
        old = factor * inverse
        mixed = acc_ref[t] * join([old, old]) + values_ref[...] * join([inverse, inverse])
        roped_ref[t] = mixed.astype(jnp.bfloat16)

    attention(
        steps, roped_ref, kv_ref, bias_ref, (s_0, s_1), (most_0, most_1), top_ref, sum_ref, values_ref,
        begin, finish,
    )

    for copy in pool_loads:
        copy.wait()
    for copy in pool_stores:
        copy.start()
    weight_copy.wait()

    def out_copy(n, columns):
        return pltpu.make_async_copy(stage_ref.at[n % 2], hidden_ref.at[:, columns], out_sems.at[n % 2])

    def project(n, carry):
        columns = pl.ds(pl.multiple_of(n * chunk, chunk), chunk)

        @pl.when(n >= 2)
        def _():
            out_copy(n, columns).wait()

        attended = join(
            [
                roped_ref[t, one * rows : (one + 1) * rows, :]
                for t in range(items)
                for one in range(head_pair)
            ]
        )
        stage_ref[n % 2] = jnp.dot(
            attended, w_ref[:, columns], preferred_element_type=jnp.float32
        ).astype(jnp.bfloat16)
        out_copy(n, columns).start()
        return carry

    lax.fori_loop(0, chunks, project, 0)
    for n in range(2):
        out_copy(n, pl.ds(0, chunk)).wait()
    for copy in pool_stores:
        copy.wait()


def rest_part(lengths, state, slots, weight, key_cache, value_cache):
    items, pair_rows, _ = state[0].shape
    rows = pair_rows // head_pair
    width = weight.shape[1]
    chunk = 512
    return pl.pallas_call(
        rest_kernel,
        out_shape=(
            pltpu.HBM((rows, width), jnp.bfloat16),
            pltpu.HBM(key_cache.shape, jnp.bfloat16),
            pltpu.HBM(value_cache.shape, jnp.bfloat16),
        ),
        in_specs=[smem_spec] + [hbm_spec] * 3 + [any_spec] * 7 + [hbm_spec] * 3,
        out_specs=(hbm_spec,) * 3,
        scratch_shapes=state_shapes(items, rows)
        + working(rows, 4)
        + [
            pltpu.VMEM(weight.shape, jnp.bfloat16),
            pltpu.VMEM((2, rows, chunk), jnp.bfloat16),
            pltpu.VMEM(key_cache.shape, jnp.bfloat16),
            pltpu.VMEM(value_cache.shape, jnp.bfloat16),
            pltpu.SemaphoreType.DMA((3, items)),
            pltpu.SemaphoreType.DMA,
            pltpu.SemaphoreType.DMA,
            pltpu.SemaphoreType.DMA((2,)),
            pltpu.SemaphoreType.DMA((2,)),
        ],
        cost_estimate=light,
        compiler_params=params(large_limit),
        name="attend_rest",
    )(lengths, *in_hbm(*state), *slots, *in_hbm(weight, key_cache, value_cache))


def place_kernel(targets_ref, arrived_ref, key_in, value_in, key_ref, value_ref, buffer_ref, load_sem, sem):
    load = pltpu.make_async_copy(arrived_ref, buffer_ref, load_sem)
    load.start()
    load.wait()

    def each(act):
        for slot in range(targets_ref.shape[0]):
            page = targets_ref[slot]

            @pl.when(page >= 0)
            def _(slot=slot, page=page):
                for kind, out_ref in enumerate((key_ref, value_ref)):
                    act(pltpu.make_async_copy(buffer_ref.at[slot, kind], out_ref.at[page], sem))

    each(lambda copy: copy.start())
    each(lambda copy: copy.wait())


def place_new(targets, arrived, key_pool, value_pool):
    return pl.pallas_call(
        place_kernel,
        out_shape=(
            pltpu.HBM(key_pool.shape, jnp.bfloat16),
            pltpu.HBM(value_pool.shape, jnp.bfloat16),
        ),
        in_specs=[smem_spec, any_spec, hbm_spec, hbm_spec],
        out_specs=(hbm_spec,) * 2,
        input_output_aliases={2: 0, 3: 1},
        scratch_shapes=[
            pltpu.VMEM(arrived.shape, jnp.bfloat16),
            pltpu.SemaphoreType.DMA,
            pltpu.SemaphoreType.DMA,
        ],
        cost_estimate=light,
        compiler_params=params(small_limit),
        name="place_new",
    )(targets, arrived, *in_hbm(key_pool, value_pool))


def after(value, *others):
    return lax.optimization_barrier((value,) + others)[0]


def body(queries, new_keys, new_values, key_cache, value_cache, out_weight, lengths, page_table):
    blk_count = lax.axis_size("blk")
    pages = key_cache.shape[0]
    window_pages = page_table.shape[1] // 2
    cap = (window_pages + blk_count - 1) // blk_count

    def other_core(value):
        return lax.ppermute(value, "group", [(0, 1), (1, 0), (2, 3), (3, 2)])

    def other_chip(value):
        return lax.ppermute(value, "group", [(0, 2), (2, 0), (1, 3), (3, 1)])

    picked = pick_old(page_table, cap, key_cache, value_cache)
    old = lax.all_to_all(picked, "blk", split_axis=0, concat_axis=0, tiled=True)
    old = old.reshape((blk_count * cap,) + old.shape[2:])

    fresh, cosine, sine = rotate_keys(lengths, new_keys[0], new_values[0])
    fresh_far = other_chip(fresh)
    fresh_core = other_core(fresh)
    roped, acc, stat = diagonal_part(after(queries[0], picked), cosine, sine, fresh)

    old = sort_old(after(page_table, stat), blk_count, cap, pages, old)
    old_far = other_chip(old)
    old_core = other_core(old)
    fresh_far_core = other_core(after(fresh_far, old))
    new, targets = pick_new(
        page_table, blk_count, cap, pages, (fresh, fresh_core, fresh_far, fresh_far_core)
    )
    arrived = lax.all_to_all(new, "blk", split_axis=0, concat_axis=0, tiled=True)
    old_far_core = other_core(after(old_far, new))
    hidden, key_out, value_out = rest_part(
        lengths, (roped, acc, stat),
        (fresh_core, fresh_far, fresh_far_core, old, old_core, old_far, old_far_core),
        out_weight, key_cache, value_cache,
    )
    key_out, value_out = place_new(targets, arrived, key_out, value_out)
    return (hidden[None], key_out, value_out)


def solution(mesh):
    return jax.shard_map(
        body,
        mesh=mesh,
        in_specs=(
            P("blk", "group", None),
            P("blk", "group", None),
            P("blk", "group", None),
            P("blk", "group", None),
            P("blk", "group", None),
            P(),
            P(),
            P(),
        ),
        out_specs=(P("blk", "group", None), P("blk", "group", None), P("blk", "group", None)),
        check_vma=False,
    )
```

```python
import jax
import jax.numpy as jnp
import numpy as np
from jax import lax
from jax.experimental import pallas as pl
from jax.experimental.pallas import tpu as pltpu
from jax.sharding import PartitionSpec as P

masked_score = -1e30
step_keys = 512
step_slots = 16
any_spec = pl.BlockSpec(memory_space=pl.ANY)
hbm_spec = pl.BlockSpec(memory_space=pltpu.HBM)
smem_spec = pl.BlockSpec(memory_space=pltpu.SMEM)
vmem_spec = pl.BlockSpec(memory_space=pltpu.VMEM)
small_limit = 16 * 1024 * 1024
head_pair = 2
large_limit = 58 * 1024 * 1024


light = pl.CostEstimate(flops=1, bytes_accessed=1, transcendentals=0)


def params(limit):
    return pltpu.CompilerParams(vmem_limit_bytes=limit)


def in_hbm(*arrays):
    return [pltpu.with_memory_space_constraint(array, pltpu.HBM) for array in arrays]


def turn(values, cosine, sine):
    front = values[:, :128].astype(jnp.float32)
    return front * cosine + pltpu.roll(front, 64, 1) * sine


def join(pieces):
    return jnp.concatenate(pieces, axis=1)


def pages_here(table_ref, r, first, count, cap, pages):
    low = lax.axis_index("blk") * pages
    found = jnp.int32(0)
    chosen = [jnp.int32(0)] * cap
    for j in range(first, first + count):
        page = table_ref[r, j] - low
        inside = (page >= 0) & (page < pages)
        chosen = [jnp.where(inside & (found == c), page, chosen[c]) for c in range(cap)]
        found = found + inside.astype(jnp.int32)
    return chosen, found


def pick_old_kernel(cap, table_ref, key_ref, value_ref, *refs):
    outs, sems = refs[:-1], refs[-1]
    for number, out_ref in enumerate(outs):
        for place in range(out_ref.shape[0] // cap):
            r = lax.axis_index("blk") ^ number if len(outs) > 1 else place
            chosen, _ = pages_here(table_ref, r, 0, table_ref.shape[1] // 2, cap, key_ref.shape[0])
            for c in range(cap):
                slot = out_ref.at[place * cap + c]
                pltpu.make_async_copy(key_ref.at[chosen[c]], slot.at[0], sems.at[number]).start()
                pltpu.make_async_copy(value_ref.at[chosen[c]], slot.at[1], sems.at[number]).start()
    for number, out_ref in enumerate(outs):
        pltpu.make_async_copy(out_ref, out_ref, sems.at[number]).wait()


def pick_old(page_table, cap, partners, key_cache, value_cache):
    slots = page_table.shape[0] * cap // partners
    return pl.pallas_call(
        lambda *refs: pick_old_kernel(cap, *refs),
        out_shape=[jax.ShapeDtypeStruct((slots, 2) + key_cache.shape[1:], jnp.bfloat16)] * partners,
        in_specs=[smem_spec, hbm_spec, hbm_spec],
        out_specs=[vmem_spec] * partners,
        scratch_shapes=[pltpu.SemaphoreType.DMA((partners,))],
        cost_estimate=light,
        compiler_params=params(small_limit),
        name="pick_old",
    )(*in_hbm(page_table, key_cache, value_cache))


def owner_of(page, pages, owners):
    factor = (1 << 20) // pages + 1
    assert all((p * factor) >> 20 == p // pages for p in range(pages * owners))
    assert pages * owners * factor < 1 << 31
    return (page * factor) >> 20


def find_slots(table_ref, first, count, cap, pages, counts_ref):
    owners = counts_ref.shape[0]
    row = lax.axis_index("blk")
    for o in range(owners):
        counts_ref[o] = 0
    slots = []
    for j in range(count):
        owner = owner_of(table_ref[row, first + j], pages, owners)
        rank = counts_ref[owner]
        counts_ref[owner] = rank + 1
        slots.append(owner * cap + rank)
    return slots


def rotate_kernel(lengths_ref, freq_ref, keys_ref, values_ref, out_ref, cos_ref, sin_ref):
    rows = keys_ref.shape[0]
    slots = rows // 32
    start = lengths_ref[lax.axis_index("blk")] + lax.axis_index("group") * rows
    positions = start + lax.broadcasted_iota(jnp.int32, (rows, 128), 0)
    angles = positions.astype(jnp.float32) * freq_ref[...]
    lane = lax.broadcasted_iota(jnp.int32, (rows, 128), 1)
    cosine = jnp.cos(angles)
    sine = jnp.sin(angles)
    sine = jnp.where(lane < 64, -sine, sine)
    cos_ref[...] = cosine
    sin_ref[...] = sine
    keys = keys_ref[...]
    turned = join([turn(keys, cosine, sine).astype(jnp.bfloat16), keys[:, 128:]])
    out_ref[:, 0] = turned.reshape(slots, 32, 256)
    out_ref[:, 1] = values_ref[...].reshape(slots, 32, 256)


def rotate_keys(lengths, keys, values):
    rows, head_dim = keys.shape
    quarter = head_dim // 4
    freq_table = np.float32(10000.0) ** (-np.arange(quarter, dtype=np.float32) / np.float32(quarter))
    freq_table = np.concatenate([freq_table, freq_table])[None].astype(np.float32)
    return pl.pallas_call(
        rotate_kernel,
        out_shape=(
            pltpu.HBM((rows // 32, 2, 32, head_dim), jnp.bfloat16),
            pltpu.HBM((rows, 128), jnp.float32),
            pltpu.HBM((rows, 128), jnp.float32),
        ),
        in_specs=[smem_spec, vmem_spec, vmem_spec, vmem_spec],
        out_specs=(vmem_spec,) * 3,
        cost_estimate=light,
        compiler_params=params(small_limit),
        name="rotate_keys",
    )(lengths, jnp.asarray(freq_table), keys, values)


def sort_kernel(pages, cap, table_ref, *refs):
    olds, (out_ref, page_of_ref, counts_ref, sem) = refs[:-4], refs[-4:]
    count = out_ref.shape[0]
    slots = find_slots(table_ref, 0, count, cap, pages, counts_ref)
    if len(olds) == 1:
        for j, slot in enumerate(slots):
            pltpu.make_async_copy(olds[0].at[slot], out_ref.at[j], sem).start()
    else:
        for slot in range(page_of_ref.shape[0]):
            page_of_ref[slot] = -1
        for j, slot in enumerate(slots):
            page_of_ref[slot] = j
        for number, old_ref in enumerate(olds):
            owner = lax.axis_index("blk") ^ number
            for c in range(cap):
                page = page_of_ref[owner * cap + c]

                @pl.when(page >= 0)
                def _(old_ref=old_ref, c=c, page=page):
                    pltpu.make_async_copy(old_ref.at[c], out_ref.at[page], sem).start()

    pltpu.make_async_copy(out_ref, out_ref, sem).wait()


def sort_old(page_table, blk_count, cap, pages, olds):
    window = page_table.shape[1] // 2
    shape = olds[0].shape[1:]
    return pl.pallas_call(
        lambda *refs: sort_kernel(pages, cap, *refs),
        out_shape=jax.ShapeDtypeStruct((window,) + shape, jnp.bfloat16),
        in_specs=[smem_spec] + [any_spec] * len(olds),
        out_specs=vmem_spec,
        scratch_shapes=[
            pltpu.SMEM((blk_count * cap,), jnp.int32),
            pltpu.SMEM((blk_count,), jnp.int32),
            pltpu.SemaphoreType.DMA,
        ],
        cost_estimate=light,
        compiler_params=params(small_limit),
        name="sort_old",
    )(page_table, *olds)


def pick_new_kernel(
    pages, cap, table_ref, own_ref, core_ref, far_ref, far_core_ref, out_ref, targets_ref,
    slots_ref, counts_ref, sem,
):
    count = slots_ref.shape[0]
    block_pages = count // 4
    group_index = lax.axis_index("group")
    for j, slot in enumerate(find_slots(table_ref, table_ref.shape[1] - count, count, cap, pages, counts_ref)):
        slots_ref[j] = slot
    for number, ref in enumerate((own_ref, core_ref, far_ref, far_core_ref)):
        block = group_index ^ number
        for place in range(block_pages):
            source = ref.at[4 * place + group_index]
            target = out_ref.at[slots_ref[block * block_pages + place]]
            pltpu.make_async_copy(source, target, sem).start()
    for r in range(table_ref.shape[0]):
        chosen, found = pages_here(table_ref, r, table_ref.shape[1] - count, count, cap, pages)
        for c in range(cap):
            targets_ref[r * cap + c] = jnp.where(found > c, chosen[c], -1)
    sent = out_ref.at[pl.ds(0, count)]
    pltpu.make_async_copy(sent, sent, sem).wait()


def pick_new(page_table, blk_count, cap, pages, sources):
    window = page_table.shape[1] // 2
    return pl.pallas_call(
        lambda *refs: pick_new_kernel(pages, cap, *refs),
        out_shape=(
            jax.ShapeDtypeStruct((blk_count * cap,) + sources[0].shape[1:], jnp.bfloat16),
            jax.ShapeDtypeStruct((blk_count * cap,), jnp.int32),
        ),
        in_specs=[smem_spec] + [any_spec] * 4,
        out_specs=(vmem_spec, smem_spec),
        scratch_shapes=[
            pltpu.SMEM((window,), jnp.int32),
            pltpu.SMEM((blk_count,), jnp.int32),
            pltpu.SemaphoreType.DMA,
        ],
        cost_estimate=light,
        compiler_params=params(small_limit),
        name="pick_new",
    )(page_table, *sources)


def lane_fold(values, combine):
    total = values[:, :128]
    for start in range(128, values.shape[1], 128):
        total = combine(total, values[:, start : start + 128])
    return total


def old_bias(rows, quarter):
    row = lax.broadcasted_iota(jnp.int32, (rows, 256), 0)
    column = lax.broadcasted_iota(jnp.int32, (rows, 256), 1)
    held = quarter ^ (column // 128)
    position = ((column % 128) // 32) * 128 + 32 * held + column % 32
    return jnp.where(position > row, 0.0, masked_score)


def fetch(source, first, kv_ref, place, count, sem):
    for kind in range(2):
        pltpu.make_async_copy(
            source.at[pl.ds(first, count), kind], kv_ref.at[kind, pl.ds(place, count)], sem
        ).start()


def fetch_pair(sources, first, kv_ref, place, sem):
    fetch(sources[0], first, kv_ref, place, 4, sem)
    fetch(sources[1], first, kv_ref, place + 4, 4, sem)


def wait_rows(kv_ref, steps, most, sem):
    for n in range(1, most + 1):

        @pl.when(steps == n)
        def _(n=n):
            filled = kv_ref.at[:, pl.ds(0, n * step_slots)]
            pltpu.make_async_copy(filled, filled, sem).wait()


def attention(steps, roped_ref, kv_ref, bias_ref, s_refs, most_refs, top_ref, sum_ref, sum_of_values, begin, finish):
    items, rows, _ = roped_ref.shape

    def block(kind, c):
        return kv_ref[kind, pl.ds(c * step_slots, step_slots)].reshape(step_keys, 256)

    def scores(t, c, which, masked):
        result = lax.dot_general(
            roped_ref[t], block(0, c), (((1,), (1,)), ((), ())), preferred_element_type=jnp.float32
        )
        if masked:
            result = result.reshape(head_pair, rows // head_pair, step_keys) + bias_ref[...]
            result = result.reshape(rows, step_keys)
        s_refs[which][c] = result
        most_refs[which][...] = jnp.maximum(most_refs[which][...], lane_fold(result, jnp.maximum))

    def weigh(c, which):
        weights = jnp.exp(s_refs[which][c] - join([top_ref[...]] * (step_keys // 128)))
        sum_ref[...] += lane_fold(weights, jnp.add)
        sum_of_values[...] += jnp.dot(
            weights.astype(jnp.bfloat16), block(1, c), preferred_element_type=jnp.float32
        )

    def settle(which):
        top_ref[...] = jnp.broadcast_to(
            jnp.max(most_refs[which][...], axis=1, keepdims=True), top_ref.shape
        )
        sum_ref[...] = jnp.zeros_like(sum_ref)
        sum_of_values[...] = jnp.zeros_like(sum_of_values)

    def loop(work):
        def step(c, carry):
            work(c, False)
            return carry

        if isinstance(steps, int):
            for c in range(steps):
                work(c, c == 0)
            return

        @pl.when(steps > 0)
        def _():
            work(0, True)

        lax.fori_loop(1, steps, step, 0)

    def one(t, which):
        begin(t + 1, most_refs[1 - which])
        settle(which)

        def work(c, masked):
            scores(t + 1, c, 1 - which, masked)
            weigh(c, which)

        loop(work)
        finish(t)

    def two(i, carry):
        one(2 * i, 0)
        one(2 * i + 1, 1)
        return carry

    begin(0, most_refs[0])
    loop(lambda c, masked: scores(0, c, 0, masked))
    pairs = (items - 1) // 2
    lax.fori_loop(0, pairs, two, 0)
    last = 2 * pairs
    if last < items - 1:
        one(last, 0)
        last += 1
    settle(last % 2)
    loop(lambda c, masked: weigh(c, last % 2))
    finish(last)


def working(rows, steps):
    return [
        pltpu.VMEM((2, steps * step_slots, 32, 256), jnp.bfloat16),
        pltpu.VMEM((steps, head_pair * rows, step_keys), jnp.float32),
        pltpu.VMEM((steps, head_pair * rows, step_keys), jnp.float32),
        pltpu.VMEM((head_pair * rows, 128), jnp.float32),
        pltpu.VMEM((head_pair * rows, 128), jnp.float32),
        pltpu.VMEM((head_pair * rows, 128), jnp.float32),
        pltpu.VMEM((head_pair * rows, 128), jnp.float32),
        pltpu.VMEM((head_pair * rows, 256), jnp.float32),
        pltpu.VMEM((rows, step_keys), jnp.float32),
    ]


def state_shapes(items, rows):
    return [
        pltpu.VMEM((items, head_pair * rows, 256), jnp.bfloat16),
        pltpu.VMEM((items, head_pair * rows, 256), jnp.float32),
        pltpu.VMEM((items, head_pair * rows, 128), jnp.float32),
    ]


def state_out(items, rows):
    return (
        pltpu.HBM((items, head_pair * rows, 256), jnp.float32),
        pltpu.HBM((items, head_pair * rows, 128), jnp.float32),
    )


def diagonal_kernel(
    query_ref, cos_ref, sin_ref, own_ref, roped_out, acc_out, stat_out,
    q_ref, roped_ref, acc_ref, stat_ref, kv_ref, s_0, s_1, most_0, most_1, top_ref, sum_ref, values_ref,
    bias_ref, query_sem, sem, out_sem,
):
    rows = q_ref.shape[0]
    items = roped_ref.shape[0]
    query_copy = pltpu.make_async_copy(query_ref, q_ref, query_sem)
    query_copy.start()
    fetch(own_ref, 0, kv_ref, 0, step_slots, sem)
    row = lax.broadcasted_iota(jnp.int32, (rows, step_keys), 0)
    column = lax.broadcasted_iota(jnp.int32, (rows, step_keys), 1)
    bias_ref[...] = jnp.where(column <= row, 0.0, masked_score)
    query_copy.wait()

    def rope(t, carry):
        for one in range(head_pair):
            raw = q_ref[:, pl.ds(pl.multiple_of((t * head_pair + one) * 256, 256), 256)]
            front = turn(raw, cos_ref[...], sin_ref[...])
            some = pl.ds(one * rows, rows)
            roped_ref[t, some, :128] = (front * 0.0625).astype(jnp.bfloat16)
            roped_ref[t, some, 128:] = raw[:, 128:] * jnp.bfloat16(0.0625)
        return carry

    lax.fori_loop(0, items, rope, 0)
    roped_copy = pltpu.make_async_copy(roped_ref, roped_out, query_sem)
    roped_copy.start()
    pltpu.make_async_copy(kv_ref, kv_ref, sem).wait()

    def begin(t, most_ref):
        most_ref[...] = jnp.full_like(most_ref, masked_score)

    def finish(t):
        lane = lax.broadcasted_iota(jnp.int32, stat_ref.shape[1:], 1)
        sums = jnp.sum(sum_ref[...], axis=1, keepdims=True)
        stat_ref[t] = jnp.where(lane < 64, top_ref[...], sums)
        acc_ref[t] = values_ref[...]
        pltpu.make_async_copy(acc_ref.at[t], acc_out.at[t], out_sem).start()
        pltpu.make_async_copy(stat_ref.at[t], stat_out.at[t], out_sem).start()

    attention(
        1, roped_ref, kv_ref, bias_ref, (s_0, s_1), (most_0, most_1), top_ref, sum_ref, values_ref,
        begin, finish,
    )
    roped_copy.wait()
    pltpu.make_async_copy(acc_ref, acc_out, out_sem).wait()
    pltpu.make_async_copy(stat_ref, stat_out, out_sem).wait()


def diagonal_part(queries, cosine, sine, own):
    rows, width = queries.shape
    items = width // (256 * head_pair)
    return pl.pallas_call(
        diagonal_kernel,
        out_shape=(pltpu.HBM((items, head_pair * rows, 256), jnp.bfloat16),) + state_out(items, rows),
        in_specs=[hbm_spec, vmem_spec, vmem_spec, hbm_spec],
        out_specs=(hbm_spec,) * 3,
        scratch_shapes=[pltpu.VMEM((rows, width), jnp.bfloat16)]
        + state_shapes(items, rows)
        + working(rows, 1)
        + [pltpu.SemaphoreType.DMA] * 3,
        cost_estimate=light,
        compiler_params=params(large_limit),
        name="attend_diagonal",
    )(*in_hbm(queries), cosine, sine, *in_hbm(own))


def rest_kernel(
    lengths_ref, roped_in, acc_in, stat_in, core_ref, far_ref, far_core_ref,
    old_ref, old_core_ref, old_far_ref, old_far_core_ref, weight_ref, key_ref, value_ref,
    hidden_ref, key_out_ref, value_out_ref,
    roped_ref, acc_ref, stat_ref, kv_ref, s_0, s_1, most_0, most_1, top_ref, sum_ref, values_ref,
    bias_ref, w_ref, stage_ref, key_pool, value_pool,
    state_sems, sem, weight_sem, pool_sems, out_sems,
):
    group_index = lax.axis_index("group")
    has_old = lengths_ref[lax.axis_index("blk")] > 0
    items = roped_ref.shape[0]
    rows = bias_ref.shape[0]
    chunk = stage_ref.shape[2]
    chunks = w_ref.shape[1] // chunk
    odd = group_index % 2
    chip = group_index // 2
    steps = jnp.where(has_old, 4, odd + 2 * chip)
    base = jnp.where(has_old, 16, 0)
    near = (old_ref, old_core_ref)
    far = (old_far_ref, old_far_core_ref)

    def copies(t):
        return [
            pltpu.make_async_copy(source.at[t], target.at[t], state_sems.at[number, t])
            for number, (source, target) in enumerate(
                ((roped_in, roped_ref), (stat_in, stat_ref), (acc_in, acc_ref))
            )
        ]

    pool_loads = [
        pltpu.make_async_copy(key_ref, key_pool, pool_sems.at[0]),
        pltpu.make_async_copy(value_ref, value_pool, pool_sems.at[1]),
    ]
    pool_stores = [
        pltpu.make_async_copy(key_pool, key_out_ref, pool_sems.at[0]),
        pltpu.make_async_copy(value_pool, value_out_ref, pool_sems.at[1]),
    ]
    for copy in copies(0):
        copy.start()

    @pl.when(odd == 1)
    def _():
        fetch(core_ref, 0, kv_ref, base, 16, sem)

    @pl.when(chip == 1)
    def _():
        place = base + 16 * jnp.where(has_old, 1, odd)
        fetch(far_ref, 0, kv_ref, place, 16, sem)
        fetch(far_core_ref, 0, kv_ref, place + 16, 16, sem)

    @pl.when(has_old)
    def _():
        for block in range(4):

            @pl.when(block >= group_index)
            def _(block=block):
                gap = jnp.where(block == group_index, 0, odd)
                place = 16 * (gap + block - group_index)
                fetch_pair(near, 4 * block, kv_ref, place, sem)
                fetch_pair(far, 4 * block, kv_ref, place + 8, sem)

    for copy in pool_loads:
        copy.start()
    for t in range(1, items):
        for copy in copies(t):
            copy.start()
    weight_copy = pltpu.make_async_copy(weight_ref, w_ref, weight_sem)
    weight_copy.start()

    bias_ref[...] = jnp.zeros_like(bias_ref)

    @pl.when(has_old)
    def _():
        bias_ref[:, :256] = old_bias(rows, group_index)
        bias_ref[:, 256:] = old_bias(rows, group_index ^ 2)

    wait_rows(kv_ref, steps, 4, sem)
    lane = lax.broadcasted_iota(jnp.int32, stat_ref.shape[1:], 1)

    def begin(t, most_ref):
        for copy in copies(t):
            copy.wait()
        most_ref[...] = jnp.where(lane < 64, stat_ref[t], masked_score)

    def finish(t):
        stat = stat_ref[t]
        factor = jnp.exp(stat[:, :1] - top_ref[...])
        sums = stat[:, 64:65] * factor + jnp.sum(sum_ref[...], axis=1, keepdims=True)
        inverse = 1.0 / sums
        old = factor * inverse
        mixed = acc_ref[t] * join([old, old]) + values_ref[...] * join([inverse, inverse])
        roped_ref[t] = mixed.astype(jnp.bfloat16)

    attention(
        steps, roped_ref, kv_ref, bias_ref, (s_0, s_1), (most_0, most_1), top_ref, sum_ref, values_ref,
        begin, finish,
    )

    for copy in pool_loads:
        copy.wait()
    for copy in pool_stores:
        copy.start()
    weight_copy.wait()

    def out_copy(n, columns):
        return pltpu.make_async_copy(stage_ref.at[n % 2], hidden_ref.at[:, columns], out_sems.at[n % 2])

    def project(n, carry):
        columns = pl.ds(pl.multiple_of(n * chunk, chunk), chunk)

        @pl.when(n >= 2)
        def _():
            out_copy(n, columns).wait()

        attended = join(
            [
                roped_ref[t, one * rows : (one + 1) * rows, :]
                for t in range(items)
                for one in range(head_pair)
            ]
        )
        stage_ref[n % 2] = jnp.dot(
            attended, w_ref[:, columns], preferred_element_type=jnp.float32
        ).astype(jnp.bfloat16)
        out_copy(n, columns).start()
        return carry

    lax.fori_loop(0, chunks, project, 0)
    for n in range(2):
        out_copy(n, pl.ds(0, chunk)).wait()
    for copy in pool_stores:
        copy.wait()


def rest_part(lengths, state, slots, weight, key_cache, value_cache):
    items, pair_rows, _ = state[0].shape
    rows = pair_rows // head_pair
    width = weight.shape[1]
    chunk = 512
    return pl.pallas_call(
        rest_kernel,
        out_shape=(
            pltpu.HBM((rows, width), jnp.bfloat16),
            pltpu.HBM(key_cache.shape, jnp.bfloat16),
            pltpu.HBM(value_cache.shape, jnp.bfloat16),
        ),
        in_specs=[smem_spec] + [hbm_spec] * 3 + [any_spec] * 7 + [hbm_spec] * 3,
        out_specs=(hbm_spec,) * 3,
        scratch_shapes=state_shapes(items, rows)
        + working(rows, 4)
        + [
            pltpu.VMEM(weight.shape, jnp.bfloat16),
            pltpu.VMEM((2, rows, chunk), jnp.bfloat16),
            pltpu.VMEM(key_cache.shape, jnp.bfloat16),
            pltpu.VMEM(value_cache.shape, jnp.bfloat16),
            pltpu.SemaphoreType.DMA((3, items)),
            pltpu.SemaphoreType.DMA,
            pltpu.SemaphoreType.DMA,
            pltpu.SemaphoreType.DMA((2,)),
            pltpu.SemaphoreType.DMA((2,)),
        ],
        cost_estimate=light,
        compiler_params=params(large_limit),
        name="attend_rest",
    )(lengths, *in_hbm(*state), *slots, *in_hbm(weight, key_cache, value_cache))


def place_kernel(targets_ref, arrived_ref, key_in, value_in, key_ref, value_ref, buffer_ref, load_sem, sem):
    load = pltpu.make_async_copy(arrived_ref, buffer_ref, load_sem)
    load.start()
    load.wait()

    def each(act):
        for slot in range(targets_ref.shape[0]):
            page = targets_ref[slot]

            @pl.when(page >= 0)
            def _(slot=slot, page=page):
                for kind, out_ref in enumerate((key_ref, value_ref)):
                    act(pltpu.make_async_copy(buffer_ref.at[slot, kind], out_ref.at[page], sem))

    each(lambda copy: copy.start())
    each(lambda copy: copy.wait())


def place_new(targets, arrived, key_pool, value_pool):
    return pl.pallas_call(
        place_kernel,
        out_shape=(
            pltpu.HBM(key_pool.shape, jnp.bfloat16),
            pltpu.HBM(value_pool.shape, jnp.bfloat16),
        ),
        in_specs=[smem_spec, any_spec, hbm_spec, hbm_spec],
        out_specs=(hbm_spec,) * 2,
        input_output_aliases={2: 0, 3: 1},
        scratch_shapes=[
            pltpu.VMEM(arrived.shape, jnp.bfloat16),
            pltpu.SemaphoreType.DMA,
            pltpu.SemaphoreType.DMA,
        ],
        cost_estimate=light,
        compiler_params=params(small_limit),
        name="place_new",
    )(targets, arrived, *in_hbm(key_pool, value_pool))


def after(value, *others):
    return lax.optimization_barrier((value,) + others)[0]


def body(queries, new_keys, new_values, key_cache, value_cache, out_weight, lengths, page_table):
    blk_count = lax.axis_size("blk")
    pages = key_cache.shape[0]
    window_pages = page_table.shape[1] // 2
    cap = (window_pages + blk_count - 1) // blk_count

    def other_core(value):
        return lax.ppermute(value, "group", [(0, 1), (1, 0), (2, 3), (3, 2)])

    def other_chip(value):
        return lax.ppermute(value, "group", [(0, 2), (2, 0), (1, 3), (3, 1)])

    partners = blk_count if blk_count <= 8 and blk_count & (blk_count - 1) == 0 else 1
    picked = pick_old(page_table, cap, partners, key_cache, value_cache)
    if partners > 1:
        olds = [picked[0]] + [None] * (partners - 1)
        for number in reversed(range(1, partners)):
            pairs = [(i, i ^ number) for i in range(blk_count)]
            olds[number] = lax.ppermute(picked[number], "blk", pairs)
    else:
        olds = [lax.all_to_all(picked[0], "blk", split_axis=0, concat_axis=0, tiled=True)]

    fresh, cosine, sine = rotate_keys(lengths, after(new_keys[0], picked[0]), new_values[0])
    fresh_far = other_chip(fresh)
    fresh_core = other_core(fresh)

    roped, acc, stat = diagonal_part(after(queries[0], picked[0]), cosine, sine, fresh)

    old = sort_old(after(page_table, stat), blk_count, cap, pages, olds)
    old_far = other_chip(old)
    old_core = other_core(old)
    fresh_far_core = other_core(after(fresh_far, old))
    new, targets = pick_new(
        page_table, blk_count, cap, pages, (fresh, fresh_core, fresh_far, fresh_far_core)
    )
    arrived = lax.all_to_all(new, "blk", split_axis=0, concat_axis=0, tiled=True)
    old_far_core = other_core(after(old_far, new))
    hidden, key_out, value_out = rest_part(
        lengths, (roped, acc, stat),
        (fresh_core, fresh_far, fresh_far_core, old, old_core, old_far, old_far_core),
        out_weight, key_cache, value_cache,
    )
    key_out, value_out = place_new(targets, arrived, key_out, value_out)
    return (hidden[None], key_out, value_out)


def solution(mesh):
    return jax.shard_map(
        body,
        mesh=mesh,
        in_specs=(
            P("blk", "group", None),
            P("blk", "group", None),
            P("blk", "group", None),
            P("blk", "group", None),
            P("blk", "group", None),
            P(),
            P(),
            P(),
        ),
        out_specs=(P("blk", "group", None), P("blk", "group", None), P("blk", "group", None)),
        check_vma=False,
    )
```

```python
import jax
import jax.numpy as jnp
import numpy as np
from jax import lax
from jax.experimental import pallas as pl
from jax.experimental.pallas import tpu as pltpu
from jax.sharding import PartitionSpec as P

masked_score = -1e30
step_keys = 512
step_slots = 16
any_spec = pl.BlockSpec(memory_space=pl.ANY)
hbm_spec = pl.BlockSpec(memory_space=pltpu.HBM)
smem_spec = pl.BlockSpec(memory_space=pltpu.SMEM)
vmem_spec = pl.BlockSpec(memory_space=pltpu.VMEM)
small_limit = 16 * 1024 * 1024
head_pair = 2
middle_limit = 32 * 1024 * 1024
large_limit = 58 * 1024 * 1024


light = pl.CostEstimate(flops=1, bytes_accessed=1, transcendentals=0)


def params(limit):
    return pltpu.CompilerParams(vmem_limit_bytes=limit)


def in_hbm(*arrays):
    return [pltpu.with_memory_space_constraint(array, pltpu.HBM) for array in arrays]


def turn(values, cosine, sine):
    front = values[:, :128].astype(jnp.float32)
    return front * cosine + pltpu.roll(front, 64, 1) * sine


def join(pieces):
    return jnp.concatenate(pieces, axis=1)


def pages_here(table_ref, r, first, count, cap, pages):
    low = lax.axis_index("blk") * pages
    found = jnp.int32(0)
    chosen = [jnp.int32(0)] * cap
    for j in range(first, first + count):
        page = table_ref[r, j] - low
        inside = (page >= 0) & (page < pages)
        chosen = [jnp.where(inside & (found == c), page, chosen[c]) for c in range(cap)]
        found = found + inside.astype(jnp.int32)
    return chosen, found


def pick_old_kernel(table_ref, key_ref, value_ref, out_ref, sem):
    requests, cap = out_ref.shape[:2]
    for r in range(requests):
        chosen, _ = pages_here(table_ref, r, 0, table_ref.shape[1] // 2, cap, key_ref.shape[0])
        for c in range(cap):
            pltpu.make_async_copy(key_ref.at[chosen[c]], out_ref.at[r, c, 0], sem).start()
            pltpu.make_async_copy(value_ref.at[chosen[c]], out_ref.at[r, c, 1], sem).start()
    pltpu.make_async_copy(out_ref, out_ref, sem).wait()


def pick_old(page_table, cap, key_cache, value_cache):
    requests = page_table.shape[0]
    return pl.pallas_call(
        pick_old_kernel,
        out_shape=jax.ShapeDtypeStruct((requests, cap, 2) + key_cache.shape[1:], jnp.bfloat16),
        in_specs=[smem_spec, hbm_spec, hbm_spec],
        out_specs=vmem_spec,
        scratch_shapes=[pltpu.SemaphoreType.DMA],
        cost_estimate=light,
        compiler_params=params(small_limit),
        name="pick_old",
    )(*in_hbm(page_table, key_cache, value_cache))


def owner_of(page, pages, owners):
    factor = (1 << 20) // pages + 1
    assert all((p * factor) >> 20 == p // pages for p in range(pages * owners))
    assert pages * owners * factor < 1 << 31
    return (page * factor) >> 20


def find_slots(table_ref, first, count, cap, pages, counts_ref):
    owners = counts_ref.shape[0]
    row = lax.axis_index("blk")
    for o in range(owners):
        counts_ref[o] = 0
    slots = []
    for j in range(count):
        owner = owner_of(table_ref[row, first + j], pages, owners)
        rank = counts_ref[owner]
        counts_ref[owner] = rank + 1
        slots.append(owner * cap + rank)
    return slots


def rotate_kernel(lengths_ref, freq_ref, keys_ref, values_ref, out_ref, cos_ref, sin_ref):
    rows = keys_ref.shape[0]
    slots = rows // 32
    start = lengths_ref[lax.axis_index("blk")] + lax.axis_index("group") * rows
    positions = start + lax.broadcasted_iota(jnp.int32, (rows, 128), 0)
    angles = positions.astype(jnp.float32) * freq_ref[...]
    lane = lax.broadcasted_iota(jnp.int32, (rows, 128), 1)
    cosine = jnp.cos(angles)
    sine = jnp.sin(angles)
    sine = jnp.where(lane < 64, -sine, sine)
    cos_ref[...] = cosine
    sin_ref[...] = sine
    keys = keys_ref[...]
    turned = join([turn(keys, cosine, sine).astype(jnp.bfloat16), keys[:, 128:]])
    out_ref[:, 0] = turned.reshape(slots, 32, 256)
    out_ref[:, 1] = values_ref[...].reshape(slots, 32, 256)


def rotate_keys(lengths, keys, values):
    rows, head_dim = keys.shape
    quarter = head_dim // 4
    freq_table = np.float32(10000.0) ** (-np.arange(quarter, dtype=np.float32) / np.float32(quarter))
    freq_table = np.concatenate([freq_table, freq_table])[None].astype(np.float32)
    return pl.pallas_call(
        rotate_kernel,
        out_shape=(
            pltpu.HBM((rows // 32, 2, 32, head_dim), jnp.bfloat16),
            pltpu.HBM((rows, 128), jnp.float32),
            pltpu.HBM((rows, 128), jnp.float32),
        ),
        in_specs=[smem_spec, vmem_spec, vmem_spec, vmem_spec],
        out_specs=(vmem_spec,) * 3,
        cost_estimate=light,
        compiler_params=params(small_limit),
        name="rotate_keys",
    )(lengths, jnp.asarray(freq_table), keys, values)


def sort_kernel(pages, cap, table_ref, old_ref, out_ref, counts_ref, sem):
    count = out_ref.shape[0]
    for j, slot in enumerate(find_slots(table_ref, 0, count, cap, pages, counts_ref)):
        pltpu.make_async_copy(old_ref.at[slot], out_ref.at[j], sem).start()
    pltpu.make_async_copy(out_ref, out_ref, sem).wait()


def sort_old(page_table, blk_count, cap, pages, old):
    window = page_table.shape[1] // 2
    return pl.pallas_call(
        lambda *refs: sort_kernel(pages, cap, *refs),
        out_shape=jax.ShapeDtypeStruct((window,) + old.shape[1:], jnp.bfloat16),
        in_specs=[smem_spec, hbm_spec],
        out_specs=vmem_spec,
        scratch_shapes=[pltpu.SMEM((blk_count,), jnp.int32), pltpu.SemaphoreType.DMA],
        cost_estimate=light,
        compiler_params=params(small_limit),
        name="sort_old",
    )(*in_hbm(page_table, old))


def pick_new_kernel(
    pages, cap, table_ref, own_ref, core_ref, far_ref, far_core_ref, out_ref, targets_ref,
    slots_ref, counts_ref, sem,
):
    count = slots_ref.shape[0]
    block_pages = count // 4
    group_index = lax.axis_index("group")
    for j, slot in enumerate(find_slots(table_ref, table_ref.shape[1] - count, count, cap, pages, counts_ref)):
        slots_ref[j] = slot
    for number, ref in enumerate((own_ref, core_ref, far_ref, far_core_ref)):
        block = group_index ^ number
        for place in range(block_pages):
            source = ref.at[4 * place + group_index]
            target = out_ref.at[slots_ref[block * block_pages + place]]
            pltpu.make_async_copy(source, target, sem).start()
    for r in range(table_ref.shape[0]):
        chosen, found = pages_here(table_ref, r, table_ref.shape[1] - count, count, cap, pages)
        for c in range(cap):
            targets_ref[r * cap + c] = jnp.where(found > c, chosen[c], -1)
    sent = out_ref.at[pl.ds(0, count)]
    pltpu.make_async_copy(sent, sent, sem).wait()


def pick_new(page_table, blk_count, cap, pages, sources):
    window = page_table.shape[1] // 2
    return pl.pallas_call(
        lambda *refs: pick_new_kernel(pages, cap, *refs),
        out_shape=(
            jax.ShapeDtypeStruct((blk_count * cap,) + sources[0].shape[1:], jnp.bfloat16),
            jax.ShapeDtypeStruct((blk_count * cap,), jnp.int32),
        ),
        in_specs=[smem_spec] + [any_spec] * 4,
        out_specs=(vmem_spec, smem_spec),
        scratch_shapes=[
            pltpu.SMEM((window,), jnp.int32),
            pltpu.SMEM((blk_count,), jnp.int32),
            pltpu.SemaphoreType.DMA,
        ],
        cost_estimate=light,
        compiler_params=params(small_limit),
        name="pick_new",
    )(*in_hbm(page_table), *sources)


def lane_fold(values, combine):
    total = values[:, :128]
    for start in range(128, values.shape[1], 128):
        total = combine(total, values[:, start : start + 128])
    return total


def old_bias(rows, quarter):
    row = lax.broadcasted_iota(jnp.int32, (rows, 256), 0)
    column = lax.broadcasted_iota(jnp.int32, (rows, 256), 1)
    held = quarter ^ (column // 128)
    position = ((column % 128) // 32) * 128 + 32 * held + column % 32
    return jnp.where(position > row, 0.0, masked_score)


def fetch(source, first, kv_ref, place, count, sem):
    for kind in range(2):
        pltpu.make_async_copy(
            source.at[pl.ds(first, count), kind], kv_ref.at[kind, pl.ds(place, count)], sem
        ).start()


def fetch_pair(sources, first, kv_ref, place, sem):
    fetch(sources[0], first, kv_ref, place, 4, sem)
    fetch(sources[1], first, kv_ref, place + 4, 4, sem)


def wait_rows(kv_ref, steps, most, sem):
    for n in range(1, most + 1):

        @pl.when(steps == n)
        def _(n=n):
            filled = kv_ref.at[:, pl.ds(0, n * step_slots)]
            pltpu.make_async_copy(filled, filled, sem).wait()


def attention(steps, roped_ref, kv_ref, bias_ref, s_refs, most_refs, top_ref, sum_ref, sum_of_values, begin, finish):
    items, rows, _ = roped_ref.shape

    def block(kind, c):
        return kv_ref[kind, pl.ds(c * step_slots, step_slots)].reshape(step_keys, 256)

    def scores(t, c, which, masked):
        result = lax.dot_general(
            roped_ref[t], block(0, c), (((1,), (1,)), ((), ())), preferred_element_type=jnp.float32
        )
        if masked:
            result = result.reshape(head_pair, rows // head_pair, step_keys) + bias_ref[...]
            result = result.reshape(rows, step_keys)
        s_refs[which][c] = result
        most_refs[which][...] = jnp.maximum(most_refs[which][...], lane_fold(result, jnp.maximum))

    def weigh(c, which):
        weights = jnp.exp(s_refs[which][c] - join([top_ref[...]] * (step_keys // 128)))
        sum_ref[...] += lane_fold(weights, jnp.add)
        sum_of_values[...] += jnp.dot(
            weights.astype(jnp.bfloat16), block(1, c), preferred_element_type=jnp.float32
        )

    def settle(which):
        top_ref[...] = jnp.broadcast_to(
            jnp.max(most_refs[which][...], axis=1, keepdims=True), top_ref.shape
        )
        sum_ref[...] = jnp.zeros_like(sum_ref)
        sum_of_values[...] = jnp.zeros_like(sum_of_values)

    def loop(work):
        def step(c, carry):
            work(c, False)
            return carry

        if isinstance(steps, int):
            for c in range(steps):
                work(c, c == 0)
            return

        @pl.when(steps > 0)
        def _():
            work(0, True)

        lax.fori_loop(1, steps, step, 0)

    def one(t, which):
        begin(t + 1, most_refs[1 - which])
        settle(which)

        def work(c, masked):
            weigh(c, which)
            scores(t + 1, c, 1 - which, masked)

        loop(work)
        finish(t)

    def two(i, carry):
        one(2 * i, 0)
        one(2 * i + 1, 1)
        return carry

    begin(0, most_refs[0])
    loop(lambda c, masked: scores(0, c, 0, masked))
    pairs = (items - 1) // 2
    lax.fori_loop(0, pairs, two, 0)
    last = 2 * pairs
    if last < items - 1:
        one(last, 0)
        last += 1
    settle(last % 2)
    loop(lambda c, masked: weigh(c, last % 2))
    finish(last)


def working(rows, steps):
    return [
        pltpu.VMEM((2, steps * step_slots, 32, 256), jnp.bfloat16),
        pltpu.VMEM((steps, head_pair * rows, step_keys), jnp.float32),
        pltpu.VMEM((steps, head_pair * rows, step_keys), jnp.float32),
        pltpu.VMEM((head_pair * rows, 128), jnp.float32),
        pltpu.VMEM((head_pair * rows, 128), jnp.float32),
        pltpu.VMEM((head_pair * rows, 128), jnp.float32),
        pltpu.VMEM((head_pair * rows, 128), jnp.float32),
        pltpu.VMEM((head_pair * rows, 256), jnp.float32),
        pltpu.VMEM((rows, step_keys), jnp.float32),
    ]


def state_shapes(items, rows):
    return [
        pltpu.VMEM((items, head_pair * rows, 256), jnp.bfloat16),
        pltpu.VMEM((items, head_pair * rows, 256), jnp.float32),
        pltpu.VMEM((items, head_pair * rows, 128), jnp.float32),
    ]


def state_out(items, rows):
    return (
        pltpu.HBM((items, head_pair * rows, 256), jnp.float32),
        pltpu.HBM((items, head_pair * rows, 128), jnp.float32),
    )


def diagonal_kernel(
    first, query_ref, cos_ref, sin_ref, own_ref, roped_out, acc_out, stat_out,
    q_ref, roped_ref, acc_ref, stat_ref, kv_ref, s_0, s_1, most_0, most_1, top_ref, sum_ref, values_ref,
    bias_ref, query_sem, sem, out_sem,
):
    rows = q_ref.shape[0]
    items = roped_ref.shape[0]
    columns = pl.ds(first * head_pair * 256, items * head_pair * 256)
    query_copy = pltpu.make_async_copy(query_ref.at[:, columns], q_ref, query_sem)
    query_copy.start()
    fetch(own_ref, 0, kv_ref, 0, step_slots, sem)
    row = lax.broadcasted_iota(jnp.int32, (rows, step_keys), 0)
    column = lax.broadcasted_iota(jnp.int32, (rows, step_keys), 1)
    bias_ref[...] = jnp.where(column <= row, 0.0, masked_score)
    query_copy.wait()

    def rope(t, carry):
        for one in range(head_pair):
            raw = q_ref[:, pl.ds(pl.multiple_of((t * head_pair + one) * 256, 256), 256)]
            front = turn(raw, cos_ref[...], sin_ref[...])
            some = pl.ds(one * rows, rows)
            roped_ref[t, some, :128] = (front * 0.0625).astype(jnp.bfloat16)
            roped_ref[t, some, 128:] = raw[:, 128:] * jnp.bfloat16(0.0625)
        return carry

    lax.fori_loop(0, items, rope, 0)
    roped_copy = pltpu.make_async_copy(roped_ref, roped_out, query_sem)
    roped_copy.start()
    pltpu.make_async_copy(kv_ref, kv_ref, sem).wait()

    def begin(t, most_ref):
        most_ref[...] = jnp.full_like(most_ref, masked_score)

    def finish(t):
        lane = lax.broadcasted_iota(jnp.int32, stat_ref.shape[1:], 1)
        sums = jnp.sum(sum_ref[...], axis=1, keepdims=True)
        stat_ref[t] = jnp.where(lane < 64, top_ref[...], sums)
        acc_ref[t] = values_ref[...]
        pltpu.make_async_copy(acc_ref.at[t], acc_out.at[t], out_sem).start()
        pltpu.make_async_copy(stat_ref.at[t], stat_out.at[t], out_sem).start()

    attention(
        1, roped_ref, kv_ref, bias_ref, (s_0, s_1), (most_0, most_1), top_ref, sum_ref, values_ref,
        begin, finish,
    )
    roped_copy.wait()
    pltpu.make_async_copy(acc_ref, acc_out, out_sem).wait()
    pltpu.make_async_copy(stat_ref, stat_out, out_sem).wait()


def diagonal_part(first, items, queries, cosine, sine, own):
    rows = queries.shape[0]
    return pl.pallas_call(
        lambda *refs: diagonal_kernel(first, *refs),
        out_shape=(pltpu.HBM((items, head_pair * rows, 256), jnp.bfloat16),) + state_out(items, rows),
        in_specs=[hbm_spec, vmem_spec, vmem_spec, hbm_spec],
        out_specs=(hbm_spec,) * 3,
        scratch_shapes=[pltpu.VMEM((rows, items * head_pair * 256), jnp.bfloat16)]
        + state_shapes(items, rows)
        + working(rows, 1)
        + [pltpu.SemaphoreType.DMA] * 3,
        cost_estimate=light,
        compiler_params=params(middle_limit),
        name="attend_diagonal",
    )(*in_hbm(queries), cosine, sine, *in_hbm(own))


def rest_kernel(
    lengths_ref, roped_a, acc_a, stat_a, roped_b, acc_b, stat_b, core_ref, far_ref, far_core_ref,
    old_ref, old_core_ref, old_far_ref, old_far_core_ref, weight_ref, key_ref, value_ref,
    hidden_ref, key_out_ref, value_out_ref,
    roped_ref, acc_ref, stat_ref, kv_ref, s_0, s_1, most_0, most_1, top_ref, sum_ref, values_ref,
    bias_ref, w_ref, stage_ref, key_pool, value_pool,
    state_sems, sem, weight_sem, pool_sems, out_sems,
):
    group_index = lax.axis_index("group")
    has_old = lengths_ref[lax.axis_index("blk")] > 0
    items = roped_ref.shape[0]
    rows = bias_ref.shape[0]
    chunk = stage_ref.shape[2]
    chunks = w_ref.shape[1] // chunk
    odd = group_index % 2
    chip = group_index // 2
    steps = jnp.where(has_old, 4, odd + 2 * chip)
    base = jnp.where(has_old, 16, 0)
    near = (old_ref, old_core_ref)
    far = (old_far_ref, old_far_core_ref)

    state = (roped_ref, stat_ref, acc_ref)
    head_start = roped_a.shape[0]

    def start_state(t):
        sources = (roped_a, stat_a, acc_a) if t < head_start else (roped_b, stat_b, acc_b)
        for number, (source, target) in enumerate(zip(sources, state)):
            place = t if t < head_start else t - head_start
            pltpu.make_async_copy(source.at[place], target.at[t], state_sems.at[number, t]).start()

    def wait_state(t):
        for number, target in enumerate(state):
            pltpu.make_async_copy(target.at[t], target.at[t], state_sems.at[number, t]).wait()

    pool_loads = [
        pltpu.make_async_copy(key_ref, key_pool, pool_sems.at[0]),
        pltpu.make_async_copy(value_ref, value_pool, pool_sems.at[1]),
    ]
    pool_stores = [
        pltpu.make_async_copy(key_pool, key_out_ref, pool_sems.at[0]),
        pltpu.make_async_copy(value_pool, value_out_ref, pool_sems.at[1]),
    ]
    start_state(0)

    @pl.when(odd == 1)
    def _():
        fetch(core_ref, 0, kv_ref, base, 16, sem)

    @pl.when(chip == 1)
    def _():
        place = base + 16 * jnp.where(has_old, 1, odd)
        fetch(far_ref, 0, kv_ref, place, 16, sem)
        fetch(far_core_ref, 0, kv_ref, place + 16, 16, sem)

    @pl.when(has_old)
    def _():
        for block in range(4):

            @pl.when(block >= group_index)
            def _(block=block):
                gap = jnp.where(block == group_index, 0, odd)
                place = 16 * (gap + block - group_index)
                fetch_pair(near, 4 * block, kv_ref, place, sem)
                fetch_pair(far, 4 * block, kv_ref, place + 8, sem)

    for copy in pool_loads:
        copy.start()
    for t in range(1, items):
        start_state(t)
    weight_copy = pltpu.make_async_copy(weight_ref, w_ref, weight_sem)
    weight_copy.start()

    bias_ref[...] = jnp.zeros_like(bias_ref)

    @pl.when(has_old)
    def _():
        bias_ref[:, :256] = old_bias(rows, group_index)
        bias_ref[:, 256:] = old_bias(rows, group_index ^ 2)

    wait_rows(kv_ref, steps, 4, sem)
    lane = lax.broadcasted_iota(jnp.int32, stat_ref.shape[1:], 1)

    def begin(t, most_ref):
        wait_state(t)
        most_ref[...] = jnp.where(lane < 64, stat_ref[t], masked_score)

    def finish(t):
        stat = stat_ref[t]
        factor = jnp.exp(stat[:, :1] - top_ref[...])
        sums = stat[:, 64:65] * factor + jnp.sum(sum_ref[...], axis=1, keepdims=True)
        inverse = 1.0 / sums
        old = factor * inverse
        mixed = acc_ref[t] * join([old, old]) + values_ref[...] * join([inverse, inverse])
        roped_ref[t] = mixed.astype(jnp.bfloat16)

    attention(
        steps, roped_ref, kv_ref, bias_ref, (s_0, s_1), (most_0, most_1), top_ref, sum_ref, values_ref,
        begin, finish,
    )

    for copy in pool_loads:
        copy.wait()
    for copy in pool_stores:
        copy.start()
    weight_copy.wait()

    def out_copy(n, columns):
        return pltpu.make_async_copy(stage_ref.at[n % 2], hidden_ref.at[:, columns], out_sems.at[n % 2])

    def project(n, carry):
        columns = pl.ds(pl.multiple_of(n * chunk, chunk), chunk)

        @pl.when(n >= 2)
        def _():
            out_copy(n, columns).wait()

        attended = join(
            [
                roped_ref[t, one * rows : (one + 1) * rows, :]
                for t in range(items)
                for one in range(head_pair)
            ]
        )
        stage_ref[n % 2] = jnp.dot(
            attended, w_ref[:, columns], preferred_element_type=jnp.float32
        ).astype(jnp.bfloat16)
        out_copy(n, columns).start()
        return carry

    lax.fori_loop(0, chunks, project, 0)
    for n in range(2):
        out_copy(n, pl.ds(0, chunk)).wait()
    for copy in pool_stores:
        copy.wait()


def rest_part(lengths, states, slots, weight, key_cache, value_cache):
    items = sum(state[0].shape[0] for state in states)
    pair_rows = states[0][0].shape[1]
    rows = pair_rows // head_pair
    width = weight.shape[1]
    chunk = 256
    return pl.pallas_call(
        rest_kernel,
        out_shape=(
            pltpu.HBM((rows, width), jnp.bfloat16),
            pltpu.HBM(key_cache.shape, jnp.bfloat16),
            pltpu.HBM(value_cache.shape, jnp.bfloat16),
        ),
        in_specs=[smem_spec] + [hbm_spec] * 6 + [any_spec] * 7 + [hbm_spec] * 3,
        out_specs=(hbm_spec,) * 3,
        scratch_shapes=state_shapes(items, rows)
        + working(rows, 4)
        + [
            pltpu.VMEM(weight.shape, jnp.bfloat16),
            pltpu.VMEM((2, rows, chunk), jnp.bfloat16),
            pltpu.VMEM(key_cache.shape, jnp.bfloat16),
            pltpu.VMEM(value_cache.shape, jnp.bfloat16),
            pltpu.SemaphoreType.DMA((3, items)),
            pltpu.SemaphoreType.DMA,
            pltpu.SemaphoreType.DMA,
            pltpu.SemaphoreType.DMA((2,)),
            pltpu.SemaphoreType.DMA((2,)),
        ],
        cost_estimate=light,
        compiler_params=params(large_limit),
        name="attend_rest",
    )(lengths, *in_hbm(*states[0], *states[1]), *slots, *in_hbm(weight, key_cache, value_cache))


def place_kernel(targets_ref, arrived_ref, key_in, value_in, key_ref, value_ref, buffer_ref, load_sem, sem):
    load = pltpu.make_async_copy(arrived_ref, buffer_ref, load_sem)
    load.start()
    load.wait()

    def each(act):
        for slot in range(targets_ref.shape[0]):
            page = targets_ref[slot]

            @pl.when(page >= 0)
            def _(slot=slot, page=page):
                for kind, out_ref in enumerate((key_ref, value_ref)):
                    act(pltpu.make_async_copy(buffer_ref.at[slot, kind], out_ref.at[page], sem))

    each(lambda copy: copy.start())
    each(lambda copy: copy.wait())


def place_new(targets, arrived, key_pool, value_pool):
    return pl.pallas_call(
        place_kernel,
        out_shape=(
            pltpu.HBM(key_pool.shape, jnp.bfloat16),
            pltpu.HBM(value_pool.shape, jnp.bfloat16),
        ),
        in_specs=[smem_spec, any_spec, hbm_spec, hbm_spec],
        out_specs=(hbm_spec,) * 2,
        input_output_aliases={2: 0, 3: 1},
        scratch_shapes=[
            pltpu.VMEM(arrived.shape, jnp.bfloat16),
            pltpu.SemaphoreType.DMA,
            pltpu.SemaphoreType.DMA,
        ],
        cost_estimate=light,
        compiler_params=params(small_limit),
        name="place_new",
    )(targets, arrived, *in_hbm(key_pool, value_pool))


def after(value, *others):
    return lax.optimization_barrier((value,) + others)[0]


def body(queries, new_keys, new_values, key_cache, value_cache, out_weight, lengths, page_table):
    blk_count = lax.axis_size("blk")
    pages = key_cache.shape[0]
    window_pages = page_table.shape[1] // 2
    cap = (window_pages + blk_count - 1) // blk_count

    def other_core(value):
        return lax.ppermute(value, "group", [(0, 1), (1, 0), (2, 3), (3, 2)])

    def other_chip(value):
        return lax.ppermute(value, "group", [(0, 2), (2, 0), (1, 3), (3, 1)])

    picked = pick_old(page_table, cap, key_cache, value_cache)
    old = lax.all_to_all(picked, "blk", split_axis=0, concat_axis=0, tiled=True)
    old = old.reshape((blk_count * cap,) + old.shape[2:])

    fresh, cosine, sine = rotate_keys(lengths, new_keys[0], new_values[0])
    fresh_far = other_chip(fresh)
    fresh_core = other_core(fresh)
    pairs = queries.shape[2] // (256 * head_pair)
    front = (pairs + 1) // 2
    state = diagonal_part(0, front, after(queries[0], picked), cosine, sine, fresh)

    old = sort_old(after(page_table, state[2]), blk_count, cap, pages, old)
    old_far = other_chip(old)
    old_core = other_core(old)
    later = diagonal_part(front, pairs - front, after(queries[0], old), cosine, sine, fresh)
    fresh_far_core = other_core(after(fresh_far, old))
    new, targets = pick_new(
        after(page_table, later[2]), blk_count, cap, pages, (fresh, fresh_core, fresh_far, fresh_far_core)
    )
    arrived = lax.all_to_all(new, "blk", split_axis=0, concat_axis=0, tiled=True)
    old_far_core = other_core(after(old_far, new))
    hidden, key_out, value_out = rest_part(
        lengths, (state, later),
        (fresh_core, fresh_far, fresh_far_core, old, old_core, old_far, old_far_core),
        out_weight, key_cache, value_cache,
    )
    key_out, value_out = place_new(targets, arrived, key_out, value_out)
    return (hidden[None], key_out, value_out)


def solution(mesh):
    return jax.shard_map(
        body,
        mesh=mesh,
        in_specs=(
            P("blk", "group", None),
            P("blk", "group", None),
            P("blk", "group", None),
            P("blk", "group", None),
            P("blk", "group", None),
            P(),
            P(),
            P(),
        ),
        out_specs=(P("blk", "group", None), P("blk", "group", None), P("blk", "group", None)),
        check_vma=False,
    )
```

```python
import jax
import jax.numpy as jnp
import numpy as np
from jax import lax
from jax.experimental import pallas as pl
from jax.experimental.pallas import tpu as pltpu
from jax.sharding import PartitionSpec as P

masked_score = -1e30
block_keys = 512
block_slots = 16
any_spec = pl.BlockSpec(memory_space=pl.ANY)
hbm_spec = pl.BlockSpec(memory_space=pltpu.HBM)
smem_spec = pl.BlockSpec(memory_space=pltpu.SMEM)
vmem_spec = pl.BlockSpec(memory_space=pltpu.VMEM)
small_limit = 16 * 1024 * 1024
head_pair = 2
large_limit = 58 * 1024 * 1024


light = pl.CostEstimate(flops=1, bytes_accessed=1, transcendentals=0)


def params(limit):
    return pltpu.CompilerParams(vmem_limit_bytes=limit)


def in_hbm(*arrays):
    return [pltpu.with_memory_space_constraint(array, pltpu.HBM) for array in arrays]


def turn(values, cosine, sine):
    front = values[:, :128].astype(jnp.float32)
    return front * cosine + pltpu.roll(front, 64, 1) * sine


def join(pieces):
    return jnp.concatenate(pieces, axis=1)


def pages_here(table_ref, r, first, count, cap, pages):
    low = lax.axis_index("blk") * pages
    found = jnp.int32(0)
    chosen = [jnp.int32(0)] * cap
    for j in range(first, first + count):
        page = table_ref[r, j] - low
        inside = (page >= 0) & (page < pages)
        chosen = [jnp.where(inside & (found == c), page, chosen[c]) for c in range(cap)]
        found = found + inside.astype(jnp.int32)
    return chosen, found


def pick_old_kernel(table_ref, key_ref, value_ref, out_ref, sem):
    requests, cap = out_ref.shape[:2]
    for r in range(requests):
        chosen, _ = pages_here(table_ref, r, 0, table_ref.shape[1] // 2, cap, key_ref.shape[0])
        for c in range(cap):
            pltpu.make_async_copy(key_ref.at[chosen[c]], out_ref.at[r, c, 0], sem).start()
            pltpu.make_async_copy(value_ref.at[chosen[c]], out_ref.at[r, c, 1], sem).start()
    pltpu.make_async_copy(out_ref, out_ref, sem).wait()


def pick_old(page_table, cap, key_cache, value_cache):
    requests = page_table.shape[0]
    return pl.pallas_call(
        pick_old_kernel,
        out_shape=jax.ShapeDtypeStruct((requests, cap, 2) + key_cache.shape[1:], jnp.bfloat16),
        in_specs=[smem_spec, hbm_spec, hbm_spec],
        out_specs=vmem_spec,
        scratch_shapes=[pltpu.SemaphoreType.DMA],
        cost_estimate=light,
        compiler_params=params(small_limit),
        name="pick_old",
    )(*in_hbm(page_table, key_cache, value_cache))


def owner_of(page, pages, owners):
    factor = (1 << 20) // pages + 1
    assert all((p * factor) >> 20 == p // pages for p in range(pages * owners))
    assert pages * owners * factor < 1 << 31
    return (page * factor) >> 20


def find_slots(table_ref, first, count, cap, pages, counts_ref):
    owners = counts_ref.shape[0]
    row = lax.axis_index("blk")
    for o in range(owners):
        counts_ref[o] = 0
    slots = []
    for j in range(count):
        owner = owner_of(table_ref[row, first + j], pages, owners)
        rank = counts_ref[owner]
        counts_ref[owner] = rank + 1
        slots.append(owner * cap + rank)
    return slots


def rotate_kernel(lengths_ref, freq_ref, keys_ref, values_ref, out_ref, cos_ref, sin_ref):
    rows = keys_ref.shape[0]
    slots = rows // 32
    start = lengths_ref[lax.axis_index("blk")] + lax.axis_index("group") * rows
    positions = start + lax.broadcasted_iota(jnp.int32, (rows, 128), 0)
    angles = positions.astype(jnp.float32) * freq_ref[...]
    lane = lax.broadcasted_iota(jnp.int32, (rows, 128), 1)
    cosine = jnp.cos(angles)
    sine = jnp.sin(angles)
    sine = jnp.where(lane < 64, -sine, sine)
    cos_ref[...] = cosine
    sin_ref[...] = sine
    keys = keys_ref[...]
    turned = join([turn(keys, cosine, sine).astype(jnp.bfloat16), keys[:, 128:]])
    out_ref[:, 0] = turned.reshape(slots, 32, 256)
    out_ref[:, 1] = values_ref[...].reshape(slots, 32, 256)


def rotate_keys(lengths, keys, values):
    rows, head_dim = keys.shape
    quarter = head_dim // 4
    freq_table = np.float32(10000.0) ** (-np.arange(quarter, dtype=np.float32) / np.float32(quarter))
    freq_table = np.concatenate([freq_table, freq_table])[None].astype(np.float32)
    return pl.pallas_call(
        rotate_kernel,
        out_shape=(
            pltpu.HBM((rows // 32, 2, 32, head_dim), jnp.bfloat16),
            pltpu.HBM((rows, 128), jnp.float32),
            pltpu.HBM((rows, 128), jnp.float32),
        ),
        in_specs=[smem_spec, vmem_spec, vmem_spec, vmem_spec],
        out_specs=(vmem_spec,) * 3,
        cost_estimate=light,
        compiler_params=params(small_limit),
        name="rotate_keys",
    )(lengths, jnp.asarray(freq_table), keys, values)


def sort_kernel(pages, cap, table_ref, old_ref, out_ref, counts_ref, sem):
    count = out_ref.shape[0]
    for j, slot in enumerate(find_slots(table_ref, 0, count, cap, pages, counts_ref)):
        pltpu.make_async_copy(old_ref.at[slot], out_ref.at[j], sem).start()
    pltpu.make_async_copy(out_ref, out_ref, sem).wait()


def sort_old(page_table, blk_count, cap, pages, old):
    window = page_table.shape[1] // 2
    return pl.pallas_call(
        lambda *refs: sort_kernel(pages, cap, *refs),
        out_shape=jax.ShapeDtypeStruct((window,) + old.shape[1:], jnp.bfloat16),
        in_specs=[smem_spec, hbm_spec],
        out_specs=vmem_spec,
        scratch_shapes=[pltpu.SMEM((blk_count,), jnp.int32), pltpu.SemaphoreType.DMA],
        cost_estimate=light,
        compiler_params=params(small_limit),
        name="sort_old",
    )(page_table, *in_hbm(old))


def pick_new_kernel(
    pages, cap, table_ref, own_ref, core_ref, far_ref, far_core_ref, out_ref, targets_ref,
    slots_ref, counts_ref, sem,
):
    count = slots_ref.shape[0]
    block_pages = count // 4
    group_index = lax.axis_index("group")
    for j, slot in enumerate(find_slots(table_ref, table_ref.shape[1] - count, count, cap, pages, counts_ref)):
        slots_ref[j] = slot
    for number, ref in enumerate((own_ref, core_ref, far_ref, far_core_ref)):
        block = group_index ^ number
        for place in range(block_pages):
            source = ref.at[4 * place + group_index]
            target = out_ref.at[slots_ref[block * block_pages + place]]
            pltpu.make_async_copy(source, target, sem).start()
    for r in range(table_ref.shape[0]):
        chosen, found = pages_here(table_ref, r, table_ref.shape[1] - count, count, cap, pages)
        for c in range(cap):
            targets_ref[r * cap + c] = jnp.where(found > c, chosen[c], -1)
    sent = out_ref.at[pl.ds(0, count)]
    pltpu.make_async_copy(sent, sent, sem).wait()


def pick_new(page_table, blk_count, cap, pages, sources):
    window = page_table.shape[1] // 2
    return pl.pallas_call(
        lambda *refs: pick_new_kernel(pages, cap, *refs),
        out_shape=(
            jax.ShapeDtypeStruct((blk_count * cap,) + sources[0].shape[1:], jnp.bfloat16),
            jax.ShapeDtypeStruct((blk_count * cap,), jnp.int32),
        ),
        in_specs=[smem_spec] + [any_spec] * 4,
        out_specs=(vmem_spec, smem_spec),
        scratch_shapes=[
            pltpu.SMEM((window,), jnp.int32),
            pltpu.SMEM((blk_count,), jnp.int32),
            pltpu.SemaphoreType.DMA,
        ],
        cost_estimate=light,
        compiler_params=params(small_limit),
        name="pick_new",
    )(page_table, *sources)


def lane_fold(values, combine):
    total = values[:, :128]
    for start in range(128, values.shape[1], 128):
        total = combine(total, values[:, start : start + 128])
    return total


def old_bias(rows, quarter):
    row = lax.broadcasted_iota(jnp.int32, (rows, 256), 0)
    column = lax.broadcasted_iota(jnp.int32, (rows, 256), 1)
    held = quarter ^ (column // 128)
    position = ((column % 128) // 32) * 128 + 32 * held + column % 32
    return jnp.where(position > row, 0.0, masked_score)


def fetch(source, first, kv_ref, place, count, sem):
    for kind in range(2):
        pltpu.make_async_copy(
            source.at[pl.ds(first, count), kind], kv_ref.at[kind, pl.ds(place, count)], sem
        ).start()


def fetch_pair(sources, first, kv_ref, place, sem):
    fetch(sources[0], first, kv_ref, place, 4, sem)
    fetch(sources[1], first, kv_ref, place + 4, 4, sem)


def wait_rows(kv_ref, blocks, most, sem):
    for n in range(1, most + 1):

        @pl.when(blocks == n)
        def _(n=n):
            filled = kv_ref.at[:, pl.ds(0, n * block_slots)]
            pltpu.make_async_copy(filled, filled, sem).wait()


def attention(steps, step_keys, roped_ref, kv_ref, bias_ref, s_refs, most_refs, top_ref, sum_ref, sum_of_values, begin, finish):
    items, rows, _ = roped_ref.shape
    step_slots = step_keys // 32
    biased = bias_ref.shape[1]

    def block(kind, c):
        return kv_ref[kind, pl.ds(c * step_slots, step_slots)].reshape(step_keys, 256)

    def scores(t, c, which, masked):
        result = lax.dot_general(
            roped_ref[t], block(0, c), (((1,), (1,)), ((), ())), preferred_element_type=jnp.float32
        )
        if masked:
            head = result[:, :biased].reshape(head_pair, rows // head_pair, biased) + bias_ref[...]
            head = head.reshape(rows, biased)
            result = join([head, result[:, biased:]]) if step_keys > biased else head
        s_refs[which][c] = result
        most_refs[which][...] = jnp.maximum(most_refs[which][...], lane_fold(result, jnp.maximum))

    def weigh(c, which):
        weights = jnp.exp(s_refs[which][c] - join([top_ref[...]] * (step_keys // 128)))
        sum_ref[...] += lane_fold(weights, jnp.add)
        sum_of_values[...] += jnp.dot(
            weights.astype(jnp.bfloat16), block(1, c), preferred_element_type=jnp.float32
        )

    def settle(which):
        top_ref[...] = jnp.broadcast_to(
            jnp.max(most_refs[which][...], axis=1, keepdims=True), top_ref.shape
        )
        sum_ref[...] = jnp.zeros_like(sum_ref)
        sum_of_values[...] = jnp.zeros_like(sum_of_values)

    def loop(work):
        def step(c, carry):
            work(c, False)
            return carry

        if isinstance(steps, int):
            for c in range(steps):
                work(c, c == 0)
            return

        @pl.when(steps > 0)
        def _():
            work(0, True)

        lax.fori_loop(1, steps, step, 0)

    def one(t, which):
        begin(t + 1, most_refs[1 - which])
        settle(which)

        def work(c, masked):
            weigh(c, which)
            scores(t + 1, c, 1 - which, masked)

        loop(work)
        finish(t)

    def two(i, carry):
        one(2 * i, 0)
        one(2 * i + 1, 1)
        return carry

    begin(0, most_refs[0])
    loop(lambda c, masked: scores(0, c, 0, masked))
    pairs = (items - 1) // 2
    lax.fori_loop(0, pairs, two, 0)
    last = 2 * pairs
    if last < items - 1:
        one(last, 0)
        last += 1
    settle(last % 2)
    loop(lambda c, masked: weigh(c, last % 2))
    finish(last)


def working(rows, steps, step_keys):
    return [
        pltpu.VMEM((2, steps * step_keys // 32, 32, 256), jnp.bfloat16),
        pltpu.VMEM((steps, head_pair * rows, step_keys), jnp.float32),
        pltpu.VMEM((steps, head_pair * rows, step_keys), jnp.float32),
        pltpu.VMEM((head_pair * rows, 128), jnp.float32),
        pltpu.VMEM((head_pair * rows, 128), jnp.float32),
        pltpu.VMEM((head_pair * rows, 128), jnp.float32),
        pltpu.VMEM((head_pair * rows, 128), jnp.float32),
        pltpu.VMEM((head_pair * rows, 256), jnp.float32),
        pltpu.VMEM((rows, block_keys), jnp.float32),
    ]


def state_shapes(items, rows):
    return [
        pltpu.VMEM((items, head_pair * rows, 256), jnp.bfloat16),
        pltpu.VMEM((items, head_pair * rows, 256), jnp.float32),
        pltpu.VMEM((items, head_pair * rows, 128), jnp.float32),
    ]


def state_out(items, rows):
    return (
        pltpu.HBM((items, head_pair * rows, 256), jnp.float32),
        pltpu.HBM((items, head_pair * rows, 128), jnp.float32),
    )


def diagonal_kernel(
    query_ref, cos_ref, sin_ref, own_ref, roped_out, acc_out, stat_out,
    q_ref, roped_ref, acc_ref, stat_ref, kv_ref, s_0, s_1, most_0, most_1, top_ref, sum_ref, values_ref,
    bias_ref, query_sem, sem, out_sem,
):
    rows = q_ref.shape[0]
    items = roped_ref.shape[0]
    query_copy = pltpu.make_async_copy(query_ref, q_ref, query_sem)
    query_copy.start()
    fetch(own_ref, 0, kv_ref, 0, block_slots, sem)
    row = lax.broadcasted_iota(jnp.int32, (rows, block_keys), 0)
    column = lax.broadcasted_iota(jnp.int32, (rows, block_keys), 1)
    bias_ref[...] = jnp.where(column <= row, 0.0, masked_score)
    query_copy.wait()

    def rope(t, carry):
        for one in range(head_pair):
            raw = q_ref[:, pl.ds(pl.multiple_of((t * head_pair + one) * 256, 256), 256)]
            front = turn(raw, cos_ref[...], sin_ref[...])
            some = pl.ds(one * rows, rows)
            roped_ref[t, some, :128] = (front * 0.0625).astype(jnp.bfloat16)
            roped_ref[t, some, 128:] = raw[:, 128:] * jnp.bfloat16(0.0625)
        return carry

    lax.fori_loop(0, items, rope, 0)
    roped_copy = pltpu.make_async_copy(roped_ref, roped_out, query_sem)
    roped_copy.start()
    pltpu.make_async_copy(kv_ref, kv_ref, sem).wait()

    def begin(t, most_ref):
        most_ref[...] = jnp.full_like(most_ref, masked_score)

    def finish(t):
        lane = lax.broadcasted_iota(jnp.int32, stat_ref.shape[1:], 1)
        sums = jnp.sum(sum_ref[...], axis=1, keepdims=True)
        stat_ref[t] = jnp.where(lane < 64, top_ref[...], sums)
        acc_ref[t] = values_ref[...]
        pltpu.make_async_copy(acc_ref.at[t], acc_out.at[t], out_sem).start()
        pltpu.make_async_copy(stat_ref.at[t], stat_out.at[t], out_sem).start()

    attention(
        1, block_keys, roped_ref, kv_ref, bias_ref, (s_0, s_1), (most_0, most_1), top_ref, sum_ref, values_ref,
        begin, finish,
    )
    roped_copy.wait()
    pltpu.make_async_copy(acc_ref, acc_out, out_sem).wait()
    pltpu.make_async_copy(stat_ref, stat_out, out_sem).wait()


def diagonal_part(queries, cosine, sine, own):
    rows, width = queries.shape
    items = width // (256 * head_pair)
    return pl.pallas_call(
        diagonal_kernel,
        out_shape=(pltpu.HBM((items, head_pair * rows, 256), jnp.bfloat16),) + state_out(items, rows),
        in_specs=[hbm_spec, vmem_spec, vmem_spec, hbm_spec],
        out_specs=(hbm_spec,) * 3,
        scratch_shapes=[pltpu.VMEM((rows, width), jnp.bfloat16)]
        + state_shapes(items, rows)
        + working(rows, 1, block_keys)
        + [pltpu.SemaphoreType.DMA] * 3,
        cost_estimate=light,
        compiler_params=params(large_limit),
        name="attend_diagonal",
    )(*in_hbm(queries), cosine, sine, *in_hbm(own))


def rest_kernel(
    lengths_ref, roped_in, acc_in, stat_in, core_ref, far_ref, far_core_ref,
    old_ref, old_core_ref, old_far_ref, old_far_core_ref, weight_ref, key_ref, value_ref,
    hidden_ref, key_out_ref, value_out_ref,
    roped_ref, acc_ref, stat_ref, kv_ref, s_0, s_1, most_0, most_1, top_ref, sum_ref, values_ref,
    bias_ref, w_ref, stage_ref, key_pool, value_pool,
    state_sems, sem, weight_sem, pool_sems, out_sems,
):
    group_index = lax.axis_index("group")
    has_old = lengths_ref[lax.axis_index("blk")] > 0
    items = roped_ref.shape[0]
    rows = bias_ref.shape[0]
    chunk = stage_ref.shape[2]
    chunks = w_ref.shape[1] // chunk
    odd = group_index % 2
    chip = group_index // 2
    blocks = jnp.where(has_old, 4, odd + 2 * chip)
    steps = jnp.where(has_old, 2, odd + chip)
    base = jnp.where(has_old, 16, 16 * odd)
    near = (old_ref, old_core_ref)
    far = (old_far_ref, old_far_core_ref)

    def copies(t):
        return [
            pltpu.make_async_copy(source.at[t], target.at[t], state_sems.at[number, t])
            for number, (source, target) in enumerate(
                ((roped_in, roped_ref), (stat_in, stat_ref), (acc_in, acc_ref))
            )
        ]

    pool_loads = [
        pltpu.make_async_copy(key_ref, key_pool, pool_sems.at[0]),
        pltpu.make_async_copy(value_ref, value_pool, pool_sems.at[1]),
    ]
    pool_stores = [
        pltpu.make_async_copy(key_pool, key_out_ref, pool_sems.at[0]),
        pltpu.make_async_copy(value_pool, value_out_ref, pool_sems.at[1]),
    ]
    for copy in copies(0):
        copy.start()

    @pl.when(odd == 1)
    def _():
        fetch(core_ref, 0, kv_ref, base, 16, sem)

    @pl.when(chip == 1)
    def _():
        place = jnp.where(has_old, 32, 32 * odd)
        fetch(far_ref, 0, kv_ref, place, 16, sem)
        fetch(far_core_ref, 0, kv_ref, place + 16, 16, sem)

    @pl.when(has_old)
    def _():
        for block in range(4):

            @pl.when(block >= group_index)
            def _(block=block):
                gap = jnp.where(block == group_index, 0, odd)
                place = 16 * (gap + block - group_index)
                fetch_pair(near, 4 * block, kv_ref, place, sem)
                fetch_pair(far, 4 * block, kv_ref, place + 8, sem)

    for copy in pool_loads:
        copy.start()
    for t in range(1, items):
        for copy in copies(t):
            copy.start()
    weight_copy = pltpu.make_async_copy(weight_ref, w_ref, weight_sem)
    weight_copy.start()

    @pl.when(jnp.logical_not(has_old))
    def _():
        bias_ref[...] = jnp.where(odd == 1, masked_score, 0.0) + jnp.zeros_like(bias_ref)
        empty = pl.ds(0, block_slots)

        @pl.when(odd == 1)
        def _():
            kv_ref[:, empty] = jnp.zeros((2, block_slots, 32, 256), jnp.bfloat16)

    @pl.when(has_old)
    def _():
        bias_ref[:, :256] = old_bias(rows, group_index)
        bias_ref[:, 256:] = old_bias(rows, group_index ^ 2)

    wait_rows(kv_ref, blocks, 4, sem)
    lane = lax.broadcasted_iota(jnp.int32, stat_ref.shape[1:], 1)

    def begin(t, most_ref):
        for copy in copies(t):
            copy.wait()
        most_ref[...] = jnp.where(lane < 64, stat_ref[t], masked_score)

    def finish(t):
        stat = stat_ref[t]
        factor = jnp.exp(stat[:, :1] - top_ref[...])
        sums = stat[:, 64:65] * factor + jnp.sum(sum_ref[...], axis=1, keepdims=True)
        inverse = 1.0 / sums
        old = factor * inverse
        mixed = acc_ref[t] * join([old, old]) + values_ref[...] * join([inverse, inverse])
        roped_ref[t] = mixed.astype(jnp.bfloat16)

    attention(
        steps, 2 * block_keys, roped_ref, kv_ref, bias_ref, (s_0, s_1), (most_0, most_1), top_ref, sum_ref, values_ref,
        begin, finish,
    )

    for copy in pool_loads:
        copy.wait()
    for copy in pool_stores:
        copy.start()
    weight_copy.wait()

    def out_copy(n, columns):
        return pltpu.make_async_copy(stage_ref.at[n % 2], hidden_ref.at[:, columns], out_sems.at[n % 2])

    def project(n, carry):
        columns = pl.ds(pl.multiple_of(n * chunk, chunk), chunk)

        @pl.when(n >= 2)
        def _():
            out_copy(n, columns).wait()

        attended = join(
            [
                roped_ref[t, one * rows : (one + 1) * rows, :]
                for t in range(items)
                for one in range(head_pair)
            ]
        )
        stage_ref[n % 2] = jnp.dot(
            attended, w_ref[:, columns], preferred_element_type=jnp.float32
        ).astype(jnp.bfloat16)
        out_copy(n, columns).start()
        return carry

    lax.fori_loop(0, chunks, project, 0)
    for n in range(2):
        out_copy(n, pl.ds(0, chunk)).wait()
    for copy in pool_stores:
        copy.wait()


def rest_part(lengths, state, slots, weight, key_cache, value_cache):
    items, pair_rows, _ = state[0].shape
    rows = pair_rows // head_pair
    width = weight.shape[1]
    chunk = 512
    return pl.pallas_call(
        rest_kernel,
        out_shape=(
            pltpu.HBM((rows, width), jnp.bfloat16),
            pltpu.HBM(key_cache.shape, jnp.bfloat16),
            pltpu.HBM(value_cache.shape, jnp.bfloat16),
        ),
        in_specs=[smem_spec] + [hbm_spec] * 3 + [any_spec] * 7 + [hbm_spec] * 3,
        out_specs=(hbm_spec,) * 3,
        scratch_shapes=state_shapes(items, rows)
        + working(rows, 2, 2 * block_keys)
        + [
            pltpu.VMEM(weight.shape, jnp.bfloat16),
            pltpu.VMEM((2, rows, chunk), jnp.bfloat16),
            pltpu.VMEM(key_cache.shape, jnp.bfloat16),
            pltpu.VMEM(value_cache.shape, jnp.bfloat16),
            pltpu.SemaphoreType.DMA((3, items)),
            pltpu.SemaphoreType.DMA,
            pltpu.SemaphoreType.DMA,
            pltpu.SemaphoreType.DMA((2,)),
            pltpu.SemaphoreType.DMA((2,)),
        ],
        cost_estimate=light,
        compiler_params=params(large_limit),
        name="attend_rest",
    )(lengths, *in_hbm(*state), *slots, *in_hbm(weight, key_cache, value_cache))


def place_kernel(targets_ref, arrived_ref, key_in, value_in, key_ref, value_ref, buffer_ref, load_sem, sem):
    load = pltpu.make_async_copy(arrived_ref, buffer_ref, load_sem)
    load.start()
    load.wait()

    def each(act):
        for slot in range(targets_ref.shape[0]):
            page = targets_ref[slot]

            @pl.when(page >= 0)
            def _(slot=slot, page=page):
                for kind, out_ref in enumerate((key_ref, value_ref)):
                    act(pltpu.make_async_copy(buffer_ref.at[slot, kind], out_ref.at[page], sem))

    each(lambda copy: copy.start())
    each(lambda copy: copy.wait())


def place_new(targets, arrived, key_pool, value_pool):
    return pl.pallas_call(
        place_kernel,
        out_shape=(
            pltpu.HBM(key_pool.shape, jnp.bfloat16),
            pltpu.HBM(value_pool.shape, jnp.bfloat16),
        ),
        in_specs=[smem_spec, any_spec, hbm_spec, hbm_spec],
        out_specs=(hbm_spec,) * 2,
        input_output_aliases={2: 0, 3: 1},
        scratch_shapes=[
            pltpu.VMEM(arrived.shape, jnp.bfloat16),
            pltpu.SemaphoreType.DMA,
            pltpu.SemaphoreType.DMA,
        ],
        cost_estimate=light,
        compiler_params=params(small_limit),
        name="place_new",
    )(targets, arrived, *in_hbm(key_pool, value_pool))


def after(value, *others):
    return lax.optimization_barrier((value,) + others)[0]


def body(queries, new_keys, new_values, key_cache, value_cache, out_weight, lengths, page_table):
    blk_count = lax.axis_size("blk")
    pages = key_cache.shape[0]
    window_pages = page_table.shape[1] // 2
    cap = (window_pages + blk_count - 1) // blk_count

    def other_core(value):
        return lax.ppermute(value, "group", [(0, 1), (1, 0), (2, 3), (3, 2)])

    def other_chip(value):
        return lax.ppermute(value, "group", [(0, 2), (2, 0), (1, 3), (3, 1)])

    picked = pick_old(page_table, cap, key_cache, value_cache)
    old = lax.all_to_all(picked, "blk", split_axis=0, concat_axis=0, tiled=True)
    old = old.reshape((blk_count * cap,) + old.shape[2:])

    fresh, cosine, sine = rotate_keys(lengths, new_keys[0], new_values[0])
    fresh_far = other_chip(fresh)
    fresh_core = other_core(fresh)
    roped, acc, stat = diagonal_part(after(queries[0], picked), cosine, sine, fresh)

    old = sort_old(after(page_table, stat), blk_count, cap, pages, old)
    old_far = other_chip(old)
    old_core = other_core(old)
    fresh_far_core = other_core(after(fresh_far, old))
    new, targets = pick_new(
        page_table, blk_count, cap, pages, (fresh, fresh_core, fresh_far, fresh_far_core)
    )
    arrived = lax.all_to_all(new, "blk", split_axis=0, concat_axis=0, tiled=True)
    old_far_core = other_core(after(old_far, new))
    hidden, key_out, value_out = rest_part(
        lengths, (roped, acc, stat),
        (fresh_core, fresh_far, fresh_far_core, old, old_core, old_far, old_far_core),
        out_weight, key_cache, value_cache,
    )
    key_out, value_out = place_new(targets, arrived, key_out, value_out)
    return (hidden[None], key_out, value_out)


def solution(mesh):
    return jax.shard_map(
        body,
        mesh=mesh,
        in_specs=(
            P("blk", "group", None),
            P("blk", "group", None),
            P("blk", "group", None),
            P("blk", "group", None),
            P("blk", "group", None),
            P(),
            P(),
            P(),
        ),
        out_specs=(P("blk", "group", None), P("blk", "group", None), P("blk", "group", None)),
        check_vma=False,
    )
```

```python
import jax
import jax.numpy as jnp
import numpy as np
from jax import lax
from jax.experimental import pallas as pl
from jax.experimental.pallas import tpu as pltpu
from jax.sharding import PartitionSpec as P

masked_score = -1e30
block_keys = 512
block_slots = 16
any_spec = pl.BlockSpec(memory_space=pl.ANY)
hbm_spec = pl.BlockSpec(memory_space=pltpu.HBM)
smem_spec = pl.BlockSpec(memory_space=pltpu.SMEM)
vmem_spec = pl.BlockSpec(memory_space=pltpu.VMEM)
small_limit = 16 * 1024 * 1024
head_pair = 2
middle_limit = 40 * 1024 * 1024
large_limit = 60 * 1024 * 1024


light = pl.CostEstimate(flops=1, bytes_accessed=1, transcendentals=0)


def params(limit):
    return pltpu.CompilerParams(vmem_limit_bytes=limit)


def in_hbm(*arrays):
    return [pltpu.with_memory_space_constraint(array, pltpu.HBM) for array in arrays]


def turn(values, cosine, sine):
    front = values[:, :128].astype(jnp.float32)
    return front * cosine + pltpu.roll(front, 64, 1) * sine


def join(pieces):
    return jnp.concatenate(pieces, axis=1)


def pages_here(table_ref, r, first, count, cap, pages):
    low = lax.axis_index("blk") * pages
    found = jnp.int32(0)
    chosen = [jnp.int32(0)] * cap
    for j in range(first, first + count):
        page = table_ref[r, j] - low
        inside = (page >= 0) & (page < pages)
        chosen = [jnp.where(inside & (found == c), page, chosen[c]) for c in range(cap)]
        found = found + inside.astype(jnp.int32)
    return chosen, found


def pick_old_kernel(table_ref, key_ref, value_ref, out_ref, sem):
    requests, cap = out_ref.shape[:2]
    for r in range(requests):
        chosen, _ = pages_here(table_ref, r, 0, table_ref.shape[1] // 2, cap, key_ref.shape[0])
        for c in range(cap):
            pltpu.make_async_copy(key_ref.at[chosen[c]], out_ref.at[r, c, 0], sem).start()
            pltpu.make_async_copy(value_ref.at[chosen[c]], out_ref.at[r, c, 1], sem).start()
    pltpu.make_async_copy(out_ref, out_ref, sem).wait()


def pick_old(page_table, cap, key_cache, value_cache):
    requests = page_table.shape[0]
    return pl.pallas_call(
        pick_old_kernel,
        out_shape=jax.ShapeDtypeStruct((requests, cap, 2) + key_cache.shape[1:], jnp.bfloat16),
        in_specs=[smem_spec, hbm_spec, hbm_spec],
        out_specs=vmem_spec,
        scratch_shapes=[pltpu.SemaphoreType.DMA],
        cost_estimate=light,
        compiler_params=params(small_limit),
        name="pick_old",
    )(*in_hbm(page_table, key_cache, value_cache))


def owner_of(page, pages, owners):
    factor = (1 << 20) // pages + 1
    assert all((p * factor) >> 20 == p // pages for p in range(pages * owners))
    assert pages * owners * factor < 1 << 31
    return (page * factor) >> 20


def find_slots(table_ref, first, count, cap, pages, counts_ref):
    owners = counts_ref.shape[0]
    row = lax.axis_index("blk")
    for o in range(owners):
        counts_ref[o] = 0
    slots = []
    for j in range(count):
        owner = owner_of(table_ref[row, first + j], pages, owners)
        rank = counts_ref[owner]
        counts_ref[owner] = rank + 1
        slots.append(owner * cap + rank)
    return slots


def rotate_kernel(lengths_ref, freq_ref, keys_ref, values_ref, out_ref, cos_ref, sin_ref):
    rows = keys_ref.shape[0]
    slots = rows // 32
    start = lengths_ref[lax.axis_index("blk")] + lax.axis_index("group") * rows
    positions = start + lax.broadcasted_iota(jnp.int32, (rows, 128), 0)
    angles = positions.astype(jnp.float32) * freq_ref[...]
    lane = lax.broadcasted_iota(jnp.int32, (rows, 128), 1)
    cosine = jnp.cos(angles)
    sine = jnp.sin(angles)
    sine = jnp.where(lane < 64, -sine, sine)
    cos_ref[...] = cosine
    sin_ref[...] = sine
    keys = keys_ref[...]
    turned = join([turn(keys, cosine, sine).astype(jnp.bfloat16), keys[:, 128:]])
    out_ref[:, 0] = turned.reshape(slots, 32, 256)
    out_ref[:, 1] = values_ref[...].reshape(slots, 32, 256)


def rotate_keys(lengths, keys, values):
    rows, head_dim = keys.shape
    quarter = head_dim // 4
    freq_table = np.float32(10000.0) ** (-np.arange(quarter, dtype=np.float32) / np.float32(quarter))
    freq_table = np.concatenate([freq_table, freq_table])[None].astype(np.float32)
    return pl.pallas_call(
        rotate_kernel,
        out_shape=(
            pltpu.HBM((rows // 32, 2, 32, head_dim), jnp.bfloat16),
            pltpu.HBM((rows, 128), jnp.float32),
            pltpu.HBM((rows, 128), jnp.float32),
        ),
        in_specs=[smem_spec, vmem_spec, vmem_spec, vmem_spec],
        out_specs=(vmem_spec,) * 3,
        cost_estimate=light,
        compiler_params=params(small_limit),
        name="rotate_keys",
    )(lengths, jnp.asarray(freq_table), keys, values)


def sort_kernel(pages, cap, table_ref, old_ref, out_ref, counts_ref, sem):
    count = out_ref.shape[0]
    for j, slot in enumerate(find_slots(table_ref, 0, count, cap, pages, counts_ref)):
        pltpu.make_async_copy(old_ref.at[slot], out_ref.at[j], sem).start()
    pltpu.make_async_copy(out_ref, out_ref, sem).wait()


def sort_old(page_table, blk_count, cap, pages, old):
    window = page_table.shape[1] // 2
    return pl.pallas_call(
        lambda *refs: sort_kernel(pages, cap, *refs),
        out_shape=jax.ShapeDtypeStruct((window,) + old.shape[1:], jnp.bfloat16),
        in_specs=[smem_spec, hbm_spec],
        out_specs=vmem_spec,
        scratch_shapes=[pltpu.SMEM((blk_count,), jnp.int32), pltpu.SemaphoreType.DMA],
        cost_estimate=light,
        compiler_params=params(small_limit),
        name="sort_old",
    )(page_table, *in_hbm(old))


def pick_new_kernel(
    pages, cap, table_ref, own_ref, core_ref, far_ref, far_core_ref, out_ref, targets_ref,
    slots_ref, counts_ref, sem,
):
    count = slots_ref.shape[0]
    block_pages = count // 4
    group_index = lax.axis_index("group")
    for j, slot in enumerate(find_slots(table_ref, table_ref.shape[1] - count, count, cap, pages, counts_ref)):
        slots_ref[j] = slot
    for number, ref in enumerate((own_ref, core_ref, far_ref, far_core_ref)):
        block = group_index ^ number
        for place in range(block_pages):
            source = ref.at[4 * place + group_index]
            target = out_ref.at[slots_ref[block * block_pages + place]]
            pltpu.make_async_copy(source, target, sem).start()
    for r in range(table_ref.shape[0]):
        chosen, found = pages_here(table_ref, r, table_ref.shape[1] - count, count, cap, pages)
        for c in range(cap):
            targets_ref[r * cap + c] = jnp.where(found > c, chosen[c], -1)
    sent = out_ref.at[pl.ds(0, count)]
    pltpu.make_async_copy(sent, sent, sem).wait()


def pick_new(page_table, blk_count, cap, pages, sources):
    window = page_table.shape[1] // 2
    return pl.pallas_call(
        lambda *refs: pick_new_kernel(pages, cap, *refs),
        out_shape=(
            jax.ShapeDtypeStruct((blk_count * cap,) + sources[0].shape[1:], jnp.bfloat16),
            jax.ShapeDtypeStruct((blk_count * cap,), jnp.int32),
        ),
        in_specs=[smem_spec] + [any_spec] * 4,
        out_specs=(vmem_spec, smem_spec),
        scratch_shapes=[
            pltpu.SMEM((window,), jnp.int32),
            pltpu.SMEM((blk_count,), jnp.int32),
            pltpu.SemaphoreType.DMA,
        ],
        cost_estimate=light,
        compiler_params=params(small_limit),
        name="pick_new",
    )(page_table, *sources)


def lane_fold(values, combine):
    total = values[:, :128]
    for start in range(128, values.shape[1], 128):
        total = combine(total, values[:, start : start + 128])
    return total


def old_bias(rows, quarter):
    row = lax.broadcasted_iota(jnp.int32, (rows, 256), 0)
    column = lax.broadcasted_iota(jnp.int32, (rows, 256), 1)
    held = quarter ^ (column // 128)
    position = ((column % 128) // 32) * 128 + 32 * held + column % 32
    return jnp.where(position > row, 0.0, masked_score)


def fetch(source, first, kv_ref, place, count, sem):
    pltpu.make_async_copy(source.at[pl.ds(first, count)], kv_ref.at[pl.ds(place, count)], sem).start()


def fetch_pair(sources, first, kv_ref, place, sem):
    fetch(sources[0], first, kv_ref, place, 4, sem)
    fetch(sources[1], first, kv_ref, place + 4, 4, sem)


def wait_rows(kv_ref, blocks, most, sem):
    for n in range(1, most + 1):

        @pl.when(blocks == n)
        def _(n=n):
            filled = kv_ref.at[pl.ds(0, n * block_slots)]
            pltpu.make_async_copy(filled, filled, sem).wait()


def attention(steps, step_keys, roped_ref, kv_ref, bias_ref, s_refs, most_refs, top_ref, sum_ref, sum_of_values, begin, finish):
    items, rows, _ = roped_ref.shape
    step_slots = step_keys // 32
    biased = bias_ref.shape[1]

    def block(kind, c):
        return kv_ref[pl.ds(c * step_slots, step_slots), kind].reshape(step_keys, 256)

    def scores(t, c, which, masked):
        result = lax.dot_general(
            roped_ref[t], block(0, c), (((1,), (1,)), ((), ())), preferred_element_type=jnp.float32
        )
        if masked:
            head = result[:, :biased].reshape(head_pair, rows // head_pair, biased) + bias_ref[...]
            head = head.reshape(rows, biased)
            result = join([head, result[:, biased:]]) if step_keys > biased else head
        s_refs[which][c] = result
        most_refs[which][...] = jnp.maximum(most_refs[which][...], lane_fold(result, jnp.maximum))

    def weigh(c, which):
        weights = jnp.exp(s_refs[which][c] - join([top_ref[...]] * (step_keys // 128)))
        sum_ref[...] += lane_fold(weights, jnp.add)
        sum_of_values[...] += jnp.dot(
            weights.astype(jnp.bfloat16), block(1, c), preferred_element_type=jnp.float32
        )

    def settle(which):
        top_ref[...] = jnp.broadcast_to(
            jnp.max(most_refs[which][...], axis=1, keepdims=True), top_ref.shape
        )
        sum_ref[...] = jnp.zeros_like(sum_ref)
        sum_of_values[...] = jnp.zeros_like(sum_of_values)

    def loop(work):
        def step(c, carry):
            work(c, False)
            return carry

        @pl.when(steps > 0)
        def _():
            work(0, True)

        lax.fori_loop(1, steps, step, 0)

    def both(t, which):
        def work(c, masked):
            weigh(c, which)
            scores(t + 1, c, 1 - which, masked)

        loop(work)

    drive(
        items, most_refs, begin, settle, finish,
        lambda: loop(lambda c, masked: scores(0, c, 0, masked)),
        both,
        lambda which: loop(lambda c, masked: weigh(c, which)),
    )


def attention_at_once(roped_ref, kv_ref, bias_ref, s_refs, most_refs, top_ref, sum_ref, sum_of_values, begin, finish):
    items, rows, _ = roped_ref.shape
    blocks, _, width = s_refs[0].shape
    biased = bias_ref.shape[1]
    slots = width // 32

    def scores(t, which):
        most = most_refs[which][...]
        query = roped_ref[t]
        for c in range(blocks):
            keys = kv_ref[c * slots : (c + 1) * slots, 0].reshape(width, 256)
            result = lax.dot_general(
                query, keys, (((1,), (1,)), ((), ())), preferred_element_type=jnp.float32
            )
            if c == 0:
                head = result[:, :biased].reshape(head_pair, rows // head_pair, biased) + bias_ref[...]
                head = head.reshape(rows, biased)
                result = join([head, result[:, biased:]]) if width > biased else head
            s_refs[which][c] = result
            most = jnp.maximum(most, lane_fold(result, jnp.maximum))
        most_refs[which][...] = most

    def weigh(which):
        top = join([top_ref[...]] * (width // 128))
        sums = None
        total = None
        for c in range(blocks):
            weights = jnp.exp(s_refs[which][c] - top)
            folded = lane_fold(weights, jnp.add)
            sums = folded if sums is None else sums + folded
            values = kv_ref[c * slots : (c + 1) * slots, 1].reshape(width, 256)
            part = jnp.dot(weights.astype(jnp.bfloat16), values, preferred_element_type=jnp.float32)
            total = part if total is None else total + part
        sum_ref[...] = sums
        sum_of_values[...] = total

    def settle(which):
        top_ref[...] = jnp.broadcast_to(
            jnp.max(most_refs[which][...], axis=1, keepdims=True), top_ref.shape
        )

    def both(t, which):
        weigh(which)
        scores(t + 1, 1 - which)

    drive(items, most_refs, begin, settle, finish, lambda: scores(0, 0), both, weigh)


def drive(items, most_refs, begin, settle, finish, only_scores, both, only_weigh):
    def one(t, which):
        begin(t + 1, most_refs[1 - which])
        settle(which)
        both(t, which)
        finish(t)

    def two(i, carry):
        one(2 * i, 0)
        one(2 * i + 1, 1)
        return carry

    begin(0, most_refs[0])
    only_scores()
    pairs = (items - 1) // 2
    lax.fori_loop(0, pairs, two, 0)
    last = 2 * pairs
    if last < items - 1:
        one(last, 0)
        last += 1
    settle(last % 2)
    only_weigh(last % 2)
    finish(last)


def working(rows, steps, step_keys):
    return [
        pltpu.VMEM((steps * step_keys // 32, 2, 32, 256), jnp.bfloat16),
        pltpu.VMEM((steps, head_pair * rows, step_keys), jnp.float32),
        pltpu.VMEM((steps, head_pair * rows, step_keys), jnp.float32),
        pltpu.VMEM((head_pair * rows, 128), jnp.float32),
        pltpu.VMEM((head_pair * rows, 128), jnp.float32),
        pltpu.VMEM((head_pair * rows, 128), jnp.float32),
        pltpu.VMEM((head_pair * rows, 128), jnp.float32),
        pltpu.VMEM((head_pair * rows, 256), jnp.float32),
        pltpu.VMEM((rows, block_keys), jnp.float32),
    ]


def state_shapes(items, rows):
    return [
        pltpu.VMEM((items, head_pair * rows, 256), jnp.bfloat16),
        pltpu.VMEM((items, head_pair * rows, 256), jnp.float32),
        pltpu.VMEM((items, head_pair * rows, 128), jnp.float32),
    ]


def state_out(items, rows):
    return (
        pltpu.HBM((items, head_pair * rows, 256), jnp.float32),
        pltpu.HBM((items, head_pair * rows, 128), jnp.float32),
    )


def diagonal_kernel(
    query_ref, cos_ref, sin_ref, own_ref, key_ref, value_ref, roped_out, acc_out, stat_out,
    key_out_ref, value_out_ref, key_pool, value_pool, q_ref, roped_ref, acc_ref, stat_ref, kv_ref, s_0, s_1, most_0, most_1, top_ref, sum_ref, values_ref,
    bias_ref, query_sem, sem, out_sem, pool_sems,
):
    rows = q_ref.shape[0]
    items = roped_ref.shape[0]
    loads = [
        pltpu.make_async_copy(key_ref, key_pool, pool_sems.at[0]),
        pltpu.make_async_copy(value_ref, value_pool, pool_sems.at[1]),
    ]
    stores = [
        pltpu.make_async_copy(key_pool, key_out_ref, pool_sems.at[0]),
        pltpu.make_async_copy(value_pool, value_out_ref, pool_sems.at[1]),
    ]
    query_copy = pltpu.make_async_copy(query_ref, q_ref, query_sem)
    query_copy.start()
    fetch(own_ref, 0, kv_ref, 0, block_slots, sem)
    for copy in loads:
        copy.start()
    row = lax.broadcasted_iota(jnp.int32, (rows, block_keys), 0)
    column = lax.broadcasted_iota(jnp.int32, (rows, block_keys), 1)
    bias_ref[...] = jnp.where(column <= row, 0.0, masked_score)
    query_copy.wait()

    def rope(t, carry):
        for one in range(head_pair):
            raw = q_ref[:, pl.ds(pl.multiple_of((t * head_pair + one) * 256, 256), 256)]
            front = turn(raw, cos_ref[...], sin_ref[...])
            some = pl.ds(one * rows, rows)
            roped_ref[t, some, :128] = (front * 0.0625).astype(jnp.bfloat16)
            roped_ref[t, some, 128:] = raw[:, 128:] * jnp.bfloat16(0.0625)
        return carry

    lax.fori_loop(0, items, rope, 0)
    roped_copy = pltpu.make_async_copy(roped_ref, roped_out, query_sem)
    roped_copy.start()
    pltpu.make_async_copy(kv_ref, kv_ref, sem).wait()
    for load, store in zip(loads, stores):
        load.wait()
        store.start()

    def begin(t, most_ref):
        most_ref[...] = jnp.full_like(most_ref, masked_score)

    def finish(t):
        lane = lax.broadcasted_iota(jnp.int32, stat_ref.shape[1:], 1)
        sums = jnp.sum(sum_ref[...], axis=1, keepdims=True)
        stat_ref[t] = jnp.where(lane < 64, top_ref[...], sums)
        acc_ref[t] = values_ref[...]
        pltpu.make_async_copy(acc_ref.at[t], acc_out.at[t], out_sem).start()
        pltpu.make_async_copy(stat_ref.at[t], stat_out.at[t], out_sem).start()

    attention_at_once(
        roped_ref, kv_ref, bias_ref, (s_0, s_1), (most_0, most_1), top_ref, sum_ref, values_ref,
        begin, finish,
    )
    roped_copy.wait()
    for copy in stores:
        copy.wait()
    pltpu.make_async_copy(acc_ref, acc_out, out_sem).wait()
    pltpu.make_async_copy(stat_ref, stat_out, out_sem).wait()


def diagonal_part(queries, cosine, sine, own, key_cache, value_cache):
    rows, width = queries.shape
    items = width // (256 * head_pair)
    return pl.pallas_call(
        diagonal_kernel,
        out_shape=(pltpu.HBM((items, head_pair * rows, 256), jnp.bfloat16),)
        + state_out(items, rows)
        + (pltpu.HBM(key_cache.shape, jnp.bfloat16), pltpu.HBM(value_cache.shape, jnp.bfloat16)),
        in_specs=[hbm_spec, vmem_spec, vmem_spec, hbm_spec, hbm_spec, hbm_spec],
        out_specs=(hbm_spec,) * 5,
        scratch_shapes=[
            pltpu.VMEM(key_cache.shape, jnp.bfloat16),
            pltpu.VMEM(value_cache.shape, jnp.bfloat16),
            pltpu.VMEM((rows, width), jnp.bfloat16),
        ]
        + state_shapes(items, rows)
        + working(rows, 1, block_keys)
        + [pltpu.SemaphoreType.DMA] * 3
        + [pltpu.SemaphoreType.DMA((2,))],
        cost_estimate=light,
        compiler_params=params(middle_limit),
        name="attend_diagonal",
    )(*in_hbm(queries), cosine, sine, *in_hbm(own, key_cache, value_cache))


def rest_kernel(
    lengths_ref, roped_in, acc_in, stat_in, core_ref, far_ref, far_core_ref,
    old_ref, old_core_ref, old_far_ref, old_far_core_ref, weight_ref, hidden_ref,
    roped_ref, acc_ref, stat_ref, kv_ref, s_0, s_1, most_0, most_1, top_ref, sum_ref, values_ref,
    bias_ref, w_ref, stage_ref, roped_sem, state_sems, sem, weight_sem, out_sems,
):
    group_index = lax.axis_index("group")
    has_old = lengths_ref[lax.axis_index("blk")] > 0
    items = roped_ref.shape[0]
    rows = bias_ref.shape[0]
    chunk = stage_ref.shape[2]
    chunks = w_ref.shape[1] // chunk
    odd = group_index % 2
    chip = group_index // 2
    blocks = jnp.where(has_old, 4, odd + 2 * chip)
    steps = odd + chip
    base = jnp.where(has_old, 16, 16 * odd)
    near = (old_ref, old_core_ref)
    far = (old_far_ref, old_far_core_ref)

    def copies(t):
        place = t % 2
        return [
            pltpu.make_async_copy(source.at[t], target.at[place], state_sems.at[number, place])
            for number, (source, target) in enumerate(((stat_in, stat_ref), (acc_in, acc_ref)))
        ]

    roped_copy = pltpu.make_async_copy(roped_in, roped_ref, roped_sem)
    roped_copy.start()
    for t in range(2):
        for copy in copies(t):
            copy.start()

    @pl.when(odd == 1)
    def _():
        fetch(core_ref, 0, kv_ref, base, 16, sem)

    @pl.when(chip == 1)
    def _():
        place = jnp.where(has_old, 32, 32 * odd)
        fetch(far_ref, 0, kv_ref, place, 16, sem)
        fetch(far_core_ref, 0, kv_ref, place + 16, 16, sem)

    @pl.when(has_old)
    def _():
        for block in range(4):

            @pl.when(block >= group_index)
            def _(block=block):
                gap = jnp.where(block == group_index, 0, odd)
                place = 16 * (gap + block - group_index)
                fetch_pair(near, 4 * block, kv_ref, place, sem)
                fetch_pair(far, 4 * block, kv_ref, place + 8, sem)

    weight_copy = pltpu.make_async_copy(weight_ref, w_ref, weight_sem)
    weight_copy.start()

    @pl.when(jnp.logical_not(has_old))
    def _():
        bias_ref[...] = jnp.where(odd == 1, masked_score, 0.0) + jnp.zeros_like(bias_ref)
        empty = pl.ds(0, block_slots)

        @pl.when(odd == 1)
        def _():
            kv_ref[empty] = jnp.zeros((block_slots, 2, 32, 256), jnp.bfloat16)

    @pl.when(has_old)
    def _():
        bias_ref[:, :256] = old_bias(rows, group_index)
        bias_ref[:, 256:] = old_bias(rows, group_index ^ 2)

    roped_copy.wait()
    wait_rows(kv_ref, blocks, 4, sem)
    lane = lax.broadcasted_iota(jnp.int32, stat_ref.shape[1:], 1)

    def begin(t, most_ref):
        for copy in copies(t):
            copy.wait()
        most_ref[...] = jnp.where(lane < 64, stat_ref[t % 2], masked_score)

    def finish(t):
        stat = stat_ref[t % 2]
        factor = jnp.exp(stat[:, :1] - top_ref[...])
        sums = stat[:, 64:65] * factor + jnp.sum(sum_ref[...], axis=1, keepdims=True)
        inverse = 1.0 / sums
        old = factor * inverse
        mixed = acc_ref[t % 2] * join([old, old]) + values_ref[...] * join([inverse, inverse])
        roped_ref[t] = mixed.astype(jnp.bfloat16)

        @pl.when(t + 2 < items)
        def _():
            for copy in copies(t + 2):
                copy.start()

    scratch = (roped_ref, kv_ref, bias_ref, (s_0, s_1), (most_0, most_1), top_ref, sum_ref, values_ref)

    @pl.when(has_old)
    def _():
        attention_at_once(*scratch, begin, finish)

    @pl.when(jnp.logical_not(has_old))
    def _():
        attention(steps, 2 * block_keys, *scratch, begin, finish)


    weight_copy.wait()

    def out_copy(n, columns):
        return pltpu.make_async_copy(stage_ref.at[n % 2], hidden_ref.at[:, columns], out_sems.at[n % 2])

    def project(n, carry):
        columns = pl.ds(pl.multiple_of(n * chunk, chunk), chunk)

        @pl.when(n >= 2)
        def _():
            out_copy(n, columns).wait()

        attended = join(
            [
                roped_ref[t, one * rows : (one + 1) * rows, :]
                for t in range(items)
                for one in range(head_pair)
            ]
        )
        stage_ref[n % 2] = jnp.dot(
            attended, w_ref[:, columns], preferred_element_type=jnp.float32
        ).astype(jnp.bfloat16)
        out_copy(n, columns).start()
        return carry

    lax.fori_loop(0, chunks, project, 0)
    for n in range(2):
        out_copy(n, pl.ds(0, chunk)).wait()


def rest_part(lengths, state, slots, weight):
    items, pair_rows, _ = state[0].shape
    rows = pair_rows // head_pair
    width = weight.shape[1]
    chunk = 512
    return pl.pallas_call(
        rest_kernel,
        out_shape=pltpu.HBM((rows, width), jnp.bfloat16),
        in_specs=[smem_spec] + [hbm_spec] * 3 + [any_spec] * 7 + [hbm_spec],
        out_specs=hbm_spec,
        scratch_shapes=[pltpu.VMEM((items, pair_rows, 256), jnp.bfloat16)]
        + state_shapes(2, rows)[1:]
        + working(rows, 2, 2 * block_keys)
        + [
            pltpu.VMEM(weight.shape, jnp.bfloat16),
            pltpu.VMEM((2, rows, chunk), jnp.bfloat16),
            pltpu.SemaphoreType.DMA,
            pltpu.SemaphoreType.DMA((2, 2)),
            pltpu.SemaphoreType.DMA,
            pltpu.SemaphoreType.DMA,
            pltpu.SemaphoreType.DMA((2,)),
        ],
        cost_estimate=light,
        compiler_params=params(large_limit),
        name="attend_rest",
    )(lengths, *in_hbm(*state), *slots, *in_hbm(weight))


def place_kernel(targets_ref, arrived_ref, key_in, value_in, key_ref, value_ref, buffer_ref, load_sem, sem):
    load = pltpu.make_async_copy(arrived_ref, buffer_ref, load_sem)
    load.start()
    load.wait()

    def each(act):
        for slot in range(targets_ref.shape[0]):
            page = targets_ref[slot]

            @pl.when(page >= 0)
            def _(slot=slot, page=page):
                for kind, out_ref in enumerate((key_ref, value_ref)):
                    act(pltpu.make_async_copy(buffer_ref.at[slot, kind], out_ref.at[page], sem))

    each(lambda copy: copy.start())
    each(lambda copy: copy.wait())


def place_new(targets, arrived, key_pool, value_pool):
    return pl.pallas_call(
        place_kernel,
        out_shape=(
            pltpu.HBM(key_pool.shape, jnp.bfloat16),
            pltpu.HBM(value_pool.shape, jnp.bfloat16),
        ),
        in_specs=[smem_spec, any_spec, hbm_spec, hbm_spec],
        out_specs=(hbm_spec,) * 2,
        input_output_aliases={2: 0, 3: 1},
        scratch_shapes=[
            pltpu.VMEM(arrived.shape, jnp.bfloat16),
            pltpu.SemaphoreType.DMA,
            pltpu.SemaphoreType.DMA,
        ],
        cost_estimate=light,
        compiler_params=params(small_limit),
        name="place_new",
    )(targets, arrived, *in_hbm(key_pool, value_pool))


def after(value, *others):
    return lax.optimization_barrier((value,) + others)[0]


def body(queries, new_keys, new_values, key_cache, value_cache, out_weight, lengths, page_table):
    blk_count = lax.axis_size("blk")
    pages = key_cache.shape[0]
    window_pages = page_table.shape[1] // 2
    cap = (window_pages + blk_count - 1) // blk_count

    def other_core(value):
        return lax.ppermute(value, "group", [(0, 1), (1, 0), (2, 3), (3, 2)])

    def other_chip(value):
        return lax.ppermute(value, "group", [(0, 2), (2, 0), (1, 3), (3, 1)])

    picked = pick_old(page_table, cap, key_cache, value_cache)
    old = lax.all_to_all(picked, "blk", split_axis=0, concat_axis=0, tiled=True)
    old = old.reshape((blk_count * cap,) + old.shape[2:])

    fresh, cosine, sine = rotate_keys(lengths, new_keys[0], new_values[0])
    fresh_far = other_chip(fresh)
    fresh_core = other_core(fresh)
    roped, acc, stat, key_out, value_out = diagonal_part(
        after(queries[0], picked), cosine, sine, fresh, key_cache, value_cache
    )

    old = sort_old(after(page_table, stat), blk_count, cap, pages, old)
    old_far = other_chip(old)
    old_core = other_core(old)
    fresh_far_core = other_core(after(fresh_far, old))
    new, targets = pick_new(
        page_table, blk_count, cap, pages, (fresh, fresh_core, fresh_far, fresh_far_core)
    )
    arrived = lax.all_to_all(new, "blk", split_axis=0, concat_axis=0, tiled=True)
    old_far_core = other_core(after(old_far, new))
    hidden = rest_part(
        lengths, (roped, acc, stat),
        (fresh_core, fresh_far, fresh_far_core, old, old_core, old_far, old_far_core),
        out_weight,
    )
    key_out, value_out = place_new(targets, arrived, key_out, value_out)
    return (hidden[None], key_out, value_out)


def solution(mesh):
    return jax.shard_map(
        body,
        mesh=mesh,
        in_specs=(
            P("blk", "group", None),
            P("blk", "group", None),
            P("blk", "group", None),
            P("blk", "group", None),
            P("blk", "group", None),
            P(),
            P(),
            P(),
        ),
        out_specs=(P("blk", "group", None), P("blk", "group", None), P("blk", "group", None)),
        check_vma=False,
    )
```

```python
import jax
import jax.numpy as jnp
import numpy as np
from jax import lax
from jax.experimental import pallas as pl
from jax.experimental.pallas import tpu as pltpu
from jax.sharding import PartitionSpec as P

masked_score = -1e30
block_keys = 512
block_slots = 16
any_spec = pl.BlockSpec(memory_space=pl.ANY)
hbm_spec = pl.BlockSpec(memory_space=pltpu.HBM)
smem_spec = pl.BlockSpec(memory_space=pltpu.SMEM)
vmem_spec = pl.BlockSpec(memory_space=pltpu.VMEM)
small_limit = 16 * 1024 * 1024
head_pair = 2
large_limit = 60 * 1024 * 1024


light = pl.CostEstimate(flops=1, bytes_accessed=1, transcendentals=0)


def params(limit):
    return pltpu.CompilerParams(vmem_limit_bytes=limit)


def in_hbm(*arrays):
    return [pltpu.with_memory_space_constraint(array, pltpu.HBM) for array in arrays]


def turn(values, cosine, sine):
    front = values[:, :128].astype(jnp.float32)
    return front * cosine + pltpu.roll(front, 64, 1) * sine


def join(pieces):
    return jnp.concatenate(pieces, axis=1)


def pages_here(table_ref, r, first, count, cap, pages):
    low = lax.axis_index("blk") * pages
    found = jnp.int32(0)
    chosen = [jnp.int32(0)] * cap
    for j in range(first, first + count):
        page = table_ref[r, j] - low
        inside = (page >= 0) & (page < pages)
        chosen = [jnp.where(inside & (found == c), page, chosen[c]) for c in range(cap)]
        found = found + inside.astype(jnp.int32)
    return chosen, found


def pick_old_kernel(table_ref, key_ref, value_ref, out_ref, sem):
    requests, cap = out_ref.shape[:2]
    for r in range(requests):
        chosen, _ = pages_here(table_ref, r, 0, table_ref.shape[1] // 2, cap, key_ref.shape[0])
        for c in range(cap):
            pltpu.make_async_copy(key_ref.at[chosen[c]], out_ref.at[r, c, 0], sem).start()
            pltpu.make_async_copy(value_ref.at[chosen[c]], out_ref.at[r, c, 1], sem).start()
    pltpu.make_async_copy(out_ref, out_ref, sem).wait()


def pick_old(page_table, cap, key_cache, value_cache):
    requests = page_table.shape[0]
    return pl.pallas_call(
        pick_old_kernel,
        out_shape=jax.ShapeDtypeStruct((requests, cap, 2) + key_cache.shape[1:], jnp.bfloat16),
        in_specs=[smem_spec, hbm_spec, hbm_spec],
        out_specs=vmem_spec,
        scratch_shapes=[pltpu.SemaphoreType.DMA],
        cost_estimate=light,
        compiler_params=params(small_limit),
        name="pick_old",
    )(*in_hbm(page_table, key_cache, value_cache))


def owner_of(page, pages, owners):
    factor = (1 << 20) // pages + 1
    assert all((p * factor) >> 20 == p // pages for p in range(pages * owners))
    assert pages * owners * factor < 1 << 31
    return (page * factor) >> 20


def find_slots(table_ref, first, count, cap, pages, counts_ref):
    owners = counts_ref.shape[0]
    row = lax.axis_index("blk")
    for o in range(owners):
        counts_ref[o] = 0
    slots = []
    for j in range(count):
        owner = owner_of(table_ref[row, first + j], pages, owners)
        rank = counts_ref[owner]
        counts_ref[owner] = rank + 1
        slots.append(owner * cap + rank)
    return slots


def rotate_kernel(lengths_ref, freq_ref, keys_ref, values_ref, out_ref, cos_ref, sin_ref):
    rows = keys_ref.shape[0]
    slots = rows // 32
    start = lengths_ref[lax.axis_index("blk")] + lax.axis_index("group") * rows
    positions = start + lax.broadcasted_iota(jnp.int32, (rows, 128), 0)
    angles = positions.astype(jnp.float32) * freq_ref[...]
    lane = lax.broadcasted_iota(jnp.int32, (rows, 128), 1)
    cosine = jnp.cos(angles)
    sine = jnp.sin(angles)
    sine = jnp.where(lane < 64, -sine, sine)
    cos_ref[...] = cosine
    sin_ref[...] = sine
    keys = keys_ref[...]
    turned = join([turn(keys, cosine, sine).astype(jnp.bfloat16), keys[:, 128:]])
    out_ref[:, 0] = turned.reshape(slots, 32, 256)
    out_ref[:, 1] = values_ref[...].reshape(slots, 32, 256)


def rotate_keys(lengths, keys, values):
    rows, head_dim = keys.shape
    quarter = head_dim // 4
    freq_table = np.float32(10000.0) ** (-np.arange(quarter, dtype=np.float32) / np.float32(quarter))
    freq_table = np.concatenate([freq_table, freq_table])[None].astype(np.float32)
    return pl.pallas_call(
        rotate_kernel,
        out_shape=(
            pltpu.HBM((rows // 32, 2, 32, head_dim), jnp.bfloat16),
            pltpu.HBM((rows, 128), jnp.float32),
            pltpu.HBM((rows, 128), jnp.float32),
        ),
        in_specs=[smem_spec, vmem_spec, vmem_spec, vmem_spec],
        out_specs=(vmem_spec,) * 3,
        cost_estimate=light,
        compiler_params=params(small_limit),
        name="rotate_keys",
    )(lengths, jnp.asarray(freq_table), keys, values)


def sort_kernel(pages, cap, table_ref, old_ref, out_ref, counts_ref, sem):
    count = out_ref.shape[0]
    for j, slot in enumerate(find_slots(table_ref, 0, count, cap, pages, counts_ref)):
        pltpu.make_async_copy(old_ref.at[slot], out_ref.at[j], sem).start()
    pltpu.make_async_copy(out_ref, out_ref, sem).wait()


def sort_old(page_table, blk_count, cap, pages, old):
    window = page_table.shape[1] // 2
    return pl.pallas_call(
        lambda *refs: sort_kernel(pages, cap, *refs),
        out_shape=jax.ShapeDtypeStruct((window,) + old.shape[1:], jnp.bfloat16),
        in_specs=[smem_spec, hbm_spec],
        out_specs=vmem_spec,
        scratch_shapes=[pltpu.SMEM((blk_count,), jnp.int32), pltpu.SemaphoreType.DMA],
        cost_estimate=light,
        compiler_params=params(small_limit),
        name="sort_old",
    )(page_table, *in_hbm(old))


def pick_new_kernel(
    pages, cap, table_ref, own_ref, core_ref, far_ref, far_core_ref, out_ref, targets_ref,
    slots_ref, counts_ref, sem,
):
    count = slots_ref.shape[0]
    block_pages = count // 4
    group_index = lax.axis_index("group")
    for j, slot in enumerate(find_slots(table_ref, table_ref.shape[1] - count, count, cap, pages, counts_ref)):
        slots_ref[j] = slot
    for number, ref in enumerate((own_ref, core_ref, far_ref, far_core_ref)):
        block = group_index ^ number
        for place in range(block_pages):
            source = ref.at[4 * place + group_index]
            target = out_ref.at[slots_ref[block * block_pages + place]]
            pltpu.make_async_copy(source, target, sem).start()
    for r in range(table_ref.shape[0]):
        chosen, found = pages_here(table_ref, r, table_ref.shape[1] - count, count, cap, pages)
        for c in range(cap):
            targets_ref[r * cap + c] = jnp.where(found > c, chosen[c], -1)
    sent = out_ref.at[pl.ds(0, count)]
    pltpu.make_async_copy(sent, sent, sem).wait()


def pick_new(page_table, blk_count, cap, pages, sources):
    window = page_table.shape[1] // 2
    return pl.pallas_call(
        lambda *refs: pick_new_kernel(pages, cap, *refs),
        out_shape=(
            jax.ShapeDtypeStruct((blk_count * cap,) + sources[0].shape[1:], jnp.bfloat16),
            jax.ShapeDtypeStruct((blk_count * cap,), jnp.int32),
        ),
        in_specs=[smem_spec] + [any_spec] * 4,
        out_specs=(vmem_spec, smem_spec),
        scratch_shapes=[
            pltpu.SMEM((window,), jnp.int32),
            pltpu.SMEM((blk_count,), jnp.int32),
            pltpu.SemaphoreType.DMA,
        ],
        cost_estimate=light,
        compiler_params=params(small_limit),
        name="pick_new",
    )(page_table, *sources)


def lane_fold(values, combine):
    total = values[:, :128]
    for start in range(128, values.shape[1], 128):
        total = combine(total, values[:, start : start + 128])
    return total


def old_bias(rows, quarter):
    row = lax.broadcasted_iota(jnp.int32, (rows, 256), 0)
    column = lax.broadcasted_iota(jnp.int32, (rows, 256), 1)
    held = quarter ^ (column // 128)
    position = ((column % 128) // 32) * 128 + 32 * held + column % 32
    return jnp.where(position > row, 0.0, masked_score)


def fetch(source, first, kv_ref, place, count, sem):
    pltpu.make_async_copy(source.at[pl.ds(first, count)], kv_ref.at[pl.ds(place, count)], sem).start()


def fetch_pair(sources, first, kv_ref, place, sem):
    fetch(sources[0], first, kv_ref, place, 4, sem)
    fetch(sources[1], first, kv_ref, place + 4, 4, sem)


def wait_rows(kv_ref, blocks, most, sem):
    for n in range(1, most + 1):

        @pl.when(blocks == n)
        def _(n=n):
            filled = kv_ref.at[pl.ds(0, n * block_slots)]
            pltpu.make_async_copy(filled, filled, sem).wait()


def attention(steps, step_keys, roped_ref, kv_ref, bias_ref, s_refs, most_refs, top_ref, sum_ref, sum_of_values, begin, finish):
    items, rows, _ = roped_ref.shape
    step_slots = step_keys // 32
    biased = bias_ref.shape[1]

    def block(kind, c):
        return kv_ref[pl.ds(c * step_slots, step_slots), kind].reshape(step_keys, 256)

    def scores(t, c, which, masked):
        result = lax.dot_general(
            roped_ref[t], block(0, c), (((1,), (1,)), ((), ())), preferred_element_type=jnp.float32
        )
        if masked:
            head = result[:, :biased].reshape(head_pair, rows // head_pair, biased) + bias_ref[...]
            head = head.reshape(rows, biased)
            result = join([head, result[:, biased:]]) if step_keys > biased else head
        s_refs[which][c] = result
        most_refs[which][...] = jnp.maximum(most_refs[which][...], lane_fold(result, jnp.maximum))

    def weigh(c, which):
        weights = jnp.exp(s_refs[which][c] - join([top_ref[...]] * (step_keys // 128)))
        sum_ref[...] += lane_fold(weights, jnp.add)
        sum_of_values[...] += jnp.dot(
            weights.astype(jnp.bfloat16), block(1, c), preferred_element_type=jnp.float32
        )

    def settle(which):
        top_ref[...] = jnp.broadcast_to(
            jnp.max(most_refs[which][...], axis=1, keepdims=True), top_ref.shape
        )
        sum_ref[...] = jnp.zeros_like(sum_ref)
        sum_of_values[...] = jnp.zeros_like(sum_of_values)

    def loop(work):
        def step(c, carry):
            work(c, False)
            return carry

        @pl.when(steps > 0)
        def _():
            work(0, True)

        lax.fori_loop(1, steps, step, 0)

    def both(t, which):
        def work(c, masked):
            weigh(c, which)
            scores(t + 1, c, 1 - which, masked)

        loop(work)

    drive(
        items, most_refs, begin, settle, finish,
        lambda: loop(lambda c, masked: scores(0, c, 0, masked)),
        both,
        lambda which: loop(lambda c, masked: weigh(c, which)),
    )


def attention_at_once(roped_ref, kv_ref, bias_ref, s_refs, most_refs, top_ref, sum_ref, sum_of_values, begin, finish):
    items, rows, _ = roped_ref.shape
    blocks, _, width = s_refs[0].shape
    biased = bias_ref.shape[1]
    slots = width // 32

    def scores(t, which):
        most = most_refs[which][...]
        query = roped_ref[t]
        for c in range(blocks):
            keys = kv_ref[c * slots : (c + 1) * slots, 0].reshape(width, 256)
            result = lax.dot_general(
                query, keys, (((1,), (1,)), ((), ())), preferred_element_type=jnp.float32
            )
            if c == 0:
                head = result[:, :biased].reshape(head_pair, rows // head_pair, biased) + bias_ref[...]
                head = head.reshape(rows, biased)
                result = join([head, result[:, biased:]]) if width > biased else head
            s_refs[which][c] = result
            most = jnp.maximum(most, lane_fold(result, jnp.maximum))
        most_refs[which][...] = most

    def weigh(which):
        top = join([top_ref[...]] * (width // 128))
        sums = None
        total = None
        for c in range(blocks):
            weights = jnp.exp(s_refs[which][c] - top)
            folded = lane_fold(weights, jnp.add)
            sums = folded if sums is None else sums + folded
            values = kv_ref[c * slots : (c + 1) * slots, 1].reshape(width, 256)
            part = jnp.dot(weights.astype(jnp.bfloat16), values, preferred_element_type=jnp.float32)
            total = part if total is None else total + part
        sum_ref[...] = sums
        sum_of_values[...] = total

    def settle(which):
        top_ref[...] = jnp.broadcast_to(
            jnp.max(most_refs[which][...], axis=1, keepdims=True), top_ref.shape
        )

    def both(t, which):
        weigh(which)
        scores(t + 1, 1 - which)

    drive(items, most_refs, begin, settle, finish, lambda: scores(0, 0), both, weigh)


def drive(items, most_refs, begin, settle, finish, only_scores, both, only_weigh):
    def one(t, which):
        begin(t + 1, most_refs[1 - which])
        settle(which)
        both(t, which)
        finish(t)

    def two(i, carry):
        one(2 * i, 0)
        one(2 * i + 1, 1)
        return carry

    begin(0, most_refs[0])
    only_scores()
    pairs = (items - 1) // 2
    lax.fori_loop(0, pairs, two, 0)
    last = 2 * pairs
    if last < items - 1:
        one(last, 0)
        last += 1
    settle(last % 2)
    only_weigh(last % 2)
    finish(last)


def working(rows, steps, step_keys):
    return [
        pltpu.VMEM((steps * step_keys // 32, 2, 32, 256), jnp.bfloat16),
        pltpu.VMEM((steps, head_pair * rows, step_keys), jnp.float32),
        pltpu.VMEM((steps, head_pair * rows, step_keys), jnp.float32),
        pltpu.VMEM((head_pair * rows, 128), jnp.float32),
        pltpu.VMEM((head_pair * rows, 128), jnp.float32),
        pltpu.VMEM((head_pair * rows, 128), jnp.float32),
        pltpu.VMEM((head_pair * rows, 128), jnp.float32),
        pltpu.VMEM((head_pair * rows, 256), jnp.float32),
        pltpu.VMEM((rows, block_keys), jnp.float32),
    ]


def state_shapes(items, rows):
    return [
        pltpu.VMEM((items, head_pair * rows, 256), jnp.bfloat16),
        pltpu.VMEM((items, head_pair * rows, 256), jnp.float32),
        pltpu.VMEM((items, head_pair * rows, 128), jnp.float32),
    ]


def state_out(items, rows):
    return (
        pltpu.HBM((items, head_pair * rows, 256), jnp.float32),
        pltpu.HBM((items, head_pair * rows, 128), jnp.float32),
    )


def diagonal_kernel(
    query_ref, cos_ref, sin_ref, own_ref, key_ref, value_ref, roped_out, acc_out, stat_out,
    key_out_ref, value_out_ref, key_pool, value_pool, q_ref, roped_ref, acc_ref, stat_ref, kv_ref, s_0, s_1, most_0, most_1, top_ref, sum_ref, values_ref,
    bias_ref, query_sem, sem, out_sem, pool_sems,
):
    rows = q_ref.shape[0]
    items = roped_ref.shape[0]
    loads = [
        pltpu.make_async_copy(key_ref, key_pool, pool_sems.at[0]),
        pltpu.make_async_copy(value_ref, value_pool, pool_sems.at[1]),
    ]
    stores = [
        pltpu.make_async_copy(key_pool, key_out_ref, pool_sems.at[0]),
        pltpu.make_async_copy(value_pool, value_out_ref, pool_sems.at[1]),
    ]
    query_copy = pltpu.make_async_copy(query_ref, q_ref, query_sem)
    query_copy.start()
    fetch(own_ref, 0, kv_ref, 0, block_slots, sem)
    for copy in loads:
        copy.start()
    row = lax.broadcasted_iota(jnp.int32, (rows, block_keys), 0)
    column = lax.broadcasted_iota(jnp.int32, (rows, block_keys), 1)
    bias_ref[...] = jnp.where(column <= row, 0.0, masked_score)
    query_copy.wait()

    def rope(t, carry):
        for one in range(head_pair):
            raw = q_ref[:, pl.ds(pl.multiple_of((t * head_pair + one) * 256, 256), 256)]
            front = turn(raw, cos_ref[...], sin_ref[...])
            some = pl.ds(one * rows, rows)
            roped_ref[t, some, :128] = (front * 0.0625).astype(jnp.bfloat16)
            roped_ref[t, some, 128:] = raw[:, 128:] * jnp.bfloat16(0.0625)
        return carry

    lax.fori_loop(0, items, rope, 0)
    roped_copy = pltpu.make_async_copy(roped_ref, roped_out, query_sem)
    roped_copy.start()
    pltpu.make_async_copy(kv_ref, kv_ref, sem).wait()
    for load, store in zip(loads, stores):
        load.wait()
        store.start()

    def begin(t, most_ref):
        most_ref[...] = jnp.full_like(most_ref, masked_score)

    def finish(t):
        lane = lax.broadcasted_iota(jnp.int32, stat_ref.shape[1:], 1)
        sums = jnp.sum(sum_ref[...], axis=1, keepdims=True)
        stat_ref[t] = jnp.where(lane < 64, top_ref[...], sums)
        acc_ref[t] = values_ref[...]
        pltpu.make_async_copy(acc_ref.at[t], acc_out.at[t], out_sem).start()
        pltpu.make_async_copy(stat_ref.at[t], stat_out.at[t], out_sem).start()

    attention_at_once(
        roped_ref, kv_ref, bias_ref, (s_0, s_1), (most_0, most_1), top_ref, sum_ref, values_ref,
        begin, finish,
    )
    roped_copy.wait()
    for copy in stores:
        copy.wait()
    pltpu.make_async_copy(acc_ref, acc_out, out_sem).wait()
    pltpu.make_async_copy(stat_ref, stat_out, out_sem).wait()


def diagonal_part(queries, cosine, sine, own, key_cache, value_cache):
    rows, width = queries.shape
    items = width // (256 * head_pair)
    return pl.pallas_call(
        diagonal_kernel,
        out_shape=(pltpu.HBM((items, head_pair * rows, 256), jnp.bfloat16),)
        + state_out(items, rows)
        + (pltpu.HBM(key_cache.shape, jnp.bfloat16), pltpu.HBM(value_cache.shape, jnp.bfloat16)),
        in_specs=[hbm_spec, vmem_spec, vmem_spec, hbm_spec, hbm_spec, hbm_spec],
        out_specs=(hbm_spec,) * 5,
        scratch_shapes=[
            pltpu.VMEM(key_cache.shape, jnp.bfloat16),
            pltpu.VMEM(value_cache.shape, jnp.bfloat16),
            pltpu.VMEM((rows, width), jnp.bfloat16),
        ]
        + state_shapes(items, rows)
        + working(rows, 1, block_keys)
        + [pltpu.SemaphoreType.DMA] * 3
        + [pltpu.SemaphoreType.DMA((2,))],
        cost_estimate=light,
        compiler_params=params(large_limit),
        name="attend_diagonal",
    )(*in_hbm(queries), cosine, sine, *in_hbm(own, key_cache, value_cache))


def rest_kernel(
    lengths_ref, roped_in, acc_in, stat_in, core_ref, far_ref, far_core_ref,
    old_ref, old_core_ref, old_far_ref, old_far_core_ref, weight_ref, hidden_ref,
    roped_ref, acc_ref, stat_ref, kv_ref, s_0, s_1, most_0, most_1, top_ref, sum_ref, values_ref,
    bias_ref, w_ref, stage_ref, roped_sem, state_sems, sem, weight_sem, out_sems,
):
    group_index = lax.axis_index("group")
    has_old = lengths_ref[lax.axis_index("blk")] > 0
    items = roped_ref.shape[0]
    rows = bias_ref.shape[0]
    chunk = stage_ref.shape[2]
    chunks = w_ref.shape[1] // chunk
    odd = group_index % 2
    chip = group_index // 2
    blocks = jnp.where(has_old, 4, odd + 2 * chip)
    steps = odd + chip
    base = jnp.where(has_old, 16, 16 * odd)
    near = (old_ref, old_core_ref)
    far = (old_far_ref, old_far_core_ref)

    def copies(t):
        place = t % 2
        return [
            pltpu.make_async_copy(source.at[t], target.at[place], state_sems.at[number, place])
            for number, (source, target) in enumerate(((stat_in, stat_ref), (acc_in, acc_ref)))
        ]

    roped_copy = pltpu.make_async_copy(roped_in, roped_ref, roped_sem)
    roped_copy.start()
    for t in range(2):
        for copy in copies(t):
            copy.start()

    @pl.when(odd == 1)
    def _():
        fetch(core_ref, 0, kv_ref, base, 16, sem)

    @pl.when(chip == 1)
    def _():
        place = jnp.where(has_old, 32, 32 * odd)
        fetch(far_ref, 0, kv_ref, place, 16, sem)
        fetch(far_core_ref, 0, kv_ref, place + 16, 16, sem)

    @pl.when(has_old)
    def _():
        for block in range(4):

            @pl.when(block >= group_index)
            def _(block=block):
                gap = jnp.where(block == group_index, 0, odd)
                place = 16 * (gap + block - group_index)
                fetch_pair(near, 4 * block, kv_ref, place, sem)
                fetch_pair(far, 4 * block, kv_ref, place + 8, sem)

    weight_copy = pltpu.make_async_copy(weight_ref, w_ref, weight_sem)

    @pl.when(jnp.logical_not(has_old))
    def _():
        bias_ref[...] = jnp.where(odd == 1, masked_score, 0.0) + jnp.zeros_like(bias_ref)
        empty = pl.ds(0, block_slots)

        @pl.when(odd == 1)
        def _():
            kv_ref[empty] = jnp.zeros((block_slots, 2, 32, 256), jnp.bfloat16)

    @pl.when(has_old)
    def _():
        bias_ref[:, :256] = old_bias(rows, group_index)
        bias_ref[:, 256:] = old_bias(rows, group_index ^ 2)

    roped_copy.wait()
    wait_rows(kv_ref, blocks, 4, sem)
    lane = lax.broadcasted_iota(jnp.int32, stat_ref.shape[1:], 1)

    def begin(t, most_ref):
        for copy in copies(t):
            copy.wait()
        most_ref[...] = jnp.where(lane < 64, stat_ref[t % 2], masked_score)

    def finish(t):
        stat = stat_ref[t % 2]
        factor = jnp.exp(stat[:, :1] - top_ref[...])
        sums = stat[:, 64:65] * factor + jnp.sum(sum_ref[...], axis=1, keepdims=True)
        inverse = 1.0 / sums
        old = factor * inverse
        mixed = acc_ref[t % 2] * join([old, old]) + values_ref[...] * join([inverse, inverse])
        roped_ref[t] = mixed.astype(jnp.bfloat16)

        @pl.when(t + 2 < items)
        def _():
            for copy in copies(t + 2):
                copy.start()

        @pl.when(t + 3 == items)
        def _():
            weight_copy.start()

    scratch = (roped_ref, kv_ref, bias_ref, (s_0, s_1), (most_0, most_1), top_ref, sum_ref, values_ref)

    @pl.when(has_old)
    def _():
        attention_at_once(*scratch, begin, finish)

    @pl.when(jnp.logical_not(has_old))
    def _():
        attention(steps, 2 * block_keys, *scratch, begin, finish)


    weight_copy.wait()

    def out_copy(n, columns):
        return pltpu.make_async_copy(stage_ref.at[n % 2], hidden_ref.at[:, columns], out_sems.at[n % 2])

    def project(n, carry):
        columns = pl.ds(pl.multiple_of(n * chunk, chunk), chunk)

        @pl.when(n >= 2)
        def _():
            out_copy(n, columns).wait()

        attended = join(
            [
                roped_ref[t, one * rows : (one + 1) * rows, :]
                for t in range(items)
                for one in range(head_pair)
            ]
        )
        stage_ref[n % 2] = jnp.dot(
            attended, w_ref[:, columns], preferred_element_type=jnp.float32
        ).astype(jnp.bfloat16)
        out_copy(n, columns).start()
        return carry

    lax.fori_loop(0, chunks, project, 0)
    for n in range(2):
        out_copy(n, pl.ds(0, chunk)).wait()


def rest_part(lengths, state, slots, weight):
    items, pair_rows, _ = state[0].shape
    rows = pair_rows // head_pair
    width = weight.shape[1]
    chunk = 512
    return pl.pallas_call(
        rest_kernel,
        out_shape=pltpu.HBM((rows, width), jnp.bfloat16),
        in_specs=[smem_spec] + [hbm_spec] * 3 + [any_spec] * 7 + [hbm_spec],
        out_specs=hbm_spec,
        scratch_shapes=[pltpu.VMEM((items, pair_rows, 256), jnp.bfloat16)]
        + state_shapes(2, rows)[1:]
        + working(rows, 2, 2 * block_keys)
        + [
            pltpu.VMEM(weight.shape, jnp.bfloat16),
            pltpu.VMEM((2, rows, chunk), jnp.bfloat16),
            pltpu.SemaphoreType.DMA,
            pltpu.SemaphoreType.DMA((2, 2)),
            pltpu.SemaphoreType.DMA,
            pltpu.SemaphoreType.DMA,
            pltpu.SemaphoreType.DMA((2,)),
        ],
        cost_estimate=light,
        compiler_params=params(large_limit),
        name="attend_rest",
    )(lengths, *in_hbm(*state), *slots, *in_hbm(weight))


def place_kernel(targets_ref, arrived_ref, key_in, value_in, key_ref, value_ref, buffer_ref, load_sem, sem):
    load = pltpu.make_async_copy(arrived_ref, buffer_ref, load_sem)
    load.start()
    load.wait()

    def each(act):
        for slot in range(targets_ref.shape[0]):
            page = targets_ref[slot]

            @pl.when(page >= 0)
            def _(slot=slot, page=page):
                for kind, out_ref in enumerate((key_ref, value_ref)):
                    act(pltpu.make_async_copy(buffer_ref.at[slot, kind], out_ref.at[page], sem))

    each(lambda copy: copy.start())
    each(lambda copy: copy.wait())


def place_new(targets, arrived, key_pool, value_pool):
    return pl.pallas_call(
        place_kernel,
        out_shape=(
            pltpu.HBM(key_pool.shape, jnp.bfloat16),
            pltpu.HBM(value_pool.shape, jnp.bfloat16),
        ),
        in_specs=[smem_spec, any_spec, hbm_spec, hbm_spec],
        out_specs=(hbm_spec,) * 2,
        input_output_aliases={2: 0, 3: 1},
        scratch_shapes=[
            pltpu.VMEM(arrived.shape, jnp.bfloat16),
            pltpu.SemaphoreType.DMA,
            pltpu.SemaphoreType.DMA,
        ],
        cost_estimate=light,
        compiler_params=params(small_limit),
        name="place_new",
    )(targets, arrived, *in_hbm(key_pool, value_pool))


def after(value, *others):
    return lax.optimization_barrier((value,) + others)[0]


def body(queries, new_keys, new_values, key_cache, value_cache, out_weight, lengths, page_table):
    blk_count = lax.axis_size("blk")
    pages = key_cache.shape[0]
    window_pages = page_table.shape[1] // 2
    cap = (window_pages + blk_count - 1) // blk_count

    def other_core(value):
        return lax.ppermute(value, "group", [(0, 1), (1, 0), (2, 3), (3, 2)])

    def other_chip(value):
        return lax.ppermute(value, "group", [(0, 2), (2, 0), (1, 3), (3, 1)])

    picked = pick_old(page_table, cap, key_cache, value_cache)
    old = lax.all_to_all(picked, "blk", split_axis=0, concat_axis=0, tiled=True)
    old = old.reshape((blk_count * cap,) + old.shape[2:])

    fresh, cosine, sine = rotate_keys(lengths, new_keys[0], new_values[0])
    fresh_far = other_chip(fresh)
    fresh_core = other_core(fresh)
    roped, acc, stat, key_out, value_out = diagonal_part(
        after(queries[0], picked), cosine, sine, fresh, key_cache, value_cache
    )

    old = sort_old(after(page_table, stat), blk_count, cap, pages, old)
    old_far = other_chip(old)
    old_core = other_core(old)
    fresh_far_core = other_core(after(fresh_far, old))
    new, targets = pick_new(
        page_table, blk_count, cap, pages, (fresh, fresh_core, fresh_far, fresh_far_core)
    )
    arrived = lax.all_to_all(new, "blk", split_axis=0, concat_axis=0, tiled=True)
    old_far_core = other_core(after(old_far, new))
    hidden = rest_part(
        lengths, (roped, acc, stat),
        (fresh_core, fresh_far, fresh_far_core, old, old_core, old_far, old_far_core),
        out_weight,
    )
    key_out, value_out = place_new(targets, arrived, key_out, value_out)
    return (hidden[None], key_out, value_out)


def solution(mesh):
    return jax.shard_map(
        body,
        mesh=mesh,
        in_specs=(
            P("blk", "group", None),
            P("blk", "group", None),
            P("blk", "group", None),
            P("blk", "group", None),
            P("blk", "group", None),
            P(),
            P(),
            P(),
        ),
        out_specs=(P("blk", "group", None), P("blk", "group", None), P("blk", "group", None)),
        check_vma=False,
    )
```

```python
import jax
import jax.numpy as jnp
import numpy as np
from jax import lax
from jax.experimental import pallas as pl
from jax.experimental.pallas import tpu as pltpu
from jax.sharding import PartitionSpec as P

masked_score = -1e30
block_keys = 512
block_slots = 16
any_spec = pl.BlockSpec(memory_space=pl.ANY)
hbm_spec = pl.BlockSpec(memory_space=pltpu.HBM)
smem_spec = pl.BlockSpec(memory_space=pltpu.SMEM)
vmem_spec = pl.BlockSpec(memory_space=pltpu.VMEM)
small_limit = 16 * 1024 * 1024
head_pair = 2
large_limit = 60 * 1024 * 1024


light = pl.CostEstimate(flops=1, bytes_accessed=1, transcendentals=0)


def params(limit):
    return pltpu.CompilerParams(vmem_limit_bytes=limit)


def in_hbm(*arrays):
    return [pltpu.with_memory_space_constraint(array, pltpu.HBM) for array in arrays]


def turn(values, cosine, sine):
    front = values[:, :128].astype(jnp.float32)
    return front * cosine + pltpu.roll(front, 64, 1) * sine


def join(pieces):
    return jnp.concatenate(pieces, axis=1)


def pages_here(table_ref, r, first, count, cap, pages):
    low = lax.axis_index("blk") * pages
    found = jnp.int32(0)
    chosen = [jnp.int32(0)] * cap
    for j in range(first, first + count):
        page = table_ref[r, j] - low
        inside = (page >= 0) & (page < pages)
        chosen = [jnp.where(inside & (found == c), page, chosen[c]) for c in range(cap)]
        found = found + inside.astype(jnp.int32)
    return chosen, found


def pick_old_kernel(table_ref, key_ref, value_ref, out_ref, sem):
    requests, cap = out_ref.shape[:2]
    for r in range(requests):
        chosen, _ = pages_here(table_ref, r, 0, table_ref.shape[1] // 2, cap, key_ref.shape[0])
        for c in range(cap):
            pltpu.make_async_copy(key_ref.at[chosen[c]], out_ref.at[r, c, 0], sem).start()
            pltpu.make_async_copy(value_ref.at[chosen[c]], out_ref.at[r, c, 1], sem).start()
    pltpu.make_async_copy(out_ref, out_ref, sem).wait()


def pick_old(page_table, cap, key_cache, value_cache):
    requests = page_table.shape[0]
    return pl.pallas_call(
        pick_old_kernel,
        out_shape=jax.ShapeDtypeStruct((requests, cap, 2) + key_cache.shape[1:], jnp.bfloat16),
        in_specs=[smem_spec, hbm_spec, hbm_spec],
        out_specs=vmem_spec,
        scratch_shapes=[pltpu.SemaphoreType.DMA],
        cost_estimate=light,
        compiler_params=params(small_limit),
        name="pick_old",
    )(*in_hbm(page_table, key_cache, value_cache))


def owner_of(page, pages, owners):
    factor = (1 << 20) // pages + 1
    assert all((p * factor) >> 20 == p // pages for p in range(pages * owners))
    assert pages * owners * factor < 1 << 31
    return (page * factor) >> 20


def find_slots(table_ref, first, count, cap, pages, counts_ref):
    owners = counts_ref.shape[0]
    row = lax.axis_index("blk")
    for o in range(owners):
        counts_ref[o] = 0
    slots = []
    for j in range(count):
        owner = owner_of(table_ref[row, first + j], pages, owners)
        rank = counts_ref[owner]
        counts_ref[owner] = rank + 1
        slots.append(owner * cap + rank)
    return slots


def rotate_kernel(lengths_ref, freq_ref, keys_ref, values_ref, out_ref, cos_ref, sin_ref):
    rows = keys_ref.shape[0]
    slots = rows // 32
    start = lengths_ref[lax.axis_index("blk")] + lax.axis_index("group") * rows
    positions = start + lax.broadcasted_iota(jnp.int32, (rows, 128), 0)
    angles = positions.astype(jnp.float32) * freq_ref[...]
    lane = lax.broadcasted_iota(jnp.int32, (rows, 128), 1)
    cosine = jnp.cos(angles)
    sine = jnp.sin(angles)
    sine = jnp.where(lane < 64, -sine, sine)
    cos_ref[...] = cosine
    sin_ref[...] = sine
    keys = keys_ref[...]
    turned = join([turn(keys, cosine, sine).astype(jnp.bfloat16), keys[:, 128:]])
    out_ref[:, 0] = turned.reshape(slots, 32, 256)
    out_ref[:, 1] = values_ref[...].reshape(slots, 32, 256)


def rotate_keys(lengths, keys, values):
    rows, head_dim = keys.shape
    quarter = head_dim // 4
    freq_table = np.float32(10000.0) ** (-np.arange(quarter, dtype=np.float32) / np.float32(quarter))
    freq_table = np.concatenate([freq_table, freq_table])[None].astype(np.float32)
    return pl.pallas_call(
        rotate_kernel,
        out_shape=(
            pltpu.HBM((rows // 32, 2, 32, head_dim), jnp.bfloat16),
            pltpu.HBM((rows, 128), jnp.float32),
            pltpu.HBM((rows, 128), jnp.float32),
        ),
        in_specs=[smem_spec, vmem_spec, vmem_spec, vmem_spec],
        out_specs=(vmem_spec,) * 3,
        cost_estimate=light,
        compiler_params=params(small_limit),
        name="rotate_keys",
    )(lengths, jnp.asarray(freq_table), keys, values)


def sort_kernel(pages, cap, table_ref, old_ref, out_ref, counts_ref, sem):
    count = out_ref.shape[0]
    for j, slot in enumerate(find_slots(table_ref, 0, count, cap, pages, counts_ref)):
        pltpu.make_async_copy(old_ref.at[slot], out_ref.at[j], sem).start()
    pltpu.make_async_copy(out_ref, out_ref, sem).wait()


def sort_old(page_table, blk_count, cap, pages, old):
    window = page_table.shape[1] // 2
    return pl.pallas_call(
        lambda *refs: sort_kernel(pages, cap, *refs),
        out_shape=jax.ShapeDtypeStruct((window,) + old.shape[1:], jnp.bfloat16),
        in_specs=[smem_spec, hbm_spec],
        out_specs=vmem_spec,
        scratch_shapes=[pltpu.SMEM((blk_count,), jnp.int32), pltpu.SemaphoreType.DMA],
        cost_estimate=light,
        compiler_params=params(small_limit),
        name="sort_old",
    )(page_table, *in_hbm(old))


def pick_new_kernel(
    pages, cap, table_ref, own_ref, core_ref, far_ref, far_core_ref, out_ref, targets_ref,
    slots_ref, counts_ref, sem,
):
    count = slots_ref.shape[0]
    block_pages = count // 4
    group_index = lax.axis_index("group")
    for j, slot in enumerate(find_slots(table_ref, table_ref.shape[1] - count, count, cap, pages, counts_ref)):
        slots_ref[j] = slot
    for number, ref in enumerate((own_ref, core_ref, far_ref, far_core_ref)):
        block = group_index ^ number
        for place in range(block_pages):
            source = ref.at[4 * place + group_index]
            target = out_ref.at[slots_ref[block * block_pages + place]]
            pltpu.make_async_copy(source, target, sem).start()
    for r in range(table_ref.shape[0]):
        chosen, found = pages_here(table_ref, r, table_ref.shape[1] - count, count, cap, pages)
        for c in range(cap):
            targets_ref[r * cap + c] = jnp.where(found > c, chosen[c], -1)
    sent = out_ref.at[pl.ds(0, count)]
    pltpu.make_async_copy(sent, sent, sem).wait()


def pick_new(page_table, blk_count, cap, pages, sources):
    window = page_table.shape[1] // 2
    return pl.pallas_call(
        lambda *refs: pick_new_kernel(pages, cap, *refs),
        out_shape=(
            jax.ShapeDtypeStruct((blk_count * cap,) + sources[0].shape[1:], jnp.bfloat16),
            jax.ShapeDtypeStruct((blk_count * cap,), jnp.int32),
        ),
        in_specs=[smem_spec] + [any_spec] * 4,
        out_specs=(vmem_spec, smem_spec),
        scratch_shapes=[
            pltpu.SMEM((window,), jnp.int32),
            pltpu.SMEM((blk_count,), jnp.int32),
            pltpu.SemaphoreType.DMA,
        ],
        cost_estimate=light,
        compiler_params=params(small_limit),
        name="pick_new",
    )(page_table, *sources)


def lane_fold(values, combine):
    total = values[:, :128]
    for start in range(128, values.shape[1], 128):
        total = combine(total, values[:, start : start + 128])
    return total


def old_bias(rows, quarter):
    row = lax.broadcasted_iota(jnp.int32, (rows, 256), 0)
    column = lax.broadcasted_iota(jnp.int32, (rows, 256), 1)
    held = quarter ^ (column // 128)
    position = ((column % 128) // 32) * 128 + 32 * held + column % 32
    return jnp.where(position > row, 0.0, masked_score)


def fetch(source, first, kv_ref, place, count, sem):
    pltpu.make_async_copy(source.at[pl.ds(first, count)], kv_ref.at[pl.ds(place, count)], sem).start()


def fetch_pair(sources, first, kv_ref, place, sem):
    fetch(sources[0], first, kv_ref, place, 4, sem)
    fetch(sources[1], first, kv_ref, place + 4, 4, sem)


def wait_rows(kv_ref, blocks, most, sem):
    for n in range(1, most + 1):

        @pl.when(blocks == n)
        def _(n=n):
            filled = kv_ref.at[pl.ds(0, n * block_slots)]
            pltpu.make_async_copy(filled, filled, sem).wait()


def attention(steps, step_keys, roped_ref, kv_ref, bias_ref, s_refs, most_refs, top_ref, sum_ref, sum_of_values, begin, finish):
    items, rows, _ = roped_ref.shape
    step_slots = step_keys // 32
    tables, _, biased = bias_ref.shape

    def block(kind, c):
        return kv_ref[pl.ds(c * step_slots, step_slots), kind].reshape(step_keys, 256)

    def scores(t, c, which):
        result = lax.dot_general(
            roped_ref[t], block(0, c), (((1,), (1,)), ((), ())), preferred_element_type=jnp.float32
        )
        bias = bias_ref[jnp.minimum(c, tables - 1)]
        head = result[:, :biased].reshape(head_pair, rows // head_pair, biased) + bias
        head = head.reshape(rows, biased)
        result = join([head, result[:, biased:]]) if step_keys > biased else head
        s_refs[which][c] = result
        most_refs[which][...] = jnp.maximum(most_refs[which][...], lane_fold(result, jnp.maximum))

    def weigh(c, which):
        weights = jnp.exp(s_refs[which][c] - join([top_ref[...]] * (step_keys // 128)))
        sum_ref[...] += lane_fold(weights, jnp.add)
        sum_of_values[...] += jnp.dot(
            weights.astype(jnp.bfloat16), block(1, c), preferred_element_type=jnp.float32
        )

    def settle(which):
        top_ref[...] = jnp.broadcast_to(
            jnp.max(most_refs[which][...], axis=1, keepdims=True), top_ref.shape
        )
        sum_ref[...] = jnp.zeros_like(sum_ref)
        sum_of_values[...] = jnp.zeros_like(sum_of_values)

    def loop(work):
        def step(c, carry):
            work(c)
            return carry

        lax.fori_loop(0, steps, step, 0)

    def both(t, which):
        def work(c):
            weigh(c, which)
            scores(t + 1, c, 1 - which)

        loop(work)

    drive(
        items, most_refs, begin, settle, finish,
        lambda: loop(lambda c: scores(0, c, 0)),
        both,
        lambda which: loop(lambda c: weigh(c, which)),
    )


def attention_at_once(roped_ref, kv_ref, bias_ref, s_refs, most_refs, top_ref, sum_ref, sum_of_values, begin, finish):
    items, rows, _ = roped_ref.shape
    blocks, _, width = s_refs[0].shape
    biased = bias_ref.shape[2]
    slots = width // 32

    def scores(t, which):
        most = most_refs[which][...]
        query = roped_ref[t]
        for c in range(blocks):
            keys = kv_ref[c * slots : (c + 1) * slots, 0].reshape(width, 256)
            result = lax.dot_general(
                query, keys, (((1,), (1,)), ((), ())), preferred_element_type=jnp.float32
            )
            if c == 0:
                head = result[:, :biased].reshape(head_pair, rows // head_pair, biased) + bias_ref[0]
                head = head.reshape(rows, biased)
                result = join([head, result[:, biased:]]) if width > biased else head
            s_refs[which][c] = result
            most = jnp.maximum(most, lane_fold(result, jnp.maximum))
        most_refs[which][...] = most

    def weigh(which):
        top = join([top_ref[...]] * (width // 128))
        sums = None
        total = None
        for c in range(blocks):
            weights = jnp.exp(s_refs[which][c] - top)
            folded = lane_fold(weights, jnp.add)
            sums = folded if sums is None else sums + folded
            values = kv_ref[c * slots : (c + 1) * slots, 1].reshape(width, 256)
            part = jnp.dot(weights.astype(jnp.bfloat16), values, preferred_element_type=jnp.float32)
            total = part if total is None else total + part
        sum_ref[...] = sums
        sum_of_values[...] = total

    def settle(which):
        top_ref[...] = jnp.broadcast_to(
            jnp.max(most_refs[which][...], axis=1, keepdims=True), top_ref.shape
        )

    def both(t, which):
        weigh(which)
        scores(t + 1, 1 - which)

    drive(items, most_refs, begin, settle, finish, lambda: scores(0, 0), both, weigh)


def drive(items, most_refs, begin, settle, finish, only_scores, both, only_weigh):
    def one(t, which):
        begin(t + 1, most_refs[1 - which])
        settle(which)
        both(t, which)
        finish(t)

    def two(i, carry):
        one(2 * i, 0)
        one(2 * i + 1, 1)
        return carry

    begin(0, most_refs[0])
    only_scores()
    pairs = (items - 1) // 2
    lax.fori_loop(0, pairs, two, 0)
    last = 2 * pairs
    if last < items - 1:
        one(last, 0)
        last += 1
    settle(last % 2)
    only_weigh(last % 2)
    finish(last)


def working(rows, steps, step_keys, tables):
    return [
        pltpu.VMEM((steps * step_keys // 32, 2, 32, 256), jnp.bfloat16),
        pltpu.VMEM((steps, head_pair * rows, step_keys), jnp.float32),
        pltpu.VMEM((steps, head_pair * rows, step_keys), jnp.float32),
        pltpu.VMEM((head_pair * rows, 128), jnp.float32),
        pltpu.VMEM((head_pair * rows, 128), jnp.float32),
        pltpu.VMEM((head_pair * rows, 128), jnp.float32),
        pltpu.VMEM((head_pair * rows, 128), jnp.float32),
        pltpu.VMEM((head_pair * rows, 256), jnp.float32),
        pltpu.VMEM((tables, rows, block_keys), jnp.float32),
    ]


def state_shapes(items, rows):
    return [
        pltpu.VMEM((items, head_pair * rows, 256), jnp.bfloat16),
        pltpu.VMEM((items, head_pair * rows, 256), jnp.float32),
        pltpu.VMEM((items, head_pair * rows, 128), jnp.float32),
    ]


def state_out(items, rows):
    return (
        pltpu.HBM((items, head_pair * rows, 256), jnp.float32),
        pltpu.HBM((items, head_pair * rows, 128), jnp.float32),
    )


def diagonal_kernel(
    query_ref, cos_in, sin_in, own_ref, key_ref, value_ref, roped_out, acc_out, stat_out,
    key_out_ref, value_out_ref, cos_ref, sin_ref, key_pool, value_pool, q_ref, roped_ref, acc_ref, stat_ref, kv_ref, s_0, s_1, most_0, most_1, top_ref, sum_ref, values_ref,
    bias_ref, query_sem, sem, out_sem, pool_sems, angle_sems,
):
    rows = q_ref.shape[0]
    items = roped_ref.shape[0]
    loads = [
        pltpu.make_async_copy(key_ref, key_pool, pool_sems.at[0]),
        pltpu.make_async_copy(value_ref, value_pool, pool_sems.at[1]),
    ]
    stores = [
        pltpu.make_async_copy(key_pool, key_out_ref, pool_sems.at[0]),
        pltpu.make_async_copy(value_pool, value_out_ref, pool_sems.at[1]),
    ]
    query_copy = pltpu.make_async_copy(query_ref, q_ref, query_sem)
    query_copy.start()
    angle_copies = [
        pltpu.make_async_copy(cos_in, cos_ref, angle_sems.at[0]),
        pltpu.make_async_copy(sin_in, sin_ref, angle_sems.at[1]),
    ]
    for copy in angle_copies:
        copy.start()
    fetch(own_ref, 0, kv_ref, 0, block_slots, sem)
    for copy in loads:
        copy.start()
    row = lax.broadcasted_iota(jnp.int32, (rows, block_keys), 0)
    column = lax.broadcasted_iota(jnp.int32, (rows, block_keys), 1)
    bias_ref[0] = jnp.where(column <= row, 0.0, masked_score)
    query_copy.wait()
    for copy in angle_copies:
        copy.wait()

    def rope(t, carry):
        for one in range(head_pair):
            raw = q_ref[:, pl.ds(pl.multiple_of((t * head_pair + one) * 256, 256), 256)]
            front = turn(raw, cos_ref[...], sin_ref[...])
            some = pl.ds(one * rows, rows)
            roped_ref[t, some, :128] = (front * 0.0625).astype(jnp.bfloat16)
            roped_ref[t, some, 128:] = raw[:, 128:] * jnp.bfloat16(0.0625)
        return carry

    lax.fori_loop(0, items, rope, 0)
    roped_copy = pltpu.make_async_copy(roped_ref, roped_out, query_sem)
    roped_copy.start()
    pltpu.make_async_copy(kv_ref, kv_ref, sem).wait()
    for load, store in zip(loads, stores):
        load.wait()
        store.start()

    def begin(t, most_ref):
        most_ref[...] = jnp.full_like(most_ref, masked_score)

    def finish(t):
        lane = lax.broadcasted_iota(jnp.int32, stat_ref.shape[1:], 1)
        sums = jnp.sum(sum_ref[...], axis=1, keepdims=True)
        stat_ref[t] = jnp.where(lane < 64, top_ref[...], sums)
        acc_ref[t] = values_ref[...]
        pltpu.make_async_copy(acc_ref.at[t], acc_out.at[t], out_sem).start()
        pltpu.make_async_copy(stat_ref.at[t], stat_out.at[t], out_sem).start()

    attention_at_once(
        roped_ref, kv_ref, bias_ref, (s_0, s_1), (most_0, most_1), top_ref, sum_ref, values_ref,
        begin, finish,
    )
    roped_copy.wait()
    for copy in stores:
        copy.wait()
    pltpu.make_async_copy(acc_ref, acc_out, out_sem).wait()
    pltpu.make_async_copy(stat_ref, stat_out, out_sem).wait()


def diagonal_part(queries, cosine, sine, own, key_cache, value_cache):
    rows, width = queries.shape
    items = width // (256 * head_pair)
    return pl.pallas_call(
        diagonal_kernel,
        out_shape=(pltpu.HBM((items, head_pair * rows, 256), jnp.bfloat16),)
        + state_out(items, rows)
        + (pltpu.HBM(key_cache.shape, jnp.bfloat16), pltpu.HBM(value_cache.shape, jnp.bfloat16)),
        in_specs=[hbm_spec] * 6,
        out_specs=(hbm_spec,) * 5,
        scratch_shapes=[
            pltpu.VMEM(cosine.shape, jnp.float32),
            pltpu.VMEM(sine.shape, jnp.float32),
            pltpu.VMEM(key_cache.shape, jnp.bfloat16),
            pltpu.VMEM(value_cache.shape, jnp.bfloat16),
            pltpu.VMEM((rows, width), jnp.bfloat16),
        ]
        + state_shapes(items, rows)
        + working(rows, 1, block_keys, 1)
        + [pltpu.SemaphoreType.DMA] * 3
        + [pltpu.SemaphoreType.DMA((2,))] * 2,
        cost_estimate=light,
        compiler_params=params(large_limit),
        name="attend_diagonal",
    )(*in_hbm(queries, cosine, sine, own, key_cache, value_cache))


def rest_kernel(
    lengths_ref, roped_in, acc_in, stat_in, core_ref, far_ref, far_core_ref,
    old_ref, old_core_ref, old_far_ref, old_far_core_ref, weight_ref, hidden_ref,
    roped_ref, acc_ref, stat_ref, kv_ref, s_0, s_1, most_0, most_1, top_ref, sum_ref, values_ref,
    bias_ref, w_ref, stage_ref, roped_sem, state_sems, sem, weight_sem, out_sems,
):
    group_index = lax.axis_index("group")
    has_old = lengths_ref[lax.axis_index("blk")] > 0
    items = roped_ref.shape[0]
    rows = bias_ref.shape[1]
    chunk = stage_ref.shape[2]
    chunks = w_ref.shape[1] // chunk
    odd = group_index % 2
    chip = group_index // 2
    blocks = jnp.where(has_old, 4, odd + 2 * chip)
    steps = jnp.where(has_old, 2, odd + chip)
    base = jnp.where(has_old, 16, 16 * odd)
    near = (old_ref, old_core_ref)
    far = (old_far_ref, old_far_core_ref)

    def copies(t):
        return [
            pltpu.make_async_copy(source.at[t], target.at[t], state_sems.at[number, t])
            for number, (source, target) in enumerate(((stat_in, stat_ref), (acc_in, acc_ref)))
        ]

    roped_copy = pltpu.make_async_copy(roped_in, roped_ref, roped_sem)
    roped_copy.start()
    @pl.when(odd == 1)
    def _():
        fetch(core_ref, 0, kv_ref, base, 16, sem)

    @pl.when(chip == 1)
    def _():
        place = jnp.where(has_old, 32, 32 * odd)
        fetch(far_ref, 0, kv_ref, place, 16, sem)
        fetch(far_core_ref, 0, kv_ref, place + 16, 16, sem)

    @pl.when(has_old)
    def _():
        for block in range(4):

            @pl.when(block >= group_index)
            def _(block=block):
                gap = jnp.where(block == group_index, 0, odd)
                place = 16 * (gap + block - group_index)
                fetch_pair(near, 4 * block, kv_ref, place, sem)
                fetch_pair(far, 4 * block, kv_ref, place + 8, sem)

    for t in range(items):
        for copy in copies(t):
            copy.start()
    weight_copy = pltpu.make_async_copy(weight_ref, w_ref, weight_sem)
    weight_copy.start()

    bias_ref[1] = jnp.zeros(bias_ref.shape[1:], jnp.float32)

    @pl.when(jnp.logical_not(has_old))
    def _():
        bias_ref[0] = jnp.where(odd == 1, masked_score, 0.0) + jnp.zeros(bias_ref.shape[1:], jnp.float32)
        empty = pl.ds(0, block_slots)

        @pl.when(odd == 1)
        def _():
            kv_ref[empty] = jnp.zeros((block_slots, 2, 32, 256), jnp.bfloat16)

    @pl.when(has_old)
    def _():
        bias_ref[0, :, :256] = old_bias(rows, group_index)
        bias_ref[0, :, 256:] = old_bias(rows, group_index ^ 2)

    roped_copy.wait()
    wait_rows(kv_ref, blocks, 4, sem)
    lane = lax.broadcasted_iota(jnp.int32, stat_ref.shape[1:], 1)

    def begin(t, most_ref):
        for copy in copies(t):
            copy.wait()
        most_ref[...] = jnp.where(lane < 64, stat_ref[t], masked_score)

    def finish(t):
        stat = stat_ref[t]
        factor = jnp.exp(stat[:, :1] - top_ref[...])
        sums = stat[:, 64:65] * factor + jnp.sum(sum_ref[...], axis=1, keepdims=True)
        inverse = 1.0 / sums
        old = factor * inverse
        mixed = acc_ref[t] * join([old, old]) + values_ref[...] * join([inverse, inverse])
        roped_ref[t] = mixed.astype(jnp.bfloat16)

    scratch = (roped_ref, kv_ref, bias_ref, (s_0, s_1), (most_0, most_1), top_ref, sum_ref, values_ref)

    attention(steps, 2 * block_keys, *scratch, begin, finish)
    weight_copy.wait()

    def out_copy(n, columns):
        return pltpu.make_async_copy(stage_ref.at[n % 2], hidden_ref.at[:, columns], out_sems.at[n % 2])

    def project(n, carry):
        columns = pl.ds(pl.multiple_of(n * chunk, chunk), chunk)

        @pl.when(n >= 2)
        def _():
            out_copy(n, columns).wait()

        attended = join(
            [
                roped_ref[t, one * rows : (one + 1) * rows, :]
                for t in range(items)
                for one in range(head_pair)
            ]
        )
        stage_ref[n % 2] = jnp.dot(
            attended, w_ref[:, columns], preferred_element_type=jnp.float32
        ).astype(jnp.bfloat16)
        out_copy(n, columns).start()
        return carry

    lax.fori_loop(0, chunks, project, 0)
    for n in range(2):
        out_copy(n, pl.ds(0, chunk)).wait()


def rest_part(lengths, state, slots, weight):
    items, pair_rows, _ = state[0].shape
    rows = pair_rows // head_pair
    width = weight.shape[1]
    chunk = 512
    return pl.pallas_call(
        rest_kernel,
        out_shape=pltpu.HBM((rows, width), jnp.bfloat16),
        in_specs=[smem_spec] + [hbm_spec] * 3 + [any_spec] * 7 + [hbm_spec],
        out_specs=hbm_spec,
        scratch_shapes=state_shapes(items, rows)
        + working(rows, 2, 2 * block_keys, 2)
        + [
            pltpu.VMEM(weight.shape, jnp.bfloat16),
            pltpu.VMEM((2, rows, chunk), jnp.bfloat16),
            pltpu.SemaphoreType.DMA,
            pltpu.SemaphoreType.DMA((2, items)),
            pltpu.SemaphoreType.DMA,
            pltpu.SemaphoreType.DMA,
            pltpu.SemaphoreType.DMA((2,)),
        ],
        cost_estimate=light,
        compiler_params=params(large_limit),
        name="attend_rest",
    )(lengths, *in_hbm(*state), *slots, *in_hbm(weight))


def place_kernel(targets_ref, arrived_ref, key_in, value_in, key_ref, value_ref, buffer_ref, load_sem, sem):
    load = pltpu.make_async_copy(arrived_ref, buffer_ref, load_sem)
    load.start()
    load.wait()

    def each(act):
        for slot in range(targets_ref.shape[0]):
            page = targets_ref[slot]

            @pl.when(page >= 0)
            def _(slot=slot, page=page):
                for kind, out_ref in enumerate((key_ref, value_ref)):
                    act(pltpu.make_async_copy(buffer_ref.at[slot, kind], out_ref.at[page], sem))

    each(lambda copy: copy.start())
    each(lambda copy: copy.wait())


def place_new(targets, arrived, key_pool, value_pool):
    return pl.pallas_call(
        place_kernel,
        out_shape=(
            pltpu.HBM(key_pool.shape, jnp.bfloat16),
            pltpu.HBM(value_pool.shape, jnp.bfloat16),
        ),
        in_specs=[smem_spec, any_spec, hbm_spec, hbm_spec],
        out_specs=(hbm_spec,) * 2,
        input_output_aliases={2: 0, 3: 1},
        scratch_shapes=[
            pltpu.VMEM(arrived.shape, jnp.bfloat16),
            pltpu.SemaphoreType.DMA,
            pltpu.SemaphoreType.DMA,
        ],
        cost_estimate=light,
        compiler_params=params(small_limit),
        name="place_new",
    )(targets, arrived, *in_hbm(key_pool, value_pool))


def after(value, *others):
    return lax.optimization_barrier((value,) + others)[0]


def body(queries, new_keys, new_values, key_cache, value_cache, out_weight, lengths, page_table):
    blk_count = lax.axis_size("blk")
    pages = key_cache.shape[0]
    window_pages = page_table.shape[1] // 2
    cap = (window_pages + blk_count - 1) // blk_count

    def other_core(value):
        return lax.ppermute(value, "group", [(0, 1), (1, 0), (2, 3), (3, 2)])

    def other_chip(value):
        return lax.ppermute(value, "group", [(0, 2), (2, 0), (1, 3), (3, 1)])

    picked = pick_old(page_table, cap, key_cache, value_cache)
    old = lax.all_to_all(picked, "blk", split_axis=0, concat_axis=0, tiled=True)
    old = old.reshape((blk_count * cap,) + old.shape[2:])

    fresh, cosine, sine = rotate_keys(lengths, new_keys[0], new_values[0])
    fresh_far = other_chip(fresh)
    fresh_core = other_core(fresh)
    roped, acc, stat, key_out, value_out = diagonal_part(
        after(queries[0], picked), cosine, sine, fresh, key_cache, value_cache
    )

    old = sort_old(after(page_table, stat), blk_count, cap, pages, old)
    old_far = other_chip(old)
    old_core = other_core(old)
    fresh_far_core = other_core(after(fresh_far, old))
    new, targets = pick_new(
        page_table, blk_count, cap, pages, (fresh, fresh_core, fresh_far, fresh_far_core)
    )
    arrived = lax.all_to_all(new, "blk", split_axis=0, concat_axis=0, tiled=True)
    old_far_core = other_core(after(old_far, new))
    hidden = rest_part(
        lengths, (roped, acc, stat),
        (fresh_core, fresh_far, fresh_far_core, old, old_core, old_far, old_far_core),
        out_weight,
    )
    key_out, value_out = place_new(targets, arrived, key_out, value_out)
    return (hidden[None], key_out, value_out)


def solution(mesh):
    return jax.shard_map(
        body,
        mesh=mesh,
        in_specs=(
            P("blk", "group", None),
            P("blk", "group", None),
            P("blk", "group", None),
            P("blk", "group", None),
            P("blk", "group", None),
            P(),
            P(),
            P(),
        ),
        out_specs=(P("blk", "group", None), P("blk", "group", None), P("blk", "group", None)),
        check_vma=False,
    )
```

```python
import jax
import jax.numpy as jnp
import numpy as np
from jax import lax
from jax.experimental import pallas as pl
from jax.experimental.pallas import tpu as pltpu
from jax.sharding import PartitionSpec as P

masked_score = -1e30
block_keys = 512
block_slots = 16
any_spec = pl.BlockSpec(memory_space=pl.ANY)
hbm_spec = pl.BlockSpec(memory_space=pltpu.HBM)
smem_spec = pl.BlockSpec(memory_space=pltpu.SMEM)
vmem_spec = pl.BlockSpec(memory_space=pltpu.VMEM)
small_limit = 16 * 1024 * 1024
head_pair = 2
large_limit = 60 * 1024 * 1024


light = pl.CostEstimate(flops=1, bytes_accessed=1, transcendentals=0)


def params(limit):
    return pltpu.CompilerParams(vmem_limit_bytes=limit)


def in_hbm(*arrays):
    return [pltpu.with_memory_space_constraint(array, pltpu.HBM) for array in arrays]


def turn(values, cosine, sine):
    front = values[:, :128].astype(jnp.float32)
    return front * cosine + pltpu.roll(front, 64, 1) * sine


def join(pieces):
    return jnp.concatenate(pieces, axis=1)


def pages_here(table_ref, r, first, count, cap, pages):
    low = lax.axis_index("blk") * pages
    found = jnp.int32(0)
    chosen = [jnp.int32(0)] * cap
    for j in range(first, first + count):
        page = table_ref[r, j] - low
        inside = (page >= 0) & (page < pages)
        chosen = [jnp.where(inside & (found == c), page, chosen[c]) for c in range(cap)]
        found = found + inside.astype(jnp.int32)
    return chosen, found


def pick_old_kernel(table_ref, key_ref, value_ref, out_ref, sem):
    requests, cap = out_ref.shape[:2]
    for r in range(requests):
        chosen, _ = pages_here(table_ref, r, 0, table_ref.shape[1] // 2, cap, key_ref.shape[0])
        for c in range(cap):
            pltpu.make_async_copy(key_ref.at[chosen[c]], out_ref.at[r, c, 0], sem).start()
            pltpu.make_async_copy(value_ref.at[chosen[c]], out_ref.at[r, c, 1], sem).start()
    pltpu.make_async_copy(out_ref, out_ref, sem).wait()


def pick_old(page_table, cap, key_cache, value_cache):
    requests = page_table.shape[0]
    return pl.pallas_call(
        pick_old_kernel,
        out_shape=jax.ShapeDtypeStruct((requests, cap, 2) + key_cache.shape[1:], jnp.bfloat16),
        in_specs=[smem_spec, hbm_spec, hbm_spec],
        out_specs=vmem_spec,
        scratch_shapes=[pltpu.SemaphoreType.DMA],
        cost_estimate=light,
        compiler_params=params(small_limit),
        name="pick_old",
    )(*in_hbm(page_table, key_cache, value_cache))


def owner_of(page, pages, owners):
    factor = (1 << 20) // pages + 1
    assert all((p * factor) >> 20 == p // pages for p in range(pages * owners))
    assert pages * owners * factor < 1 << 31
    return (page * factor) >> 20


def find_slots(table_ref, first, count, cap, pages, counts_ref):
    owners = counts_ref.shape[0]
    row = lax.axis_index("blk")
    for o in range(owners):
        counts_ref[o] = 0
    slots = []
    for j in range(count):
        owner = owner_of(table_ref[row, first + j], pages, owners)
        rank = counts_ref[owner]
        counts_ref[owner] = rank + 1
        slots.append(owner * cap + rank)
    return slots


def rotate_kernel(lengths_ref, freq_ref, keys_ref, values_ref, out_ref, cos_ref, sin_ref):
    rows = keys_ref.shape[0]
    slots = rows // 32
    start = lengths_ref[lax.axis_index("blk")] + lax.axis_index("group") * rows
    positions = start + lax.broadcasted_iota(jnp.int32, (rows, 128), 0)
    angles = positions.astype(jnp.float32) * freq_ref[...]
    lane = lax.broadcasted_iota(jnp.int32, (rows, 128), 1)
    cosine = jnp.cos(angles)
    sine = jnp.sin(angles)
    sine = jnp.where(lane < 64, -sine, sine)
    cos_ref[...] = cosine
    sin_ref[...] = sine
    keys = keys_ref[...]
    turned = join([turn(keys, cosine, sine).astype(jnp.bfloat16), keys[:, 128:]])
    out_ref[:, 0] = turned.reshape(slots, 32, 256)
    out_ref[:, 1] = values_ref[...].reshape(slots, 32, 256)


def rotate_keys(lengths, keys, values):
    rows, head_dim = keys.shape
    quarter = head_dim // 4
    freq_table = np.float32(10000.0) ** (-np.arange(quarter, dtype=np.float32) / np.float32(quarter))
    freq_table = np.concatenate([freq_table, freq_table])[None].astype(np.float32)
    return pl.pallas_call(
        rotate_kernel,
        out_shape=(
            pltpu.HBM((rows // 32, 2, 32, head_dim), jnp.bfloat16),
            pltpu.HBM((rows, 128), jnp.float32),
            pltpu.HBM((rows, 128), jnp.float32),
        ),
        in_specs=[smem_spec, vmem_spec, vmem_spec, vmem_spec],
        out_specs=(vmem_spec,) * 3,
        cost_estimate=light,
        compiler_params=params(small_limit),
        name="rotate_keys",
    )(lengths, jnp.asarray(freq_table), keys, values)


def sort_kernel(pages, cap, table_ref, old_ref, out_ref, counts_ref, sem):
    count = out_ref.shape[0]
    for j, slot in enumerate(find_slots(table_ref, 0, count, cap, pages, counts_ref)):
        pltpu.make_async_copy(old_ref.at[slot], out_ref.at[j], sem).start()
    pltpu.make_async_copy(out_ref, out_ref, sem).wait()


def sort_old(page_table, blk_count, cap, pages, old):
    window = page_table.shape[1] // 2
    return pl.pallas_call(
        lambda *refs: sort_kernel(pages, cap, *refs),
        out_shape=jax.ShapeDtypeStruct((window,) + old.shape[1:], jnp.bfloat16),
        in_specs=[smem_spec, hbm_spec],
        out_specs=vmem_spec,
        scratch_shapes=[pltpu.SMEM((blk_count,), jnp.int32), pltpu.SemaphoreType.DMA],
        cost_estimate=light,
        compiler_params=params(small_limit),
        name="sort_old",
    )(page_table, *in_hbm(old))


def pick_new_kernel(
    pages, cap, table_ref, own_ref, core_ref, far_ref, far_core_ref, out_ref, targets_ref,
    slots_ref, counts_ref, sem,
):
    count = slots_ref.shape[0]
    block_pages = count // 4
    group_index = lax.axis_index("group")
    for j, slot in enumerate(find_slots(table_ref, table_ref.shape[1] - count, count, cap, pages, counts_ref)):
        slots_ref[j] = slot
    for number, ref in enumerate((own_ref, core_ref, far_ref, far_core_ref)):
        block = group_index ^ number
        for place in range(block_pages):
            source = ref.at[4 * place + group_index]
            target = out_ref.at[slots_ref[block * block_pages + place]]
            pltpu.make_async_copy(source, target, sem).start()
    for r in range(table_ref.shape[0]):
        chosen, found = pages_here(table_ref, r, table_ref.shape[1] - count, count, cap, pages)
        for c in range(cap):
            targets_ref[r * cap + c] = jnp.where(found > c, chosen[c], -1)
    sent = out_ref.at[pl.ds(0, count)]
    pltpu.make_async_copy(sent, sent, sem).wait()


def pick_new(page_table, blk_count, cap, pages, sources):
    window = page_table.shape[1] // 2
    return pl.pallas_call(
        lambda *refs: pick_new_kernel(pages, cap, *refs),
        out_shape=(
            jax.ShapeDtypeStruct((blk_count * cap,) + sources[0].shape[1:], jnp.bfloat16),
            jax.ShapeDtypeStruct((blk_count * cap,), jnp.int32),
        ),
        in_specs=[smem_spec] + [any_spec] * 4,
        out_specs=(vmem_spec, smem_spec),
        scratch_shapes=[
            pltpu.SMEM((window,), jnp.int32),
            pltpu.SMEM((blk_count,), jnp.int32),
            pltpu.SemaphoreType.DMA,
        ],
        cost_estimate=light,
        compiler_params=params(small_limit),
        name="pick_new",
    )(page_table, *sources)


def lane_fold(values, combine):
    total = values[:, :128]
    for start in range(128, values.shape[1], 128):
        total = combine(total, values[:, start : start + 128])
    return total


def old_bias(rows, quarter):
    row = lax.broadcasted_iota(jnp.int32, (rows, 256), 0)
    column = lax.broadcasted_iota(jnp.int32, (rows, 256), 1)
    held = quarter ^ (column // 128)
    position = ((column % 128) // 32) * 128 + 32 * held + column % 32
    return jnp.where(position > row, 0.0, masked_score)


def fetch(source, first, kv_ref, place, count, sem):
    pltpu.make_async_copy(source.at[pl.ds(first, count)], kv_ref.at[pl.ds(place, count)], sem).start()


def fetch_pair(sources, first, kv_ref, place, sem):
    fetch(sources[0], first, kv_ref, place, 4, sem)
    fetch(sources[1], first, kv_ref, place + 4, 4, sem)


def wait_rows(kv_ref, blocks, most, sem):
    for n in range(1, most + 1):

        @pl.when(blocks == n)
        def _(n=n):
            filled = kv_ref.at[pl.ds(0, n * block_slots)]
            pltpu.make_async_copy(filled, filled, sem).wait()


def attention(steps, most_steps, step_keys, roped_ref, kv_ref, bias_ref, s_refs, most_refs, top_ref, sum_ref, sum_of_values, begin, finish):
    items, rows, _ = roped_ref.shape
    step_slots = step_keys // 32
    biased = bias_ref.shape[2]

    def block(kind, c):
        return kv_ref[c * step_slots : (c + 1) * step_slots, kind].reshape(step_keys, 256)

    def scores(t, c, which):
        result = lax.dot_general(
            roped_ref[t], block(0, c), (((1,), (1,)), ((), ())), preferred_element_type=jnp.float32
        )
        if c == 0:
            head = result[:, :biased].reshape(head_pair, rows // head_pair, biased) + bias_ref[0]
            head = head.reshape(rows, biased)
            result = join([head, result[:, biased:]]) if step_keys > biased else head
        s_refs[which][c] = result
        most_refs[which][...] = jnp.maximum(most_refs[which][...], lane_fold(result, jnp.maximum))

    def weigh(c, which):
        weights = jnp.exp(s_refs[which][c] - join([top_ref[...]] * (step_keys // 128)))
        sum_ref[...] += lane_fold(weights, jnp.add)
        sum_of_values[...] += jnp.dot(
            weights.astype(jnp.bfloat16), block(1, c), preferred_element_type=jnp.float32
        )

    def settle(which):
        top_ref[...] = jnp.broadcast_to(
            jnp.max(most_refs[which][...], axis=1, keepdims=True), top_ref.shape
        )
        sum_ref[...] = jnp.zeros_like(sum_ref)
        sum_of_values[...] = jnp.zeros_like(sum_of_values)

    def loop(work):
        for c in range(most_steps):

            @pl.when(steps > c)
            def _(c=c):
                work(c)

    def both(t, which):
        def work(c):
            weigh(c, which)
            scores(t + 1, c, 1 - which)

        loop(work)

    drive(
        items, most_refs, begin, settle, finish,
        lambda: loop(lambda c: scores(0, c, 0)),
        both,
        lambda which: loop(lambda c: weigh(c, which)),
    )


def attention_at_once(roped_ref, kv_ref, bias_ref, s_refs, most_refs, top_ref, sum_ref, sum_of_values, begin, finish):
    items, rows, _ = roped_ref.shape
    blocks, _, width = s_refs[0].shape
    biased = bias_ref.shape[2]
    slots = width // 32

    def scores(t, which):
        most = most_refs[which][...]
        query = roped_ref[t]
        for c in range(blocks):
            keys = kv_ref[c * slots : (c + 1) * slots, 0].reshape(width, 256)
            result = lax.dot_general(
                query, keys, (((1,), (1,)), ((), ())), preferred_element_type=jnp.float32
            )
            if c == 0:
                head = result[:, :biased].reshape(head_pair, rows // head_pair, biased) + bias_ref[0]
                head = head.reshape(rows, biased)
                result = join([head, result[:, biased:]]) if width > biased else head
            s_refs[which][c] = result
            most = jnp.maximum(most, lane_fold(result, jnp.maximum))
        most_refs[which][...] = most

    def weigh(which):
        top = join([top_ref[...]] * (width // 128))
        sums = None
        total = None
        for c in range(blocks):
            weights = jnp.exp(s_refs[which][c] - top)
            folded = lane_fold(weights, jnp.add)
            sums = folded if sums is None else sums + folded
            values = kv_ref[c * slots : (c + 1) * slots, 1].reshape(width, 256)
            part = jnp.dot(weights.astype(jnp.bfloat16), values, preferred_element_type=jnp.float32)
            total = part if total is None else total + part
        sum_ref[...] = sums
        sum_of_values[...] = total

    def settle(which):
        top_ref[...] = jnp.broadcast_to(
            jnp.max(most_refs[which][...], axis=1, keepdims=True), top_ref.shape
        )

    def both(t, which):
        weigh(which)
        scores(t + 1, 1 - which)

    drive(items, most_refs, begin, settle, finish, lambda: scores(0, 0), both, weigh)


def drive(items, most_refs, begin, settle, finish, only_scores, both, only_weigh):
    def one(t, which):
        begin(t + 1, most_refs[1 - which])
        settle(which)
        both(t, which)
        finish(t)

    def two(i, carry):
        one(2 * i, 0)
        one(2 * i + 1, 1)
        return carry

    begin(0, most_refs[0])
    only_scores()
    pairs = (items - 1) // 2
    lax.fori_loop(0, pairs, two, 0)
    last = 2 * pairs
    if last < items - 1:
        one(last, 0)
        last += 1
    settle(last % 2)
    only_weigh(last % 2)
    finish(last)


def working(rows, steps, step_keys, tables):
    return [
        pltpu.VMEM((steps * step_keys // 32, 2, 32, 256), jnp.bfloat16),
        pltpu.VMEM((steps, head_pair * rows, step_keys), jnp.float32),
        pltpu.VMEM((steps, head_pair * rows, step_keys), jnp.float32),
        pltpu.VMEM((head_pair * rows, 128), jnp.float32),
        pltpu.VMEM((head_pair * rows, 128), jnp.float32),
        pltpu.VMEM((head_pair * rows, 128), jnp.float32),
        pltpu.VMEM((head_pair * rows, 128), jnp.float32),
        pltpu.VMEM((head_pair * rows, 256), jnp.float32),
        pltpu.VMEM((tables, rows, block_keys), jnp.float32),
    ]


def state_shapes(items, rows):
    return [
        pltpu.VMEM((items, head_pair * rows, 256), jnp.bfloat16),
        pltpu.VMEM((items, head_pair * rows, 256), jnp.float32),
        pltpu.VMEM((items, head_pair * rows, 128), jnp.float32),
    ]


def state_out(items, rows):
    return (
        pltpu.HBM((items, head_pair * rows, 256), jnp.float32),
        pltpu.HBM((items, head_pair * rows, 128), jnp.float32),
    )


def diagonal_kernel(
    query_ref, cos_in, sin_in, own_ref, key_ref, value_ref, roped_out, acc_out, stat_out,
    key_out_ref, value_out_ref, cos_ref, sin_ref, key_pool, value_pool, q_ref, roped_ref, acc_ref, stat_ref, kv_ref, s_0, s_1, most_0, most_1, top_ref, sum_ref, values_ref,
    bias_ref, query_sem, sem, out_sem, pool_sems, angle_sems,
):
    rows = q_ref.shape[0]
    items = roped_ref.shape[0]
    loads = [
        pltpu.make_async_copy(key_ref, key_pool, pool_sems.at[0]),
        pltpu.make_async_copy(value_ref, value_pool, pool_sems.at[1]),
    ]
    stores = [
        pltpu.make_async_copy(key_pool, key_out_ref, pool_sems.at[0]),
        pltpu.make_async_copy(value_pool, value_out_ref, pool_sems.at[1]),
    ]
    query_copy = pltpu.make_async_copy(query_ref, q_ref, query_sem)
    query_copy.start()
    angle_copies = [
        pltpu.make_async_copy(cos_in, cos_ref, angle_sems.at[0]),
        pltpu.make_async_copy(sin_in, sin_ref, angle_sems.at[1]),
    ]
    for copy in angle_copies:
        copy.start()
    fetch(own_ref, 0, kv_ref, 0, block_slots, sem)
    for copy in loads:
        copy.start()
    row = lax.broadcasted_iota(jnp.int32, (rows, block_keys), 0)
    column = lax.broadcasted_iota(jnp.int32, (rows, block_keys), 1)
    bias_ref[0] = jnp.where(column <= row, 0.0, masked_score)
    query_copy.wait()
    for copy in angle_copies:
        copy.wait()

    def rope(t, carry):
        for one in range(head_pair):
            raw = q_ref[:, pl.ds(pl.multiple_of((t * head_pair + one) * 256, 256), 256)]
            front = turn(raw, cos_ref[...], sin_ref[...])
            some = pl.ds(one * rows, rows)
            roped_ref[t, some, :128] = (front * 0.0625).astype(jnp.bfloat16)
            roped_ref[t, some, 128:] = raw[:, 128:] * jnp.bfloat16(0.0625)
        return carry

    lax.fori_loop(0, items, rope, 0)
    roped_copy = pltpu.make_async_copy(roped_ref, roped_out, query_sem)
    roped_copy.start()
    pltpu.make_async_copy(kv_ref, kv_ref, sem).wait()
    for load, store in zip(loads, stores):
        load.wait()
        store.start()

    def begin(t, most_ref):
        most_ref[...] = jnp.full_like(most_ref, masked_score)

    def finish(t):
        lane = lax.broadcasted_iota(jnp.int32, stat_ref.shape[1:], 1)
        sums = jnp.sum(sum_ref[...], axis=1, keepdims=True)
        stat_ref[t] = jnp.where(lane < 64, top_ref[...], sums)
        acc_ref[t] = values_ref[...]
        pltpu.make_async_copy(acc_ref.at[t], acc_out.at[t], out_sem).start()
        pltpu.make_async_copy(stat_ref.at[t], stat_out.at[t], out_sem).start()

    attention_at_once(
        roped_ref, kv_ref, bias_ref, (s_0, s_1), (most_0, most_1), top_ref, sum_ref, values_ref,
        begin, finish,
    )
    roped_copy.wait()
    for copy in stores:
        copy.wait()
    pltpu.make_async_copy(acc_ref, acc_out, out_sem).wait()
    pltpu.make_async_copy(stat_ref, stat_out, out_sem).wait()


def diagonal_part(queries, cosine, sine, own, key_cache, value_cache):
    rows, width = queries.shape
    items = width // (256 * head_pair)
    return pl.pallas_call(
        diagonal_kernel,
        out_shape=(pltpu.HBM((items, head_pair * rows, 256), jnp.bfloat16),)
        + state_out(items, rows)
        + (pltpu.HBM(key_cache.shape, jnp.bfloat16), pltpu.HBM(value_cache.shape, jnp.bfloat16)),
        in_specs=[hbm_spec] * 6,
        out_specs=(hbm_spec,) * 5,
        scratch_shapes=[
            pltpu.VMEM(cosine.shape, jnp.float32),
            pltpu.VMEM(sine.shape, jnp.float32),
            pltpu.VMEM(key_cache.shape, jnp.bfloat16),
            pltpu.VMEM(value_cache.shape, jnp.bfloat16),
            pltpu.VMEM((rows, width), jnp.bfloat16),
        ]
        + state_shapes(items, rows)
        + working(rows, 1, block_keys, 1)
        + [pltpu.SemaphoreType.DMA] * 3
        + [pltpu.SemaphoreType.DMA((2,))] * 2,
        cost_estimate=light,
        compiler_params=params(large_limit),
        name="attend_diagonal",
    )(*in_hbm(queries, cosine, sine, own, key_cache, value_cache))


def rest_kernel(
    lengths_ref, roped_in, acc_in, stat_in, core_ref, far_ref, far_core_ref,
    old_ref, old_core_ref, old_far_ref, old_far_core_ref, weight_ref, hidden_ref,
    roped_ref, acc_ref, stat_ref, kv_ref, s_0, s_1, most_0, most_1, top_ref, sum_ref, values_ref,
    bias_ref, w_ref, stage_ref, roped_sem, state_sems, sem, weight_sem, out_sems,
):
    group_index = lax.axis_index("group")
    has_old = lengths_ref[lax.axis_index("blk")] > 0
    items = roped_ref.shape[0]
    rows = bias_ref.shape[1]
    chunk = stage_ref.shape[2]
    chunks = w_ref.shape[1] // chunk
    odd = group_index % 2
    chip = group_index // 2
    blocks = jnp.where(has_old, 4, odd + 2 * chip)
    steps = jnp.where(has_old, 2, odd + chip)
    base = jnp.where(has_old, 16, 16 * odd)
    near = (old_ref, old_core_ref)
    far = (old_far_ref, old_far_core_ref)

    def copies(t):
        return [
            pltpu.make_async_copy(source.at[t], target.at[t], state_sems.at[number, t])
            for number, (source, target) in enumerate(((stat_in, stat_ref), (acc_in, acc_ref)))
        ]

    roped_copy = pltpu.make_async_copy(roped_in, roped_ref, roped_sem)
    roped_copy.start()
    @pl.when(odd == 1)
    def _():
        fetch(core_ref, 0, kv_ref, base, 16, sem)

    @pl.when(chip == 1)
    def _():
        place = jnp.where(has_old, 32, 32 * odd)
        fetch(far_ref, 0, kv_ref, place, 16, sem)
        fetch(far_core_ref, 0, kv_ref, place + 16, 16, sem)

    @pl.when(has_old)
    def _():
        for block in range(4):

            @pl.when(block >= group_index)
            def _(block=block):
                gap = jnp.where(block == group_index, 0, odd)
                place = 16 * (gap + block - group_index)
                fetch_pair(near, 4 * block, kv_ref, place, sem)
                fetch_pair(far, 4 * block, kv_ref, place + 8, sem)

    for t in range(items):
        for copy in copies(t):
            copy.start()
    weight_copy = pltpu.make_async_copy(weight_ref, w_ref, weight_sem)
    weight_copy.start()

    @pl.when(jnp.logical_not(has_old))
    def _():
        bias_ref[0] = jnp.where(odd == 1, masked_score, 0.0) + jnp.zeros(bias_ref.shape[1:], jnp.float32)
        empty = pl.ds(0, block_slots)

        @pl.when(odd == 1)
        def _():
            kv_ref[empty] = jnp.zeros((block_slots, 2, 32, 256), jnp.bfloat16)

    @pl.when(has_old)
    def _():
        bias_ref[0, :, :256] = old_bias(rows, group_index)
        bias_ref[0, :, 256:] = old_bias(rows, group_index ^ 2)

    roped_copy.wait()
    wait_rows(kv_ref, blocks, 4, sem)
    lane = lax.broadcasted_iota(jnp.int32, stat_ref.shape[1:], 1)

    def begin(t, most_ref):
        for copy in copies(t):
            copy.wait()
        most_ref[...] = jnp.where(lane < 64, stat_ref[t], masked_score)

    def finish(t):
        stat = stat_ref[t]
        factor = jnp.exp(stat[:, :1] - top_ref[...])
        sums = stat[:, 64:65] * factor + jnp.sum(sum_ref[...], axis=1, keepdims=True)
        inverse = 1.0 / sums
        old = factor * inverse
        mixed = acc_ref[t] * join([old, old]) + values_ref[...] * join([inverse, inverse])
        roped_ref[t] = mixed.astype(jnp.bfloat16)

    scratch = (roped_ref, kv_ref, bias_ref, (s_0, s_1), (most_0, most_1), top_ref, sum_ref, values_ref)

    attention(steps, 2, 2 * block_keys, *scratch, begin, finish)
    weight_copy.wait()

    def out_copy(n, columns):
        return pltpu.make_async_copy(stage_ref.at[n % 2], hidden_ref.at[:, columns], out_sems.at[n % 2])

    def project(n, carry):
        columns = pl.ds(pl.multiple_of(n * chunk, chunk), chunk)

        @pl.when(n >= 2)
        def _():
            out_copy(n, columns).wait()

        attended = join(
            [
                roped_ref[t, one * rows : (one + 1) * rows, :]
                for t in range(items)
                for one in range(head_pair)
            ]
        )
        stage_ref[n % 2] = jnp.dot(
            attended, w_ref[:, columns], preferred_element_type=jnp.float32
        ).astype(jnp.bfloat16)
        out_copy(n, columns).start()
        return carry

    lax.fori_loop(0, chunks, project, 0)
    for n in range(2):
        out_copy(n, pl.ds(0, chunk)).wait()


def rest_part(lengths, state, slots, weight):
    items, pair_rows, _ = state[0].shape
    rows = pair_rows // head_pair
    width = weight.shape[1]
    chunk = 512
    return pl.pallas_call(
        rest_kernel,
        out_shape=pltpu.HBM((rows, width), jnp.bfloat16),
        in_specs=[smem_spec] + [hbm_spec] * 3 + [any_spec] * 7 + [hbm_spec],
        out_specs=hbm_spec,
        scratch_shapes=state_shapes(items, rows)
        + working(rows, 2, 2 * block_keys, 1)
        + [
            pltpu.VMEM(weight.shape, jnp.bfloat16),
            pltpu.VMEM((2, rows, chunk), jnp.bfloat16),
            pltpu.SemaphoreType.DMA,
            pltpu.SemaphoreType.DMA((2, items)),
            pltpu.SemaphoreType.DMA,
            pltpu.SemaphoreType.DMA,
            pltpu.SemaphoreType.DMA((2,)),
        ],
        cost_estimate=light,
        compiler_params=params(large_limit),
        name="attend_rest",
    )(lengths, *in_hbm(*state), *slots, *in_hbm(weight))


def place_kernel(targets_ref, arrived_ref, key_in, value_in, key_ref, value_ref, buffer_ref, load_sem, sem):
    load = pltpu.make_async_copy(arrived_ref, buffer_ref, load_sem)
    load.start()
    load.wait()

    def each(act):
        for slot in range(targets_ref.shape[0]):
            page = targets_ref[slot]

            @pl.when(page >= 0)
            def _(slot=slot, page=page):
                for kind, out_ref in enumerate((key_ref, value_ref)):
                    act(pltpu.make_async_copy(buffer_ref.at[slot, kind], out_ref.at[page], sem))

    each(lambda copy: copy.start())
    each(lambda copy: copy.wait())


def place_new(targets, arrived, key_pool, value_pool):
    return pl.pallas_call(
        place_kernel,
        out_shape=(
            pltpu.HBM(key_pool.shape, jnp.bfloat16),
            pltpu.HBM(value_pool.shape, jnp.bfloat16),
        ),
        in_specs=[smem_spec, any_spec, hbm_spec, hbm_spec],
        out_specs=(hbm_spec,) * 2,
        input_output_aliases={2: 0, 3: 1},
        scratch_shapes=[
            pltpu.VMEM(arrived.shape, jnp.bfloat16),
            pltpu.SemaphoreType.DMA,
            pltpu.SemaphoreType.DMA,
        ],
        cost_estimate=light,
        compiler_params=params(small_limit),
        name="place_new",
    )(targets, arrived, *in_hbm(key_pool, value_pool))


def after(value, *others):
    return lax.optimization_barrier((value,) + others)[0]


def body(queries, new_keys, new_values, key_cache, value_cache, out_weight, lengths, page_table):
    blk_count = lax.axis_size("blk")
    pages = key_cache.shape[0]
    window_pages = page_table.shape[1] // 2
    cap = (window_pages + blk_count - 1) // blk_count

    def other_core(value):
        return lax.ppermute(value, "group", [(0, 1), (1, 0), (2, 3), (3, 2)])

    def other_chip(value):
        return lax.ppermute(value, "group", [(0, 2), (2, 0), (1, 3), (3, 1)])

    picked = pick_old(page_table, cap, key_cache, value_cache)
    old = lax.all_to_all(picked, "blk", split_axis=0, concat_axis=0, tiled=True)
    old = old.reshape((blk_count * cap,) + old.shape[2:])

    fresh, cosine, sine = rotate_keys(lengths, new_keys[0], new_values[0])
    fresh_far = other_chip(fresh)
    fresh_core = other_core(fresh)
    roped, acc, stat, key_out, value_out = diagonal_part(
        after(queries[0], picked), cosine, sine, fresh, key_cache, value_cache
    )

    old = sort_old(after(page_table, stat), blk_count, cap, pages, old)
    old_far = other_chip(old)
    old_core = other_core(old)
    fresh_far_core = other_core(after(fresh_far, old))
    new, targets = pick_new(
        page_table, blk_count, cap, pages, (fresh, fresh_core, fresh_far, fresh_far_core)
    )
    arrived = lax.all_to_all(new, "blk", split_axis=0, concat_axis=0, tiled=True)
    old_far_core = other_core(after(old_far, new))
    hidden = rest_part(
        lengths, (roped, acc, stat),
        (fresh_core, fresh_far, fresh_far_core, old, old_core, old_far, old_far_core),
        out_weight,
    )
    key_out, value_out = place_new(targets, arrived, key_out, value_out)
    return (hidden[None], key_out, value_out)


def solution(mesh):
    return jax.shard_map(
        body,
        mesh=mesh,
        in_specs=(
            P("blk", "group", None),
            P("blk", "group", None),
            P("blk", "group", None),
            P("blk", "group", None),
            P("blk", "group", None),
            P(),
            P(),
            P(),
        ),
        out_specs=(P("blk", "group", None), P("blk", "group", None), P("blk", "group", None)),
        check_vma=False,
    )
```

```python
import jax
import jax.numpy as jnp
import numpy as np
from jax import lax
from jax.experimental import pallas as pl
from jax.experimental.pallas import tpu as pltpu
from jax.sharding import PartitionSpec as P

masked_score = -1e30
block_keys = 512
block_slots = 16
any_spec = pl.BlockSpec(memory_space=pl.ANY)
hbm_spec = pl.BlockSpec(memory_space=pltpu.HBM)
smem_spec = pl.BlockSpec(memory_space=pltpu.SMEM)
vmem_spec = pl.BlockSpec(memory_space=pltpu.VMEM)
small_limit = 16 * 1024 * 1024
head_pair = 2
large_limit = 60 * 1024 * 1024


light = pl.CostEstimate(flops=1, bytes_accessed=1, transcendentals=0)


def params(limit):
    return pltpu.CompilerParams(vmem_limit_bytes=limit)


def in_hbm(*arrays):
    return [pltpu.with_memory_space_constraint(array, pltpu.HBM) for array in arrays]


def turn(values, cosine, sine):
    front = values[:, :128].astype(jnp.float32)
    return front * cosine + pltpu.roll(front, 64, 1) * sine


def join(pieces):
    return jnp.concatenate(pieces, axis=1)


def pages_here(table_ref, r, first, count, cap, pages):
    low = lax.axis_index("blk") * pages
    found = jnp.int32(0)
    chosen = [jnp.int32(0)] * cap
    for j in range(first, first + count):
        page = table_ref[r, j] - low
        inside = (page >= 0) & (page < pages)
        chosen = [jnp.where(inside & (found == c), page, chosen[c]) for c in range(cap)]
        found = found + inside.astype(jnp.int32)
    return chosen, found


def pick_old_kernel(table_ref, key_ref, value_ref, out_ref, sem):
    requests, cap = out_ref.shape[:2]
    for r in range(requests):
        chosen, _ = pages_here(table_ref, r, 0, table_ref.shape[1] // 2, cap, key_ref.shape[0])
        for c in range(cap):
            pltpu.make_async_copy(key_ref.at[chosen[c]], out_ref.at[r, c, 0], sem).start()
            pltpu.make_async_copy(value_ref.at[chosen[c]], out_ref.at[r, c, 1], sem).start()
    pltpu.make_async_copy(out_ref, out_ref, sem).wait()


def pick_old(page_table, cap, key_cache, value_cache):
    requests = page_table.shape[0]
    return pl.pallas_call(
        pick_old_kernel,
        out_shape=jax.ShapeDtypeStruct((requests, cap, 2) + key_cache.shape[1:], jnp.bfloat16),
        in_specs=[smem_spec, hbm_spec, hbm_spec],
        out_specs=vmem_spec,
        scratch_shapes=[pltpu.SemaphoreType.DMA],
        cost_estimate=light,
        compiler_params=params(small_limit),
        name="pick_old",
    )(*in_hbm(page_table, key_cache, value_cache))


def owner_of(page, pages, owners):
    factor = (1 << 20) // pages + 1
    assert all((p * factor) >> 20 == p // pages for p in range(pages * owners))
    assert pages * owners * factor < 1 << 31
    return (page * factor) >> 20


def find_slots(table_ref, first, count, cap, pages, counts_ref):
    owners = counts_ref.shape[0]
    row = lax.axis_index("blk")
    for o in range(owners):
        counts_ref[o] = 0
    slots = []
    for j in range(count):
        owner = owner_of(table_ref[row, first + j], pages, owners)
        rank = counts_ref[owner]
        counts_ref[owner] = rank + 1
        slots.append(owner * cap + rank)
    return slots


def rotate_kernel(lengths_ref, freq_ref, keys_ref, values_ref, out_ref, cos_ref, sin_ref):
    rows = keys_ref.shape[0]
    slots = rows // 32
    start = lengths_ref[lax.axis_index("blk")] + lax.axis_index("group") * rows
    positions = start + lax.broadcasted_iota(jnp.int32, (rows, 128), 0)
    angles = positions.astype(jnp.float32) * freq_ref[...]
    lane = lax.broadcasted_iota(jnp.int32, (rows, 128), 1)
    cosine = jnp.cos(angles)
    sine = jnp.sin(angles)
    sine = jnp.where(lane < 64, -sine, sine)
    cos_ref[...] = cosine
    sin_ref[...] = sine
    keys = keys_ref[...]
    turned = join([turn(keys, cosine, sine).astype(jnp.bfloat16), keys[:, 128:]])
    out_ref[:, 0] = turned.reshape(slots, 32, 256)
    out_ref[:, 1] = values_ref[...].reshape(slots, 32, 256)


def rotate_keys(lengths, keys, values):
    rows, head_dim = keys.shape
    quarter = head_dim // 4
    freq_table = np.float32(10000.0) ** (-np.arange(quarter, dtype=np.float32) / np.float32(quarter))
    freq_table = np.concatenate([freq_table, freq_table])[None].astype(np.float32)
    return pl.pallas_call(
        rotate_kernel,
        out_shape=(
            pltpu.HBM((rows // 32, 2, 32, head_dim), jnp.bfloat16),
            pltpu.HBM((rows, 128), jnp.float32),
            pltpu.HBM((rows, 128), jnp.float32),
        ),
        in_specs=[smem_spec, vmem_spec, vmem_spec, vmem_spec],
        out_specs=(vmem_spec,) * 3,
        cost_estimate=light,
        compiler_params=params(small_limit),
        name="rotate_keys",
    )(lengths, jnp.asarray(freq_table), keys, values)


def sort_kernel(pages, cap, table_ref, old_ref, out_ref, counts_ref, sem):
    count = out_ref.shape[0]
    for j, slot in enumerate(find_slots(table_ref, 0, count, cap, pages, counts_ref)):
        pltpu.make_async_copy(old_ref.at[slot], out_ref.at[j], sem).start()
    pltpu.make_async_copy(out_ref, out_ref, sem).wait()


def sort_old(page_table, blk_count, cap, pages, old):
    window = page_table.shape[1] // 2
    return pl.pallas_call(
        lambda *refs: sort_kernel(pages, cap, *refs),
        out_shape=jax.ShapeDtypeStruct((window,) + old.shape[1:], jnp.bfloat16),
        in_specs=[smem_spec, hbm_spec],
        out_specs=vmem_spec,
        scratch_shapes=[pltpu.SMEM((blk_count,), jnp.int32), pltpu.SemaphoreType.DMA],
        cost_estimate=light,
        compiler_params=params(small_limit),
        name="sort_old",
    )(page_table, *in_hbm(old))


def pick_new_kernel(
    pages, cap, table_ref, own_ref, core_ref, far_ref, far_core_ref, out_ref, targets_ref,
    slots_ref, counts_ref, sem,
):
    count = slots_ref.shape[0]
    block_pages = count // 4
    group_index = lax.axis_index("group")
    for j, slot in enumerate(find_slots(table_ref, table_ref.shape[1] - count, count, cap, pages, counts_ref)):
        slots_ref[j] = slot
    for number, ref in enumerate((own_ref, core_ref, far_ref, far_core_ref)):
        block = group_index ^ number
        for place in range(block_pages):
            source = ref.at[4 * place + group_index]
            target = out_ref.at[slots_ref[block * block_pages + place]]
            pltpu.make_async_copy(source, target, sem).start()
    for r in range(table_ref.shape[0]):
        chosen, found = pages_here(table_ref, r, table_ref.shape[1] - count, count, cap, pages)
        for c in range(cap):
            targets_ref[r * cap + c] = jnp.where(found > c, chosen[c], -1)
    sent = out_ref.at[pl.ds(0, count)]
    pltpu.make_async_copy(sent, sent, sem).wait()


def pick_new(page_table, blk_count, cap, pages, sources):
    window = page_table.shape[1] // 2
    return pl.pallas_call(
        lambda *refs: pick_new_kernel(pages, cap, *refs),
        out_shape=(
            jax.ShapeDtypeStruct((blk_count * cap,) + sources[0].shape[1:], jnp.bfloat16),
            jax.ShapeDtypeStruct((blk_count * cap,), jnp.int32),
        ),
        in_specs=[smem_spec] + [any_spec] * 4,
        out_specs=(vmem_spec, smem_spec),
        scratch_shapes=[
            pltpu.SMEM((window,), jnp.int32),
            pltpu.SMEM((blk_count,), jnp.int32),
            pltpu.SemaphoreType.DMA,
        ],
        cost_estimate=light,
        compiler_params=params(small_limit),
        name="pick_new",
    )(page_table, *sources)


def lane_fold(values, combine):
    total = values[:, :128]
    for start in range(128, values.shape[1], 128):
        total = combine(total, values[:, start : start + 128])
    return total


def old_bias(rows, quarter):
    row = lax.broadcasted_iota(jnp.int32, (rows, 256), 0)
    column = lax.broadcasted_iota(jnp.int32, (rows, 256), 1)
    held = quarter ^ (column // 128)
    position = ((column % 128) // 32) * 128 + 32 * held + column % 32
    return jnp.where(position > row, 0.0, masked_score)


def fetch(source, first, kv_ref, place, count, sem):
    for kind in range(2):
        pltpu.make_async_copy(
            source.at[pl.ds(first, count), kind], kv_ref.at[kind, pl.ds(place, count)], sem
        ).start()


def fetch_pair(sources, first, kv_ref, place, sem):
    fetch(sources[0], first, kv_ref, place, 4, sem)
    fetch(sources[1], first, kv_ref, place + 4, 4, sem)


def wait_rows(kv_ref, blocks, most, sem):
    for n in range(1, most + 1):

        @pl.when(blocks == n)
        def _(n=n):
            filled = kv_ref.at[:, pl.ds(0, n * block_slots)]
            pltpu.make_async_copy(filled, filled, sem).wait()


def attention(steps, most_steps, step_keys, roped_ref, kv_ref, bias_ref, s_refs, most_refs, top_ref, sum_ref, sum_of_values, begin, finish):
    items, rows, _ = roped_ref.shape
    step_slots = step_keys // 32
    biased = bias_ref.shape[2]

    def block(kind, c):
        return kv_ref[kind, c * step_slots : (c + 1) * step_slots].reshape(step_keys, 256)

    def scores(t, c, which):
        result = lax.dot_general(
            roped_ref[t], block(0, c), (((1,), (1,)), ((), ())), preferred_element_type=jnp.float32
        )
        if c == 0:
            head = result[:, :biased].reshape(head_pair, rows // head_pair, biased) + bias_ref[0]
            head = head.reshape(rows, biased)
            result = join([head, result[:, biased:]]) if step_keys > biased else head
        s_refs[which][c] = result
        most_refs[which][...] = jnp.maximum(most_refs[which][...], lane_fold(result, jnp.maximum))

    def weigh(c, which):
        weights = jnp.exp(s_refs[which][c] - join([top_ref[...]] * (step_keys // 128)))
        sum_ref[...] += lane_fold(weights, jnp.add)
        sum_of_values[...] += jnp.dot(
            weights.astype(jnp.bfloat16), block(1, c), preferred_element_type=jnp.float32
        )

    def settle(which):
        top_ref[...] = jnp.broadcast_to(
            jnp.max(most_refs[which][...], axis=1, keepdims=True), top_ref.shape
        )
        sum_ref[...] = jnp.zeros_like(sum_ref)
        sum_of_values[...] = jnp.zeros_like(sum_of_values)

    def loop(work):
        for c in range(most_steps):

            @pl.when(steps > c)
            def _(c=c):
                work(c)

    def both(t, which):
        def work(c):
            weigh(c, which)
            scores(t + 1, c, 1 - which)

        loop(work)

    drive(
        items, most_refs, begin, settle, finish,
        lambda: loop(lambda c: scores(0, c, 0)),
        both,
        lambda which: loop(lambda c: weigh(c, which)),
    )


def attention_at_once(roped_ref, kv_ref, bias_ref, s_refs, most_refs, top_ref, sum_ref, sum_of_values, begin, finish):
    items, rows, _ = roped_ref.shape
    blocks, _, width = s_refs[0].shape
    biased = bias_ref.shape[2]
    slots = width // 32

    def scores(t, which):
        most = most_refs[which][...]
        query = roped_ref[t]
        for c in range(blocks):
            keys = kv_ref[0, c * slots : (c + 1) * slots].reshape(width, 256)
            result = lax.dot_general(
                query, keys, (((1,), (1,)), ((), ())), preferred_element_type=jnp.float32
            )
            if c == 0:
                head = result[:, :biased].reshape(head_pair, rows // head_pair, biased) + bias_ref[0]
                head = head.reshape(rows, biased)
                result = join([head, result[:, biased:]]) if width > biased else head
            s_refs[which][c] = result
            most = jnp.maximum(most, lane_fold(result, jnp.maximum))
        most_refs[which][...] = most

    def weigh(which):
        top = join([top_ref[...]] * (width // 128))
        sums = None
        total = None
        for c in range(blocks):
            weights = jnp.exp(s_refs[which][c] - top)
            folded = lane_fold(weights, jnp.add)
            sums = folded if sums is None else sums + folded
            values = kv_ref[1, c * slots : (c + 1) * slots].reshape(width, 256)
            part = jnp.dot(weights.astype(jnp.bfloat16), values, preferred_element_type=jnp.float32)
            total = part if total is None else total + part
        sum_ref[...] = sums
        sum_of_values[...] = total

    def settle(which):
        top_ref[...] = jnp.broadcast_to(
            jnp.max(most_refs[which][...], axis=1, keepdims=True), top_ref.shape
        )

    def both(t, which):
        weigh(which)
        scores(t + 1, 1 - which)

    drive(items, most_refs, begin, settle, finish, lambda: scores(0, 0), both, weigh)


def drive(items, most_refs, begin, settle, finish, only_scores, both, only_weigh):
    def one(t, which):
        begin(t + 1, most_refs[1 - which])
        settle(which)
        both(t, which)
        finish(t)

    def two(i, carry):
        one(2 * i, 0)
        one(2 * i + 1, 1)
        return carry

    begin(0, most_refs[0])
    only_scores()
    pairs = (items - 1) // 2
    lax.fori_loop(0, pairs, two, 0)
    last = 2 * pairs
    if last < items - 1:
        one(last, 0)
        last += 1
    settle(last % 2)
    only_weigh(last % 2)
    finish(last)


def working(rows, steps, step_keys, tables):
    return [
        pltpu.VMEM((2, steps * step_keys // 32, 32, 256), jnp.bfloat16),
        pltpu.VMEM((steps, head_pair * rows, step_keys), jnp.float32),
        pltpu.VMEM((steps, head_pair * rows, step_keys), jnp.float32),
        pltpu.VMEM((head_pair * rows, 128), jnp.float32),
        pltpu.VMEM((head_pair * rows, 128), jnp.float32),
        pltpu.VMEM((head_pair * rows, 128), jnp.float32),
        pltpu.VMEM((head_pair * rows, 128), jnp.float32),
        pltpu.VMEM((head_pair * rows, 256), jnp.float32),
        pltpu.VMEM((tables, rows, block_keys), jnp.float32),
    ]


def state_shapes(items, rows):
    return [
        pltpu.VMEM((items, head_pair * rows, 256), jnp.bfloat16),
        pltpu.VMEM((items, head_pair * rows, 256), jnp.float32),
        pltpu.VMEM((items, head_pair * rows, 128), jnp.float32),
    ]


def state_out(items, rows):
    return (
        pltpu.HBM((items, head_pair * rows, 256), jnp.float32),
        pltpu.HBM((items, head_pair * rows, 128), jnp.float32),
    )


def diagonal_kernel(
    query_ref, cos_in, sin_in, own_ref, key_ref, value_ref, roped_out, acc_out, stat_out,
    key_out_ref, value_out_ref, cos_ref, sin_ref, key_pool, value_pool, q_ref, roped_ref, acc_ref, stat_ref, kv_ref, s_0, s_1, most_0, most_1, top_ref, sum_ref, values_ref,
    bias_ref, query_sem, sem, out_sem, pool_sems, angle_sems,
):
    rows = q_ref.shape[0]
    items = roped_ref.shape[0]
    loads = [
        pltpu.make_async_copy(key_ref, key_pool, pool_sems.at[0]),
        pltpu.make_async_copy(value_ref, value_pool, pool_sems.at[1]),
    ]
    stores = [
        pltpu.make_async_copy(key_pool, key_out_ref, pool_sems.at[0]),
        pltpu.make_async_copy(value_pool, value_out_ref, pool_sems.at[1]),
    ]
    query_copy = pltpu.make_async_copy(query_ref, q_ref, query_sem)
    query_copy.start()
    angle_copies = [
        pltpu.make_async_copy(cos_in, cos_ref, angle_sems.at[0]),
        pltpu.make_async_copy(sin_in, sin_ref, angle_sems.at[1]),
    ]
    for copy in angle_copies:
        copy.start()
    fetch(own_ref, 0, kv_ref, 0, block_slots, sem)
    for copy in loads:
        copy.start()
    row = lax.broadcasted_iota(jnp.int32, (rows, block_keys), 0)
    column = lax.broadcasted_iota(jnp.int32, (rows, block_keys), 1)
    bias_ref[0] = jnp.where(column <= row, 0.0, masked_score)
    query_copy.wait()
    for copy in angle_copies:
        copy.wait()

    def rope(t, carry):
        for one in range(head_pair):
            raw = q_ref[:, pl.ds(pl.multiple_of((t * head_pair + one) * 256, 256), 256)]
            front = turn(raw, cos_ref[...], sin_ref[...])
            some = pl.ds(one * rows, rows)
            roped_ref[t, some, :128] = (front * 0.0625).astype(jnp.bfloat16)
            roped_ref[t, some, 128:] = raw[:, 128:] * jnp.bfloat16(0.0625)
        return carry

    lax.fori_loop(0, items, rope, 0)
    roped_copy = pltpu.make_async_copy(roped_ref, roped_out, query_sem)
    roped_copy.start()
    pltpu.make_async_copy(kv_ref, kv_ref, sem).wait()
    for load, store in zip(loads, stores):
        load.wait()
        store.start()

    def begin(t, most_ref):
        most_ref[...] = jnp.full_like(most_ref, masked_score)

    def finish(t):
        lane = lax.broadcasted_iota(jnp.int32, stat_ref.shape[1:], 1)
        sums = jnp.sum(sum_ref[...], axis=1, keepdims=True)
        stat_ref[t] = jnp.where(lane < 64, top_ref[...], sums)
        acc_ref[t] = values_ref[...]
        pltpu.make_async_copy(acc_ref.at[t], acc_out.at[t], out_sem).start()
        pltpu.make_async_copy(stat_ref.at[t], stat_out.at[t], out_sem).start()

    attention_at_once(
        roped_ref, kv_ref, bias_ref, (s_0, s_1), (most_0, most_1), top_ref, sum_ref, values_ref,
        begin, finish,
    )
    roped_copy.wait()
    for copy in stores:
        copy.wait()
    pltpu.make_async_copy(acc_ref, acc_out, out_sem).wait()
    pltpu.make_async_copy(stat_ref, stat_out, out_sem).wait()


def diagonal_part(queries, cosine, sine, own, key_cache, value_cache):
    rows, width = queries.shape
    items = width // (256 * head_pair)
    return pl.pallas_call(
        diagonal_kernel,
        out_shape=(pltpu.HBM((items, head_pair * rows, 256), jnp.bfloat16),)
        + state_out(items, rows)
        + (pltpu.HBM(key_cache.shape, jnp.bfloat16), pltpu.HBM(value_cache.shape, jnp.bfloat16)),
        in_specs=[hbm_spec] * 6,
        out_specs=(hbm_spec,) * 5,
        scratch_shapes=[
            pltpu.VMEM(cosine.shape, jnp.float32),
            pltpu.VMEM(sine.shape, jnp.float32),
            pltpu.VMEM(key_cache.shape, jnp.bfloat16),
            pltpu.VMEM(value_cache.shape, jnp.bfloat16),
            pltpu.VMEM((rows, width), jnp.bfloat16),
        ]
        + state_shapes(items, rows)
        + working(rows, 1, block_keys, 1)
        + [pltpu.SemaphoreType.DMA] * 3
        + [pltpu.SemaphoreType.DMA((2,))] * 2,
        cost_estimate=light,
        compiler_params=params(large_limit),
        name="attend_diagonal",
    )(*in_hbm(queries, cosine, sine, own, key_cache, value_cache))


def rest_kernel(
    lengths_ref, roped_in, acc_in, stat_in, core_ref, far_ref, far_core_ref,
    old_ref, old_core_ref, old_far_ref, old_far_core_ref, weight_ref, hidden_ref,
    roped_ref, acc_ref, stat_ref, kv_ref, s_0, s_1, most_0, most_1, top_ref, sum_ref, values_ref,
    bias_ref, w_ref, stage_ref, roped_sem, state_sems, sem, weight_sem, out_sems,
):
    group_index = lax.axis_index("group")
    has_old = lengths_ref[lax.axis_index("blk")] > 0
    items = roped_ref.shape[0]
    rows = bias_ref.shape[1]
    chunk = stage_ref.shape[2]
    chunks = w_ref.shape[1] // chunk
    odd = group_index % 2
    chip = group_index // 2
    blocks = jnp.where(has_old, 4, odd + 2 * chip)
    steps = jnp.where(has_old, 2, odd + chip)
    base = jnp.where(has_old, 16, 16 * odd)
    near = (old_ref, old_core_ref)
    far = (old_far_ref, old_far_core_ref)

    def copies(t):
        return [
            pltpu.make_async_copy(source.at[t], target.at[t], state_sems.at[number, t])
            for number, (source, target) in enumerate(((stat_in, stat_ref), (acc_in, acc_ref)))
        ]

    roped_copy = pltpu.make_async_copy(roped_in, roped_ref, roped_sem)
    roped_copy.start()
    @pl.when(odd == 1)
    def _():
        fetch(core_ref, 0, kv_ref, base, 16, sem)

    @pl.when(chip == 1)
    def _():
        place = jnp.where(has_old, 32, 32 * odd)
        fetch(far_ref, 0, kv_ref, place, 16, sem)
        fetch(far_core_ref, 0, kv_ref, place + 16, 16, sem)

    @pl.when(has_old)
    def _():
        for block in range(4):

            @pl.when(block >= group_index)
            def _(block=block):
                gap = jnp.where(block == group_index, 0, odd)
                place = 16 * (gap + block - group_index)
                fetch_pair(near, 4 * block, kv_ref, place, sem)
                fetch_pair(far, 4 * block, kv_ref, place + 8, sem)

    for t in range(items):
        for copy in copies(t):
            copy.start()
    weight_copy = pltpu.make_async_copy(weight_ref, w_ref, weight_sem)
    weight_copy.start()

    @pl.when(jnp.logical_not(has_old))
    def _():
        bias_ref[0] = jnp.where(odd == 1, masked_score, 0.0) + jnp.zeros(bias_ref.shape[1:], jnp.float32)
        empty = pl.ds(0, block_slots)

        @pl.when(odd == 1)
        def _():
            kv_ref[:, empty] = jnp.zeros((2, block_slots, 32, 256), jnp.bfloat16)

    @pl.when(has_old)
    def _():
        bias_ref[0, :, :256] = old_bias(rows, group_index)
        bias_ref[0, :, 256:] = old_bias(rows, group_index ^ 2)

    roped_copy.wait()
    wait_rows(kv_ref, blocks, 4, sem)
    lane = lax.broadcasted_iota(jnp.int32, stat_ref.shape[1:], 1)

    def begin(t, most_ref):
        for copy in copies(t):
            copy.wait()
        most_ref[...] = jnp.where(lane < 64, stat_ref[t], masked_score)

    def finish(t):
        stat = stat_ref[t]
        factor = jnp.exp(stat[:, :1] - top_ref[...])
        sums = stat[:, 64:65] * factor + jnp.sum(sum_ref[...], axis=1, keepdims=True)
        inverse = 1.0 / sums
        old = factor * inverse
        mixed = acc_ref[t] * join([old, old]) + values_ref[...] * join([inverse, inverse])
        roped_ref[t] = mixed.astype(jnp.bfloat16)

    scratch = (roped_ref, kv_ref, bias_ref, (s_0, s_1), (most_0, most_1), top_ref, sum_ref, values_ref)

    attention(steps, 2, 2 * block_keys, *scratch, begin, finish)
    weight_copy.wait()

    def out_copy(n, columns):
        return pltpu.make_async_copy(stage_ref.at[n % 2], hidden_ref.at[:, columns], out_sems.at[n % 2])

    def project(n, carry):
        columns = pl.ds(pl.multiple_of(n * chunk, chunk), chunk)

        @pl.when(n >= 2)
        def _():
            out_copy(n, columns).wait()

        attended = join(
            [
                roped_ref[t, one * rows : (one + 1) * rows, :]
                for t in range(items)
                for one in range(head_pair)
            ]
        )
        stage_ref[n % 2] = jnp.dot(
            attended, w_ref[:, columns], preferred_element_type=jnp.float32
        ).astype(jnp.bfloat16)
        out_copy(n, columns).start()
        return carry

    lax.fori_loop(0, chunks, project, 0)
    for n in range(2):
        out_copy(n, pl.ds(0, chunk)).wait()


def rest_part(lengths, state, slots, weight):
    items, pair_rows, _ = state[0].shape
    rows = pair_rows // head_pair
    width = weight.shape[1]
    chunk = 512
    return pl.pallas_call(
        rest_kernel,
        out_shape=pltpu.HBM((rows, width), jnp.bfloat16),
        in_specs=[smem_spec] + [hbm_spec] * 3 + [any_spec] * 7 + [hbm_spec],
        out_specs=hbm_spec,
        scratch_shapes=state_shapes(items, rows)
        + working(rows, 2, 2 * block_keys, 1)
        + [
            pltpu.VMEM(weight.shape, jnp.bfloat16),
            pltpu.VMEM((2, rows, chunk), jnp.bfloat16),
            pltpu.SemaphoreType.DMA,
            pltpu.SemaphoreType.DMA((2, items)),
            pltpu.SemaphoreType.DMA,
            pltpu.SemaphoreType.DMA,
            pltpu.SemaphoreType.DMA((2,)),
        ],
        cost_estimate=light,
        compiler_params=params(large_limit),
        name="attend_rest",
    )(lengths, *in_hbm(*state), *slots, *in_hbm(weight))


def place_kernel(targets_ref, arrived_ref, key_in, value_in, key_ref, value_ref, buffer_ref, load_sem, sem):
    load = pltpu.make_async_copy(arrived_ref, buffer_ref, load_sem)
    load.start()
    load.wait()

    def each(act):
        for slot in range(targets_ref.shape[0]):
            page = targets_ref[slot]

            @pl.when(page >= 0)
            def _(slot=slot, page=page):
                for kind, out_ref in enumerate((key_ref, value_ref)):
                    act(pltpu.make_async_copy(buffer_ref.at[slot, kind], out_ref.at[page], sem))

    each(lambda copy: copy.start())
    each(lambda copy: copy.wait())


def place_new(targets, arrived, key_pool, value_pool):
    return pl.pallas_call(
        place_kernel,
        out_shape=(
            pltpu.HBM(key_pool.shape, jnp.bfloat16),
            pltpu.HBM(value_pool.shape, jnp.bfloat16),
        ),
        in_specs=[smem_spec, any_spec, hbm_spec, hbm_spec],
        out_specs=(hbm_spec,) * 2,
        input_output_aliases={2: 0, 3: 1},
        scratch_shapes=[
            pltpu.VMEM(arrived.shape, jnp.bfloat16),
            pltpu.SemaphoreType.DMA,
            pltpu.SemaphoreType.DMA,
        ],
        cost_estimate=light,
        compiler_params=params(small_limit),
        name="place_new",
    )(targets, arrived, *in_hbm(key_pool, value_pool))


def after(value, *others):
    return lax.optimization_barrier((value,) + others)[0]


def body(queries, new_keys, new_values, key_cache, value_cache, out_weight, lengths, page_table):
    blk_count = lax.axis_size("blk")
    pages = key_cache.shape[0]
    window_pages = page_table.shape[1] // 2
    cap = (window_pages + blk_count - 1) // blk_count

    def other_core(value):
        return lax.ppermute(value, "group", [(0, 1), (1, 0), (2, 3), (3, 2)])

    def other_chip(value):
        return lax.ppermute(value, "group", [(0, 2), (2, 0), (1, 3), (3, 1)])

    picked = pick_old(page_table, cap, key_cache, value_cache)
    old = lax.all_to_all(picked, "blk", split_axis=0, concat_axis=0, tiled=True)
    old = old.reshape((blk_count * cap,) + old.shape[2:])

    fresh, cosine, sine = rotate_keys(lengths, new_keys[0], new_values[0])
    fresh_far = other_chip(fresh)
    fresh_core = other_core(fresh)
    roped, acc, stat, key_out, value_out = diagonal_part(
        after(queries[0], picked), cosine, sine, fresh, key_cache, value_cache
    )

    old = sort_old(after(page_table, stat), blk_count, cap, pages, old)
    old_far = other_chip(old)
    old_core = other_core(old)
    fresh_far_core = other_core(after(fresh_far, old))
    new, targets = pick_new(
        page_table, blk_count, cap, pages, (fresh, fresh_core, fresh_far, fresh_far_core)
    )
    arrived = lax.all_to_all(new, "blk", split_axis=0, concat_axis=0, tiled=True)
    old_far_core = other_core(after(old_far, new))
    hidden = rest_part(
        lengths, (roped, acc, stat),
        (fresh_core, fresh_far, fresh_far_core, old, old_core, old_far, old_far_core),
        out_weight,
    )
    key_out, value_out = place_new(targets, arrived, key_out, value_out)
    return (hidden[None], key_out, value_out)


def solution(mesh):
    return jax.shard_map(
        body,
        mesh=mesh,
        in_specs=(
            P("blk", "group", None),
            P("blk", "group", None),
            P("blk", "group", None),
            P("blk", "group", None),
            P("blk", "group", None),
            P(),
            P(),
            P(),
        ),
        out_specs=(P("blk", "group", None), P("blk", "group", None), P("blk", "group", None)),
        check_vma=False,
    )
```

```python
import jax
import jax.numpy as jnp
import numpy as np
from jax import lax
from jax.experimental import pallas as pl
from jax.experimental.pallas import tpu as pltpu
from jax.sharding import PartitionSpec as P

masked_score = -1e30
block_keys = 512
block_slots = 16
any_spec = pl.BlockSpec(memory_space=pl.ANY)
hbm_spec = pl.BlockSpec(memory_space=pltpu.HBM)
smem_spec = pl.BlockSpec(memory_space=pltpu.SMEM)
vmem_spec = pl.BlockSpec(memory_space=pltpu.VMEM)
small_limit = 16 * 1024 * 1024
head_pair = 2
large_limit = 60 * 1024 * 1024


light = pl.CostEstimate(flops=1, bytes_accessed=1, transcendentals=0)


def params(limit):
    return pltpu.CompilerParams(vmem_limit_bytes=limit)


def in_hbm(*arrays):
    return [pltpu.with_memory_space_constraint(array, pltpu.HBM) for array in arrays]


def turn(values, cosine, sine):
    front = values[:, :128].astype(jnp.float32)
    return front * cosine + pltpu.roll(front, 64, 1) * sine


def join(pieces):
    return jnp.concatenate(pieces, axis=1)


def pages_here(table_ref, r, first, count, cap, pages):
    low = lax.axis_index("blk") * pages
    found = jnp.int32(0)
    chosen = [jnp.int32(0)] * cap
    for j in range(first, first + count):
        page = table_ref[r, j] - low
        inside = (page >= 0) & (page < pages)
        chosen = [jnp.where(inside & (found == c), page, chosen[c]) for c in range(cap)]
        found = found + inside.astype(jnp.int32)
    return chosen, found


def pick_old_kernel(table_ref, key_ref, value_ref, out_ref, sem):
    requests, cap = out_ref.shape[:2]
    for r in range(requests):
        chosen, _ = pages_here(table_ref, r, 0, table_ref.shape[1] // 2, cap, key_ref.shape[0])
        for c in range(cap):
            pltpu.make_async_copy(key_ref.at[chosen[c]], out_ref.at[r, c, 0], sem).start()
            pltpu.make_async_copy(value_ref.at[chosen[c]], out_ref.at[r, c, 1], sem).start()
    pltpu.make_async_copy(out_ref, out_ref, sem).wait()


def pick_old(page_table, cap, key_cache, value_cache):
    requests = page_table.shape[0]
    return pl.pallas_call(
        pick_old_kernel,
        out_shape=jax.ShapeDtypeStruct((requests, cap, 2) + key_cache.shape[1:], jnp.bfloat16),
        in_specs=[smem_spec, hbm_spec, hbm_spec],
        out_specs=vmem_spec,
        scratch_shapes=[pltpu.SemaphoreType.DMA],
        cost_estimate=light,
        compiler_params=params(small_limit),
        name="pick_old",
    )(*in_hbm(page_table, key_cache, value_cache))


def owner_of(page, pages, owners):
    factor = (1 << 20) // pages + 1
    assert all((p * factor) >> 20 == p // pages for p in range(pages * owners))
    assert pages * owners * factor < 1 << 31
    return (page * factor) >> 20


def find_slots(table_ref, first, count, cap, pages, counts_ref):
    owners = counts_ref.shape[0]
    row = lax.axis_index("blk")
    for o in range(owners):
        counts_ref[o] = 0
    slots = []
    for j in range(count):
        owner = owner_of(table_ref[row, first + j], pages, owners)
        rank = counts_ref[owner]
        counts_ref[owner] = rank + 1
        slots.append(owner * cap + rank)
    return slots


def rotate_kernel(lengths_ref, freq_ref, keys_ref, values_ref, out_ref, cos_ref, sin_ref):
    rows = keys_ref.shape[0]
    slots = rows // 32
    start = lengths_ref[lax.axis_index("blk")] + lax.axis_index("group") * rows
    positions = start + lax.broadcasted_iota(jnp.int32, (rows, 128), 0)
    angles = positions.astype(jnp.float32) * freq_ref[...]
    lane = lax.broadcasted_iota(jnp.int32, (rows, 128), 1)
    cosine = jnp.cos(angles)
    sine = jnp.sin(angles)
    sine = jnp.where(lane < 64, -sine, sine)
    cos_ref[...] = cosine
    sin_ref[...] = sine
    keys = keys_ref[...]
    turned = join([turn(keys, cosine, sine).astype(jnp.bfloat16), keys[:, 128:]])
    out_ref[:, 0] = turned.reshape(slots, 32, 256)
    out_ref[:, 1] = values_ref[...].reshape(slots, 32, 256)


def rotate_keys(lengths, keys, values):
    rows, head_dim = keys.shape
    quarter = head_dim // 4
    freq_table = np.float32(10000.0) ** (-np.arange(quarter, dtype=np.float32) / np.float32(quarter))
    freq_table = np.concatenate([freq_table, freq_table])[None].astype(np.float32)
    return pl.pallas_call(
        rotate_kernel,
        out_shape=(
            pltpu.HBM((rows // 32, 2, 32, head_dim), jnp.bfloat16),
            pltpu.HBM((rows, 128), jnp.float32),
            pltpu.HBM((rows, 128), jnp.float32),
        ),
        in_specs=[smem_spec, vmem_spec, vmem_spec, vmem_spec],
        out_specs=(vmem_spec,) * 3,
        cost_estimate=light,
        compiler_params=params(small_limit),
        name="rotate_keys",
    )(lengths, jnp.asarray(freq_table), keys, values)


def sort_kernel(pages, cap, table_ref, old_ref, out_ref, counts_ref, sem):
    count = out_ref.shape[0]
    for j, slot in enumerate(find_slots(table_ref, 0, count, cap, pages, counts_ref)):
        pltpu.make_async_copy(old_ref.at[slot], out_ref.at[j], sem).start()
    pltpu.make_async_copy(out_ref, out_ref, sem).wait()


def sort_old(page_table, blk_count, cap, pages, old):
    window = page_table.shape[1] // 2
    return pl.pallas_call(
        lambda *refs: sort_kernel(pages, cap, *refs),
        out_shape=jax.ShapeDtypeStruct((window,) + old.shape[1:], jnp.bfloat16),
        in_specs=[smem_spec, hbm_spec],
        out_specs=vmem_spec,
        scratch_shapes=[pltpu.SMEM((blk_count,), jnp.int32), pltpu.SemaphoreType.DMA],
        cost_estimate=light,
        compiler_params=params(small_limit),
        name="sort_old",
    )(page_table, *in_hbm(old))


def pick_new_kernel(
    pages, cap, table_ref, own_ref, core_ref, far_ref, far_core_ref, out_ref, targets_ref,
    slots_ref, counts_ref, sem,
):
    count = slots_ref.shape[0]
    block_pages = count // 4
    group_index = lax.axis_index("group")
    for j, slot in enumerate(find_slots(table_ref, table_ref.shape[1] - count, count, cap, pages, counts_ref)):
        slots_ref[j] = slot
    for number, ref in enumerate((own_ref, core_ref, far_ref, far_core_ref)):
        block = group_index ^ number
        for place in range(block_pages):
            source = ref.at[4 * place + group_index]
            target = out_ref.at[slots_ref[block * block_pages + place]]
            pltpu.make_async_copy(source, target, sem).start()
    for r in range(table_ref.shape[0]):
        chosen, found = pages_here(table_ref, r, table_ref.shape[1] - count, count, cap, pages)
        for c in range(cap):
            targets_ref[r * cap + c] = jnp.where(found > c, chosen[c], -1)
    sent = out_ref.at[pl.ds(0, count)]
    pltpu.make_async_copy(sent, sent, sem).wait()


def pick_new(page_table, blk_count, cap, pages, sources):
    window = page_table.shape[1] // 2
    return pl.pallas_call(
        lambda *refs: pick_new_kernel(pages, cap, *refs),
        out_shape=(
            jax.ShapeDtypeStruct((blk_count * cap,) + sources[0].shape[1:], jnp.bfloat16),
            jax.ShapeDtypeStruct((blk_count * cap,), jnp.int32),
        ),
        in_specs=[smem_spec] + [any_spec] * 4,
        out_specs=(vmem_spec, smem_spec),
        scratch_shapes=[
            pltpu.SMEM((window,), jnp.int32),
            pltpu.SMEM((blk_count,), jnp.int32),
            pltpu.SemaphoreType.DMA,
        ],
        cost_estimate=light,
        compiler_params=params(small_limit),
        name="pick_new",
    )(page_table, *sources)


def lane_fold(values, combine):
    total = values[:, :128]
    for start in range(128, values.shape[1], 128):
        total = combine(total, values[:, start : start + 128])
    return total


def old_bias(rows, quarter):
    row = lax.broadcasted_iota(jnp.int32, (rows, 256), 0)
    column = lax.broadcasted_iota(jnp.int32, (rows, 256), 1)
    held = quarter ^ (column // 128)
    position = ((column % 128) // 32) * 128 + 32 * held + column % 32
    return jnp.where(position > row, 0.0, masked_score)


def fetch(source, first, kv_ref, place, count, sem):
    for kind in range(2):
        pltpu.make_async_copy(
            source.at[pl.ds(first, count), kind], kv_ref.at[kind, pl.ds(place, count)], sem
        ).start()


def fetch_pair(sources, first, kv_ref, place, sem):
    fetch(sources[0], first, kv_ref, place, 4, sem)
    fetch(sources[1], first, kv_ref, place + 4, 4, sem)


def wait_rows(kv_ref, blocks, most, sem):
    for n in range(1, most + 1):

        @pl.when(blocks == n)
        def _(n=n):
            filled = kv_ref.at[:, pl.ds(0, n * block_slots)]
            pltpu.make_async_copy(filled, filled, sem).wait()


def attention(steps, step_keys, roped_ref, kv_ref, bias_ref, s_refs, most_refs, top_ref, sum_ref, sum_of_values, begin, finish):
    items, rows, _ = roped_ref.shape
    step_slots = step_keys // 32
    biased = bias_ref.shape[2]

    def block(kind, c):
        return kv_ref[kind, pl.ds(c * step_slots, step_slots)].reshape(step_keys, 256)

    def scores(t, c, which, masked):
        result = lax.dot_general(
            roped_ref[t], block(0, c), (((1,), (1,)), ((), ())), preferred_element_type=jnp.float32
        )
        if masked:
            head = result[:, :biased].reshape(head_pair, rows // head_pair, biased) + bias_ref[0]
            head = head.reshape(rows, biased)
            result = join([head, result[:, biased:]]) if step_keys > biased else head
        s_refs[which][c] = result
        most_refs[which][...] = jnp.maximum(most_refs[which][...], lane_fold(result, jnp.maximum))

    def weigh(c, which):
        weights = jnp.exp(s_refs[which][c] - join([top_ref[...]] * (step_keys // 128)))
        sum_ref[...] += lane_fold(weights, jnp.add)
        sum_of_values[...] += jnp.dot(
            weights.astype(jnp.bfloat16), block(1, c), preferred_element_type=jnp.float32
        )

    def settle(which):
        top_ref[...] = jnp.broadcast_to(
            jnp.max(most_refs[which][...], axis=1, keepdims=True), top_ref.shape
        )
        sum_ref[...] = jnp.zeros_like(sum_ref)
        sum_of_values[...] = jnp.zeros_like(sum_of_values)

    def loop(work):
        def step(c, carry):
            work(c, False)
            return carry

        @pl.when(steps > 0)
        def _():
            work(0, True)

        lax.fori_loop(1, steps, step, 0)

    def both(t, which):
        def work(c, masked):
            weigh(c, which)
            scores(t + 1, c, 1 - which, masked)

        loop(work)

    drive(
        items, most_refs, begin, settle, finish,
        lambda: loop(lambda c, masked: scores(0, c, 0, masked)),
        both,
        lambda which: loop(lambda c, masked: weigh(c, which)),
    )


def attention_at_once(roped_ref, kv_ref, bias_ref, s_refs, most_refs, top_ref, sum_ref, sum_of_values, begin, finish):
    items, rows, _ = roped_ref.shape
    blocks, _, width = s_refs[0].shape
    biased = bias_ref.shape[2]
    slots = width // 32

    def scores(t, which):
        most = most_refs[which][...]
        query = roped_ref[t]
        for c in range(blocks):
            keys = kv_ref[0, c * slots : (c + 1) * slots].reshape(width, 256)
            result = lax.dot_general(
                query, keys, (((1,), (1,)), ((), ())), preferred_element_type=jnp.float32
            )
            if c == 0:
                head = result[:, :biased].reshape(head_pair, rows // head_pair, biased) + bias_ref[0]
                head = head.reshape(rows, biased)
                result = join([head, result[:, biased:]]) if width > biased else head
            s_refs[which][c] = result
            most = jnp.maximum(most, lane_fold(result, jnp.maximum))
        most_refs[which][...] = most

    def weigh(which):
        top = join([top_ref[...]] * (width // 128))
        sums = None
        total = None
        for c in range(blocks):
            weights = jnp.exp(s_refs[which][c] - top)
            folded = lane_fold(weights, jnp.add)
            sums = folded if sums is None else sums + folded
            values = kv_ref[1, c * slots : (c + 1) * slots].reshape(width, 256)
            part = jnp.dot(weights.astype(jnp.bfloat16), values, preferred_element_type=jnp.float32)
            total = part if total is None else total + part
        sum_ref[...] = sums
        sum_of_values[...] = total

    def settle(which):
        top_ref[...] = jnp.broadcast_to(
            jnp.max(most_refs[which][...], axis=1, keepdims=True), top_ref.shape
        )

    def both(t, which):
        weigh(which)
        scores(t + 1, 1 - which)

    drive(items, most_refs, begin, settle, finish, lambda: scores(0, 0), both, weigh)


def drive(items, most_refs, begin, settle, finish, only_scores, both, only_weigh):
    def one(t, which):
        begin(t + 1, most_refs[1 - which])
        settle(which)
        both(t, which)
        finish(t)

    def two(i, carry):
        one(2 * i, 0)
        one(2 * i + 1, 1)
        return carry

    begin(0, most_refs[0])
    only_scores()
    pairs = (items - 1) // 2
    lax.fori_loop(0, pairs, two, 0)
    last = 2 * pairs
    if last < items - 1:
        one(last, 0)
        last += 1
    settle(last % 2)
    only_weigh(last % 2)
    finish(last)


def working(rows, steps, step_keys, tables):
    return [
        pltpu.VMEM((2, steps * step_keys // 32, 32, 256), jnp.bfloat16),
        pltpu.VMEM((steps, head_pair * rows, step_keys), jnp.float32),
        pltpu.VMEM((steps, head_pair * rows, step_keys), jnp.float32),
        pltpu.VMEM((head_pair * rows, 128), jnp.float32),
        pltpu.VMEM((head_pair * rows, 128), jnp.float32),
        pltpu.VMEM((head_pair * rows, 128), jnp.float32),
        pltpu.VMEM((head_pair * rows, 128), jnp.float32),
        pltpu.VMEM((head_pair * rows, 256), jnp.float32),
        pltpu.VMEM((tables, rows, block_keys), jnp.float32),
    ]


def state_shapes(items, rows):
    return [
        pltpu.VMEM((items, head_pair * rows, 256), jnp.bfloat16),
        pltpu.VMEM((items, head_pair * rows, 256), jnp.float32),
        pltpu.VMEM((items, head_pair * rows, 128), jnp.float32),
    ]


def state_out(items, rows):
    return (
        pltpu.HBM((items, head_pair * rows, 256), jnp.float32),
        pltpu.HBM((items, head_pair * rows, 128), jnp.float32),
    )


def diagonal_kernel(
    query_ref, cos_in, sin_in, own_ref, key_ref, value_ref, roped_out, acc_out, stat_out,
    key_out_ref, value_out_ref, cos_ref, sin_ref, key_pool, value_pool, q_ref, roped_ref, acc_ref, stat_ref, kv_ref, s_0, s_1, most_0, most_1, top_ref, sum_ref, values_ref,
    bias_ref, query_sem, sem, out_sem, pool_sems, angle_sems,
):
    rows = q_ref.shape[0]
    items = roped_ref.shape[0]
    loads = [
        pltpu.make_async_copy(key_ref, key_pool, pool_sems.at[0]),
        pltpu.make_async_copy(value_ref, value_pool, pool_sems.at[1]),
    ]
    stores = [
        pltpu.make_async_copy(key_pool, key_out_ref, pool_sems.at[0]),
        pltpu.make_async_copy(value_pool, value_out_ref, pool_sems.at[1]),
    ]
    query_copy = pltpu.make_async_copy(query_ref, q_ref, query_sem)
    query_copy.start()
    angle_copies = [
        pltpu.make_async_copy(cos_in, cos_ref, angle_sems.at[0]),
        pltpu.make_async_copy(sin_in, sin_ref, angle_sems.at[1]),
    ]
    for copy in angle_copies:
        copy.start()
    fetch(own_ref, 0, kv_ref, 0, block_slots, sem)
    for copy in loads:
        copy.start()
    row = lax.broadcasted_iota(jnp.int32, (rows, block_keys), 0)
    column = lax.broadcasted_iota(jnp.int32, (rows, block_keys), 1)
    bias_ref[0] = jnp.where(column <= row, 0.0, masked_score)
    query_copy.wait()
    for copy in angle_copies:
        copy.wait()

    def rope(t, carry):
        for one in range(head_pair):
            raw = q_ref[:, pl.ds(pl.multiple_of((t * head_pair + one) * 256, 256), 256)]
            front = turn(raw, cos_ref[...], sin_ref[...])
            some = pl.ds(one * rows, rows)
            roped_ref[t, some, :128] = (front * 0.0625).astype(jnp.bfloat16)
            roped_ref[t, some, 128:] = raw[:, 128:] * jnp.bfloat16(0.0625)
        return carry

    lax.fori_loop(0, items, rope, 0)
    roped_copy = pltpu.make_async_copy(roped_ref, roped_out, query_sem)
    roped_copy.start()
    pltpu.make_async_copy(kv_ref, kv_ref, sem).wait()
    for load, store in zip(loads, stores):
        load.wait()
        store.start()

    def begin(t, most_ref):
        most_ref[...] = jnp.full_like(most_ref, masked_score)

    def finish(t):
        lane = lax.broadcasted_iota(jnp.int32, stat_ref.shape[1:], 1)
        sums = jnp.sum(sum_ref[...], axis=1, keepdims=True)
        stat_ref[t] = jnp.where(lane < 64, top_ref[...], sums)
        acc_ref[t] = values_ref[...]
        pltpu.make_async_copy(acc_ref.at[t], acc_out.at[t], out_sem).start()
        pltpu.make_async_copy(stat_ref.at[t], stat_out.at[t], out_sem).start()

    attention_at_once(
        roped_ref, kv_ref, bias_ref, (s_0, s_1), (most_0, most_1), top_ref, sum_ref, values_ref,
        begin, finish,
    )
    roped_copy.wait()
    for copy in stores:
        copy.wait()
    pltpu.make_async_copy(acc_ref, acc_out, out_sem).wait()
    pltpu.make_async_copy(stat_ref, stat_out, out_sem).wait()


def diagonal_part(queries, cosine, sine, own, key_cache, value_cache):
    rows, width = queries.shape
    items = width // (256 * head_pair)
    return pl.pallas_call(
        diagonal_kernel,
        out_shape=(pltpu.HBM((items, head_pair * rows, 256), jnp.bfloat16),)
        + state_out(items, rows)
        + (pltpu.HBM(key_cache.shape, jnp.bfloat16), pltpu.HBM(value_cache.shape, jnp.bfloat16)),
        in_specs=[hbm_spec] * 6,
        out_specs=(hbm_spec,) * 5,
        scratch_shapes=[
            pltpu.VMEM(cosine.shape, jnp.float32),
            pltpu.VMEM(sine.shape, jnp.float32),
            pltpu.VMEM(key_cache.shape, jnp.bfloat16),
            pltpu.VMEM(value_cache.shape, jnp.bfloat16),
            pltpu.VMEM((rows, width), jnp.bfloat16),
        ]
        + state_shapes(items, rows)
        + working(rows, 1, block_keys, 1)
        + [pltpu.SemaphoreType.DMA] * 3
        + [pltpu.SemaphoreType.DMA((2,))] * 2,
        cost_estimate=light,
        compiler_params=params(large_limit),
        name="attend_diagonal",
    )(*in_hbm(queries, cosine, sine, own, key_cache, value_cache))


def rest_kernel(
    lengths_ref, roped_in, acc_in, stat_in, core_ref, far_ref, far_core_ref,
    old_ref, old_core_ref, old_far_ref, old_far_core_ref, weight_ref, hidden_ref,
    roped_ref, acc_ref, stat_ref, kv_ref, s_0, s_1, most_0, most_1, top_ref, sum_ref, values_ref,
    bias_ref, w_ref, stage_ref, roped_sem, state_sems, sem, weight_sem, out_sems,
):
    group_index = lax.axis_index("group")
    has_old = lengths_ref[lax.axis_index("blk")] > 0
    items = roped_ref.shape[0]
    rows = bias_ref.shape[1]
    chunk = stage_ref.shape[2]
    chunks = w_ref.shape[1] // chunk
    odd = group_index % 2
    chip = group_index // 2
    blocks = jnp.where(has_old, 4, odd + 2 * chip)
    steps = jnp.where(has_old, 2, odd + chip)
    base = jnp.where(has_old, 16, 16 * odd)
    near = (old_ref, old_core_ref)
    far = (old_far_ref, old_far_core_ref)

    def copies(t):
        return [
            pltpu.make_async_copy(source.at[t], target.at[t], state_sems.at[number, t])
            for number, (source, target) in enumerate(((stat_in, stat_ref), (acc_in, acc_ref)))
        ]

    roped_copy = pltpu.make_async_copy(roped_in, roped_ref, roped_sem)
    roped_copy.start()
    @pl.when(odd == 1)
    def _():
        fetch(core_ref, 0, kv_ref, base, 16, sem)

    @pl.when(chip == 1)
    def _():
        place = jnp.where(has_old, 32, 32 * odd)
        fetch(far_ref, 0, kv_ref, place, 16, sem)
        fetch(far_core_ref, 0, kv_ref, place + 16, 16, sem)

    @pl.when(has_old)
    def _():
        for block in range(4):

            @pl.when(block >= group_index)
            def _(block=block):
                gap = jnp.where(block == group_index, 0, odd)
                place = 16 * (gap + block - group_index)
                fetch_pair(near, 4 * block, kv_ref, place, sem)
                fetch_pair(far, 4 * block, kv_ref, place + 8, sem)

    for t in range(items):
        for copy in copies(t):
            copy.start()
    weight_copy = pltpu.make_async_copy(weight_ref, w_ref, weight_sem)
    weight_copy.start()

    @pl.when(jnp.logical_not(has_old))
    def _():
        bias_ref[0] = jnp.where(odd == 1, masked_score, 0.0) + jnp.zeros(bias_ref.shape[1:], jnp.float32)
        empty = pl.ds(0, block_slots)

        @pl.when(odd == 1)
        def _():
            kv_ref[:, empty] = jnp.zeros((2, block_slots, 32, 256), jnp.bfloat16)

    @pl.when(has_old)
    def _():
        bias_ref[0, :, :256] = old_bias(rows, group_index)
        bias_ref[0, :, 256:] = old_bias(rows, group_index ^ 2)

    roped_copy.wait()
    wait_rows(kv_ref, blocks, 4, sem)
    lane = lax.broadcasted_iota(jnp.int32, stat_ref.shape[1:], 1)

    def begin(t, most_ref):
        for copy in copies(t):
            copy.wait()
        most_ref[...] = jnp.where(lane < 64, stat_ref[t], masked_score)

    def finish(t):
        stat = stat_ref[t]
        factor = jnp.exp(stat[:, :1] - top_ref[...])
        sums = stat[:, 64:65] * factor + jnp.sum(sum_ref[...], axis=1, keepdims=True)
        inverse = 1.0 / sums
        old = factor * inverse
        mixed = acc_ref[t] * join([old, old]) + values_ref[...] * join([inverse, inverse])
        roped_ref[t] = mixed.astype(jnp.bfloat16)

    scratch = (roped_ref, kv_ref, bias_ref, (s_0, s_1), (most_0, most_1), top_ref, sum_ref, values_ref)

    attention(steps, 2 * block_keys, *scratch, begin, finish)
    weight_copy.wait()

    def out_copy(n, columns):
        return pltpu.make_async_copy(stage_ref.at[n % 2], hidden_ref.at[:, columns], out_sems.at[n % 2])

    def project(n, carry):
        columns = pl.ds(pl.multiple_of(n * chunk, chunk), chunk)

        @pl.when(n >= 2)
        def _():
            out_copy(n, columns).wait()

        attended = join(
            [
                roped_ref[t, one * rows : (one + 1) * rows, :]
                for t in range(items)
                for one in range(head_pair)
            ]
        )
        stage_ref[n % 2] = jnp.dot(
            attended, w_ref[:, columns], preferred_element_type=jnp.float32
        ).astype(jnp.bfloat16)
        out_copy(n, columns).start()
        return carry

    lax.fori_loop(0, chunks, project, 0)
    for n in range(2):
        out_copy(n, pl.ds(0, chunk)).wait()


def rest_part(lengths, state, slots, weight):
    items, pair_rows, _ = state[0].shape
    rows = pair_rows // head_pair
    width = weight.shape[1]
    chunk = 512
    return pl.pallas_call(
        rest_kernel,
        out_shape=pltpu.HBM((rows, width), jnp.bfloat16),
        in_specs=[smem_spec] + [hbm_spec] * 3 + [any_spec] * 7 + [hbm_spec],
        out_specs=hbm_spec,
        scratch_shapes=state_shapes(items, rows)
        + working(rows, 2, 2 * block_keys, 1)
        + [
            pltpu.VMEM(weight.shape, jnp.bfloat16),
            pltpu.VMEM((2, rows, chunk), jnp.bfloat16),
            pltpu.SemaphoreType.DMA,
            pltpu.SemaphoreType.DMA((2, items)),
            pltpu.SemaphoreType.DMA,
            pltpu.SemaphoreType.DMA,
            pltpu.SemaphoreType.DMA((2,)),
        ],
        cost_estimate=light,
        compiler_params=params(large_limit),
        name="attend_rest",
    )(lengths, *in_hbm(*state), *slots, *in_hbm(weight))


def place_kernel(targets_ref, arrived_ref, key_in, value_in, key_ref, value_ref, buffer_ref, load_sem, sem):
    load = pltpu.make_async_copy(arrived_ref, buffer_ref, load_sem)
    load.start()
    load.wait()

    def each(act):
        for slot in range(targets_ref.shape[0]):
            page = targets_ref[slot]

            @pl.when(page >= 0)
            def _(slot=slot, page=page):
                for kind, out_ref in enumerate((key_ref, value_ref)):
                    act(pltpu.make_async_copy(buffer_ref.at[slot, kind], out_ref.at[page], sem))

    each(lambda copy: copy.start())
    each(lambda copy: copy.wait())


def place_new(targets, arrived, key_pool, value_pool):
    return pl.pallas_call(
        place_kernel,
        out_shape=(
            pltpu.HBM(key_pool.shape, jnp.bfloat16),
            pltpu.HBM(value_pool.shape, jnp.bfloat16),
        ),
        in_specs=[smem_spec, any_spec, hbm_spec, hbm_spec],
        out_specs=(hbm_spec,) * 2,
        input_output_aliases={2: 0, 3: 1},
        scratch_shapes=[
            pltpu.VMEM(arrived.shape, jnp.bfloat16),
            pltpu.SemaphoreType.DMA,
            pltpu.SemaphoreType.DMA,
        ],
        cost_estimate=light,
        compiler_params=params(small_limit),
        name="place_new",
    )(targets, arrived, *in_hbm(key_pool, value_pool))


def after(value, *others):
    return lax.optimization_barrier((value,) + others)[0]


def body(queries, new_keys, new_values, key_cache, value_cache, out_weight, lengths, page_table):
    blk_count = lax.axis_size("blk")
    pages = key_cache.shape[0]
    window_pages = page_table.shape[1] // 2
    cap = (window_pages + blk_count - 1) // blk_count

    def other_core(value):
        return lax.ppermute(value, "group", [(0, 1), (1, 0), (2, 3), (3, 2)])

    def other_chip(value):
        return lax.ppermute(value, "group", [(0, 2), (2, 0), (1, 3), (3, 1)])

    picked = pick_old(page_table, cap, key_cache, value_cache)
    old = lax.all_to_all(picked, "blk", split_axis=0, concat_axis=0, tiled=True)
    old = old.reshape((blk_count * cap,) + old.shape[2:])

    fresh, cosine, sine = rotate_keys(lengths, new_keys[0], new_values[0])
    fresh_far = other_chip(fresh)
    fresh_core = other_core(fresh)
    roped, acc, stat, key_out, value_out = diagonal_part(
        after(queries[0], picked), cosine, sine, fresh, key_cache, value_cache
    )

    old = sort_old(after(page_table, stat), blk_count, cap, pages, old)
    old_far = other_chip(old)
    old_core = other_core(old)
    fresh_far = after(fresh_far, old)
    fresh_far_core = other_core(fresh_far)
    new, targets = pick_new(
        page_table, blk_count, cap, pages, (fresh, fresh_core, fresh_far, fresh_far_core)
    )
    arrived = lax.all_to_all(new, "blk", split_axis=0, concat_axis=0, tiled=True)
    old_far_core = other_core(after(old_far, new))
    hidden = rest_part(
        lengths, (roped, acc, stat),
        (fresh_core, fresh_far, fresh_far_core, old, old_core, old_far, old_far_core),
        out_weight,
    )
    key_out, value_out = place_new(targets, arrived, key_out, value_out)
    return (hidden[None], key_out, value_out)


def solution(mesh):
    return jax.shard_map(
        body,
        mesh=mesh,
        in_specs=(
            P("blk", "group", None),
            P("blk", "group", None),
            P("blk", "group", None),
            P("blk", "group", None),
            P("blk", "group", None),
            P(),
            P(),
            P(),
        ),
        out_specs=(P("blk", "group", None), P("blk", "group", None), P("blk", "group", None)),
        check_vma=False,
    )
```

```python
import jax
import jax.numpy as jnp
import numpy as np
from jax import lax
from jax.experimental import pallas as pl
from jax.experimental.pallas import tpu as pltpu
from jax.sharding import PartitionSpec as P

masked_score = -1e30
block_keys = 512
block_slots = 16
any_spec = pl.BlockSpec(memory_space=pl.ANY)
hbm_spec = pl.BlockSpec(memory_space=pltpu.HBM)
smem_spec = pl.BlockSpec(memory_space=pltpu.SMEM)
vmem_spec = pl.BlockSpec(memory_space=pltpu.VMEM)
small_limit = 16 * 1024 * 1024
head_pair = 2
large_limit = 60 * 1024 * 1024


light = pl.CostEstimate(flops=1, bytes_accessed=1, transcendentals=0)


def params(limit):
    return pltpu.CompilerParams(vmem_limit_bytes=limit)


def in_hbm(*arrays):
    return [pltpu.with_memory_space_constraint(array, pltpu.HBM) for array in arrays]


def turn(values, cosine, sine):
    front = values[:, :128].astype(jnp.float32)
    return front * cosine + pltpu.roll(front, 64, 1) * sine


def join(pieces):
    return jnp.concatenate(pieces, axis=1)


def pages_here(table_ref, r, first, count, cap, pages):
    low = lax.axis_index("blk") * pages
    found = jnp.int32(0)
    chosen = [jnp.int32(0)] * cap
    for j in range(first, first + count):
        page = table_ref[r, j] - low
        inside = (page >= 0) & (page < pages)
        chosen = [jnp.where(inside & (found == c), page, chosen[c]) for c in range(cap)]
        found = found + inside.astype(jnp.int32)
    return chosen, found


def pick_old_kernel(table_ref, key_ref, value_ref, out_ref, found_ref, sem):
    requests, cap = out_ref.shape[:2]
    pages = key_ref.shape[0]
    low = lax.axis_index("blk") * pages
    for r in range(requests):
        count = jnp.int32(0)
        for j in range(table_ref.shape[1] // 2):
            page = table_ref[r, j] - low
            found_ref[jnp.minimum(count, cap)] = page
            count = count + ((page >= 0) & (page < pages)).astype(jnp.int32)
        for c in range(cap):
            page = jnp.where(count > c, found_ref[c], 0)
            pltpu.make_async_copy(key_ref.at[page], out_ref.at[r, c, 0], sem).start()
            pltpu.make_async_copy(value_ref.at[page], out_ref.at[r, c, 1], sem).start()
    pltpu.make_async_copy(out_ref, out_ref, sem).wait()


def pick_old(page_table, cap, key_cache, value_cache):
    requests = page_table.shape[0]
    return pl.pallas_call(
        pick_old_kernel,
        out_shape=jax.ShapeDtypeStruct((requests, cap, 2) + key_cache.shape[1:], jnp.bfloat16),
        in_specs=[smem_spec, hbm_spec, hbm_spec],
        out_specs=vmem_spec,
        scratch_shapes=[pltpu.SMEM((cap + 1,), jnp.int32), pltpu.SemaphoreType.DMA],
        cost_estimate=light,
        compiler_params=params(small_limit),
        name="pick_old",
    )(*in_hbm(page_table, key_cache, value_cache))


def owner_of(page, pages, owners):
    factor = (1 << 20) // pages + 1
    assert all((p * factor) >> 20 == p // pages for p in range(pages * owners))
    assert pages * owners * factor < 1 << 31
    return (page * factor) >> 20


def find_slots(table_ref, first, count, cap, pages, counts_ref):
    owners = counts_ref.shape[0]
    row = lax.axis_index("blk")
    for o in range(owners):
        counts_ref[o] = 0
    slots = []
    for j in range(count):
        owner = owner_of(table_ref[row, first + j], pages, owners)
        rank = counts_ref[owner]
        counts_ref[owner] = rank + 1
        slots.append(owner * cap + rank)
    return slots


def rotate_kernel(lengths_ref, freq_ref, keys_ref, values_ref, out_ref, cos_ref, sin_ref):
    rows = keys_ref.shape[0]
    slots = rows // 32
    start = lengths_ref[lax.axis_index("blk")] + lax.axis_index("group") * rows
    positions = start + lax.broadcasted_iota(jnp.int32, (rows, 128), 0)
    angles = positions.astype(jnp.float32) * freq_ref[...]
    lane = lax.broadcasted_iota(jnp.int32, (rows, 128), 1)
    cosine = jnp.cos(angles)
    sine = jnp.sin(angles)
    sine = jnp.where(lane < 64, -sine, sine)
    cos_ref[...] = cosine
    sin_ref[...] = sine
    keys = keys_ref[...]
    turned = join([turn(keys, cosine, sine).astype(jnp.bfloat16), keys[:, 128:]])
    out_ref[:, 0] = turned.reshape(slots, 32, 256)
    out_ref[:, 1] = values_ref[...].reshape(slots, 32, 256)


def rotate_keys(lengths, keys, values):
    rows, head_dim = keys.shape
    quarter = head_dim // 4
    freq_table = np.float32(10000.0) ** (-np.arange(quarter, dtype=np.float32) / np.float32(quarter))
    freq_table = np.concatenate([freq_table, freq_table])[None].astype(np.float32)
    return pl.pallas_call(
        rotate_kernel,
        out_shape=(
            pltpu.HBM((rows // 32, 2, 32, head_dim), jnp.bfloat16),
            pltpu.HBM((rows, 128), jnp.float32),
            pltpu.HBM((rows, 128), jnp.float32),
        ),
        in_specs=[smem_spec, vmem_spec, vmem_spec, vmem_spec],
        out_specs=(vmem_spec,) * 3,
        cost_estimate=light,
        compiler_params=params(small_limit),
        name="rotate_keys",
    )(lengths, jnp.asarray(freq_table), keys, values)


def sort_kernel(pages, cap, table_ref, old_ref, out_ref, counts_ref, sem):
    count = out_ref.shape[0]
    for j, slot in enumerate(find_slots(table_ref, 0, count, cap, pages, counts_ref)):
        pltpu.make_async_copy(old_ref.at[slot], out_ref.at[j], sem).start()
    pltpu.make_async_copy(out_ref, out_ref, sem).wait()


def sort_old(page_table, blk_count, cap, pages, old):
    window = page_table.shape[1] // 2
    return pl.pallas_call(
        lambda *refs: sort_kernel(pages, cap, *refs),
        out_shape=jax.ShapeDtypeStruct((window,) + old.shape[1:], jnp.bfloat16),
        in_specs=[smem_spec, hbm_spec],
        out_specs=vmem_spec,
        scratch_shapes=[pltpu.SMEM((blk_count,), jnp.int32), pltpu.SemaphoreType.DMA],
        cost_estimate=light,
        compiler_params=params(small_limit),
        name="sort_old",
    )(page_table, *in_hbm(old))


def pick_new_kernel(
    pages, cap, table_ref, own_ref, core_ref, far_ref, far_core_ref, out_ref, targets_ref,
    slots_ref, counts_ref, sem,
):
    count = slots_ref.shape[0]
    block_pages = count // 4
    group_index = lax.axis_index("group")
    for j, slot in enumerate(find_slots(table_ref, table_ref.shape[1] - count, count, cap, pages, counts_ref)):
        slots_ref[j] = slot
    for number, ref in enumerate((own_ref, core_ref, far_ref, far_core_ref)):
        block = group_index ^ number
        for place in range(block_pages):
            source = ref.at[4 * place + group_index]
            target = out_ref.at[slots_ref[block * block_pages + place]]
            pltpu.make_async_copy(source, target, sem).start()
    for r in range(table_ref.shape[0]):
        chosen, found = pages_here(table_ref, r, table_ref.shape[1] - count, count, cap, pages)
        for c in range(cap):
            targets_ref[r * cap + c] = jnp.where(found > c, chosen[c], -1)
    sent = out_ref.at[pl.ds(0, count)]
    pltpu.make_async_copy(sent, sent, sem).wait()


def pick_new(page_table, blk_count, cap, pages, sources):
    window = page_table.shape[1] // 2
    return pl.pallas_call(
        lambda *refs: pick_new_kernel(pages, cap, *refs),
        out_shape=(
            jax.ShapeDtypeStruct((blk_count * cap,) + sources[0].shape[1:], jnp.bfloat16),
            jax.ShapeDtypeStruct((blk_count * cap,), jnp.int32),
        ),
        in_specs=[smem_spec] + [any_spec] * 4,
        out_specs=(vmem_spec, smem_spec),
        scratch_shapes=[
            pltpu.SMEM((window,), jnp.int32),
            pltpu.SMEM((blk_count,), jnp.int32),
            pltpu.SemaphoreType.DMA,
        ],
        cost_estimate=light,
        compiler_params=params(small_limit),
        name="pick_new",
    )(page_table, *sources)


def lane_fold(values, combine):
    total = values[:, :128]
    for start in range(128, values.shape[1], 128):
        total = combine(total, values[:, start : start + 128])
    return total


def old_bias(rows, quarter):
    row = lax.broadcasted_iota(jnp.int32, (rows, 256), 0)
    column = lax.broadcasted_iota(jnp.int32, (rows, 256), 1)
    held = quarter ^ (column // 128)
    position = ((column % 128) // 32) * 128 + 32 * held + column % 32
    return jnp.where(position > row, 0.0, masked_score)


def fetch(source, first, kv_ref, place, count, sem):
    for kind in range(2):
        pltpu.make_async_copy(
            source.at[pl.ds(first, count), kind], kv_ref.at[kind, pl.ds(place, count)], sem
        ).start()


def fetch_pair(sources, first, kv_ref, place, sem):
    fetch(sources[0], first, kv_ref, place, 4, sem)
    fetch(sources[1], first, kv_ref, place + 4, 4, sem)


def wait_rows(kv_ref, blocks, most, sem):
    for n in range(1, most + 1):

        @pl.when(blocks == n)
        def _(n=n):
            filled = kv_ref.at[:, pl.ds(0, n * block_slots)]
            pltpu.make_async_copy(filled, filled, sem).wait()


def attention(steps, most_steps, step_keys, roped_ref, kv_ref, bias_ref, s_refs, most_refs, top_ref, sum_ref, sum_of_values, begin, finish):
    items, rows, _ = roped_ref.shape
    step_slots = step_keys // 32
    biased = bias_ref.shape[2]

    def block(kind, c):
        return kv_ref[kind, c * step_slots : (c + 1) * step_slots].reshape(step_keys, 256)

    def scores(t, c, which):
        result = lax.dot_general(
            roped_ref[t], block(0, c), (((1,), (1,)), ((), ())), preferred_element_type=jnp.float32
        )
        if c == 0:
            head = result[:, :biased].reshape(head_pair, rows // head_pair, biased) + bias_ref[0]
            head = head.reshape(rows, biased)
            result = join([head, result[:, biased:]]) if step_keys > biased else head
        s_refs[which][c] = result
        most_refs[which][...] = jnp.maximum(most_refs[which][...], lane_fold(result, jnp.maximum))

    def weigh(c, which):
        weights = jnp.exp(s_refs[which][c] - join([top_ref[...]] * (step_keys // 128)))
        sum_ref[...] += lane_fold(weights, jnp.add)
        sum_of_values[...] += jnp.dot(
            weights.astype(jnp.bfloat16), block(1, c), preferred_element_type=jnp.float32
        )

    def settle(which):
        top_ref[...] = jnp.broadcast_to(
            jnp.max(most_refs[which][...], axis=1, keepdims=True), top_ref.shape
        )
        sum_ref[...] = jnp.zeros_like(sum_ref)
        sum_of_values[...] = jnp.zeros_like(sum_of_values)

    def loop(work):
        for c in range(most_steps):

            @pl.when(steps > c)
            def _(c=c):
                work(c)

    def both(t, which):
        def work(c):
            weigh(c, which)
            scores(t + 1, c, 1 - which)

        loop(work)

    drive(
        items, most_refs, begin, settle, finish,
        lambda: loop(lambda c: scores(0, c, 0)),
        both,
        lambda which: loop(lambda c: weigh(c, which)),
    )


def attention_at_once(roped_ref, kv_ref, bias_ref, s_refs, most_refs, top_ref, sum_ref, sum_of_values, begin, finish):
    items, rows, _ = roped_ref.shape
    blocks, _, width = s_refs[0].shape
    biased = bias_ref.shape[2]
    slots = width // 32

    def scores(t, which):
        most = most_refs[which][...]
        query = roped_ref[t]
        for c in range(blocks):
            keys = kv_ref[0, c * slots : (c + 1) * slots].reshape(width, 256)
            result = lax.dot_general(
                query, keys, (((1,), (1,)), ((), ())), preferred_element_type=jnp.float32
            )
            if c == 0:
                head = result[:, :biased].reshape(head_pair, rows // head_pair, biased) + bias_ref[0]
                head = head.reshape(rows, biased)
                result = join([head, result[:, biased:]]) if width > biased else head
            s_refs[which][c] = result
            most = jnp.maximum(most, lane_fold(result, jnp.maximum))
        most_refs[which][...] = most

    def weigh(which):
        top = join([top_ref[...]] * (width // 128))
        sums = None
        total = None
        for c in range(blocks):
            weights = jnp.exp(s_refs[which][c] - top)
            folded = lane_fold(weights, jnp.add)
            sums = folded if sums is None else sums + folded
            values = kv_ref[1, c * slots : (c + 1) * slots].reshape(width, 256)
            part = jnp.dot(weights.astype(jnp.bfloat16), values, preferred_element_type=jnp.float32)
            total = part if total is None else total + part
        sum_ref[...] = sums
        sum_of_values[...] = total

    def settle(which):
        top_ref[...] = jnp.broadcast_to(
            jnp.max(most_refs[which][...], axis=1, keepdims=True), top_ref.shape
        )

    def both(t, which):
        weigh(which)
        scores(t + 1, 1 - which)

    drive(items, most_refs, begin, settle, finish, lambda: scores(0, 0), both, weigh)


def drive(items, most_refs, begin, settle, finish, only_scores, both, only_weigh):
    def one(t, which):
        begin(t + 1, most_refs[1 - which])
        settle(which)
        both(t, which)
        finish(t)

    def two(i, carry):
        one(2 * i, 0)
        one(2 * i + 1, 1)
        return carry

    begin(0, most_refs[0])
    only_scores()
    pairs = (items - 1) // 2
    lax.fori_loop(0, pairs, two, 0)
    last = 2 * pairs
    if last < items - 1:
        one(last, 0)
        last += 1
    settle(last % 2)
    only_weigh(last % 2)
    finish(last)


def working(rows, steps, step_keys, tables):
    return [
        pltpu.VMEM((2, steps * step_keys // 32, 32, 256), jnp.bfloat16),
        pltpu.VMEM((steps, head_pair * rows, step_keys), jnp.float32),
        pltpu.VMEM((steps, head_pair * rows, step_keys), jnp.float32),
        pltpu.VMEM((head_pair * rows, 128), jnp.float32),
        pltpu.VMEM((head_pair * rows, 128), jnp.float32),
        pltpu.VMEM((head_pair * rows, 128), jnp.float32),
        pltpu.VMEM((head_pair * rows, 128), jnp.float32),
        pltpu.VMEM((head_pair * rows, 256), jnp.float32),
        pltpu.VMEM((tables, rows, block_keys), jnp.float32),
    ]


def state_shapes(items, rows):
    return [
        pltpu.VMEM((items, head_pair * rows, 256), jnp.bfloat16),
        pltpu.VMEM((items, head_pair * rows, 256), jnp.float32),
        pltpu.VMEM((items, head_pair * rows, 128), jnp.float32),
    ]


def state_out(items, rows):
    return (
        pltpu.HBM((items, head_pair * rows, 256), jnp.float32),
        pltpu.HBM((items, head_pair * rows, 128), jnp.float32),
    )


def diagonal_kernel(
    query_ref, cos_in, sin_in, own_ref, key_ref, value_ref, roped_out, acc_out, stat_out,
    key_out_ref, value_out_ref, cos_ref, sin_ref, key_pool, value_pool, q_ref, roped_ref, acc_ref, stat_ref, kv_ref, s_0, s_1, most_0, most_1, top_ref, sum_ref, values_ref,
    bias_ref, query_sem, sem, out_sem, pool_sems, angle_sems,
):
    rows = q_ref.shape[0]
    items = roped_ref.shape[0]
    loads = [
        pltpu.make_async_copy(key_ref, key_pool, pool_sems.at[0]),
        pltpu.make_async_copy(value_ref, value_pool, pool_sems.at[1]),
    ]
    stores = [
        pltpu.make_async_copy(key_pool, key_out_ref, pool_sems.at[0]),
        pltpu.make_async_copy(value_pool, value_out_ref, pool_sems.at[1]),
    ]
    query_copy = pltpu.make_async_copy(query_ref, q_ref, query_sem)
    query_copy.start()
    angle_copies = [
        pltpu.make_async_copy(cos_in, cos_ref, angle_sems.at[0]),
        pltpu.make_async_copy(sin_in, sin_ref, angle_sems.at[1]),
    ]
    for copy in angle_copies:
        copy.start()
    fetch(own_ref, 0, kv_ref, 0, block_slots, sem)
    for copy in loads:
        copy.start()
    row = lax.broadcasted_iota(jnp.int32, (rows, block_keys), 0)
    column = lax.broadcasted_iota(jnp.int32, (rows, block_keys), 1)
    bias_ref[0] = jnp.where(column <= row, 0.0, masked_score)
    query_copy.wait()
    for copy in angle_copies:
        copy.wait()

    def rope(t, carry):
        for one in range(head_pair):
            raw = q_ref[:, pl.ds(pl.multiple_of((t * head_pair + one) * 256, 256), 256)]
            front = turn(raw, cos_ref[...], sin_ref[...])
            some = pl.ds(one * rows, rows)
            roped_ref[t, some, :128] = (front * 0.0625).astype(jnp.bfloat16)
            roped_ref[t, some, 128:] = raw[:, 128:] * jnp.bfloat16(0.0625)
        return carry

    lax.fori_loop(0, items, rope, 0)
    roped_copy = pltpu.make_async_copy(roped_ref, roped_out, query_sem)
    roped_copy.start()
    pltpu.make_async_copy(kv_ref, kv_ref, sem).wait()
    for load, store in zip(loads, stores):
        load.wait()
        store.start()

    def begin(t, most_ref):
        most_ref[...] = jnp.full_like(most_ref, masked_score)

    def finish(t):
        lane = lax.broadcasted_iota(jnp.int32, stat_ref.shape[1:], 1)
        sums = jnp.sum(sum_ref[...], axis=1, keepdims=True)
        stat_ref[t] = jnp.where(lane < 64, top_ref[...], sums)
        acc_ref[t] = values_ref[...]
        pltpu.make_async_copy(acc_ref.at[t], acc_out.at[t], out_sem).start()
        pltpu.make_async_copy(stat_ref.at[t], stat_out.at[t], out_sem).start()

    attention_at_once(
        roped_ref, kv_ref, bias_ref, (s_0, s_1), (most_0, most_1), top_ref, sum_ref, values_ref,
        begin, finish,
    )
    roped_copy.wait()
    for copy in stores:
        copy.wait()
    pltpu.make_async_copy(acc_ref, acc_out, out_sem).wait()
    pltpu.make_async_copy(stat_ref, stat_out, out_sem).wait()


def diagonal_part(queries, cosine, sine, own, key_cache, value_cache):
    rows, width = queries.shape
    items = width // (256 * head_pair)
    return pl.pallas_call(
        diagonal_kernel,
        out_shape=(pltpu.HBM((items, head_pair * rows, 256), jnp.bfloat16),)
        + state_out(items, rows)
        + (pltpu.HBM(key_cache.shape, jnp.bfloat16), pltpu.HBM(value_cache.shape, jnp.bfloat16)),
        in_specs=[hbm_spec] * 6,
        out_specs=(hbm_spec,) * 5,
        scratch_shapes=[
            pltpu.VMEM(cosine.shape, jnp.float32),
            pltpu.VMEM(sine.shape, jnp.float32),
            pltpu.VMEM(key_cache.shape, jnp.bfloat16),
            pltpu.VMEM(value_cache.shape, jnp.bfloat16),
            pltpu.VMEM((rows, width), jnp.bfloat16),
        ]
        + state_shapes(items, rows)
        + working(rows, 1, block_keys, 1)
        + [pltpu.SemaphoreType.DMA] * 3
        + [pltpu.SemaphoreType.DMA((2,))] * 2,
        cost_estimate=light,
        compiler_params=params(large_limit),
        name="attend_diagonal",
    )(*in_hbm(queries, cosine, sine, own, key_cache, value_cache))


def rest_kernel(
    lengths_ref, roped_in, acc_in, stat_in, core_ref, far_ref, far_core_ref,
    old_ref, old_core_ref, old_far_ref, old_far_core_ref, weight_ref, hidden_ref,
    roped_ref, acc_ref, stat_ref, kv_ref, s_0, s_1, most_0, most_1, top_ref, sum_ref, values_ref,
    bias_ref, w_ref, stage_ref, state_sems, sem, weight_sem, out_sems,
):
    group_index = lax.axis_index("group")
    has_old = lengths_ref[lax.axis_index("blk")] > 0
    items = roped_ref.shape[0]
    rows = bias_ref.shape[1]
    chunk = stage_ref.shape[2]
    chunks = w_ref.shape[1] // chunk
    odd = group_index % 2
    chip = group_index // 2
    blocks = jnp.where(has_old, 4, odd + 2 * chip)
    steps = jnp.where(has_old, 2, odd + chip)
    base = jnp.where(has_old, 16, 16 * odd)
    near = (old_ref, old_core_ref)
    far = (old_far_ref, old_far_core_ref)

    def copies(t):
        return [
            pltpu.make_async_copy(source.at[t], target.at[t], state_sems.at[number, t])
            for number, (source, target) in enumerate(
                ((roped_in, roped_ref), (stat_in, stat_ref), (acc_in, acc_ref))
            )
        ]

    for copy in copies(0):
        copy.start()

    @pl.when(odd == 1)
    def _():
        fetch(core_ref, 0, kv_ref, base, 16, sem)

    @pl.when(chip == 1)
    def _():
        place = jnp.where(has_old, 32, 32 * odd)
        fetch(far_ref, 0, kv_ref, place, 16, sem)
        fetch(far_core_ref, 0, kv_ref, place + 16, 16, sem)

    @pl.when(has_old)
    def _():
        for block in range(4):

            @pl.when(block >= group_index)
            def _(block=block):
                gap = jnp.where(block == group_index, 0, odd)
                place = 16 * (gap + block - group_index)
                fetch_pair(near, 4 * block, kv_ref, place, sem)
                fetch_pair(far, 4 * block, kv_ref, place + 8, sem)

    for t in range(1, items):
        for copy in copies(t):
            copy.start()
    weight_copy = pltpu.make_async_copy(weight_ref, w_ref, weight_sem)
    weight_copy.start()

    @pl.when(jnp.logical_not(has_old))
    def _():
        bias_ref[0] = jnp.where(odd == 1, masked_score, 0.0) + jnp.zeros(bias_ref.shape[1:], jnp.float32)
        empty = pl.ds(0, block_slots)

        @pl.when(odd == 1)
        def _():
            kv_ref[:, empty] = jnp.zeros((2, block_slots, 32, 256), jnp.bfloat16)

    @pl.when(has_old)
    def _():
        bias_ref[0, :, :256] = old_bias(rows, group_index)
        bias_ref[0, :, 256:] = old_bias(rows, group_index ^ 2)

    wait_rows(kv_ref, blocks, 4, sem)
    lane = lax.broadcasted_iota(jnp.int32, stat_ref.shape[1:], 1)

    def begin(t, most_ref):
        for copy in copies(t):
            copy.wait()
        most_ref[...] = jnp.where(lane < 64, stat_ref[t], masked_score)

    def finish(t):
        stat = stat_ref[t]
        factor = jnp.exp(stat[:, :1] - top_ref[...])
        sums = stat[:, 64:65] * factor + jnp.sum(sum_ref[...], axis=1, keepdims=True)
        inverse = 1.0 / sums
        old = factor * inverse
        mixed = acc_ref[t] * join([old, old]) + values_ref[...] * join([inverse, inverse])
        roped_ref[t] = mixed.astype(jnp.bfloat16)

    scratch = (roped_ref, kv_ref, bias_ref, (s_0, s_1), (most_0, most_1), top_ref, sum_ref, values_ref)

    attention(steps, 2, 2 * block_keys, *scratch, begin, finish)
    weight_copy.wait()

    def out_copy(n, columns):
        return pltpu.make_async_copy(stage_ref.at[n % 2], hidden_ref.at[:, columns], out_sems.at[n % 2])

    def project(n, carry):
        columns = pl.ds(pl.multiple_of(n * chunk, chunk), chunk)

        @pl.when(n >= 2)
        def _():
            out_copy(n, columns).wait()

        attended = join(
            [
                roped_ref[t, one * rows : (one + 1) * rows, :]
                for t in range(items)
                for one in range(head_pair)
            ]
        )
        stage_ref[n % 2] = jnp.dot(
            attended, w_ref[:, columns], preferred_element_type=jnp.float32
        ).astype(jnp.bfloat16)
        out_copy(n, columns).start()
        return carry

    lax.fori_loop(0, chunks, project, 0)
    for n in range(2):
        out_copy(n, pl.ds(0, chunk)).wait()


def rest_part(lengths, state, slots, weight):
    items, pair_rows, _ = state[0].shape
    rows = pair_rows // head_pair
    width = weight.shape[1]
    chunk = 512
    return pl.pallas_call(
        rest_kernel,
        out_shape=pltpu.HBM((rows, width), jnp.bfloat16),
        in_specs=[smem_spec] + [hbm_spec] * 3 + [any_spec] * 7 + [hbm_spec],
        out_specs=hbm_spec,
        scratch_shapes=state_shapes(items, rows)
        + working(rows, 2, 2 * block_keys, 1)
        + [
            pltpu.VMEM(weight.shape, jnp.bfloat16),
            pltpu.VMEM((2, rows, chunk), jnp.bfloat16),
            pltpu.SemaphoreType.DMA((3, items)),
            pltpu.SemaphoreType.DMA,
            pltpu.SemaphoreType.DMA,
            pltpu.SemaphoreType.DMA((2,)),
        ],
        cost_estimate=light,
        compiler_params=params(large_limit),
        name="attend_rest",
    )(lengths, *in_hbm(*state), *slots, *in_hbm(weight))


def place_kernel(targets_ref, arrived_ref, key_in, value_in, key_ref, value_ref, buffer_ref, load_sem, sem):
    load = pltpu.make_async_copy(arrived_ref, buffer_ref, load_sem)
    load.start()
    load.wait()

    def each(act):
        for slot in range(targets_ref.shape[0]):
            page = targets_ref[slot]

            @pl.when(page >= 0)
            def _(slot=slot, page=page):
                for kind, out_ref in enumerate((key_ref, value_ref)):
                    act(pltpu.make_async_copy(buffer_ref.at[slot, kind], out_ref.at[page], sem))

    each(lambda copy: copy.start())
    each(lambda copy: copy.wait())


def place_new(targets, arrived, key_pool, value_pool):
    return pl.pallas_call(
        place_kernel,
        out_shape=(
            pltpu.HBM(key_pool.shape, jnp.bfloat16),
            pltpu.HBM(value_pool.shape, jnp.bfloat16),
        ),
        in_specs=[smem_spec, any_spec, hbm_spec, hbm_spec],
        out_specs=(hbm_spec,) * 2,
        input_output_aliases={2: 0, 3: 1},
        scratch_shapes=[
            pltpu.VMEM(arrived.shape, jnp.bfloat16),
            pltpu.SemaphoreType.DMA,
            pltpu.SemaphoreType.DMA,
        ],
        cost_estimate=light,
        compiler_params=params(small_limit),
        name="place_new",
    )(targets, arrived, *in_hbm(key_pool, value_pool))


def after(value, *others):
    return lax.optimization_barrier((value,) + others)[0]


def body(queries, new_keys, new_values, key_cache, value_cache, out_weight, lengths, page_table):
    blk_count = lax.axis_size("blk")
    pages = key_cache.shape[0]
    window_pages = page_table.shape[1] // 2
    cap = (window_pages + blk_count - 1) // blk_count

    def other_core(value):
        return lax.ppermute(value, "group", [(0, 1), (1, 0), (2, 3), (3, 2)])

    def other_chip(value):
        return lax.ppermute(value, "group", [(0, 2), (2, 0), (1, 3), (3, 1)])

    picked = pick_old(page_table, cap, key_cache, value_cache)
    old = lax.all_to_all(picked, "blk", split_axis=0, concat_axis=0, tiled=True)
    old = old.reshape((blk_count * cap,) + old.shape[2:])

    fresh, cosine, sine = rotate_keys(lengths, new_keys[0], new_values[0])
    fresh_far = other_chip(fresh)
    fresh_core = other_core(fresh)
    roped, acc, stat, key_out, value_out = diagonal_part(
        after(queries[0], picked), cosine, sine, fresh, key_cache, value_cache
    )

    old = sort_old(after(page_table, stat), blk_count, cap, pages, old)
    old_far = other_chip(old)
    old_core = other_core(old)
    fresh_far_core = other_core(after(fresh_far, old))
    new, targets = pick_new(
        page_table, blk_count, cap, pages, (fresh, fresh_core, fresh_far, fresh_far_core)
    )
    arrived = lax.all_to_all(new, "blk", split_axis=0, concat_axis=0, tiled=True)
    old_far_core = other_core(after(old_far, new))
    hidden = rest_part(
        lengths, (roped, acc, stat),
        (fresh_core, fresh_far, fresh_far_core, old, old_core, old_far, old_far_core),
        out_weight,
    )
    key_out, value_out = place_new(targets, arrived, key_out, value_out)
    return (hidden[None], key_out, value_out)


def solution(mesh):
    return jax.shard_map(
        body,
        mesh=mesh,
        in_specs=(
            P("blk", "group", None),
            P("blk", "group", None),
            P("blk", "group", None),
            P("blk", "group", None),
            P("blk", "group", None),
            P(),
            P(),
            P(),
        ),
        out_specs=(P("blk", "group", None), P("blk", "group", None), P("blk", "group", None)),
        check_vma=False,
    )
```
